32 devices in a mesh: section: 2 (over core), tile: 16 (over z, y, x).
Axes of the slice: x: 2, y: 2, z: 4, core: 2. Of those that a mesh axis runs over, the one named last changes fastest.
Arguments:
- features: bfloat16 [4, 2, 128, 128, 256], P('section', None, 'tile'), may hold values from -6 to 6
- levels: int32 [4, 128], replicated, may hold values from 0 to 15, never falling along the last dimension, each value on 1 to 64 neighbouring positions
- tower_weight: bfloat16 [2, 2, 3, 768, 256], P('section'), may hold values from -0.125 to 0.125
- tower_bias: float32 [2, 2, 256], P('section'), may hold values from -3 to 3
- class_weight: bfloat16 [3, 768, 720], P(None, None, 'section'), may hold values from -0.125 to 0.125
- class_bias: float32 [720], P('section'), may hold values from -3 to 3
- box_weight: bfloat16 [3, 768, 36], P(None, None, 'section'), may hold values from -0.125 to 0.125
- box_bias: float32 [36], P('section'), may hold values from -3 to 3
- class_cotangent: bfloat16 [4, 128, 128, 720], P(None, 'tile', None, 'section'), may hold values from -6 to 6
- box_cotangent: bfloat16 [4, 128, 128, 36], P(None, 'tile', None, 'section'), may hold values from -6 to 6
Outputs:
- class_prob: bfloat16 [4, 128, 128, 720], P(None, 'tile', None, 'section')
- box_pred: bfloat16 [4, 128, 128, 36], P(None, 'tile', None, 'section')
- feature_grad: bfloat16 [4, 2, 128, 128, 256], P('section', None, 'tile')
- tower_weight_grad: float32 [2, 2, 3, 768, 256], P('section')
- tower_bias_grad: float32 [2, 2, 256], P('section')
- class_weight_grad: float32 [3, 768, 720], P(None, None, 'section')
- class_bias_grad: float32 [720], P('section')
- box_weight_grad: float32 [3, 768, 36], P(None, None, 'section')
- box_bias_grad: float32 [36], P('section')
The draws below stay inside these ranges and needn't reach their ends.
Inputs may be any that keep to these rules, and one draw needn't show every extreme that they name: levels[b, r] is the number of the feature map (one FPN level of one image) that row r of micro-batch b belongs to; it never falls along r, and each map spans 1 to 64 rows, one of them exactly that many.
All inputs are finite; a program needn't handle non-finite values.
Results may differ from the reference program's by a relative error of at most 0.0075.
Values may be sent and summed in bfloat16 or wider, within the bound.
No kernel may reach another device: no remote copies, remote signals or barrier semaphores. Data moves between devices by JAX's collectives and lax.ppermute only.
A program may use at most 384 MiB of HBM per device.

```python
import math
import jax
import jax.numpy as jnp
import numpy as np
from jax import lax

C = 256
KCLS = 720
KBOX = 36
WID = 128
MB = 4
LAYERS = 2
ROWS_ALL = 128


def block_scale(own_key, shape, pieces, low, top_value):
    level, own = 1.0, jax.random.fold_in(own_key, 6)
    for dim, shards_of in pieces:
        steps = jnp.exp(jax.random.uniform(jax.random.fold_in(own, dim), (shards_of,), jnp.float32, low / len(pieces), top_value / len(pieces)))
        level = level * jnp.repeat(steps, shape[dim] // shards_of).reshape([-1 if axis == dim else 1 for axis in range(len(shape))])
    return level


def length_profile(number_of, total, limit, lean):
    weights = [(1 << 20) // math.isqrt(rank ** lean) + 1 for rank in range(2, number_of + 1)]
    surplus, given = total - limit - (number_of - 1), [1] * (number_of - 1)
    while surplus > 0:
        movable = [i for i in range(number_of - 1) if given[i] < limit]
        pool, remaining = sum([weights[i] for i in movable]), surplus
        for i in movable:
            more = min(limit - given[i], max(1, remaining * weights[i] // pool), surplus)
            given[i] = given[i] + more
            surplus = surplus - more
    return np.array([limit] + given)


def ragged_sizes(rng, number_of, total, reach, slope):
    if number_of == 2:
        one = jax.random.randint(rng, (), max(1, total - reach), min(reach, total - 1) + 1)
        return jnp.stack([one, total - one])
    lengths = jnp.asarray(length_profile(number_of, total, reach, slope), jnp.int32)
    couples = (number_of - 1) // 2
    giver, sink = lengths[1:1 + 2 * couples:2], lengths[2:2 + 2 * couples:2]
    slack = jnp.minimum(giver - 1, reach - sink)
    shifted = jax.random.randint(jax.random.fold_in(rng, 1), (couples,), 0, 1 << 20) % (slack + 1)
    lengths = lengths.at[1:1 + 2 * couples:2].set(giver - shifted).at[2:2 + 2 * couples:2].set(sink + shifted)
    return lengths[jax.random.permutation(jax.random.fold_in(rng, 2), number_of)]


def normal_values(stream_key, dims, deviation, limit, split=(), kind=jnp.bfloat16):
    loudness = block_scale(stream_key, dims, split, -0.22, 0.18) if split else 1.0
    values = jax.random.normal(stream_key, dims, jnp.float32) * deviation * loudness
    return jnp.minimum(jnp.maximum(values, -limit), limit).astype(kind)


def setup_inputs(seed: int = 0) -> dict:
    key_of = jax.random.split(jax.random.key(seed), 11)
    features = normal_values(key_of[0], (MB, 2, ROWS_ALL, WID, C), 1.0, 6.0, ((0, 2), (2, 16)))
    levels = jax.vmap(lambda own: jnp.searchsorted(jnp.cumsum(ragged_sizes(own, max(ROWS_ALL // 8, 3), ROWS_ALL, ROWS_ALL // 2, 0)), jnp.arange(ROWS_ALL), side="right"))(jax.random.split(key_of[1], MB)).reshape((MB, ROWS_ALL)).astype(jnp.int32)
    tower_weight = normal_values(key_of[2], (LAYERS, 2, 3, 3 * C, C), (9 * C) ** -0.5, 0.125, ((0, 2),))
    tower_bias = normal_values(key_of[3], (LAYERS, 2, C), 0.5, 3.0, ((0, 2),), jnp.float32)
    class_weight = normal_values(key_of[4], (3, 3 * C, KCLS), (9 * C) ** -0.5, 0.125, ((2, 2),))
    class_bias = normal_values(key_of[5], (KCLS,), 0.5, 3.0, ((0, 2),), jnp.float32)
    box_weight = normal_values(key_of[6], (3, 3 * C, KBOX), (9 * C) ** -0.5, 0.125, ((2, 2),))
    box_bias = normal_values(key_of[7], (KBOX,), 0.5, 3.0, ((0, 2),), jnp.float32)
    class_cotangent = normal_values(key_of[8], (MB, ROWS_ALL, WID, KCLS), 1.0, 6.0, ((1, 16), (3, 2)))
    box_cotangent = normal_values(key_of[9], (MB, ROWS_ALL, WID, KBOX), 1.0, 6.0, ((1, 16), (3, 2)))
    return {"features": features, "levels": levels, "tower_weight": tower_weight, "tower_bias": tower_bias, "class_weight": class_weight, "class_bias": class_bias, "box_weight": box_weight, "box_bias": box_bias, "class_cotangent": class_cotangent, "box_cotangent": box_cotangent}


@jax.custom_vjp
def low(v):
    return lax.optimization_barrier(v.astype(jnp.bfloat16)).astype(jnp.float32)

@jax.custom_vjp
def low_back(v):
    return v

def low_keep(v):
    return (low(v), None)

def low_pass(kept, grad):
    return (grad,)

def back_keep(v):
    return (v, None)

def back_low(kept, grad):
    return (low(grad),)
low.defvjp(low_keep, low_pass)
low_back.defvjp(back_keep, back_low)

def shift_cols(value, offset):
    width = value.shape[-2]
    zeros = jnp.zeros(value.shape[:-2] + (abs(offset),) + value.shape[-1:], value.dtype)
    if offset > 0:
        return jnp.concatenate([value[..., offset:, :], zeros], axis=-2)
    if offset < 0:
        return jnp.concatenate([zeros, value[..., :width + offset, :]], axis=-2)
    return value

def conv_ref(source, line, weight, form):
    rows = source.shape[-3]
    config = [(0, 0)] * (source.ndim - 3) + [(1, 1), (0, 0), (0, 0)]
    padded = jnp.pad(source, config)
    line_pad = jnp.pad(line, (1, 1), constant_values=-1)
    total = jnp.float32(0.0)
    for k in range(3):
        keep_rows = (line_pad[k:k + rows] == line).astype(jnp.float32)
        part = padded[..., k:k + rows, :, :] * keep_rows[:, None, None]
        patches = jnp.concatenate([shift_cols(part, -1), part, shift_cols(part, 1)], axis=-1)
        total = total + jnp.einsum(form, patches, weight[..., k, :, :], precision=lax.Precision.HIGHEST)
    return total

def one_batch(params, line, batch_features):
    tower_weight, tower_bias, class_weight, class_bias, box_weight, box_bias = params
    hidden = batch_features
    for layer in range(LAYERS):
        before = conv_ref(hidden, line, tower_weight[layer], 'trwi,tio->trwo') + tower_bias[layer][:, None, None, :]
        before = low_back(before)
        hidden = low(before * jax.nn.sigmoid(before))
        if layer < LAYERS - 1:
            hidden = low_back(hidden)
    logit = conv_ref(hidden[0], line, class_weight, 'rwi,io->rwo') + class_bias
    logit = low_back(logit)
    boxes = conv_ref(hidden[1], line, box_weight, 'rwi,io->rwo') + box_bias
    return (jax.nn.sigmoid(logit), boxes)

def reference(features, levels, tower_weight, tower_bias, class_weight, class_bias, box_weight, box_bias, class_cotangent, box_cotangent):

    def forward(feats, params):

        def step(pair):
            return jax.checkpoint(one_batch)(params, pair[0], pair[1])
        return lax.map(step, (levels, feats))
    params = (tower_weight.astype(jnp.float32), tower_bias.astype(jnp.float32), class_weight.astype(jnp.float32), class_bias.astype(jnp.float32), box_weight.astype(jnp.float32), box_bias.astype(jnp.float32))
    outputs, pullback = jax.vjp(forward, features.astype(jnp.float32), params)
    feature_grad, grads = pullback((class_cotangent.astype(jnp.float32), box_cotangent.astype(jnp.float32)))
    class_prob, box_pred = outputs
    return (class_prob.astype(jnp.bfloat16), box_pred.astype(jnp.bfloat16), feature_grad.astype(jnp.bfloat16), grads[0], grads[1], grads[2], grads[3], grads[4], grads[5])
```

```python
import functools

import jax
import jax.numpy as jnp
from jax import lax
from jax.experimental import pallas as pl
from jax.experimental.pallas import tpu as pltpu
from jax.sharding import PartitionSpec as P

BF = jnp.bfloat16
F32 = jnp.float32
LANES = 128
HALF = 64
SMEM = pl.BlockSpec(memory_space=pltpu.SMEM)
ANY = pl.BlockSpec(memory_space=pl.ANY)


def dot(a, b):
    return jnp.dot(a, b, preferred_element_type=F32)


def dot_nt(a, b):
    return lax.dot_general(a, b, (((1,), (1,)), ((), ())), preferred_element_type=F32)


def dot_tn(a, b):
    return lax.dot_general(a, b, (((0,), (0,)), ((), ())), preferred_element_type=F32)


def down(v):
    return jnp.concatenate([jnp.zeros_like(v[..., :1, :]), v[..., :-1, :]], axis=-2)


def up(v):
    return jnp.concatenate([v[..., 1:, :], jnp.zeros_like(v[..., :1, :])], axis=-2)


def keep_if(v, flag):
    return v * jnp.full((1, v.shape[-1]), flag, F32).astype(v.dtype)


def build(x, rows, e, b, before=None, after=None, taps=True):
    count = len(rows)
    width = rows[0]().shape[0]
    for q in range(-1, count + 1):
        if q < 0:
            get = before
        elif q < count:
            get = rows[q]
        else:
            get = after
        if get is None:
            dest = 0 if q < 0 else count - 1
            part = x.shape[1] // 3
            first = 0 if q < 0 else 2 * part
            x[dest * width : (dest + 1) * width, first : first + part] = jnp.zeros((width, part), x.dtype)
            continue
        v = get()
        p = jnp.concatenate([down(v), v, up(v)], axis=1) if taps else v
        n = p.shape[1]
        if 0 <= q < count:
            x[q * width : (q + 1) * width, n : 2 * n] = p
        if q + 1 < count:
            x[(q + 1) * width : (q + 2) * width, 0:n] = keep_if(p, e[b, q + 1])
        if q >= 1:
            x[(q - 1) * width : q * width, 2 * n : 3 * n] = keep_if(p, e[b, q])


def rows_of(ref, lead, count):
    return [functools.partial(lambda r: ref[lead + (r,)], r) for r in range(count)]


def pick_halo(info, rx, rd, hs, lead):
    @pl.when(info[1] == 0)
    def _():
        hs[0] = rd[lead]
        hs[1] = rx[lead]

    @pl.when(info[1] != 0)
    def _():
        hs[0] = rx[lead]
        hs[1] = rd[lead]


def put_edges(info, first, last, sx, sd, lead):
    @pl.when(info[1] == 0)
    def _():
        sx[lead] = last
        sd[lead] = first

    @pl.when(info[1] != 0)
    def _():
        sx[lead] = first
        sd[lead] = last


def start_weights(info, layer, own, other, wv, sem):
    for t in range(wv.shape[0]):

        @pl.when(info[0] == layer)
        def _():
            pltpu.make_async_copy(own.at[t], wv.at[t], sem.at[t]).start()

        @pl.when(info[0] != layer)
        def _():
            pltpu.make_async_copy(other.at[t], wv.at[t], sem.at[t]).start()


def wait_weights(own, wv, sem, t):
    for i in range(wv.shape[0]):

        @pl.when(t == i)
        def _():
            pltpu.make_async_copy(own.at[i], wv.at[i], sem.at[i]).wait()


def forward_kernel(layer, info, e, h, rx, rd, own, other, bias, hn, sp, sx, sd, x, wv, hs, sem):
    t, b = pl.program_id(0), pl.program_id(1)
    rows, width = h.shape[2], h.shape[3]

    @pl.when(jnp.logical_and(t == 0, b == 0))
    def _():
        start_weights(info, layer, own, other, wv, sem)

    pick_halo(info, rx, rd, hs, (0, 0))
    build(x, rows_of(h, (0, 0), rows), e, b, lambda: hs[0], lambda: hs[1])

    @pl.when(b == 0)
    def _():
        wait_weights(own, wv, sem, t)

    z = dot(x[...], wv[t]) + bias[0]
    sg = jax.nn.sigmoid(z)
    hv = (z * sg).astype(BF).reshape(rows, width, z.shape[1])
    hn[0, 0] = hv
    sp[0, 0] = (sg * (1.0 + z * (1.0 - sg))).astype(BF).reshape(hv.shape)
    put_edges(info, hv[0], hv[rows - 1], sx, sd, (0, 0))


def forward(layer, info, e, h, rx, rd, own, other, bias):
    nb, nt, rows, width, c = h.shape
    shape = h.shape
    row_spec = pl.BlockSpec((1, 1, rows, width, c), lambda t, b: (b, t, 0, 0, 0))
    edge_spec = pl.BlockSpec((1, 1, width, c), lambda t, b: (b, t, 0, 0))
    taps = own.shape[1]
    return pl.pallas_call(
        functools.partial(forward_kernel, layer),
        grid=(nt, nb),
        in_specs=[SMEM, SMEM, row_spec, edge_spec, edge_spec, ANY, ANY, pl.BlockSpec((1, 1, c), lambda t, b: (t, 0, 0))],
        out_specs=[row_spec, row_spec, edge_spec, edge_spec],
        out_shape=[jax.ShapeDtypeStruct(shape, BF)] * 2 + [jax.ShapeDtypeStruct((nb, nt, width, c), BF)] * 2,
        scratch_shapes=[
            pltpu.VMEM((rows * width, taps), BF),
            pltpu.VMEM((nt, taps, c), BF),
            pltpu.VMEM((2, width, c), BF),
            pltpu.SemaphoreType.DMA((nt,)),
        ],
        compiler_params=pltpu.CompilerParams(vmem_limit_bytes=40 << 20),
        cost_estimate=pl.CostEstimate(flops=2 * nb * nt * rows * width * taps * c, bytes_accessed=20 << 20, transcendentals=0),
        name=f"forward{layer}",
    )(info, e, h, rx, rd, own, other, bias)


def box_taps(g):
    v = g.astype(F32)
    axis = v.ndim - 1
    return (up(v) + pltpu.roll(v, 18, axis) + pltpu.roll(down(v), 36, axis)).astype(BF)


def head_kernel(
    info, e, h, rx, rd, wc, wb, cb, bb, cot, cot_r, gb, prob, psend, boxo, dl, cx, cd, x, xb, lg, hs, de, ge
):
    b, nb = pl.program_id(0), pl.num_programs(0)
    rows, width, c = h.shape[2], h.shape[3], h.shape[4]
    kc = cot.shape[-1]
    kp = wc.shape[1] // 2
    kb = boxo.shape[-1]
    pick_halo(info, rx, rd, hs, (0, 0))
    build(x, rows_of(h, (0, 0), rows), e, b, lambda: hs[0], lambda: hs[1])
    lg[...] = dot(x[...], wc[...])
    pick_halo(info, rx, rd, hs, (0, 1))
    build(xb, rows_of(h, (0, 1), rows), e, b, lambda: hs[0], lambda: hs[1], taps=False)
    s = dot(xb[...], wb[...]).reshape(rows, width, LANES)
    box = down(s) + pltpu.roll(s, LANES - kb, 2) + pltpu.roll(up(s), LANES - 2 * kb, 2) + bb[...]
    boxo[0] = box[:, :, :kb].astype(BF)
    lane = lax.broadcasted_iota(jnp.int32, (width, kp), 1)
    shift = (kc - HALF) % LANES
    for r in range(rows):
        logit = lg[r * width : (r + 1) * width, :] + cb[...]
        p = jax.nn.sigmoid(logit)
        q = p * (1.0 - p)
        prob[0, r] = p[:, :kc].astype(BF)
        own = jnp.concatenate([cot[0, r].astype(F32), jnp.zeros((width, kp - kc), F32)], axis=1)
        d0 = own * q[:, :kp]
        d1 = jnp.where(lane < kc, cot_r[0, r].astype(F32) * q[:, kp:], 0.0)
        d = jnp.concatenate([d0, d1], axis=1).astype(BF)
        dl[0, r] = d
        other = p[:, kp:]
        moved = pltpu.roll(box[r], shift, 1)
        wide = jnp.concatenate([moved] * (kp // LANES), axis=1)
        psend[0, r] = jnp.where(lane < kc, other, wide).astype(BF)
        if r == 0 or r == rows - 1:
            i = 0 if r == 0 else 1
            de[i, pl.ds(b * width, width), :] = d
            ge[i, pl.ds(b * width, width), :] = box_taps(gb[0, r])

    @pl.when(b == nb - 1)
    def _():
        n = cx.shape[0]
        taps = 3 * c
        for i in range(2):
            k = 2 * i
            s = dot_nt(de[i], wc[k * taps : (k + 1) * taps, :]).reshape(n, width, taps)
            dc = up(s[:, :, :c]) + s[:, :, c : 2 * c] + down(s[:, :, 2 * c :])
            db = dot_nt(ge[i], wb[k * c : (k + 1) * c, :]).reshape(n, width, c)
            edge = e.shape[1] - 1 if i else 0
            for bi in range(n):
                dcb = keep_if(dc[bi].astype(BF), e[bi, edge])
                dbb = keep_if(db[bi].astype(BF), e[bi, edge])

                @pl.when((info[1] == 0) == (i == 1))
                def _():
                    cx[bi, 0] = dcb
                    cx[bi, 1] = dbb

                @pl.when((info[1] == 0) == (i == 0))
                def _():
                    cd[bi, 0] = dcb
                    cd[bi, 1] = dbb


def head(info, e, h, rx, rd, wc, wb, cb, bb, cot, cot_r, gb):
    nb, nt, rows, width, c = h.shape
    kc, kp, kb = cot.shape[-1], wc.shape[1] // 2, 18
    taps = wc.shape[0]
    m = rows * width

    def at_b(shape):
        return pl.BlockSpec((1,) + shape, lambda b, info: (b,) + (0,) * len(shape))

    def whole(shape):
        return pl.BlockSpec(shape, lambda b, info: (0,) * len(shape))

    return pl.pallas_call(
        head_kernel,
        grid_spec=pltpu.PrefetchScalarGridSpec(
            num_scalar_prefetch=1,
            grid=(nb,),
            in_specs=[
                SMEM,
                at_b((nt, rows, width, c)),
                at_b((nt, width, c)),
                at_b((nt, width, c)),
                whole(wc.shape),
                whole(wb.shape),
                whole(cb.shape),
                whole(bb.shape),
                pl.BlockSpec((1, rows, width, kc), lambda b, info: (info[0] * nb + b, 0, 0, 0)),
                at_b((rows, width, kp)),
                at_b((rows, width, LANES)),
            ],
            out_specs=[
                at_b((rows, width, kc)),
                at_b((rows, width, kp)),
                at_b((rows, width, kb)),
                at_b((rows, width, 2 * kp)),
                whole((nb, nt, width, c)),
                whole((nb, nt, width, c)),
            ],
            scratch_shapes=[
                pltpu.VMEM((m, taps), BF),
                pltpu.VMEM((m, 3 * c), BF),
                pltpu.VMEM((m, 2 * kp), F32),
                pltpu.VMEM((2, width, c), BF),
                pltpu.VMEM((2, nb * width, 2 * kp), BF),
                pltpu.VMEM((2, nb * width, LANES), BF),
            ],
        ),
        out_shape=[
            jax.ShapeDtypeStruct((nb, rows, width, kc), BF),
            jax.ShapeDtypeStruct((nb, rows, width, kp), BF),
            jax.ShapeDtypeStruct((nb, rows, width, kb), BF),
            jax.ShapeDtypeStruct((nb, rows, width, 2 * kp), BF),
            jax.ShapeDtypeStruct((nb, nt, width, c), BF),
            jax.ShapeDtypeStruct((nb, nt, width, c), BF),
        ],
        compiler_params=pltpu.CompilerParams(vmem_limit_bytes=60 << 20),
        cost_estimate=pl.CostEstimate(flops=2 * nb * m * taps * 2 * kp, bytes_accessed=20 << 20, transcendentals=0),
        name="head",
    )(info, e, h, rx, rd, wc, wb, cb, bb, cot, cot_r, gb)


def head_weights_kernel(info, e, h, rx, rd, dl, gb, own, other, cbg, wbg, bbg, x, xb, acc, hs):
    b, nb = pl.program_id(0), pl.num_programs(0)
    rows, width, c = h.shape[2], h.shape[3], h.shape[4]
    kp = own.shape[1]

    @pl.when(b == 0)
    def _():
        acc[...] = jnp.zeros_like(acc)
        cbg[...] = jnp.zeros_like(cbg)
        wbg[...] = jnp.zeros_like(wbg)
        bbg[...] = jnp.zeros_like(bbg)

    pick_halo(info, rx, rd, hs, (0, 0))
    build(x, rows_of(h, (0, 0), rows), e, b, lambda: hs[0], lambda: hs[1])
    g = dl[0].reshape(rows * width, 2 * kp)
    acc[...] += dot_tn(x[...], g)
    cbg[...] += jnp.sum(g.astype(F32), axis=0, keepdims=True)
    pick_halo(info, rx, rd, hs, (0, 1))
    build(xb, rows_of(h, (0, 1), rows), e, b, lambda: hs[0], lambda: hs[1], taps=False)
    wbg[...] += dot_tn(xb[...], box_taps(gb[0]).reshape(rows * width, LANES))
    bbg[...] += jnp.sum(gb[0].reshape(rows * width, LANES).astype(F32), axis=0, keepdims=True)

    @pl.when(b == nb - 1)
    def _():
        own[...] = acc[:, :kp]
        other[...] = acc[:, kp:].astype(BF)


def head_weights(info, e, h, rx, rd, dl, gb):
    nb, nt, rows, width, c = h.shape
    kp = dl.shape[-1] // 2
    taps = 9 * c
    m = rows * width

    def at_b(shape):
        return pl.BlockSpec((1,) + shape, lambda b: (b,) + (0,) * len(shape))

    def whole(shape):
        return pl.BlockSpec(shape, lambda b: (0,) * len(shape))

    return pl.pallas_call(
        head_weights_kernel,
        grid=(nb,),
        in_specs=[
            SMEM,
            SMEM,
            at_b((nt, rows, width, c)),
            at_b((nt, width, c)),
            at_b((nt, width, c)),
            at_b((rows, width, 2 * kp)),
            at_b((rows, width, LANES)),
        ],
        out_specs=[whole((taps, kp)), whole((taps, kp)), whole((1, 2 * kp)), whole((3 * c, LANES)), whole((1, LANES))],
        out_shape=[
            jax.ShapeDtypeStruct((taps, kp), F32),
            jax.ShapeDtypeStruct((taps, kp), BF),
            jax.ShapeDtypeStruct((1, 2 * kp), F32),
            jax.ShapeDtypeStruct((3 * c, LANES), F32),
            jax.ShapeDtypeStruct((1, LANES), F32),
        ],
        scratch_shapes=[
            pltpu.VMEM((m, taps), BF),
            pltpu.VMEM((m, 3 * c), BF),
            pltpu.VMEM((taps, 2 * kp), F32),
            pltpu.VMEM((2, width, c), BF),
        ],
        compiler_params=pltpu.CompilerParams(vmem_limit_bytes=60 << 20),
        cost_estimate=pl.CostEstimate(flops=2 * nb * m * taps * 2 * kp, bytes_accessed=20 << 20, transcendentals=0),
        name="head_weights",
    )(info, e, h, rx, rd, dl, gb)


def head_inputs_kernel(info, e, dl, gb, rx, rd, wc, wb, sp, dz, sx, sd, x, xb, hs):
    b = pl.program_id(0)
    rows, width, c = sp.shape[2], sp.shape[3], sp.shape[4]
    kp2 = dl.shape[-1]
    taps = 3 * c
    build(x, rows_of(dl, (0,), rows), e, b, taps=False)
    s = dot_nt(x[:, kp2 : 2 * kp2], wc[taps : 2 * taps, :])
    s = s + dot_nt(x[:, :kp2], wc[2 * taps :, :])
    s = s + dot_nt(x[:, 2 * kp2 :], wc[:taps, :])
    s = s.reshape(rows, width, taps)
    dc = up(s[:, :, :c]) + s[:, :, c : 2 * c] + down(s[:, :, 2 * c :])
    g3 = box_taps(gb[0])
    build(xb, [functools.partial(lambda r: g3[r], r) for r in range(rows)], e, b, taps=False)
    db = dot_nt(xb[:, LANES : 2 * LANES], wb[c : 2 * c, :])
    db = db + dot_nt(xb[:, :LANES], wb[2 * c :, :])
    db = db + dot_nt(xb[:, 2 * LANES :], wb[:c, :])
    for t, dh in ((0, dc), (1, db.reshape(rows, width, c))):
        pick_halo(info, rx, rd, hs, (0, t))
        for r in range(rows):
            v = dh[r]
            if r == 0:
                v = v + hs[0].astype(F32)
            if r == rows - 1:
                v = v + hs[1].astype(F32)
            dz[0, t, r] = (v * sp[0, t, r].astype(F32)).astype(BF)
        put_edges(info, dz[0, t, 0], dz[0, t, rows - 1], sx, sd, (0, t))


def head_inputs(info, e, dl, gb, rx, rd, wc, wb, sp):
    nb, nt, rows, width, c = sp.shape
    kp2 = dl.shape[-1]
    m = rows * width

    def at_b(shape):
        return pl.BlockSpec((1,) + shape, lambda b: (b,) + (0,) * len(shape))

    def whole(shape):
        return pl.BlockSpec(shape, lambda b: (0,) * len(shape))

    return pl.pallas_call(
        head_inputs_kernel,
        grid=(nb,),
        in_specs=[
            SMEM,
            SMEM,
            at_b((rows, width, kp2)),
            at_b((rows, width, LANES)),
            at_b((nt, width, c)),
            at_b((nt, width, c)),
            whole(wc.shape),
            whole(wb.shape),
            at_b((nt, rows, width, c)),
        ],
        out_specs=[at_b((nt, rows, width, c)), at_b((nt, width, c)), at_b((nt, width, c))],
        out_shape=[
            jax.ShapeDtypeStruct(sp.shape, BF),
            jax.ShapeDtypeStruct((nb, nt, width, c), BF),
            jax.ShapeDtypeStruct((nb, nt, width, c), BF),
        ],
        scratch_shapes=[
            pltpu.VMEM((m, 3 * kp2), BF),
            pltpu.VMEM((m, 3 * LANES), BF),
            pltpu.VMEM((2, width, c), BF),
        ],
        compiler_params=pltpu.CompilerParams(vmem_limit_bytes=60 << 20),
        cost_estimate=pl.CostEstimate(flops=2 * nb * m * 9 * c * kp2, bytes_accessed=20 << 20, transcendentals=0),
        name="head_inputs",
    )(info, e, dl, gb, rx, rd, wc, wb, sp)


def weights_kernel(info, e, h, rx, rd, dz, keep, send, bias, x, acc, hs):
    t, b, nb = pl.program_id(0), pl.program_id(1), pl.num_programs(1)
    rows, width, c = h.shape[2], h.shape[3], h.shape[4]
    pick_halo(info, rx, rd, hs, (0, 0))
    build(x, rows_of(h, (0, 0), rows), e, b, lambda: hs[0], lambda: hs[1])
    g = dz[0, 0].reshape(rows * width, c)
    part = dot_tn(x[...], g)
    total = jnp.sum(g.astype(F32), axis=0, keepdims=True)

    @pl.when(b == 0)
    def _():
        acc[...] = part
        bias[0] = total

    @pl.when(b != 0)
    def _():
        acc[...] += part
        bias[0] += total

    @pl.when(jnp.logical_and(b == nb - 1, t == info[0]))
    def _():
        keep[...] = acc[...]

    @pl.when(jnp.logical_and(b == nb - 1, t != info[0]))
    def _():
        send[...] = acc[...].astype(BF)


def weights(layer, info, e, h, rx, rd, dz):
    nb, nt, rows, width, c = h.shape
    row_spec = pl.BlockSpec((1, 1, rows, width, c), lambda t, b: (b, t, 0, 0, 0))
    edge_spec = pl.BlockSpec((1, 1, width, c), lambda t, b: (b, t, 0, 0))
    taps = 9 * c
    return pl.pallas_call(
        weights_kernel,
        grid=(nt, nb),
        in_specs=[SMEM, SMEM, row_spec, edge_spec, edge_spec, row_spec],
        out_specs=[
            pl.BlockSpec((taps, c), lambda t, b: (0, 0)),
            pl.BlockSpec((taps, c), lambda t, b: (0, 0)),
            pl.BlockSpec((1, 1, c), lambda t, b: (t, 0, 0)),
        ],
        out_shape=[
            jax.ShapeDtypeStruct((taps, c), F32),
            jax.ShapeDtypeStruct((taps, c), BF),
            jax.ShapeDtypeStruct((nt, 1, c), F32),
        ],
        scratch_shapes=[
            pltpu.VMEM((rows * width, taps), BF),
            pltpu.VMEM((taps, c), F32),
            pltpu.VMEM((2, width, c), BF),
        ],
        compiler_params=pltpu.CompilerParams(vmem_limit_bytes=40 << 20),
        cost_estimate=pl.CostEstimate(flops=2 * nb * nt * rows * width * taps * c, bytes_accessed=20 << 20, transcendentals=0),
        name=f"weights{layer}",
    )(info, e, h, rx, rd, dz)


def inputs_kernel(layer, info, e, dz, rx, rd, own, other, *rest):
    if layer:
        sp, out, sx, sd, x, wv, wt, hs, sem = rest
    else:
        out, x, wv, wt, hs, sem = rest
    t, b = pl.program_id(0), pl.program_id(1)
    rows, width, c = dz.shape[2], dz.shape[3], dz.shape[4]

    @pl.when(jnp.logical_and(t == 0, b == 0))
    def _():
        start_weights(info, layer, own, other, wv, sem)

    pick_halo(info, rx, rd, hs, (0, 0))
    build(x, rows_of(dz, (0, 0), rows), e, b, lambda: hs[0], lambda: hs[1])

    @pl.when(b == 0)
    def _():
        wait_weights(own, wv, sem, t)
        for i in range(9):
            wt[:, (8 - i) * c : (9 - i) * c] = wv[t, i * c : (i + 1) * c, :]

    dh = dot_nt(x[...], wt[...]).astype(BF)
    if not layer:
        out[0, 0] = dh.reshape(rows, width, c)
        return
    dz_next = (dh.astype(F32).reshape(rows, width, c) * sp[0, 0].astype(F32)).astype(BF)
    out[0, 0] = dz_next
    put_edges(info, dz_next[0], dz_next[rows - 1], sx, sd, (0, 0))


def inputs(layer, info, e, dz, rx, rd, own, other, sp=None):
    nb, nt, rows, width, c = dz.shape
    row_spec = pl.BlockSpec((1, 1, rows, width, c), lambda t, b: (b, t, 0, 0, 0))
    edge_spec = pl.BlockSpec((1, 1, width, c), lambda t, b: (b, t, 0, 0))
    edge = jax.ShapeDtypeStruct((nb, nt, width, c), BF)
    taps = own.shape[1]
    return pl.pallas_call(
        functools.partial(inputs_kernel, layer),
        grid=(nt, nb),
        in_specs=[SMEM, SMEM, row_spec, edge_spec, edge_spec, ANY, ANY] + ([row_spec] if layer else []),
        out_specs=[row_spec] + ([edge_spec, edge_spec] if layer else []),
        out_shape=[jax.ShapeDtypeStruct(dz.shape, BF)] + ([edge, edge] if layer else []),
        scratch_shapes=[
            pltpu.VMEM((rows * width, taps), BF),
            pltpu.VMEM((nt, taps, c), BF),
            pltpu.VMEM((c, taps), BF),
            pltpu.VMEM((2, width, c), BF),
            pltpu.SemaphoreType.DMA((nt,)),
        ],
        compiler_params=pltpu.CompilerParams(vmem_limit_bytes=40 << 20),
        cost_estimate=pl.CostEstimate(flops=2 * nb * nt * rows * width * taps * c, bytes_accessed=20 << 20, transcendentals=0),
        name=f"inputs{layer}",
    )(info, e, dz, rx, rd, own, other, *([sp] if layer else []))


def swap_section(value):
    return lax.ppermute(value, "section", [(0, 1), (1, 0)])


def swap_edges(sx, sd):
    count = lax.axis_size("tile")
    even = [p for i in range(0, count - 1, 2) for p in ((i, i + 1), (i + 1, i))]
    odd = [p for i in range(1, count - 1, 2) for p in ((i, i + 1), (i + 1, i))]
    return lax.ppermute(sx, "tile", even), lax.ppermute(sd, "tile", odd)


def sum_tiles(pieces):
    count = lax.axis_size("tile")
    index = lax.axis_index("tile")
    bits = count.bit_length() - 1

    def exchange(value, bit):
        return lax.ppermute(value, "tile", [(i, i ^ (1 << bit)) for i in range(count)])

    done = []
    for order, total in pieces:
        for bit in order(bits):
            mine = (index >> bit) & 1
            both = total.reshape((2, total.shape[0] // 2) + total.shape[1:])
            sent = exchange(lax.dynamic_index_in_dim(both, 1 - mine, 0, False).astype(BF), bit)
            total = lax.dynamic_index_in_dim(both, mine, 0, False) + sent.astype(F32)
        part = total.astype(BF)
        for bit in reversed(order(bits)):
            mine = (index >> bit) & 1
            got = exchange(part, bit)
            part = jnp.where(mine == 0, jnp.concatenate([part, got]), jnp.concatenate([got, part]))
        done.append(part)
    return done


def x_first(bits):
    return list(range(bits))


def y_first(bits):
    return [1, 0] + list(range(2, bits)) if bits > 1 else list(range(bits))


def halves(total):
    n = total.shape[0] // 2
    return [(x_first, total[:n]), (y_first, total[n:])]


def on_device(
    features,
    levels,
    tower_weight,
    tower_bias,
    class_weight,
    class_bias,
    box_weight,
    box_bias,
    class_cotangent,
    box_cotangent,
):
    section = lax.axis_index("section")
    tile = lax.axis_index("tile")
    nb, nt, rows, width, c = features.shape
    kc, kb = class_weight.shape[-1], box_weight.shape[-1]
    kp = -(-kc // LANES) * LANES
    taps = 9 * c

    lines = lax.dynamic_slice_in_dim(levels, section * nb, nb, 0)
    lines = jnp.pad(lines, ((0, 0), (1, 1)), constant_values=-1)
    lines = lax.dynamic_slice_in_dim(lines, tile * rows, rows + 2, 1)
    e = (lines[:, 1:] == lines[:, :-1]).astype(F32)
    info = jnp.stack([section, tile % 2]).astype(jnp.int32)
    even = tile % 2 == 0

    first, last = features[:, :, 0], features[:, :, rows - 1]
    rx0, rd0 = swap_edges(jnp.where(even, last, first), jnp.where(even, first, last))
    w_own = tower_weight.reshape(nt, taps, c)
    w_other = swap_section(w_own)
    bias_own = jnp.concatenate([tower_bias.reshape(-1), class_bias, box_bias])
    bias_other = swap_section(bias_own)
    tb_own, tb_other = bias_own[: nt * c].reshape(nt, 1, c), bias_other[: nt * c].reshape(nt, 1, c)
    tb0 = jnp.where(section == 0, tb_own, tb_other)
    tb1 = jnp.where(section == 0, tb_other, tb_own)
    cb = jnp.concatenate([jnp.pad(v[nt * c : nt * c + kc], (0, kp - kc)) for v in (bias_own, bias_other)])[None]
    bb = jnp.concatenate([jnp.pad(v[nt * c + kc :], (0, HALF - kb)) for v in (bias_own, bias_other)])[None]

    theirs = (1 - section) * nb
    mine = section * nb
    cot_send = jnp.concatenate(
        [
            lax.dynamic_slice_in_dim(class_cotangent, theirs, nb, 0),
            lax.dynamic_slice_in_dim(box_cotangent, theirs, nb, 0),
            jnp.zeros((nb, rows, width, kp - kc - kb), BF),
        ],
        axis=-1,
    )
    cot_r = swap_section(cot_send)
    gap = jnp.zeros((nb, rows, width, HALF - kb), BF)
    gb = jnp.concatenate(
        [lax.dynamic_slice_in_dim(box_cotangent, mine, nb, 0), gap, cot_r[..., kc : kc + kb], gap], axis=-1
    )

    wide = jnp.pad(class_weight.reshape(taps, kc), ((0, 0), (0, kp - kc)))
    wc = jnp.concatenate([wide, swap_section(wide)], axis=1)
    small = box_weight.reshape(3, 3, c, kb).transpose(0, 2, 1, 3).reshape(3 * c, 3 * kb)
    small = jnp.pad(small, ((0, 0), (0, HALF - 3 * kb)))
    wb = jnp.concatenate([small, swap_section(small)], axis=1)

    h1, sp0, sx, sd = forward(0, info, e, features, rx0, rd0, w_own, w_other, tb0)
    rx1, rd1 = swap_edges(sx, sd)
    h2, sp1, sx, sd = forward(1, info, e, h1, rx1, rd1, w_own, w_other, tb1)
    rx2, rd2 = swap_edges(sx, sd)
    prob, psend, boxo, dl, cx, cd = head(info, e, h2, rx2, rd2, wc, wb, cb, bb, class_cotangent, cot_r, gb)
    rx, rd = swap_edges(cx, cd)
    prob_r = swap_section(psend)

    wc_own, wc_send, cbg, wbg, bbg = head_weights(info, e, h2, rx2, rd2, dl, gb)
    class_sum = wc_own + swap_section(wc_send).astype(F32)
    class_done = sum_tiles(halves(class_sum))
    dz1, sx, sd = head_inputs(info, e, dl, gb, rx, rd, wc, wb, sp1)
    rx, rd = swap_edges(sx, sd)
    keep1, send1, bg1 = weights(1, info, e, h1, rx1, rd1, dz1)
    dz0, sx, sd = inputs(1, info, e, dz1, rx, rd, w_own, w_other, sp0)
    rx, rd = swap_edges(sx, sd)
    sum1 = keep1 + swap_section(send1).astype(F32)
    keep0, send0, bg0 = weights(0, info, e, features, rx0, rd0, dz0)
    sum0 = keep0 + swap_section(send0).astype(F32)
    (feature_grad,) = inputs(0, info, e, dz0, rx, rd, w_own, w_other)

    def small_parts(own):
        a = 0 if own else 1
        bias_here = jnp.where(section == 0, *((bg0, bg1) if own else (bg1, bg0))).reshape(-1)
        flat = [
            bias_here,
            cbg[0, a * kp : (a + 1) * kp],
            jnp.pad(bbg[0, a * HALF : (a + 1) * HALF], (0, LANES - HALF)),
            wbg[:, a * HALF : (a + 1) * HALF].reshape(-1),
        ]
        flat = jnp.concatenate(flat)
        pad = -flat.shape[0] % (c * 2 * lax.axis_size("tile"))
        return jnp.pad(flat, (0, pad)).reshape(-1, c)

    small_sum = small_parts(True) + swap_section(small_parts(False))
    n = taps // 2
    m = small_sum.shape[0] // 2
    first_half = jnp.concatenate([sum1[:n], sum0[:n], small_sum[:m]])
    second_half = jnp.concatenate([sum1[n:], sum0[n:], small_sum[m:]])
    done = sum_tiles([(x_first, first_half), (y_first, second_half)])
    l1, l0, tiny = (
        jnp.concatenate([v[at : at + size] for v in done])
        for at, size in ((0, n), (n, n), (2 * n, m))
    )
    mine_l = jnp.where(section == 0, l0, l1)
    other_l = swap_section(jnp.where(section == 0, l1, l0))
    tower_wgrad = jnp.where(section == 0, jnp.stack([mine_l, other_l]), jnp.stack([other_l, mine_l]))
    tower_wgrad = tower_wgrad.astype(F32).reshape(1, nt, 3, 3 * c, c)
    tiny = tiny.reshape(-1).astype(F32)
    at = nt * c
    tower_bgrad = tiny[:at].reshape(1, nt, c)
    class_bgrad = tiny[at : at + kc]
    at += kp
    box_bgrad = tiny[at : at + kb]
    at += LANES
    box_wgrad = tiny[at : at + 3 * c * HALF].reshape(3, c, HALF)[:, :, : 3 * kb].reshape(3, c, 3, kb)
    box_wgrad = box_wgrad.transpose(0, 2, 1, 3).reshape(3, 3 * c, kb)
    class_wgrad = jnp.concatenate(class_done)[:, :kc].astype(F32).reshape(3, 3 * c, kc)

    def both(own, received):
        return jnp.where(section == 0, jnp.concatenate([own, received]), jnp.concatenate([received, own]))

    return (
        both(prob, prob_r[..., :kc]),
        both(boxo, prob_r[..., kc : kc + kb]),
        feature_grad,
        tower_wgrad,
        tower_bgrad,
        class_wgrad,
        class_bgrad,
        box_wgrad,
        box_bgrad,
    )


def solution(mesh):
    in_specs = (
        P("section", None, "tile", None, None),
        P(),
        P("section", None, None, None, None),
        P("section", None, None),
        P(None, None, "section"),
        P("section"),
        P(None, None, "section"),
        P("section"),
        P(None, "tile", None, "section"),
        P(None, "tile", None, "section"),
    )
    out_specs = (
        P(None, "tile", None, "section"),
        P(None, "tile", None, "section"),
        P("section", None, "tile", None, None),
        P("section", None, None, None, None),
        P("section", None, None),
        P(None, None, "section"),
        P("section"),
        P(None, None, "section"),
        P("section"),
    )
    return jax.shard_map(on_device, mesh=mesh, in_specs=in_specs, out_specs=out_specs, check_vma=False)
```

```python
import functools

import jax
import jax.numpy as jnp
from jax import lax
from jax.experimental import pallas as pl
from jax.experimental.pallas import tpu as pltpu
from jax.sharding import PartitionSpec as P

BF = jnp.bfloat16
F32 = jnp.float32
LANES = 128
VMEM = 24 << 20
VMEM_HEAD = 44 << 20
SMEM = pl.BlockSpec(memory_space=pltpu.SMEM)
HBM = pl.BlockSpec(memory_space=pltpu.HBM)


def dot(a, b):
    return jnp.dot(a, b, preferred_element_type=F32)


def dot_nt(a, b):
    return lax.dot_general(a, b, (((1,), (1,)), ((), ())), preferred_element_type=F32)


def dot_tn(a, b):
    return lax.dot_general(a, b, (((0,), (0,)), ((), ())), preferred_element_type=F32)


def down(v):
    return jnp.concatenate([jnp.zeros_like(v[..., :1, :]), v[..., :-1, :]], axis=-2)


def up(v):
    return jnp.concatenate([v[..., 1:, :], jnp.zeros_like(v[..., :1, :])], axis=-2)


def keep_if(v, flag):
    return v * jnp.full((1, v.shape[-1]), flag, F32).astype(v.dtype)


def build(x, rows, e, b, before=None, after=None, taps=True):
    count = len(rows)
    width = rows[0]().shape[0]
    for q in range(-1, count + 1):
        if q < 0:
            get = before
        elif q < count:
            get = rows[q]
        else:
            get = after
        if get is None:
            dest = 0 if q < 0 else count - 1
            part = x.shape[1] // 3
            first = 0 if q < 0 else 2 * part
            x[dest * width : (dest + 1) * width, first : first + part] = jnp.zeros((width, part), x.dtype)
            continue
        v = get()
        p = jnp.concatenate([down(v), v, up(v)], axis=1) if taps else v
        n = p.shape[1]
        if 0 <= q < count:
            x[q * width : (q + 1) * width, n : 2 * n] = p
        if q + 1 < count:
            x[(q + 1) * width : (q + 2) * width, 0:n] = keep_if(p, e[b, q + 1])
        if q >= 1:
            x[(q - 1) * width : q * width, 2 * n : 3 * n] = keep_if(p, e[b, q])


def rows_of(ref, lead, count):
    return [functools.partial(lambda r: ref[lead + (r,)], r) for r in range(count)]


def pick_halo(info, rx, rd, hs, lead):
    @pl.when(info[1] == 0)
    def _():
        hs[0] = rd[lead]
        hs[1] = rx[lead]

    @pl.when(info[1] != 0)
    def _():
        hs[0] = rx[lead]
        hs[1] = rd[lead]


def put_edges(info, first, last, sx, sd, lead):
    @pl.when(info[1] == 0)
    def _():
        sx[lead] = last
        sd[lead] = first

    @pl.when(info[1] != 0)
    def _():
        sx[lead] = first
        sd[lead] = last


def start_weights(info, layer, own, other, wv, sem):
    for t in range(wv.shape[0]):

        @pl.when(info[0] == layer)
        def _():
            pltpu.make_async_copy(own.at[t], wv.at[t], sem.at[t]).start()

        @pl.when(info[0] != layer)
        def _():
            pltpu.make_async_copy(other.at[t], wv.at[t], sem.at[t]).start()


def wait_weights(own, wv, sem, t):
    for i in range(wv.shape[0]):

        @pl.when(t == i)
        def _():
            pltpu.make_async_copy(own.at[i], wv.at[i], sem.at[i]).wait()


def activate(z):
    sg = jax.nn.sigmoid(z)
    hv = z * sg
    return hv.astype(BF), (sg + hv * (1.0 - sg)).astype(BF)


def forward_kernel(layer, info, e, h, own, other, bias, hn, sp, zp, x, wv, sem):
    t, b = pl.program_id(0), pl.program_id(1)
    rows, width = h.shape[2], h.shape[3]

    @pl.when(jnp.logical_and(t == 0, b == 0))
    def _():
        start_weights(info, layer, own, other, wv, sem)

    build(x, rows_of(h, (0, 0), rows), e, b)

    @pl.when(b == 0)
    def _():
        wait_weights(own, wv, sem, t)

    z = dot(x[...], wv[t]) + bias[0]
    hv, sv = activate(z)
    hn[0, 0] = hv.reshape(h.shape[2:])
    sp[0, 0] = sv.reshape(h.shape[2:])
    zp[0, 0, 0] = z[:width]
    zp[0, 0, 1] = z[(rows - 1) * width :]


def forward(layer, info, e, h, own, other, bias):
    nb, nt, rows, width, c = h.shape
    row_spec = pl.BlockSpec((1, 1, rows, width, c), lambda t, b: (b, t, 0, 0, 0))
    taps = own.shape[1]
    return pl.pallas_call(
        functools.partial(forward_kernel, layer),
        grid=(nt, nb),
        in_specs=[SMEM, SMEM, row_spec, HBM, HBM, pl.BlockSpec((1, 1, c), lambda t, b: (t, 0, 0))],
        out_specs=[row_spec, row_spec, pl.BlockSpec((1, 1, 2, width, c), lambda t, b: (b, t, 0, 0, 0))],
        out_shape=[jax.ShapeDtypeStruct(h.shape, BF)] * 2 + [jax.ShapeDtypeStruct((nb, nt, 2, width, c), F32)],
        scratch_shapes=[
            pltpu.VMEM((rows * width, taps), BF),
            pltpu.VMEM((nt, taps, c), BF),
            pltpu.SemaphoreType.DMA((nt,)),
        ],
        compiler_params=pltpu.CompilerParams(vmem_limit_bytes=VMEM),
        cost_estimate=pl.CostEstimate(flops=2 * nb * nt * rows * width * taps * c, bytes_accessed=20 << 20, transcendentals=0),
        name=f"forward{layer}",
    )(info, e, h, own, other, bias)


def edge_kernel(layer, info, e, zp, rx, rd, own, other, hin, sin, hn, sp, sx, sd, wv, sem):
    t, i = pl.program_id(0), pl.program_id(1)
    nb, width, c = zp.shape[0], zp.shape[3], zp.shape[4]
    nt, taps = wv.shape[0], wv.shape[2]

    def copies(ref):
        for tt in range(nt):
            for ii in range(2):
                yield tt, ii, pltpu.make_async_copy(ref.at[tt, pl.ds(2 * ii * taps, taps)], wv.at[tt, ii], sem.at[tt, ii])

    @pl.when(jnp.logical_and(t == 0, i == 0))
    def _():
        @pl.when(info[0] == layer)
        def _():
            for _, _, copy in copies(own):
                copy.start()

        @pl.when(info[0] != layer)
        def _():
            for _, _, copy in copies(other):
                copy.start()

    for tt, ii, copy in copies(own):

        @pl.when(jnp.logical_and(t == tt, i == ii))
        def _():
            copy.wait()

    from_x = (info[1] == 0) == (i == 1)
    edge = jnp.where(i == 0, 0, e.shape[1] - 1)
    for b in range(nb):
        v = jnp.where(jnp.full((1, c), from_x.astype(jnp.int32), jnp.int32) != 0, rx[b, 0].astype(F32), rd[b, 0].astype(F32))
        p = jnp.concatenate([down(v), v, up(v)], axis=1) * e[b, edge]
        z = zp[b, 0, 0] + dot(p.astype(BF), wv[t, i])
        hv, sv = activate(z)
        hn[b, 0, 0] = hv
        sp[b, 0, 0] = sv

        @pl.when(from_x)
        def _():
            sx[b, 0] = hv

        @pl.when(jnp.logical_not(from_x))
        def _():
            sd[b, 0] = hv


def edges(layer, info, e, zp, rx, rd, own, other, hn, sp):
    nb, nt, rows, width, c = hn.shape
    taps = own.shape[1] // 3
    row_spec = pl.BlockSpec((nb, 1, 1, width, c), lambda t, i: (0, t, i * (rows - 1), 0, 0))
    edge_spec = pl.BlockSpec((nb, 1, width, c), lambda t, i: (0, t, 0, 0))
    edge = jax.ShapeDtypeStruct((nb, nt, width, c), BF)
    return pl.pallas_call(
        functools.partial(edge_kernel, layer),
        grid=(nt, 2),
        in_specs=[
            SMEM,
            SMEM,
            pl.BlockSpec((nb, 1, 1, width, c), lambda t, i: (0, t, i, 0, 0)),
            edge_spec,
            edge_spec,
            HBM,
            HBM,
            HBM,
            HBM,
        ],
        out_specs=[row_spec, row_spec, edge_spec, edge_spec],
        out_shape=[jax.ShapeDtypeStruct(hn.shape, BF)] * 2 + [edge] * 2,
        input_output_aliases={7: 0, 8: 1},
        scratch_shapes=[pltpu.VMEM((nt, 2, taps, c), BF), pltpu.SemaphoreType.DMA((nt, 2))],
        compiler_params=pltpu.CompilerParams(vmem_limit_bytes=VMEM),
        cost_estimate=pl.CostEstimate(flops=4 * nb * nt * width * taps * c, bytes_accessed=8 << 20, transcendentals=0),
        name=f"edges{layer}",
    )(info, e, zp, rx, rd, own, other, hn, sp)


def tap_columns(ref, b, e, rows, width, gt):
    n = ref(0).shape[0]
    lane = lax.broadcasted_iota(jnp.int32, (n, width), 1)
    for s, k in ((rows, 0), (rows + 1, 0), (0, 1), (rows + 1, 1), (0, 2), (1, 2)):
        gt[0, 3 * k * n : 3 * (k + 1) * n, s * width : (s + 1) * width] = jnp.zeros((3 * n, width), gt.dtype)
    for r in range(rows):
        g = ref(r)
        left = jnp.where(lane < width - 1, pltpu.roll(g, width - 1, 1), 0.0)
        right = jnp.where(lane > 0, pltpu.roll(g, 1, 1), 0.0)
        for k in range(3):
            flag = e[b, r] if k == 0 else e[b, r + 1] if k == 2 else None
            for j, v in enumerate((left, g, right)):
                v = v if flag is None else v * flag
                at = (3 * k + j) * n
                gt[0, at : at + n, (r + k) * width : (r + k + 1) * width] = v.astype(gt.dtype)


def pack_rows(hx, rows, width, hs, row):
    hx[0:width] = hs[0]
    for r in range(rows):
        hx[(r + 1) * width : (r + 2) * width] = row(r)
    hx[(rows + 1) * width :] = hs[1]


def head_row(logit, cot, cot_r, kc, kp):
    gap = jnp.zeros((kp - kc, logit.shape[1]), F32)
    p = jax.nn.sigmoid(logit)
    q = p * (1.0 - p)
    d = [cot.astype(F32) * q[:kc], gap, cot_r.astype(F32) * q[kp : kp + kc], gap]
    return p[:kc].astype(BF), p[kp : kp + kc].astype(BF), jnp.concatenate(d, axis=0).astype(BF).T


def side(v, lane, j):
    width = v.shape[-1]
    if j == 0:
        return jnp.where(lane > 0, pltpu.roll(v, 1, 1), 0.0)
    if j == 2:
        return jnp.where(lane < width - 1, pltpu.roll(v, width - 1, 1), 0.0)
    return v


def head_kernel(
    info, e, h, wk, wb, cb, bb, cot, cot_r, gb, gb_r,
    prob, psend, boxo, bsend, dl, gt, cb_x, cb_d, lp, bp, x, hx, lg, y,
):
    b = pl.program_id(0)
    rows, width, c = h.shape[2], h.shape[3], h.shape[4]
    kc, kb = cot.shape[2], gb.shape[2]
    kp, kq = wk.shape[1] // 2, bb.shape[0] // 2
    taps = 3 * c
    build(x, rows_of(h, (0, 0), rows), e, b)
    lg[...] = dot_nt(wk[0], x[:, :taps])
    lg[...] += dot_nt(wk[1], x[:, taps : 2 * taps])
    lg[...] += dot_nt(wk[2], x[:, 2 * taps :])

    def row(r, _):
        at = pl.ds(pl.multiple_of(r * width, width), width)
        prob[0, r], psend[0, r], dl[0, r] = head_row(lg[:, at] + cb[...], cot[0, r], cot_r[0, r], kc, kp)
        return 0

    lax.fori_loop(0, rows, row, 0)
    lp[0, 0] = lg[:, :width]
    lp[0, 1] = lg[:, (rows - 1) * width :]
    for r in range(rows):
        hx[r * width : (r + 1) * width] = h[0, 1, r]
    y[...] = dot_nt(wb[...], hx[...])
    n = 2 * kq
    lane = lax.broadcasted_iota(jnp.int32, (n, width), 1)
    for r in range(rows):
        v = bb[...]
        for j in range(3):
            s = y[(3 + j) * n : (4 + j) * n, r * width : (r + 1) * width]
            if r > 0:
                s = s + y[j * n : (j + 1) * n, (r - 1) * width : r * width] * e[b, r]
            if r < rows - 1:
                s = s + y[(6 + j) * n : (7 + j) * n, (r + 1) * width : (r + 2) * width] * e[b, r + 1]
            v = v + side(s, lane, j)
        boxo[0, r] = v[:kb].astype(BF)
        bsend[0, r] = v[kq : kq + kb].astype(BF)
        if r == 0 or r == rows - 1:
            bp[0, min(r, 1)] = v
    small = jnp.zeros((kq - kb, width), F32)
    tap_columns(
        lambda r: jnp.concatenate([gb[0, r].astype(F32), small, gb_r[0, r].astype(F32), small], axis=0), b, e, rows, width, gt
    )
    for i in range(2):
        s = i * (rows + 1)
        db = dot_tn(gt[0, :, s * width : (s + 1) * width], wb[...]).astype(BF)

        @pl.when((info[1] == 0) == (i == 1))
        def _():
            cb_x[0] = db

        @pl.when((info[1] == 0) == (i == 0))
        def _():
            cb_d[0] = db


def head(info, e, h, wk, wb, cb, bb, cot, cot_r, gb, gb_r):
    nb, nt, rows, width, c = h.shape
    kc, kb, kp2, kq2 = cot.shape[2], gb.shape[2], wk.shape[1], bb.shape[0]
    batches = cot.shape[0]
    m = rows * width
    ext = (rows + 2) * width

    def at_b(shape):
        return pl.BlockSpec((1,) + shape, lambda b, info: (b,) + (0,) * len(shape))

    def at_all(shape):
        return pl.BlockSpec((1,) + shape, lambda b, info: (info[0] * nb + b,) + (0,) * len(shape))

    def whole(shape):
        return pl.BlockSpec(shape, lambda b, info: (0,) * len(shape), pipeline_mode=pl.Buffered(1))

    return pl.pallas_call(
        head_kernel,
        grid_spec=pltpu.PrefetchScalarGridSpec(
            num_scalar_prefetch=1,
            grid=(nb,),
            in_specs=[
                SMEM,
                at_b((nt, rows, width, c)),
                whole(wk.shape),
                whole(wb.shape),
                whole(cb.shape),
                whole(bb.shape),
                at_all((rows, kc, width)),
                at_all((rows, kc, width)),
                at_all((rows, kb, width)),
                at_all((rows, kb, width)),
            ],
            out_specs=[
                at_all((rows, kc, width)),
                at_b((rows, kc, width)),
                at_all((rows, kb, width)),
                at_b((rows, kb, width)),
                at_b((rows, width, kp2)),
                at_b((9 * kq2, ext)),
                at_b((width, c)),
                at_b((width, c)),
                at_b((2, kp2, width)),
                at_b((2, kq2, width)),
            ],
            scratch_shapes=[
                pltpu.VMEM((m, 9 * c), BF),
                pltpu.VMEM((m, c), BF),
                pltpu.VMEM((kp2, m), F32),
                pltpu.VMEM((9 * kq2, m), F32),
            ],
        ),
        out_shape=[
            jax.ShapeDtypeStruct((batches, rows, kc, width), BF),
            jax.ShapeDtypeStruct((nb, rows, kc, width), BF),
            jax.ShapeDtypeStruct((batches, rows, kb, width), BF),
            jax.ShapeDtypeStruct((nb, rows, kb, width), BF),
            jax.ShapeDtypeStruct((nb, rows, width, kp2), BF),
            jax.ShapeDtypeStruct((nb, 9 * kq2, ext), BF),
            jax.ShapeDtypeStruct((nb, width, c), BF),
            jax.ShapeDtypeStruct((nb, width, c), BF),
            jax.ShapeDtypeStruct((nb, 2, kp2, width), F32),
            jax.ShapeDtypeStruct((nb, 2, kq2, width), F32),
        ],
        compiler_params=pltpu.CompilerParams(vmem_limit_bytes=VMEM_HEAD),
        cost_estimate=pl.CostEstimate(flops=2 * nb * m * 9 * c * kp2, bytes_accessed=20 << 20, transcendentals=0),
        name="head",
    )(info, e, h, wk, wb, cb, bb, cot, cot_r, gb, gb_r)


def head_edge_kernel(
    info, e, rx, rd, wk, wb, cb, lp, bp, cot, cot_r, cb_x, cb_d, prob_i, psend_i, boxo_i, bsend_i, dl_i,
    prob, psend, boxo, bsend, dl, cx, cd, hs, ds,
):
    i = pl.program_id(0)
    nb, nt, width, c = rx.shape
    kc, kb = cot.shape[2], boxo.shape[2]
    kp, kq = wk.shape[1] // 2, bp.shape[2] // 2
    taps = 3 * c
    n = 2 * kq
    edge = jnp.where(i == 0, 0, e.shape[1] - 1)
    from_x = (info[1] == 0) == (i == 1)

    @pl.when(from_x)
    def _():
        hs[...] = rx[...]

    @pl.when(jnp.logical_not(from_x))
    def _():
        hs[...] = rd[...]

    p = []
    for b in range(nb):
        v = hs[b, 0]
        p.append(keep_if(jnp.concatenate([down(v), v, up(v)], axis=1), e[b, edge]))
    logit = dot_nt(wk[0], jnp.concatenate(p, axis=0))
    lane = lax.broadcasted_iota(jnp.int32, (n, width), 1)
    for b in range(nb):
        lg = logit[:, b * width : (b + 1) * width] + lp[b, 0] + cb[...]
        prob[b, 0], psend[b, 0], d = head_row(lg, cot[b, 0], cot_r[b, 0], kc, kp)
        dl[b, 0] = d
        ds[b * width : (b + 1) * width, :] = d
        y = dot_nt(wb[...], hs[b, 1]) * e[b, edge]
        v = bp[b, 0]
        for j in range(3):
            v = v + side(y[j * n : (j + 1) * n, :], lane, j)
        boxo[b, 0] = v[:kb].astype(BF)
        bsend[b, 0] = v[kq : kq + kb].astype(BF)
    s = dot(ds[...], wk[0]).reshape(nb, width, taps)
    dc = up(s[:, :, :c]) + s[:, :, c : 2 * c] + down(s[:, :, 2 * c :])
    for b in range(nb):
        v = keep_if(dc[b].astype(BF), e[b, edge])

        @pl.when(from_x)
        def _():
            cx[b, 0] = v
            cx[b, 1] = cb_x[b]

        @pl.when(jnp.logical_not(from_x))
        def _():
            cd[b, 0] = v
            cd[b, 1] = cb_d[b]


def head_edges(info, e, rx, rd, wk, wb, cb, lp, bp, cot, cot_r, cb_x, cb_d, prob, psend, boxo, bsend, dl):
    nb, nt, width, c = rx.shape
    rows = cot.shape[1]
    kc, kb, kp2, kq2 = cot.shape[2], boxo.shape[2], wk.shape[1], bp.shape[2]

    def whole(shape):
        return pl.BlockSpec(shape, lambda i, info: (0,) * len(shape), pipeline_mode=pl.Buffered(1))

    def at_i(shape):
        return pl.BlockSpec(shape, lambda i, info: (0, i) + (0,) * (len(shape) - 2))

    def edge_of(shape):
        return pl.BlockSpec(shape, lambda i, info: (0, i * (rows - 1)) + (0,) * (len(shape) - 2))

    def edge_all(shape):
        return pl.BlockSpec(shape, lambda i, info: (info[0], i * (rows - 1)) + (0,) * (len(shape) - 2))

    edge = jax.ShapeDtypeStruct((nb, nt, width, c), BF)
    arrays = (prob, psend, boxo, bsend, dl)
    return pl.pallas_call(
        head_edge_kernel,
        grid_spec=pltpu.PrefetchScalarGridSpec(
            num_scalar_prefetch=1,
            grid=(2,),
            in_specs=[
                SMEM,
                whole(rx.shape),
                whole(rd.shape),
                pl.BlockSpec((1,) + wk.shape[1:], lambda i, info: (2 * i, 0, 0)),
                pl.BlockSpec((3 * kq2, c), lambda i, info: (2 * i, 0)),
                whole(cb.shape),
                at_i((nb, 1, kp2, width)),
                at_i((nb, 1, kq2, width)),
                edge_all((nb, 1, kc, width)),
                edge_all((nb, 1, kc, width)),
                whole(cb_x.shape),
                whole(cb_d.shape),
            ]
            + [HBM] * len(arrays),
            out_specs=[
                edge_all((nb, 1, kc, width)),
                edge_of((nb, 1, kc, width)),
                edge_all((nb, 1, kb, width)),
                edge_of((nb, 1, kb, width)),
                edge_of((nb, 1, width, kp2)),
                pl.BlockSpec(rx.shape, lambda i, info: (0, 0, 0, 0)),
                pl.BlockSpec(rx.shape, lambda i, info: (0, 0, 0, 0)),
            ],
            scratch_shapes=[pltpu.VMEM(rx.shape, BF), pltpu.VMEM((nb * width, kp2), BF)],
        ),
        out_shape=[jax.ShapeDtypeStruct(v.shape, BF) for v in arrays] + [edge, edge],
        input_output_aliases={13 + i: i for i in range(len(arrays))},
        compiler_params=pltpu.CompilerParams(vmem_limit_bytes=VMEM),
        cost_estimate=pl.CostEstimate(flops=8 * nb * width * 3 * c * kp2, bytes_accessed=8 << 20, transcendentals=0),
        name="head_edges",
    )(info, e, rx, rd, wk, wb, cb, lp, bp, cot, cot_r, cb_x, cb_d, *arrays)


def head_weights_kernel(info, e, h, rx, rd, dl, gt, own, other, x, hx, acc, accb, small, hs, *, kc, kb):
    b, nb = pl.program_id(0), pl.num_programs(0)
    rows, width, c = h.shape[2], h.shape[3], h.shape[4]
    kp, kq = dl.shape[-1] // 2, accb.shape[0] // 18
    taps = 3 * c
    pick_halo(info, rx, rd, hs, (0, 0))
    build(x, rows_of(h, (0, 0), rows), e, b, lambda: hs[0], lambda: hs[1])
    pick_halo(info, rx, rd, hs, (0, 1))
    pack_rows(hx, rows, width, hs, lambda r: h[0, 1, r])
    g = dl[0].reshape(rows * width, 2 * kp)

    @pl.when(b == 0)
    def _():
        acc[...] = jnp.zeros_like(acc)
        accb[...] = jnp.zeros_like(accb)
        small[...] = jnp.zeros_like(small)

    acc[...] += dot_tn(g, x[...])
    accb[...] += dot(gt[0], hx[...])
    small[:, : 2 * kp] += jnp.sum(g.astype(F32), axis=0, keepdims=True)
    ones = jnp.ones((8, gt.shape[2]), BF)
    s = dot_nt(ones, gt[0, 8 * kq : 10 * kq, :])[:1]
    small[:, 2 * kp :] += jnp.concatenate([s, jnp.zeros((1, LANES - 2 * kq), F32)], axis=1)

    def fill(ref, a):
        for k in range(3):
            ref[k * kc : (k + 1) * kc, :] = acc[a * kp : a * kp + kc, k * taps : (k + 1) * taps]
            at = 3 * kc + k * kq
            for j in range(3):
                first = (3 * k + j) * 2 * kq + a * kq
                ref[at : at + kq, j * c : (j + 1) * c] = accb[first : first + kq, :]
        end = 3 * (kc + kq)
        if end < ref.shape[0]:
            ref[end:, :] = jnp.zeros((ref.shape[0] - end, taps), F32)
        at = 3 * kc + kb
        ref[at : at + 1, :kp] = small[:, a * kp : (a + 1) * kp]
        ref[at : at + 1, kp : kp + LANES] = pltpu.roll(small[:, 2 * kp :], (LANES - a * kq) % LANES, 1)

    @pl.when(b == nb - 1)
    def _():
        fill(own, 1)
        other[...] = own[...].astype(BF)
        fill(own, 0)


def head_weights(info, e, h, rx, rd, dl, gt, kc, kb):
    nb, nt, rows, width, c = h.shape
    kp2 = dl.shape[-1]
    kq2 = gt.shape[1] // 9
    m = rows * width
    size = -(-3 * (kc + kq2 // 2) // LANES) * LANES

    def at_b(shape):
        return pl.BlockSpec((1,) + shape, lambda b: (b,) + (0,) * len(shape))

    def whole(shape):
        return pl.BlockSpec(shape, lambda b: (0,) * len(shape), pipeline_mode=pl.Buffered(1))

    return pl.pallas_call(
        functools.partial(head_weights_kernel, kc=kc, kb=kb),
        grid=(nb,),
        in_specs=[
            SMEM,
            SMEM,
            at_b((nt, rows, width, c)),
            at_b((nt, width, c)),
            at_b((nt, width, c)),
            at_b((rows, width, kp2)),
            at_b(gt.shape[1:]),
        ],
        out_specs=[whole((size, 3 * c)), whole((size, 3 * c))],
        out_shape=[jax.ShapeDtypeStruct((size, 3 * c), F32), jax.ShapeDtypeStruct((size, 3 * c), BF)],
        scratch_shapes=[
            pltpu.VMEM((m, 9 * c), BF),
            pltpu.VMEM(((rows + 2) * width, c), BF),
            pltpu.VMEM((kp2, 9 * c), F32),
            pltpu.VMEM((9 * kq2, c), F32),
            pltpu.VMEM((1, kp2 + LANES), F32),
            pltpu.VMEM((2, width, c), BF),
        ],
        compiler_params=pltpu.CompilerParams(vmem_limit_bytes=VMEM_HEAD),
        cost_estimate=pl.CostEstimate(flops=2 * nb * m * 9 * c * kp2, bytes_accessed=20 << 20, transcendentals=0),
        name="head_weights",
    )(info, e, h, rx, rd, dl, gt)


def head_inputs_kernel(info, e, dl, gt, rx, rd, wk, wb, sp, dz, sx, sd, x, hs):
    b = pl.program_id(0)
    rows, width, c = sp.shape[2], sp.shape[3], sp.shape[4]
    kp2 = dl.shape[-1]
    taps = 3 * c
    build(x, rows_of(dl, (0,), rows), e, b, taps=False)
    s = dot(x[:, kp2 : 2 * kp2], wk[1])
    s = s + dot(x[:, :kp2], wk[2])
    s = s + dot(x[:, 2 * kp2 :], wk[0])
    s = s.reshape(rows, width, taps)
    dc = up(s[:, :, :c]) + s[:, :, c : 2 * c] + down(s[:, :, 2 * c :])
    db = dot_tn(gt[0, :, width : (rows + 1) * width], wb[...]).reshape(rows, width, c)
    for t, dh in ((0, dc), (1, db)):
        pick_halo(info, rx, rd, hs, (0, t))
        for r in range(rows):
            v = dh[r]
            if r == 0:
                v = v + hs[0].astype(F32)
            if r == rows - 1:
                v = v + hs[1].astype(F32)
            dz[0, t, r] = (v * sp[0, t, r].astype(F32)).astype(BF)
        put_edges(info, dz[0, t, 0], dz[0, t, rows - 1], sx, sd, (0, t))


def head_inputs(info, e, dl, gt, rx, rd, wk, wb, sp):
    nb, nt, rows, width, c = sp.shape
    kp2 = dl.shape[-1]
    m = rows * width

    def at_b(shape):
        return pl.BlockSpec((1,) + shape, lambda b: (b,) + (0,) * len(shape))

    def whole(shape):
        return pl.BlockSpec(shape, lambda b: (0,) * len(shape), pipeline_mode=pl.Buffered(1))

    return pl.pallas_call(
        head_inputs_kernel,
        grid=(nb,),
        in_specs=[
            SMEM,
            SMEM,
            at_b((rows, width, kp2)),
            at_b(gt.shape[1:]),
            at_b((nt, width, c)),
            at_b((nt, width, c)),
            whole(wk.shape),
            whole(wb.shape),
            at_b((nt, rows, width, c)),
        ],
        out_specs=[at_b((nt, rows, width, c)), at_b((nt, width, c)), at_b((nt, width, c))],
        out_shape=[
            jax.ShapeDtypeStruct(sp.shape, BF),
            jax.ShapeDtypeStruct((nb, nt, width, c), BF),
            jax.ShapeDtypeStruct((nb, nt, width, c), BF),
        ],
        scratch_shapes=[pltpu.VMEM((m, 3 * kp2), BF), pltpu.VMEM((2, width, c), BF)],
        compiler_params=pltpu.CompilerParams(vmem_limit_bytes=VMEM_HEAD),
        cost_estimate=pl.CostEstimate(flops=2 * nb * m * 9 * c * kp2, bytes_accessed=20 << 20, transcendentals=0),
        name="head_inputs",
    )(info, e, dl, gt, rx, rd, wk, wb, sp)


def weights_kernel(info, e, h, rx, rd, dz, keep, send, x, acc, bias, hs):
    t, b, nb = pl.program_id(0), pl.program_id(1), pl.num_programs(1)
    rows, width, c = h.shape[2], h.shape[3], h.shape[4]
    pick_halo(info, rx, rd, hs, (0, 0))
    build(x, rows_of(h, (0, 0), rows), e, b, lambda: hs[0], lambda: hs[1])
    g = dz[0, 0].reshape(rows * width, c)
    part = dot_tn(x[...], g)
    total = jnp.sum(g.astype(F32), axis=0, keepdims=True)
    taps = acc.shape[0]
    tail = (keep.shape[0] - taps, c)

    @pl.when(b == 0)
    def _():
        acc[...] = part
        bias[...] = total

    @pl.when(b != 0)
    def _():
        acc[...] += part
        bias[...] += total

    @pl.when(jnp.logical_and(b == nb - 1, t == info[0]))
    def _():
        keep[:taps, :] = acc[...]
        keep[taps:, :] = jnp.broadcast_to(bias[...], tail)

    @pl.when(jnp.logical_and(b == nb - 1, t != info[0]))
    def _():
        send[:taps, :] = acc[...].astype(BF)
        send[taps:, :] = jnp.broadcast_to(bias[...].astype(BF), tail)


def weights(layer, info, e, h, rx, rd, dz):
    nb, nt, rows, width, c = h.shape
    row_spec = pl.BlockSpec((1, 1, rows, width, c), lambda t, b: (b, t, 0, 0, 0))
    edge_spec = pl.BlockSpec((1, 1, width, c), lambda t, b: (b, t, 0, 0))
    taps = 9 * c
    return pl.pallas_call(
        weights_kernel,
        grid=(nt, nb),
        in_specs=[SMEM, SMEM, row_spec, edge_spec, edge_spec, row_spec],
        out_specs=[pl.BlockSpec((taps + LANES, c), lambda t, b: (0, 0))] * 2,
        out_shape=[jax.ShapeDtypeStruct((taps + LANES, c), F32), jax.ShapeDtypeStruct((taps + LANES, c), BF)],
        scratch_shapes=[
            pltpu.VMEM((rows * width, taps), BF),
            pltpu.VMEM((taps, c), F32),
            pltpu.VMEM((1, c), F32),
            pltpu.VMEM((2, width, c), BF),
        ],
        compiler_params=pltpu.CompilerParams(vmem_limit_bytes=VMEM),
        cost_estimate=pl.CostEstimate(flops=2 * nb * nt * rows * width * taps * c, bytes_accessed=20 << 20, transcendentals=0),
        name=f"weights{layer}",
    )(info, e, h, rx, rd, dz)


def inputs_kernel(layer, info, e, dz, rx, rd, own, other, *rest):
    if layer:
        sp, out, sx, sd, x, wv, wt, hs, sem = rest
    else:
        out, x, wv, wt, hs, sem = rest
    t, b = pl.program_id(0), pl.program_id(1)
    rows, width, c = dz.shape[2], dz.shape[3], dz.shape[4]

    @pl.when(jnp.logical_and(t == 0, b == 0))
    def _():
        start_weights(info, layer, own, other, wv, sem)

    pick_halo(info, rx, rd, hs, (0, 0))
    build(x, rows_of(dz, (0, 0), rows), e, b, lambda: hs[0], lambda: hs[1])

    @pl.when(b == 0)
    def _():
        wait_weights(own, wv, sem, t)
        for i in range(9):
            wt[:, (8 - i) * c : (9 - i) * c] = wv[t, i * c : (i + 1) * c, :]

    dh = dot_nt(x[...], wt[...]).astype(BF)
    if not layer:
        out[0, 0] = dh.reshape(rows, width, c)
        return
    dz_next = (dh.astype(F32).reshape(rows, width, c) * sp[0, 0].astype(F32)).astype(BF)
    out[0, 0] = dz_next
    put_edges(info, dz_next[0], dz_next[rows - 1], sx, sd, (0, 0))


def inputs(layer, info, e, dz, rx, rd, own, other, sp=None):
    nb, nt, rows, width, c = dz.shape
    row_spec = pl.BlockSpec((1, 1, rows, width, c), lambda t, b: (b, t, 0, 0, 0))
    edge_spec = pl.BlockSpec((1, 1, width, c), lambda t, b: (b, t, 0, 0))
    edge = jax.ShapeDtypeStruct((nb, nt, width, c), BF)
    taps = own.shape[1]
    return pl.pallas_call(
        functools.partial(inputs_kernel, layer),
        grid=(nt, nb),
        in_specs=[SMEM, SMEM, row_spec, edge_spec, edge_spec, HBM, HBM] + ([row_spec] if layer else []),
        out_specs=[row_spec] + ([edge_spec, edge_spec] if layer else []),
        out_shape=[jax.ShapeDtypeStruct(dz.shape, BF)] + ([edge, edge] if layer else []),
        scratch_shapes=[
            pltpu.VMEM((rows * width, taps), BF),
            pltpu.VMEM((nt, taps, c), BF),
            pltpu.VMEM((c, taps), BF),
            pltpu.VMEM((2, width, c), BF),
            pltpu.SemaphoreType.DMA((nt,)),
        ],
        compiler_params=pltpu.CompilerParams(vmem_limit_bytes=VMEM),
        cost_estimate=pl.CostEstimate(flops=2 * nb * nt * rows * width * taps * c, bytes_accessed=20 << 20, transcendentals=0),
        name=f"inputs{layer}",
    )(info, e, dz, rx, rd, own, other, *([sp] if layer else []))


def swap_section(value):
    return lax.ppermute(value, "section", [(0, 1), (1, 0)])


def swap_edges(sx, sd):
    count = lax.axis_size("tile")
    even = [p for i in range(0, count - 1, 2) for p in ((i, i + 1), (i + 1, i))]
    odd = [p for i in range(1, count - 1, 2) for p in ((i, i + 1), (i + 1, i))]
    return lax.ppermute(sx, "tile", even), lax.ppermute(sd, "tile", odd)


class TileSum:
    def __init__(self, *terms):
        lanes = terms[0].shape[1] // 2
        self.parts = [[v[:, s] for v in terms] for s in (slice(0, lanes), slice(lanes, None))]
        self.count = lax.axis_size("tile")
        self.index = lax.axis_index("tile")
        bits = self.count.bit_length() - 1
        plan = [(0, 1), (1, 0)] + [(bit,) for bit in range(2, bits)]
        self.plan = [(True, step) for step in plan] + [(False, step) for step in reversed(plan)]
        self.sent = None

    def exchange(self, value, bit):
        return lax.ppermute(value, "tile", [(i, i ^ (1 << bit)) for i in range(self.count)])

    def start(self, *others):
        self.halving, self.bits = self.plan.pop(0)
        if self.halving:
            if len(self.bits) < len(self.parts):
                self.parts = [[jnp.concatenate(v, axis=1) for v in zip(*self.parts)]]
            split = [[v.reshape(2, v.shape[0] // 2, v.shape[1]) for v in terms] for terms in self.parts]
            pick = [(self.index >> bit) & 1 for bit in self.bits]
            sends = [
                total(lax.dynamic_index_in_dim(v, 1 - m, 0, False) for v in terms).astype(BF) for terms, m in zip(split, pick)
            ]
            self.parts = [[lax.dynamic_index_in_dim(v, m, 0, False) for v in terms] for terms, m in zip(split, pick)]
        else:
            if isinstance(self.parts[0], list):
                self.parts = [total(terms).astype(BF) for terms in self.parts]
            if len(self.bits) > len(self.parts):
                lanes = self.parts[0].shape[1] // 2
                self.parts = [self.parts[0][:, :lanes], self.parts[0][:, lanes:]]
            sends = self.parts
        sends = after(sends, *others)
        self.sent = [self.exchange(v, bit) for v, bit in zip(sends, self.bits)]
        return sends

    def finish(self, *others):
        got = after(self.sent, *others)
        if self.halving:
            self.parts = [terms + [v] for terms, v in zip(self.parts, got)]
        else:
            mine = [(self.index >> bit) & 1 for bit in self.bits]
            self.parts = [
                jnp.where(m == 0, jnp.concatenate([v, g]), jnp.concatenate([g, v]))
                for v, g, m in zip(self.parts, got, mine)
            ]

    def result(self):
        while self.plan:
            self.start()
            self.finish()
        return jnp.concatenate(self.parts, axis=1)


def total(values):
    values = [v.astype(F32) for v in values]
    return functools.reduce(jnp.add, values)


def after(value, *others):
    return lax.optimization_barrier((value,) + others)[0]


def on_device(
    features,
    levels,
    tower_weight,
    tower_bias,
    class_weight,
    class_bias,
    box_weight,
    box_bias,
    class_cotangent,
    box_cotangent,
):
    section = lax.axis_index("section")
    tile = lax.axis_index("tile")
    nb, nt, rows, width, c = features.shape
    kc, kb = class_weight.shape[-1], box_weight.shape[-1]
    kp = -(-kc // LANES) * LANES
    kq = -(-kb // 8) * 8
    taps = 9 * c

    lines = lax.dynamic_slice_in_dim(levels, section * nb, nb, 0)
    lines = jnp.pad(lines, ((0, 0), (1, 1)), constant_values=-1)
    lines = lax.dynamic_slice_in_dim(lines, tile * rows, rows + 2, 1)
    e = (lines[:, 1:] == lines[:, :-1]).astype(F32)
    info = jnp.stack([section, tile % 2]).astype(jnp.int32)
    even = tile % 2 == 0

    first, last = features[:, :, 0], features[:, :, rows - 1]
    rx0, rd0 = swap_edges(jnp.where(even, last, first), jnp.where(even, first, last))
    w_own = tower_weight.reshape(nt, taps, c)
    w_other = swap_section(w_own)
    bias_own = jnp.concatenate([tower_bias.reshape(-1), class_bias, box_bias])
    bias_other = swap_section(bias_own)
    tb_own, tb_other = bias_own[: nt * c].reshape(nt, 1, c), bias_other[: nt * c].reshape(nt, 1, c)
    tb0 = jnp.where(section == 0, tb_own, tb_other)
    tb1 = jnp.where(section == 0, tb_other, tb_own)

    def spread(at, size, padded):
        v = jnp.concatenate([jnp.pad(u[at : at + size], (0, padded - size)) for u in (bias_own, bias_other)])
        return jnp.broadcast_to(v[:, None], (2 * padded, LANES))

    cb, bb = spread(nt * c, kc, kp), spread(nt * c + kc, kb, kq)
    cot = class_cotangent.transpose(0, 1, 3, 2)
    cot_r = swap_section(cot)
    gb = box_cotangent.transpose(0, 1, 3, 2)
    gb_r = swap_section(gb)
    thin = class_weight.transpose(0, 2, 1)
    wk = jnp.concatenate([jnp.pad(v, ((0, 0), (0, kp - kc), (0, 0))) for v in (thin, swap_section(thin))], axis=1)
    small = box_weight.transpose(0, 2, 1)
    small = [v.reshape(3, kb, 3, c).transpose(0, 2, 1, 3) for v in (small, swap_section(small))]
    wb = jnp.concatenate([jnp.pad(v, ((0, 0), (0, 0), (0, kq - kb), (0, 0))) for v in small], axis=2)
    wb = wb.reshape(18 * kq, c)

    h1, sp0, zp = forward(0, info, e, features, w_own, w_other, tb0)
    h1, sp0, sx, sd = edges(0, info, e, zp, rx0, rd0, w_own, w_other, h1, sp0)
    rx1, rd1 = swap_edges(sx, sd)
    h2, sp1, zp = forward(1, info, e, h1, w_own, w_other, tb1)
    h2, sp1, sx, sd = edges(1, info, e, zp, rx1, rd1, w_own, w_other, h2, sp1)
    rx2, rd2 = swap_edges(sx, sd)
    prob, psend, boxo, bsend, dl, gt, cb_x, cb_d, lp, bp = head(info, e, h2, wk, wb, cb, bb, cot, cot_r, gb, gb_r)
    prob, psend, boxo, bsend, dl, cx, cd = head_edges(
        info, e, rx2, rd2, wk, wb, cb, lp, bp, cot, cot_r, cb_x, cb_d, prob, psend, boxo, bsend, dl
    )
    rx, rd = swap_edges(cx, cd)

    own, send = head_weights(info, e, h2, rx2, rd2, dl, gt, kc, kb)
    head_sum = TileSum(own, swap_section(send))
    info = after(info, head_sum.start())
    dz1, sx, sd = head_inputs(info, e, dl, gt, rx, rd, wk, wb, sp1)
    rx, rd = swap_edges(sx, sd)
    head_sum.finish(sx)
    info = after(info, head_sum.start(sx))
    prob_r, bsend_r = swap_section(after(psend, sx)), swap_section(after(bsend, sx))
    keep1, send1 = weights(1, info, e, h1, rx1, rd1, dz1)
    recv1 = swap_section(send1)
    head_sum.finish(send1)
    info = after(info, head_sum.start(send1))
    dz0, sx, sd = inputs(1, info, e, dz1, rx, rd, w_own, w_other, sp0)
    rx, rd = swap_edges(sx, sd)
    head_sum.finish(sx)
    sum1 = TileSum(keep1, recv1)
    info = after(info, head_sum.start(sx), sum1.start(sx))
    keep0, send0 = weights(0, info, e, features, rx0, rd0, dz0)
    recv0 = swap_section(send0)
    head_sum.finish(send0)
    sum1.finish(send0)
    sum0 = TileSum(keep0, recv0)
    info = after(info, head_sum.start(send0), sum1.start(send0), sum0.start(send0))
    (feature_grad,) = inputs(0, info, e, dz0, rx, rd, w_own, w_other)
    for s in (head_sum, sum1, sum0):
        s.finish(feature_grad)
    head_done, l1, l0 = head_sum.result(), sum1.result(), sum0.result()

    mine_l = jnp.where(section == 0, l0, l1)
    other_l = swap_section(jnp.where(section == 0, l1, l0))
    towers = jnp.where(section == 0, jnp.stack([mine_l, other_l]), jnp.stack([other_l, mine_l])).astype(F32)
    end = 3 * kc
    box = head_done[end : end + 3 * kq].astype(F32)
    theirs = (1 - section) * nb
    prob = lax.dynamic_update_slice_in_dim(prob, prob_r, theirs, 0)
    boxo = lax.dynamic_update_slice_in_dim(boxo, bsend_r, theirs, 0)
    return (
        prob.transpose(0, 1, 3, 2),
        boxo.transpose(0, 1, 3, 2),
        feature_grad,
        towers[:, :taps].reshape(1, nt, 3, 3 * c, c),
        towers[:, taps].reshape(1, nt, c),
        head_done[:end].astype(F32).reshape(3, kc, 3 * c).transpose(0, 2, 1),
        box[kb, :kc],
        box.reshape(3, kq, 3 * c)[:, :kb].transpose(0, 2, 1),
        box[kb, kp : kp + kb],
    )


def solution(mesh):
    in_specs = (
        P("section", None, "tile", None, None),
        P(),
        P("section", None, None, None, None),
        P("section", None, None),
        P(None, None, "section"),
        P("section"),
        P(None, None, "section"),
        P("section"),
        P(None, "tile", None, "section"),
        P(None, "tile", None, "section"),
    )
    out_specs = (
        P(None, "tile", None, "section"),
        P(None, "tile", None, "section"),
        P("section", None, "tile", None, None),
        P("section", None, None, None, None),
        P("section", None, None),
        P(None, None, "section"),
        P("section"),
        P(None, None, "section"),
        P("section"),
    )
    return jax.shard_map(on_device, mesh=mesh, in_specs=in_specs, out_specs=out_specs, check_vma=False)
```

```python
import functools

import jax
import jax.numpy as jnp
from jax import lax
from jax.experimental import pallas as pl
from jax.experimental.pallas import tpu as pltpu
from jax.sharding import PartitionSpec as P

BF = jnp.bfloat16
F32 = jnp.float32
LANES = 128


def cost(us):
    return pl.CostEstimate(flops=int(us * 2e9), bytes_accessed=0, transcendentals=0)


def ordered(kernel, inputs, after):
    def body(*refs):
        return kernel(*refs[:inputs], *refs[inputs + len(after) :])

    return body
SMEM = pl.BlockSpec(memory_space=pltpu.SMEM)
HBM = pl.BlockSpec(memory_space=pltpu.HBM)
ANY = pl.BlockSpec(memory_space=pl.ANY)


TOKEN = jax.ShapeDtypeStruct((8, LANES), F32)
TOKEN_SPEC = pl.BlockSpec((8, LANES), lambda *_: (0, 0))


def dot(a, b):
    return jnp.dot(a, b, preferred_element_type=F32)


def dot_nt(a, b):
    return lax.dot_general(a, b, (((1,), (1,)), ((), ())), preferred_element_type=F32)


def dot_tn(a, b):
    return lax.dot_general(a, b, (((0,), (0,)), ((), ())), preferred_element_type=F32)


def down(v):
    return jnp.concatenate([jnp.zeros_like(v[..., :1, :]), v[..., :-1, :]], axis=-2)


def up(v):
    return jnp.concatenate([v[..., 1:, :], jnp.zeros_like(v[..., :1, :])], axis=-2)


def keep_if(v, flag):
    return v * jnp.full((1, v.shape[-1]), flag, F32).astype(v.dtype)


def build(x, rows, e, b, before=None, after=None, taps=True):
    count = len(rows)
    width = rows[0]().shape[0]
    for q in range(-1, count + 1):
        if q < 0:
            get = before
        elif q < count:
            get = rows[q]
        else:
            get = after
        if get is None:
            dest = 0 if q < 0 else count - 1
            part = x.shape[1] // 3
            first = 0 if q < 0 else 2 * part
            x[dest * width : (dest + 1) * width, first : first + part] = jnp.zeros((width, part), x.dtype)
            continue
        v = get()
        p = jnp.concatenate([down(v), v, up(v)], axis=1) if taps else v
        n = p.shape[1]
        if 0 <= q < count:
            x[q * width : (q + 1) * width, n : 2 * n] = p
        if q + 1 < count:
            x[(q + 1) * width : (q + 2) * width, 0:n] = keep_if(p, e[b, q + 1])
        if q >= 1:
            x[(q - 1) * width : q * width, 2 * n : 3 * n] = keep_if(p, e[b, q])


class Borders:
    def __init__(self, info, lev, rows):
        self.info, self.lev, self.rows = info, lev, rows

    def __getitem__(self, at):
        b, i = at
        lines, count = self.lev.shape
        line = self.info[0] * (lines // 2) + b
        r = self.info[2] * self.rows + i
        same = self.lev[line, jnp.maximum(r - 1, 0)] == self.lev[line, jnp.minimum(r, count - 1)]
        return jnp.where(jnp.logical_and(same, jnp.logical_and(r > 0, r < count)), 1.0, 0.0)


def rows_of(ref, lead, count):
    return [functools.partial(lambda r: ref[lead + (r,)], r) for r in range(count)]


def pick_halo(info, rx, rd, hs, lead):
    @pl.when(info[1] == 0)
    def _():
        hs[0] = rd[lead]
        hs[1] = rx[lead]

    @pl.when(info[1] != 0)
    def _():
        hs[0] = rx[lead]
        hs[1] = rd[lead]


def put_edges(info, first, last, sx, sd, lead):
    @pl.when(info[1] == 0)
    def _():
        sx[lead] = last
        sd[lead] = first

    @pl.when(info[1] != 0)
    def _():
        sx[lead] = first
        sd[lead] = last


def start_weights(info, layer, own, other, wv, sem):
    for t in range(wv.shape[0]):

        @pl.when(info[0] == layer)
        def _():
            pltpu.make_async_copy(own.at[t], wv.at[t], sem.at[t]).start()

        @pl.when(info[0] != layer)
        def _():
            pltpu.make_async_copy(other.at[t], wv.at[t], sem.at[t]).start()


def wait_weights(own, wv, sem, t):
    for i in range(wv.shape[0]):

        @pl.when(t == i)
        def _():
            pltpu.make_async_copy(own.at[i], wv.at[i], sem.at[i]).wait()


def activate(z):
    sg = jax.nn.sigmoid(z)
    hv = z * sg
    return hv.astype(BF), (sg + hv * (1.0 - sg)).astype(BF)


def forward_kernel(layer, info, lev, h, own, other, bias, bias_r, hn, sp, zp, token, x, wv, sem):
    t, b = pl.program_id(0), pl.program_id(1)
    rows, width = h.shape[2], h.shape[3]
    e = Borders(info, lev, rows)

    @pl.when(jnp.logical_and(t == 0, b == 0))
    def _():
        start_weights(info, layer, own, other, wv, sem)

    build(x, rows_of(h, (0, 0), rows), e, b)

    @pl.when(b == 0)
    def _():
        wait_weights(own, wv, sem, t)

    c = h.shape[4]
    chosen = jnp.full((1, c), info[0] == layer, jnp.int32) != 0
    row = pl.ds(t, 1)
    z = dot(x[...], wv[t]) + jnp.where(chosen, bias[row, :c], bias_r[row, :c])
    hv, sv = activate(z)
    hn[0, 0] = hv.reshape(h.shape[2:])
    sp[0, 0] = sv.reshape(h.shape[2:])
    zp[0, 0, 0] = z[:width]
    zp[0, 0, 1] = z[(rows - 1) * width :]
    token[...] = jnp.zeros_like(token)


def forward(layer, info, lev, h, own, other, bias, bias_r, after=()):
    nb, nt, rows, width, c = h.shape
    row_spec = pl.BlockSpec((1, 1, rows, width, c), lambda t, b: (b, t, 0, 0, 0))
    taps = own.shape[1]
    return pl.pallas_call(
        ordered(functools.partial(forward_kernel, layer), 7, after),
        grid=(nt, nb),
        in_specs=[SMEM, SMEM, row_spec, HBM, HBM] + [pl.BlockSpec(bias.shape, lambda t, b: (0, 0))] * 2 + [ANY] * len(after),
        out_specs=[row_spec, row_spec, pl.BlockSpec((1, 1, 2, width, c), lambda t, b: (b, t, 0, 0, 0)), TOKEN_SPEC],
        out_shape=[jax.ShapeDtypeStruct(h.shape, BF)] * 2 + [jax.ShapeDtypeStruct((nb, nt, 2, width, c), F32), TOKEN],
        scratch_shapes=[
            pltpu.VMEM((rows * width, taps), BF),
            pltpu.VMEM((nt, taps, c), BF),
            pltpu.SemaphoreType.DMA((nt,)),
        ],
        compiler_params=pltpu.CompilerParams(vmem_limit_bytes=12 << 20),
        cost_estimate=cost(8),
        name=f"forward{layer}",
    )(info, lev, h, own, other, bias, bias_r, *after)


def edge_kernel(layer, rows, info, lev, zp, rx, rd, own, other, hin, sin, hn, sp, sx, sd, wv, sem):
    t, i = pl.program_id(0), pl.program_id(1)
    nb, width, c = zp.shape[0], zp.shape[3], zp.shape[4]
    nt, taps = wv.shape[0], wv.shape[2]
    e = Borders(info, lev, rows)

    def copies(ref):
        for tt in range(nt):
            for ii in range(2):
                yield tt, ii, pltpu.make_async_copy(ref.at[tt, pl.ds(2 * ii * taps, taps)], wv.at[tt, ii], sem.at[tt, ii])

    @pl.when(jnp.logical_and(t == 0, i == 0))
    def _():
        @pl.when(info[0] == layer)
        def _():
            for _, _, copy in copies(own):
                copy.start()

        @pl.when(info[0] != layer)
        def _():
            for _, _, copy in copies(other):
                copy.start()

    for tt, ii, copy in copies(own):

        @pl.when(jnp.logical_and(t == tt, i == ii))
        def _():
            copy.wait()

    from_x = (info[1] == 0) == (i == 1)
    edge = i * rows
    for b in range(nb):
        v = jnp.where(jnp.full((1, c), from_x.astype(jnp.int32), jnp.int32) != 0, rx[b, 0].astype(F32), rd[b, 0].astype(F32))
        p = jnp.concatenate([down(v), v, up(v)], axis=1) * e[b, edge]
        z = zp[b, 0, 0] + dot(p.astype(BF), wv[t, i])
        hv, sv = activate(z)
        hn[b, 0, 0] = hv
        sp[b, 0, 0] = sv

        @pl.when(from_x)
        def _():
            sx[b, 0] = hv

        @pl.when(jnp.logical_not(from_x))
        def _():
            sd[b, 0] = hv


def edges(layer, info, lev, zp, rx, rd, own, other, hn, sp):
    nb, nt, rows, width, c = hn.shape
    taps = own.shape[1] // 3
    row_spec = pl.BlockSpec((nb, 1, 1, width, c), lambda t, i: (0, t, i * (rows - 1), 0, 0))
    edge_spec = pl.BlockSpec((nb, 1, width, c), lambda t, i: (0, t, 0, 0))
    edge = jax.ShapeDtypeStruct((nb, nt, width, c), BF)
    return pl.pallas_call(
        functools.partial(edge_kernel, layer, rows),
        grid=(nt, 2),
        in_specs=[
            SMEM,
            SMEM,
            pl.BlockSpec((nb, 1, 1, width, c), lambda t, i: (0, t, i, 0, 0)),
            edge_spec,
            edge_spec,
            HBM,
            HBM,
            HBM,
            HBM,
        ],
        out_specs=[row_spec, row_spec, edge_spec, edge_spec],
        out_shape=[jax.ShapeDtypeStruct(hn.shape, BF)] * 2 + [edge] * 2,
        input_output_aliases={7: 0, 8: 1},
        scratch_shapes=[pltpu.VMEM((nt, 2, taps, c), BF), pltpu.SemaphoreType.DMA((nt, 2))],
        compiler_params=pltpu.CompilerParams(vmem_limit_bytes=6 << 20),
        cost_estimate=cost(4),
        name=f"edges{layer}",
    )(info, lev, zp, rx, rd, own, other, hn, sp)


def tap_columns(ref, b, e, rows, width, gt):
    n = ref(0).shape[0]
    lane = lax.broadcasted_iota(jnp.int32, (n, width), 1)
    for s, k in ((rows, 0), (rows + 1, 0), (0, 1), (rows + 1, 1), (0, 2), (1, 2)):
        gt[0, 3 * k * n : 3 * (k + 1) * n, s * width : (s + 1) * width] = jnp.zeros((3 * n, width), gt.dtype)
    for r in range(rows):
        g = ref(r)
        left = jnp.where(lane < width - 1, pltpu.roll(g, width - 1, 1), 0.0)
        right = jnp.where(lane > 0, pltpu.roll(g, 1, 1), 0.0)
        for k in range(3):
            flag = e[b, r] if k == 0 else e[b, r + 1] if k == 2 else None
            for j, v in enumerate((left, g, right)):
                v = v if flag is None else v * flag
                at = (3 * k + j) * n
                gt[0, at : at + n, (r + k) * width : (r + k + 1) * width] = v.astype(gt.dtype)


def pack_rows(hx, rows, width, hs, row):
    hx[0:width] = hs[0]
    for r in range(rows):
        hx[(r + 1) * width : (r + 2) * width] = row(r)
    hx[(rows + 1) * width :] = hs[1]


def head_row(logit, cot, cot_r, kc, kp):
    gap = jnp.zeros((kp - kc, logit.shape[1]), F32)
    p = jax.nn.sigmoid(logit)
    q = p * (1.0 - p)
    d = [cot.astype(F32) * q[:kc], gap, cot_r.astype(F32) * q[kp : kp + kc], gap]
    return p[:kc].astype(BF), p[kp : kp + kc].astype(BF), jnp.concatenate(d, axis=0).astype(BF).T


def side(v, lane, j):
    width = v.shape[-1]
    if j == 0:
        return jnp.where(lane > 0, pltpu.roll(v, 1, 1), 0.0)
    if j == 2:
        return jnp.where(lane < width - 1, pltpu.roll(v, width - 1, 1), 0.0)
    return v


def head_kernel(
    info, lev, h, wk, wb, cb, cot, gb, cot_r,
    prob, psend, dl, gt, cb_x, cb_d, lp, bo, x, hx, lg, y,
):
    b = pl.program_id(0)
    rows, width, c = h.shape[2], h.shape[3], h.shape[4]
    kc, kb = cot.shape[2], gb.shape[1]
    kp, kq = wk.shape[1] // 2, wb.shape[0] // 18
    e = Borders(info, lev, rows)

    taps = 3 * c
    build(x, rows_of(h, (0, 0), rows), e, b)
    lg[...] = dot_nt(wk[0], x[:, :taps])
    lg[...] += dot_nt(wk[1], x[:, taps : 2 * taps])
    lg[...] += dot_nt(wk[2], x[:, 2 * taps :])

    def row(r, _):
        at = pl.ds(pl.multiple_of(r * width, width), width)
        prob[0, r], psend[0, r, :kc], dl[0, r] = head_row(lg[:, at] + cb[: 2 * kp], cot[0, r], cot_r[0, r, :kc], kc, kp)
        return 0

    lax.fori_loop(0, rows, row, 0)
    lp[0, 0] = lg[:, :width] + cb[: 2 * kp]
    lp[0, 1] = lg[:, (rows - 1) * width :] + cb[: 2 * kp]
    for r in range(rows):
        hx[r * width : (r + 1) * width] = h[0, 1, r]
    y[...] = dot_nt(wb[...], hx[...])
    n = 2 * kq
    lane = lax.broadcasted_iota(jnp.int32, (n, width), 1)
    for r in range(rows):
        v = cb[2 * kp : 2 * kp + n]
        for j in range(3):
            s = y[(3 + j) * n : (4 + j) * n, r * width : (r + 1) * width]
            if r > 0:
                s = s + y[j * n : (j + 1) * n, (r - 1) * width : r * width] * e[b, r]
            if r < rows - 1:
                s = s + y[(6 + j) * n : (7 + j) * n, (r + 1) * width : (r + 2) * width] * e[b, r + 1]
            v = v + side(s, lane, j)
        bo[0, r] = v
        rest = jnp.zeros((kp - kc - kb, width), F32)
        psend[0, r, kc:] = jnp.concatenate([v[kq : kq + kb], rest], axis=0).astype(BF)
    small = jnp.zeros((kq - kb, width), F32)
    g = gb[0].astype(F32)

    def columns(r):
        return jnp.concatenate([g[:, r], small, cot_r[0, r, kc:].astype(F32)[:kb], small], axis=0)

    tap_columns(columns, b, e, rows, width, gt)
    for i in range(2):
        s = i * (rows + 1)
        db = dot_tn(gt[0, :, s * width : (s + 1) * width], wb[...]).astype(BF)

        @pl.when((info[1] == 0) == (i == 1))
        def _():
            cb_x[0] = db

        @pl.when((info[1] == 0) == (i == 0))
        def _():
            cb_d[0] = db


def head(info, lev, h, wk, wb, cb, cot, gb, cot_r, after=()):
    nb, nt, rows, width, c = h.shape
    kc, kb, kp2, kq2 = cot.shape[2], gb.shape[1], wk.shape[1], wb.shape[0] // 9
    batches = cot.shape[0]
    m = rows * width
    ext = (rows + 2) * width

    def at_b(shape):
        return pl.BlockSpec((1,) + shape, lambda b, info: (b,) + (0,) * len(shape))

    def at_all(shape):
        return pl.BlockSpec((1,) + shape, lambda b, info: (info[0] * nb + b,) + (0,) * len(shape))

    def whole(shape):
        return pl.BlockSpec(shape, lambda b, info: (0,) * len(shape), pipeline_mode=pl.Buffered(1))

    return pl.pallas_call(
        ordered(head_kernel, 9, after),
        grid_spec=pltpu.PrefetchScalarGridSpec(
            num_scalar_prefetch=1,
            grid=(nb,),
            in_specs=[
                SMEM,
                at_b((nt, rows, width, c)),
                whole(wk.shape),
                whole(wb.shape),
                whole(cb.shape),
                at_all((rows, kc, width)),
                at_all((kb, rows, width)),
                at_b((rows, kp2 // 2, width)),
            ]
            + [ANY] * len(after),
            out_specs=[
                at_all((rows, kc, width)),
                at_b((rows, kp2 // 2, width)),
                at_b((rows, width, kp2)),
                at_b((9 * kq2, ext)),
                at_b((width, c)),
                at_b((width, c)),
                at_b((2, kp2, width)),
                at_b((rows, kq2, width)),
            ],
            scratch_shapes=[
                pltpu.VMEM((m, 9 * c), BF),
                pltpu.VMEM((m, c), BF),
                pltpu.VMEM((kp2, m), F32),
                pltpu.VMEM((9 * kq2, m), F32),
            ],
        ),
        out_shape=[
            jax.ShapeDtypeStruct((batches, rows, kc, width), BF),
            jax.ShapeDtypeStruct((nb, rows, kp2 // 2, width), BF),
            jax.ShapeDtypeStruct((nb, rows, width, kp2), BF),
            jax.ShapeDtypeStruct((nb, 9 * kq2, ext), BF),
            jax.ShapeDtypeStruct((nb, width, c), BF),
            jax.ShapeDtypeStruct((nb, width, c), BF),
            jax.ShapeDtypeStruct((nb, 2, kp2, width), F32),
            jax.ShapeDtypeStruct((nb, rows, kq2, width), F32),
        ],
        compiler_params=pltpu.CompilerParams(vmem_limit_bytes=17 << 20),
        cost_estimate=cost(14),
        name="head",
    )(info, lev, h, wk, wb, cb, cot, gb, cot_r, *after)


def head_edge_kernel(
    info, lev, rx, rd, wk, wb, lp, bo, cot, cot_r, cb_x, cb_d, prob_i, psend_i, dl_i,
    prob, psend, dl, boxo, cx, cd, hs, ds, bs, bx,
):
    i = pl.program_id(0)
    nb, nt, width, c = rx.shape
    kc, kb, rows = cot.shape[2], boxo.shape[1], boxo.shape[2]
    kp, kq = wk.shape[1] // 2, bo.shape[2] // 2
    taps = 3 * c
    n = 2 * kq
    e = Borders(info, lev, rows)
    edge = i * rows
    from_x = (info[1] == 0) == (i == 1)

    @pl.when(from_x)
    def _():
        hs[...] = rx[...]

    @pl.when(jnp.logical_not(from_x))
    def _():
        hs[...] = rd[...]

    p = []
    for b in range(nb):
        v = hs[b, 0]
        p.append(keep_if(jnp.concatenate([down(v), v, up(v)], axis=1), e[b, edge]))
    logit = dot_nt(wk[0], jnp.concatenate(p, axis=0))
    lane = lax.broadcasted_iota(jnp.int32, (n, width), 1)
    for b in range(nb):
        lg = logit[:, b * width : (b + 1) * width] + lp[b, 0]
        prob[b, 0], psend[b, 0, :kc], d = head_row(lg, cot[b, 0], cot_r[b, 0, :kc], kc, kp)
        dl[b, 0] = d
        ds[b * width : (b + 1) * width, :] = d
        y = dot_nt(wb[...], hs[b, 1]) * e[b, edge]
        v = bo[b, i * (rows - 1)]
        for j in range(3):
            v = v + side(y[j * n : (j + 1) * n, :], lane, j)
        bs[b, i] = v
        gap = jnp.zeros((kp - kc - kb, width), F32)
        psend[b, 0, kc:] = jnp.concatenate([v[kq : kq + kb], gap], axis=0).astype(BF)

    @pl.when(i == 1)
    def _():
        for b in range(nb):
            for r in range(rows):
                v = bs[b, 0] if r == 0 else bs[b, 1] if r == rows - 1 else bo[b, r]
                bx[:, r, :] = v
            boxo[b] = bx[:kb].astype(BF)

    s = dot(ds[...], wk[0]).reshape(nb, width, taps)
    dc = up(s[:, :, :c]) + s[:, :, c : 2 * c] + down(s[:, :, 2 * c :])
    for b in range(nb):
        v = keep_if(dc[b].astype(BF), e[b, edge])

        @pl.when(from_x)
        def _():
            cx[b, 0] = v
            cx[b, 1] = cb_x[b]

        @pl.when(jnp.logical_not(from_x))
        def _():
            cd[b, 0] = v
            cd[b, 1] = cb_d[b]


def head_edges(info, lev, rx, rd, wk, wb, lp, bo, cot, cot_r, cb_x, cb_d, prob, psend, dl, kb):
    nb, nt, width, c = rx.shape
    rows = cot.shape[1]
    kc, kp2, kq2 = cot.shape[2], wk.shape[1], bo.shape[2]

    def whole(shape):
        return pl.BlockSpec(shape, lambda i, info: (0,) * len(shape), pipeline_mode=pl.Buffered(1))

    def at_i(shape):
        return pl.BlockSpec(shape, lambda i, info: (0, i) + (0,) * (len(shape) - 2))

    def edge_of(shape):
        return pl.BlockSpec(shape, lambda i, info: (0, i * (rows - 1)) + (0,) * (len(shape) - 2))

    def edge_all(shape):
        return pl.BlockSpec(shape, lambda i, info: (info[0], i * (rows - 1)) + (0,) * (len(shape) - 2))

    edge = jax.ShapeDtypeStruct((nb, nt, width, c), BF)
    arrays = (prob, psend, dl)
    return pl.pallas_call(
        head_edge_kernel,
        grid_spec=pltpu.PrefetchScalarGridSpec(
            num_scalar_prefetch=1,
            grid=(2,),
            in_specs=[
                SMEM,
                whole(rx.shape),
                whole(rd.shape),
                pl.BlockSpec((1,) + wk.shape[1:], lambda i, info: (2 * i, 0, 0)),
                pl.BlockSpec((3 * kq2, c), lambda i, info: (2 * i, 0)),
                at_i((nb, 1, kp2, width)),
                whole(bo.shape),
                edge_all((nb, 1, kc, width)),
                edge_of((nb, 1, kp2 // 2, width)),
                whole(cb_x.shape),
                whole(cb_d.shape),
            ]
            + [HBM] * len(arrays),
            out_specs=[
                edge_all((nb, 1, kc, width)),
                edge_of((nb, 1, kp2 // 2, width)),
                edge_of((nb, 1, width, kp2)),
                pl.BlockSpec((nb, kb, rows, width), lambda i, info: (info[0], 0, 0, 0)),
                pl.BlockSpec(rx.shape, lambda i, info: (0, 0, 0, 0)),
                pl.BlockSpec(rx.shape, lambda i, info: (0, 0, 0, 0)),
            ],
            scratch_shapes=[
                pltpu.VMEM(rx.shape, BF),
                pltpu.VMEM((nb * width, kp2), BF),
                pltpu.VMEM((nb, 2, kq2, width), F32),
                pltpu.VMEM((kq2, rows, width), F32),
            ],
        ),
        out_shape=[jax.ShapeDtypeStruct(v.shape, BF) for v in arrays]
        + [jax.ShapeDtypeStruct((cot.shape[0], kb, rows, width), BF)]
        + [edge, edge],
        input_output_aliases={12 + i: i for i in range(len(arrays))},
        compiler_params=pltpu.CompilerParams(vmem_limit_bytes=8 << 20),
        cost_estimate=cost(6),
        name="head_edges",
    )(info, lev, rx, rd, wk, wb, lp, bo, cot, cot_r, cb_x, cb_d, *arrays)


def head_weights_kernel(info, lev, h, rx, rd, dl, gt, own, other, x, hx, acc, accb, small, hs, *, kc, kb):
    b, nb = pl.program_id(0), pl.num_programs(0)
    rows, width, c = h.shape[2], h.shape[3], h.shape[4]
    kp, kq = dl.shape[-1] // 2, accb.shape[0] // 18
    taps = 3 * c
    e = Borders(info, lev, rows)
    pick_halo(info, rx, rd, hs, (0, 0))
    build(x, rows_of(h, (0, 0), rows), e, b, lambda: hs[0], lambda: hs[1])
    pick_halo(info, rx, rd, hs, (0, 1))
    pack_rows(hx, rows, width, hs, lambda r: h[0, 1, r])
    g = dl[0].reshape(rows * width, 2 * kp)

    @pl.when(b == 0)
    def _():
        acc[...] = jnp.zeros_like(acc)
        accb[...] = jnp.zeros_like(accb)
        small[...] = jnp.zeros_like(small)

    acc[...] += dot_tn(g, x[...])
    accb[...] += dot(gt[0], hx[...])
    small[:, : 2 * kp] += jnp.sum(g.astype(F32), axis=0, keepdims=True)
    ones = jnp.ones((8, gt.shape[2]), BF)
    s = dot_nt(ones, gt[0, 8 * kq : 10 * kq, :])[:1]
    small[:, 2 * kp :] += jnp.concatenate([s, jnp.zeros((1, LANES - 2 * kq), F32)], axis=1)

    def fill(ref, a):
        for k in range(3):
            ref[k * kc : (k + 1) * kc, :] = acc[a * kp : a * kp + kc, k * taps : (k + 1) * taps]
            at = 3 * kc + k * kq
            for j in range(3):
                first = (3 * k + j) * 2 * kq + a * kq
                ref[at : at + kq, j * c : (j + 1) * c] = accb[first : first + kq, :]
        end = 3 * (kc + kq)
        if end < ref.shape[0]:
            ref[end:, :] = jnp.zeros((ref.shape[0] - end, taps), F32)
        at = 3 * kc + kb
        ref[at : at + 1, :kp] = small[:, a * kp : (a + 1) * kp]
        ref[at : at + 1, kp : kp + LANES] = pltpu.roll(small[:, 2 * kp :], (LANES - a * kq) % LANES, 1)

    @pl.when(b == nb - 1)
    def _():
        fill(own, 1)
        other[...] = own[...].astype(BF)
        fill(own, 0)


def head_weights(info, lev, h, rx, rd, dl, gt, kc, kb, after=()):
    nb, nt, rows, width, c = h.shape
    kp2 = dl.shape[-1]
    kq2 = gt.shape[1] // 9
    m = rows * width
    size = -(-3 * (kc + kq2 // 2) // LANES) * LANES

    def at_b(shape):
        return pl.BlockSpec((1,) + shape, lambda b: (b,) + (0,) * len(shape))

    def whole(shape):
        return pl.BlockSpec(shape, lambda b: (0,) * len(shape), pipeline_mode=pl.Buffered(1))

    return pl.pallas_call(
        ordered(functools.partial(head_weights_kernel, kc=kc, kb=kb), 7, after),
        grid=(nb,),
        in_specs=[
            SMEM,
            SMEM,
            at_b((nt, rows, width, c)),
            at_b((nt, width, c)),
            at_b((nt, width, c)),
            at_b((rows, width, kp2)),
            at_b(gt.shape[1:]),
        ]
        + [ANY] * len(after),
        out_specs=[whole((size, 3 * c)), whole((size, 3 * c))],
        out_shape=[jax.ShapeDtypeStruct((size, 3 * c), F32), jax.ShapeDtypeStruct((size, 3 * c), BF)],
        scratch_shapes=[
            pltpu.VMEM((m, 9 * c), BF),
            pltpu.VMEM(((rows + 2) * width, c), BF),
            pltpu.VMEM((kp2, 9 * c), F32),
            pltpu.VMEM((9 * kq2, c), F32),
            pltpu.VMEM((1, kp2 + LANES), F32),
            pltpu.VMEM((2, width, c), BF),
        ],
        compiler_params=pltpu.CompilerParams(vmem_limit_bytes=21 << 20),
        cost_estimate=cost(12),
        name="head_weights",
    )(info, lev, h, rx, rd, dl, gt, *after)


def head_inputs_kernel(info, lev, dl, gt, rx, rd, wk, wb, sp, *rest):
    dz, sx, sd, *_, x, hs = rest
    b = pl.program_id(0)
    rows, width, c = sp.shape[2], sp.shape[3], sp.shape[4]
    kp2 = dl.shape[-1]
    taps = 3 * c
    e = Borders(info, lev, rows)
    build(x, rows_of(dl, (0,), rows), e, b, taps=False)
    s = dot(x[:, kp2 : 2 * kp2], wk[1])
    s = s + dot(x[:, :kp2], wk[2])
    s = s + dot(x[:, 2 * kp2 :], wk[0])
    s = s.reshape(rows, width, taps)
    dc = up(s[:, :, :c]) + s[:, :, c : 2 * c] + down(s[:, :, 2 * c :])
    db = dot_tn(gt[0, :, width : (rows + 1) * width], wb[...]).reshape(rows, width, c)
    for t, dh in ((0, dc), (1, db)):
        pick_halo(info, rx, rd, hs, (0, t))
        for r in range(rows):
            v = dh[r]
            if r == 0:
                v = v + hs[0].astype(F32)
            if r == rows - 1:
                v = v + hs[1].astype(F32)
            dz[0, t, r] = (v * sp[0, t, r].astype(F32)).astype(BF)
        put_edges(info, dz[0, t, 0], dz[0, t, rows - 1], sx, sd, (0, t))


def head_inputs(info, lev, dl, gt, rx, rd, wk, wb, sp, gate, after=()):
    nb, nt, rows, width, c = sp.shape
    kp2 = dl.shape[-1]
    m = rows * width

    def at_b(shape):
        return pl.BlockSpec((1,) + shape, lambda b: (b,) + (0,) * len(shape))

    def whole(shape):
        return pl.BlockSpec(shape, lambda b: (0,) * len(shape), pipeline_mode=pl.Buffered(1))

    return pl.pallas_call(
        ordered(head_inputs_kernel, 9, gate + after),
        grid=(nb,),
        in_specs=[
            SMEM,
            SMEM,
            at_b((rows, width, kp2)),
            at_b(gt.shape[1:]),
            at_b((nt, width, c)),
            at_b((nt, width, c)),
            whole(wk.shape),
            whole(wb.shape),
            at_b((nt, rows, width, c)),
        ]
        + [ANY] * len(gate + after),
        out_specs=[at_b((nt, rows, width, c)), at_b((nt, width, c)), at_b((nt, width, c))] + [ANY] * len(gate),
        out_shape=[
            jax.ShapeDtypeStruct(sp.shape, BF),
            jax.ShapeDtypeStruct((nb, nt, width, c), BF),
            jax.ShapeDtypeStruct((nb, nt, width, c), BF),
        ]
        + [jax.ShapeDtypeStruct(v.shape, v.dtype) for v in gate],
        input_output_aliases={9 + k: 3 + k for k in range(len(gate))},
        scratch_shapes=[pltpu.VMEM((m, 3 * kp2), BF), pltpu.VMEM((2, width, c), BF)],
        compiler_params=pltpu.CompilerParams(vmem_limit_bytes=14 << 20),
        cost_estimate=cost(9),
        name="head_inputs",
    )(info, lev, dl, gt, rx, rd, wk, wb, sp, *gate, *after)


def weights_kernel(info, lev, h, rx, rd, dz, keep, send, token, x, acc, bias, hs):
    t, b, nb = pl.program_id(0), pl.program_id(1), pl.num_programs(1)
    rows, width, c = h.shape[2], h.shape[3], h.shape[4]
    e = Borders(info, lev, rows)
    pick_halo(info, rx, rd, hs, (0, 0))
    build(x, rows_of(h, (0, 0), rows), e, b, lambda: hs[0], lambda: hs[1])
    g = dz[0, 0].reshape(rows * width, c)
    part = dot_tn(x[...], g)
    total = jnp.sum(g.astype(F32), axis=0, keepdims=True)
    taps = acc.shape[0]

    @pl.when(b == 0)
    def _():
        acc[...] = part
        bias[...] = total

    @pl.when(b != 0)
    def _():
        acc[...] += part
        bias[...] += total

    token[...] = jnp.zeros_like(token)
    for i, out in enumerate((send, keep)):

        @pl.when(jnp.logical_and(b == nb - 1, t == i))
        def _():
            out[:taps, :] = acc[...].astype(out.dtype)
            out[taps:, :] = jnp.broadcast_to(bias[...].astype(out.dtype), (out.shape[0] - taps, c))


def weights(layer, info, lev, h, rx, rd, dz, after=()):
    nb, nt, rows, width, c = h.shape

    def tower(t, info):
        return jnp.where(t == 0, 1 - info[0], info[0])

    row_spec = pl.BlockSpec((1, 1, rows, width, c), lambda t, b, info: (b, tower(t, info), 0, 0, 0))
    edge_spec = pl.BlockSpec((1, 1, width, c), lambda t, b, info: (b, tower(t, info), 0, 0))
    taps = 9 * c
    return pl.pallas_call(
        ordered(weights_kernel, 6, after),
        grid_spec=pltpu.PrefetchScalarGridSpec(
            num_scalar_prefetch=1,
            grid=(nt, nb),
            in_specs=[SMEM, row_spec, edge_spec, edge_spec, row_spec] + [ANY] * len(after),
            out_specs=[pl.BlockSpec((taps + LANES, c), lambda t, b, info: (0, 0))] * 2 + [TOKEN_SPEC],
            scratch_shapes=[
                pltpu.VMEM((rows * width, taps), BF),
                pltpu.VMEM((taps, c), F32),
                pltpu.VMEM((1, c), F32),
                pltpu.VMEM((2, width, c), BF),
            ],
        ),
        out_shape=[jax.ShapeDtypeStruct((taps + LANES, c), F32), jax.ShapeDtypeStruct((taps + LANES, c), BF), TOKEN],
        compiler_params=pltpu.CompilerParams(vmem_limit_bytes=14 << 20),
        cost_estimate=cost(8),
        name=f"weights{layer}",
    )(info, lev, h, rx, rd, dz, *after)


def inputs_kernel(layer, info, lev, dz, rx, rd, own, other, *rest):
    if layer:
        sp, out, sx, sd, x, wv, wt, hs, sem = rest
    else:
        out, token, *_, x, wv, wt, hs, sem = rest
    t, b = pl.program_id(0), pl.program_id(1)
    rows, width, c = dz.shape[2], dz.shape[3], dz.shape[4]
    e = Borders(info, lev, rows)

    @pl.when(jnp.logical_and(t == 0, b == 0))
    def _():
        start_weights(info, layer, own, other, wv, sem)

    pick_halo(info, rx, rd, hs, (0, 0))
    build(x, rows_of(dz, (0, 0), rows), e, b, lambda: hs[0], lambda: hs[1])

    @pl.when(b == 0)
    def _():
        wait_weights(own, wv, sem, t)
        for i in range(9):
            wt[:, (8 - i) * c : (9 - i) * c] = wv[t, i * c : (i + 1) * c, :]

    dh = dot_nt(x[...], wt[...]).astype(BF)
    if not layer:
        out[0, 0] = dh.reshape(rows, width, c)
        token[...] = jnp.zeros_like(token)
        return
    dz_next = (dh.astype(F32).reshape(rows, width, c) * sp[0, 0].astype(F32)).astype(BF)
    out[0, 0] = dz_next
    put_edges(info, dz_next[0], dz_next[rows - 1], sx, sd, (0, 0))


def inputs(layer, info, lev, dz, rx, rd, own, other, sp=None, gate=(), after=()):
    nb, nt, rows, width, c = dz.shape
    row_spec = pl.BlockSpec((1, 1, rows, width, c), lambda t, b: (b, t, 0, 0, 0))
    edge_spec = pl.BlockSpec((1, 1, width, c), lambda t, b: (b, t, 0, 0))
    edge = jax.ShapeDtypeStruct((nb, nt, width, c), BF)
    taps = own.shape[1]
    return pl.pallas_call(
        ordered(functools.partial(inputs_kernel, layer), 8 if layer else 7, gate + after),
        grid=(nt, nb),
        in_specs=[SMEM, SMEM, row_spec, edge_spec, edge_spec, HBM, HBM] + ([row_spec] if layer else []) + [ANY] * len(gate + after),
        out_specs=[row_spec] + ([edge_spec, edge_spec] if layer else [TOKEN_SPEC]) + [ANY] * len(gate),
        out_shape=[jax.ShapeDtypeStruct(dz.shape, BF)]
        + ([edge, edge] if layer else [TOKEN])
        + [jax.ShapeDtypeStruct(v.shape, v.dtype) for v in gate],
        input_output_aliases={7 + k: 2 + k for k in range(len(gate))},
        scratch_shapes=[
            pltpu.VMEM((rows * width, taps), BF),
            pltpu.VMEM((nt, taps, c), BF),
            pltpu.VMEM((c, taps), BF),
            pltpu.VMEM((2, width, c), BF),
            pltpu.SemaphoreType.DMA((nt,)),
        ],
        compiler_params=pltpu.CompilerParams(vmem_limit_bytes=13 << 20),
        cost_estimate=cost(9),
        name=f"inputs{layer}",
    )(info, lev, dz, rx, rd, own, other, *([sp] if layer else []), *gate, *after)


def swap_section(value):
    return lax.ppermute(value, "section", [(0, 1), (1, 0)])


def swap_edges(sx, sd):
    count = lax.axis_size("tile")
    even = [p for i in range(0, count - 1, 2) for p in ((i, i + 1), (i + 1, i))]
    odd = [p for i in range(1, count - 1, 2) for p in ((i, i + 1), (i + 1, i))]
    return lax.ppermute(sx, "tile", even), lax.ppermute(sd, "tile", odd)


def combine_kernel(plan, info, *refs):
    ins, outs = list(refs[: sum(sum(p) for p in plan)]), refs[sum(sum(p) for p in plan) :]
    for counts, out in zip(plan, outs):
        lanes = out.shape[1] // len(counts)
        for i, count in enumerate(counts):
            terms = [ins.pop(0)[...].astype(F32) for _ in range(count)]
            out[:, i * lanes : (i + 1) * lanes] = functools.reduce(jnp.add, terms).astype(out.dtype)


def combine(name, info, shape, outs, gate=(), after=()):
    rows, lanes = shape
    views = [v for parts in outs for terms in parts for v in terms]

    def spec(view):
        return pl.BlockSpec(shape, lambda i, info: (view[1](info), view[2]))

    plan = [[len(terms) for terms in parts] for parts in outs]
    return pl.pallas_call(
        ordered(functools.partial(combine_kernel, plan), 1 + len(views), gate + after),
        grid_spec=pltpu.PrefetchScalarGridSpec(
            num_scalar_prefetch=1,
            grid=(1,),
            in_specs=[spec(v) for v in views] + [ANY] * len(gate + after),
            out_specs=[pl.BlockSpec((rows, lanes * len(parts)), lambda i, info: (0, 0)) for parts in outs]
            + [ANY] * len(gate),
        ),
        out_shape=[jax.ShapeDtypeStruct((rows, lanes * len(parts)), BF) for parts in outs]
        + [jax.ShapeDtypeStruct(v.shape, v.dtype) for v in gate],
        input_output_aliases={1 + len(views) + k: len(outs) + k for k in range(len(gate))},
        compiler_params=pltpu.CompilerParams(vmem_limit_bytes=16 << 20),
        cost_estimate=cost(2),
        name=name,
    )(info, *[v[0] for v in views], *gate, *after)


def join_kernel(bits, split, info, *refs):
    n = len(bits)
    for i, bit in enumerate(bits):
        cur, got = refs[2 * i], refs[2 * i + 1]
        outs = refs[2 * n :] if split else refs[2 * n + i : 2 * n + i + 1]
        m, lanes = cur.shape[0], cur.shape[1] // len(outs)
        mine = (info[2] >> bit) & 1
        for j, out in enumerate(outs):
            at = slice(j * lanes, (j + 1) * lanes)

            @pl.when(mine == 0)
            def _():
                out[:m, :] = cur[:, at]
                out[m:, :] = got[:, at]

            @pl.when(mine != 0)
            def _():
                out[:m, :] = got[:, at]
                out[m:, :] = cur[:, at]


def join(name, info, bits, pairs, split=False, after=()):
    arrays = [v for pair in pairs for v in pair]
    shapes = [(2 * cur.shape[0], cur.shape[1]) for cur, _ in pairs]
    if split:
        shapes = [(shapes[0][0], shapes[0][1] // 2)] * 2

    def whole(shape):
        return pl.BlockSpec(shape, lambda i, info: (0, 0))

    return pl.pallas_call(
        ordered(functools.partial(join_kernel, bits, split), 1 + len(arrays), after),
        grid_spec=pltpu.PrefetchScalarGridSpec(
            num_scalar_prefetch=1,
            grid=(1,),
            in_specs=[whole(v.shape) for v in arrays] + [ANY] * len(after),
            out_specs=[whole(s) for s in shapes],
        ),
        out_shape=[jax.ShapeDtypeStruct(s, BF) for s in shapes],
        compiler_params=pltpu.CompilerParams(vmem_limit_bytes=16 << 20),
        cost_estimate=cost(2),
        name=name,
    )(info, *arrays, *after)


class TileSum:
    def __init__(self, name, info, whole, *terms):
        self.name, self.info = name, info
        rows, lanes = terms[0].shape
        self.shape = (rows, lanes // 2)
        self.parts = [[(v, lambda info: 0, i) for v in terms] for i in range(2)]
        self.count = lax.axis_size("tile")
        bits = self.count.bit_length() - 1
        near = [(0, 1), (1, 0)]
        self.plan = [("halve", step) for step in near]
        if whole or bits > 4:
            self.plan += [("add", (bit,)) for bit in range(2, bits)]
        else:
            self.plan += [("halve", (bit,)) for bit in range(2, bits)]
            self.plan += [("double", (bit,)) for bit in reversed(range(2, bits))]
        self.plan += [("double", step) for step in reversed(near)]
        self.step = 0
        self.sends = None

    def exchange(self, value, bit):
        return lax.ppermute(value, "tile", [(i, i ^ (1 << bit)) for i in range(self.count)])

    def start(self, *after, gate=()):
        kind, bits = self.plan.pop(0)
        name = f"{self.name}_{self.step}"
        self.step += 1
        if kind == "halve":
            rows, lanes = self.shape
            self.shape = (rows // 2, lanes)
            bit_of = bits * 2 if len(bits) == 1 else bits

            def half(view, bit, other):
                array, row, lane = view
                return array, lambda info: 2 * row(info) + (((info[2] >> bit) & 1) ^ other), lane

            sent = [[half(v, bit, 1) for v in terms] for terms, bit in zip(self.parts, bit_of)]
            self.parts = [[half(v, bit, 0) for v in terms] for terms, bit in zip(self.parts, bit_of)]
            outs = [sent] if len(bits) == 1 else [[terms] for terms in sent]
            sends = combine(name, self.info, self.shape, outs, gate, after)
        elif kind == "add" or self.kind != "double":
            outs = [self.parts] if len(bits) == 1 else [[terms] for terms in self.parts]
            sends = combine(name, self.info, self.shape, outs, gate, after)
        else:
            sends = join(name, self.info, self.bits, self.pairs, len(bits) > len(self.pairs), after)
        passed = tuple(sends[len(bits) :])
        sends = tuple(sends[: len(bits)])
        self.kind, self.bits, self.sends = kind, bits, sends
        got = [self.exchange(v, bit) for v, bit in zip(sends, bits)]
        if kind == "halve":
            lane = (lambda i: i) if len(bits) == 1 else (lambda i: 0)
            pick = (lambda i: got[0]) if len(bits) == 1 else (lambda i: got[i])
            self.parts = [terms + [(pick(i), lambda info: 0, lane(i))] for i, terms in enumerate(self.parts)]
        elif kind == "add":
            self.parts = [[(v, lambda info: 0, i) for v in (sends[0], got[0])] for i in range(2)]
        else:
            self.pairs = list(zip(sends, got))
        return sends + passed

    def result(self, *after):
        return join(f"{self.name}_{self.step}", self.info, self.bits, self.pairs, False, after)


def pick_kernel(info, cot, gb, out):
    rows, kc, kb = cot.shape[1], cot.shape[2], gb.shape[1]
    g = gb[0].astype(F32)
    gap = jnp.zeros((out.shape[2] - kc - kb, out.shape[3]), F32)
    for r in range(rows):
        out[0, r] = jnp.concatenate([cot[0, r].astype(F32), g[:, r], gap], axis=0).astype(BF)


def pick(info, cot, gb, nb, kp, after=()):
    def at_all(shape):
        return pl.BlockSpec((1,) + shape[1:], lambda b, info: ((1 - info[0]) * nb + b,) + (0,) * (len(shape) - 1))

    shape = (nb, cot.shape[1], kp, cot.shape[3])
    return pl.pallas_call(
        ordered(pick_kernel, 3, after),
        grid_spec=pltpu.PrefetchScalarGridSpec(
            num_scalar_prefetch=1,
            grid=(nb,),
            in_specs=[at_all(cot.shape), at_all(gb.shape)] + [ANY] * len(after),
            out_specs=pl.BlockSpec((1,) + shape[1:], lambda b, info: (b, 0, 0, 0)),
        ),
        out_shape=jax.ShapeDtypeStruct(shape, BF),
        compiler_params=pltpu.CompilerParams(vmem_limit_bytes=8 << 20),
        cost_estimate=cost(2),
        name="pick",
    )(info, cot, gb, *after)


def gather_kernel(tower, classes, boxes, out):
    out[...] = jnp.zeros_like(out)
    nt, c = tower.shape[1], tower.shape[2]
    out[:nt, :c] = tower[0]
    out[nt : nt + 1, : classes.shape[0]] = classes[...].reshape(1, -1)
    out[nt + 1 : nt + 2, : boxes.shape[0]] = boxes[...].reshape(1, -1)


def gather(tower, classes, boxes, lanes):
    return pl.pallas_call(
        gather_kernel,
        out_shape=jax.ShapeDtypeStruct((8, lanes), F32),
        cost_estimate=cost(1),
        name="gather",
    )(tower, classes, boxes)


def pick_weights_kernel(thin, small, out):
    gap = jnp.zeros((out.shape[1] - thin.shape[1] - small.shape[1], out.shape[2]), F32)
    out[0] = jnp.concatenate([thin[0].astype(F32), small[0].astype(F32), gap], axis=0).astype(BF)


def pick_weights(thin, small, kp, after=()):
    def at_k(shape):
        return pl.BlockSpec((1,) + shape[1:], lambda k: (k, 0, 0))

    shape = (thin.shape[0], kp, thin.shape[2])
    return pl.pallas_call(
        ordered(pick_weights_kernel, 2, after),
        grid=(shape[0],),
        in_specs=[at_k(thin.shape), at_k(small.shape)] + [ANY] * len(after),
        out_specs=at_k(shape),
        out_shape=jax.ShapeDtypeStruct(shape, BF),
        compiler_params=pltpu.CompilerParams(vmem_limit_bytes=6 << 20),
        cost_estimate=cost(2),
        name="pick_weights",
    )(thin, small, *after)


def pack_kernel(own, other, bias, bias_r, wk, wb, cb, *, kc, kb, kq, towers):
    k = pl.program_id(0)
    kp = own.shape[1]
    c = wb.shape[1]
    gap = jnp.zeros((kp - kc, wk.shape[2]), F32)
    for half, v in enumerate((own, other)):
        wk[0, half * kp : (half + 1) * kp, :] = jnp.concatenate([v[0].astype(F32)[:kc], gap], axis=0).astype(BF)
    u, v = own[0].astype(F32)[kc : kc + kb], other[0].astype(F32)[kc : kc + kb]
    small = jnp.zeros((kq - kb, c), F32)
    for j in range(3):
        at = slice(j * c, (j + 1) * c)
        rows = jnp.concatenate([u[:, at], small, v[:, at], small], axis=0).astype(BF)
        wb[pl.ds(pl.multiple_of((3 * k + j) * 2 * kq, 2 * kq), 2 * kq), :] = rows

    @pl.when(k == 0)
    def _():
        wide = jnp.zeros((1, kp - kc), F32)
        thin = jnp.zeros((1, kq - kb), F32)
        rest = jnp.zeros((1, cb.shape[0] - 2 * kp - kq - kb), F32)
        classes, boxes = slice(towers, towers + 1), slice(towers + 1, towers + 2)
        parts = [bias[classes, :kc], wide, bias_r[classes, :kc], wide, bias[boxes, :kb], thin, bias_r[boxes, :kb], rest]
        cb[...] = jnp.broadcast_to(jnp.concatenate(parts, axis=1), (cb.shape[1], cb.shape[0])).T


def pack(own, other, bias, bias_r, kc, kb, kq, towers, after=()):
    k, kp, c3 = own.shape
    at_k = pl.BlockSpec((1, kp, c3), lambda k: (k, 0, 0))

    def whole(shape):
        return pl.BlockSpec(shape, lambda k: (0,) * len(shape))

    shapes = [(k, 2 * kp, c3), (18 * kq, c3 // 3), (2 * kp + LANES, LANES)]
    return pl.pallas_call(
        ordered(functools.partial(pack_kernel, kc=kc, kb=kb, kq=kq, towers=towers), 4, after),
        grid=(k,),
        in_specs=[at_k, at_k, whole(bias.shape), whole(bias.shape)] + [ANY] * len(after),
        out_specs=[pl.BlockSpec((1,) + shapes[0][1:], lambda k: (k, 0, 0)), whole(shapes[1]), whole(shapes[2])],
        out_shape=[jax.ShapeDtypeStruct(s, t) for s, t in zip(shapes, (BF, BF, F32))],
        compiler_params=pltpu.CompilerParams(vmem_limit_bytes=10 << 20),
        cost_estimate=cost(3),
        name="pack",
    )(own, other, bias, bias_r, *after)


def place_kernel(info, prob_i, box_i, got, prob, box, bx):
    rows, kc, kb = prob.shape[1], prob.shape[2], box.shape[1]
    for r in range(rows):
        prob[0, r] = got[0, r, :kc]
        bx[:, r, :] = got[0, r, kc:].astype(F32)[:kb]
    box[0] = bx[...].astype(BF)


def place(info, prob, box, got, after=()):
    nb = got.shape[0]

    def at_all(shape):
        return pl.BlockSpec((1,) + shape[1:], lambda b, info: ((1 - info[0]) * nb + b,) + (0,) * (len(shape) - 1))

    return pl.pallas_call(
        ordered(place_kernel, 4, after),
        grid_spec=pltpu.PrefetchScalarGridSpec(
            num_scalar_prefetch=1,
            grid=(nb,),
            in_specs=[HBM, HBM, pl.BlockSpec((1,) + got.shape[1:], lambda b, info: (b, 0, 0, 0))] + [ANY] * len(after),
            out_specs=[at_all(prob.shape), at_all(box.shape)],
            scratch_shapes=[pltpu.VMEM(box.shape[1:], F32)],
        ),
        out_shape=[jax.ShapeDtypeStruct(v.shape, BF) for v in (prob, box)],
        input_output_aliases={1: 0, 2: 1},
        compiler_params=pltpu.CompilerParams(vmem_limit_bytes=8 << 20),
        cost_estimate=cost(2),
        name="place",
    )(info, prob, box, got, *after)


def after(value, *others):
    return lax.optimization_barrier((value,) + others)[0]


def on_device(
    features,
    levels,
    tower_weight,
    tower_bias,
    class_weight,
    class_bias,
    box_weight,
    box_bias,
    class_cotangent,
    box_cotangent,
):
    section = lax.axis_index("section")
    tile = lax.axis_index("tile")
    nb, nt, rows, width, c = features.shape
    kc, kb = class_weight.shape[-1], box_weight.shape[-1]
    kp = -(-kc // LANES) * LANES
    kq = -(-kb // 8) * 8
    taps = 9 * c
    lev = levels
    info = jnp.stack([section, tile % 2, tile]).astype(jnp.int32)
    even = tile % 2 == 0

    sx = lax.dynamic_index_in_dim(features, jnp.where(even, rows - 1, 0), 2, False)
    sd = lax.dynamic_index_in_dim(features, jnp.where(even, 0, rows - 1), 2, False)
    rx0, rd0 = swap_edges(sx, sd)
    bias = gather(tower_bias, class_bias, box_bias, kp)
    bias_r = swap_section(bias)
    w_own = tower_weight.reshape(nt, taps, c)
    w_other = swap_section(w_own)

    h1, sp0, zp, token = forward(0, info, lev, features, w_own, w_other, bias, bias_r, (sx, sd))
    thin, small = class_weight.transpose(0, 2, 1), box_weight.transpose(0, 2, 1)
    cot, gb = class_cotangent.transpose(0, 1, 3, 2), box_cotangent.transpose(0, 3, 1, 2)
    w_out = pick_weights(thin, small, kp, (token,))
    w_out_r = swap_section(w_out)
    cot_r = swap_section(pick(info, cot, gb, nb, kp, (token,)))
    h1, sp0, sx, sd = edges(0, info, lev, zp, rx0, rd0, w_own, w_other, h1, sp0)
    rx1, rd1 = swap_edges(sx, sd)
    h2, sp1, zp, _ = forward(1, info, lev, h1, w_own, w_other, bias, bias_r)
    wk, wb, cb = pack(w_out, w_out_r, bias, bias_r, kc, kb, kq, nt, (zp,))
    h2, sp1, sx, sd = edges(1, info, lev, zp, rx1, rd1, w_own, w_other, h2, sp1)
    rx2, rd2 = swap_edges(sx, sd)
    prob, psend, dl, gt, cb_x, cb_d, lp, bo = head(info, lev, h2, wk, wb, cb, cot, gb, cot_r)
    prob, psend, dl, boxo, cx, cd = head_edges(
        info, lev, rx2, rd2, wk, wb, lp, bo, cot, cot_r, cb_x, cb_d, prob, psend, dl, kb
    )
    rx, rd = swap_edges(cx, cd)

    keep, send = head_weights(info, lev, h2, rx2, rd2, dl, gt, kc, kb)
    dz1, sx, sd, send = head_inputs(info, lev, dl, gt, rx, rd, wk, wb, sp1, (send,), (keep,))
    rx, rd = swap_edges(sx, sd)
    head_sum = TileSum("sum_head", info, True, keep, swap_section(send))
    s = head_sum.start(dz1)
    keep1, send1, token = weights(1, info, lev, h1, rx1, rd1, dz1, s)
    *s, send1 = head_sum.start(token, rx, rd, gate=(send1,))
    dz0, sx, sd = inputs(1, info, lev, dz1, rx, rd, w_own, w_other, sp0, (), tuple(s))
    rx, rd = swap_edges(sx, sd)
    sum1 = TileSum("sum_one", info, False, keep1, swap_section(send1))
    s = head_sum.start(dz0)
    s = s + sum1.start(*s)
    keep0, send0, token = weights(0, info, lev, features, rx0, rd0, dz0, s)
    *s, send0 = head_sum.start(token, rx, rd, gate=(send0,))
    sum0 = TileSum("sum_zero", info, False, keep0, swap_section(send0))
    s = tuple(s)
    s = tuple(s) + sum0.start(*s)
    feature_grad, token, psend = inputs(0, info, lev, dz0, rx, rd, w_own, w_other, None, (psend,), s)
    prob_r = swap_section(psend)
    done = (token,)
    while sum0.plan:
        s = sum0.start(*done)
        if len(sum0.plan) == 4:
            prob, boxo = place(info, prob, boxo, prob_r, s)
        for other in (head_sum, sum1):
            if other.plan:
                other.start(*s)
        done = ()
    head_done, l1, l0 = (jnp.concatenate(v.result(), axis=1) for v in (head_sum, sum1, sum0))

    mine_l = jnp.where(section == 0, l0, l1)
    other_l = swap_section(jnp.where(section == 0, l1, l0))
    towers = jnp.where(section == 0, jnp.stack([mine_l[:taps], other_l[:taps]]), jnp.stack([other_l[:taps], mine_l[:taps]]))
    biases = jnp.where(section == 0, jnp.stack([mine_l[taps], other_l[taps]]), jnp.stack([other_l[taps], mine_l[taps]]))
    end = 3 * kc
    box = head_done[end : end + 3 * kq].astype(F32)
    return (
        prob.transpose(0, 1, 3, 2),
        boxo.transpose(0, 2, 3, 1),
        feature_grad,
        towers.astype(F32).reshape(1, nt, 3, 3 * c, c),
        biases.astype(F32).reshape(1, nt, c),
        head_done[:end].astype(F32).reshape(3, kc, 3 * c).transpose(0, 2, 1),
        box[kb, :kc],
        box.reshape(3, kq, 3 * c)[:, :kb].transpose(0, 2, 1),
        box[kb, kp : kp + kb],
    )


def solution(mesh):
    in_specs = (
        P("section", None, "tile", None, None),
        P(),
        P("section", None, None, None, None),
        P("section", None, None),
        P(None, None, "section"),
        P("section"),
        P(None, None, "section"),
        P("section"),
        P(None, "tile", None, "section"),
        P(None, "tile", None, "section"),
    )
    out_specs = (
        P(None, "tile", None, "section"),
        P(None, "tile", None, "section"),
        P("section", None, "tile", None, None),
        P("section", None, None, None, None),
        P("section", None, None),
        P(None, None, "section"),
        P("section"),
        P(None, None, "section"),
        P("section"),
    )
    return jax.shard_map(on_device, mesh=mesh, in_specs=in_specs, out_specs=out_specs, check_vma=False)
```

```python
import functools

import jax
import jax.numpy as jnp
from jax import lax
from jax.experimental import pallas as pl
from jax.experimental.pallas import tpu as pltpu
from jax.sharding import PartitionSpec as P

BF = jnp.bfloat16
F32 = jnp.float32
LANES = 128


def cost(us):
    return pl.CostEstimate(flops=int(us * 2e9), bytes_accessed=0, transcendentals=0)


def ordered(kernel, inputs, after):
    def body(*refs):
        return kernel(*refs[:inputs], *refs[inputs + len(after) :])

    return body
SMEM = pl.BlockSpec(memory_space=pltpu.SMEM)
HBM = pl.BlockSpec(memory_space=pltpu.HBM)
ANY = pl.BlockSpec(memory_space=pl.ANY)


TOKEN = jax.ShapeDtypeStruct((8, LANES), F32)
TOKEN_SPEC = pl.BlockSpec((8, LANES), lambda *_: (0, 0))


def dot(a, b):
    return jnp.dot(a, b, preferred_element_type=F32)


def dot_nt(a, b):
    return lax.dot_general(a, b, (((1,), (1,)), ((), ())), preferred_element_type=F32)


def dot_tn(a, b):
    return lax.dot_general(a, b, (((0,), (0,)), ((), ())), preferred_element_type=F32)


def down(v):
    return jnp.concatenate([jnp.zeros_like(v[..., :1, :]), v[..., :-1, :]], axis=-2)


def up(v):
    return jnp.concatenate([v[..., 1:, :], jnp.zeros_like(v[..., :1, :])], axis=-2)


def keep_if(v, flag):
    return v * jnp.full((1, v.shape[-1]), flag, F32).astype(v.dtype)


def build(x, rows, e, b, before=None, after=None, taps=True):
    count = len(rows)
    width = rows[0]().shape[0]
    for q in range(-1, count + 1):
        if q < 0:
            get = before
        elif q < count:
            get = rows[q]
        else:
            get = after
        if get is None:
            dest = 0 if q < 0 else count - 1
            part = x.shape[1] // 3
            first = 0 if q < 0 else 2 * part
            x[dest * width : (dest + 1) * width, first : first + part] = jnp.zeros((width, part), x.dtype)
            continue
        v = get()
        p = jnp.concatenate([down(v), v, up(v)], axis=1) if taps else v
        n = p.shape[1]
        if 0 <= q < count:
            x[q * width : (q + 1) * width, n : 2 * n] = p
        if q + 1 < count:
            x[(q + 1) * width : (q + 2) * width, 0:n] = keep_if(p, e[b, q + 1])
        if q >= 1:
            x[(q - 1) * width : q * width, 2 * n : 3 * n] = keep_if(p, e[b, q])


class Borders:
    def __init__(self, info, lev, rows):
        self.info, self.lev, self.rows = info, lev, rows

    def __getitem__(self, at):
        b, i = at
        lines, count = self.lev.shape
        line = self.info[0] * (lines // 2) + b
        r = self.info[2] * self.rows + i
        same = self.lev[line, jnp.maximum(r - 1, 0)] == self.lev[line, jnp.minimum(r, count - 1)]
        return jnp.where(jnp.logical_and(same, jnp.logical_and(r > 0, r < count)), 1.0, 0.0)


def rows_of(ref, lead, count):
    return [functools.partial(lambda r: ref[lead + (r,)], r) for r in range(count)]


def pick_halo(info, rx, rd, hs, lead):
    @pl.when(info[1] == 0)
    def _():
        hs[0] = rd[lead]
        hs[1] = rx[lead]

    @pl.when(info[1] != 0)
    def _():
        hs[0] = rx[lead]
        hs[1] = rd[lead]


def put_edges(info, first, last, sx, sd, lead):
    @pl.when(info[1] == 0)
    def _():
        sx[lead] = last
        sd[lead] = first

    @pl.when(info[1] != 0)
    def _():
        sx[lead] = first
        sd[lead] = last


def start_weights(info, layer, own, other, wv, sem):
    for t in range(wv.shape[0]):

        @pl.when(info[0] == layer)
        def _():
            pltpu.make_async_copy(own.at[t], wv.at[t], sem.at[t]).start()

        @pl.when(info[0] != layer)
        def _():
            pltpu.make_async_copy(other.at[t], wv.at[t], sem.at[t]).start()


def wait_weights(own, wv, sem, t):
    for i in range(wv.shape[0]):

        @pl.when(t == i)
        def _():
            pltpu.make_async_copy(own.at[i], wv.at[i], sem.at[i]).wait()


def activate(z):
    sg = jax.nn.sigmoid(z)
    hv = z * sg
    return hv.astype(BF), (sg + hv * (1.0 - sg)).astype(BF)


def forward_kernel(layer, info, lev, h, own, other, bias, bias_r, hn, sp, zp, token, x, wv, sem):
    t, b = pl.program_id(0), pl.program_id(1)
    rows, width = h.shape[2], h.shape[3]
    e = Borders(info, lev, rows)

    @pl.when(jnp.logical_and(t == 0, b == 0))
    def _():
        start_weights(info, layer, own, other, wv, sem)

    build(x, rows_of(h, (0, 0), rows), e, b)

    @pl.when(b == 0)
    def _():
        wait_weights(own, wv, sem, t)

    c = h.shape[4]
    chosen = jnp.full((1, c), info[0] == layer, jnp.int32) != 0
    row = pl.ds(t, 1)
    z = dot(x[...], wv[t]) + jnp.where(chosen, bias[row, :c], bias_r[row, :c])
    hv, sv = activate(z)
    hn[0, 0] = hv.reshape(h.shape[2:])
    sp[0, 0] = sv.reshape(h.shape[2:])
    zp[0, 0, 0] = z[:width]
    zp[0, 0, 1] = z[(rows - 1) * width :]
    token[...] = jnp.zeros_like(token)


def forward(layer, info, lev, h, own, other, bias, bias_r, after=()):
    nb, nt, rows, width, c = h.shape
    row_spec = pl.BlockSpec((1, 1, rows, width, c), lambda t, b: (b, t, 0, 0, 0))
    taps = own.shape[1]
    return pl.pallas_call(
        ordered(functools.partial(forward_kernel, layer), 7, after),
        grid=(nt, nb),
        in_specs=[SMEM, SMEM, row_spec, HBM, HBM] + [pl.BlockSpec(bias.shape, lambda t, b: (0, 0))] * 2 + [ANY] * len(after),
        out_specs=[row_spec, row_spec, pl.BlockSpec((1, 1, 2, width, c), lambda t, b: (b, t, 0, 0, 0)), TOKEN_SPEC],
        out_shape=[jax.ShapeDtypeStruct(h.shape, BF)] * 2 + [jax.ShapeDtypeStruct((nb, nt, 2, width, c), F32), TOKEN],
        scratch_shapes=[
            pltpu.VMEM((rows * width, taps), BF),
            pltpu.VMEM((nt, taps, c), BF),
            pltpu.SemaphoreType.DMA((nt,)),
        ],
        compiler_params=pltpu.CompilerParams(vmem_limit_bytes=12 << 20),
        cost_estimate=cost(8),
        name=f"forward{layer}",
    )(info, lev, h, own, other, bias, bias_r, *after)


def edge_kernel(layer, rows, info, lev, zp, rx, rd, own, other, hin, sin, hn, sp, sx, sd, wv, sem):
    t, i = pl.program_id(0), pl.program_id(1)
    nb, width, c = zp.shape[0], zp.shape[3], zp.shape[4]
    nt, taps = wv.shape[0], wv.shape[2]
    e = Borders(info, lev, rows)

    def copies(ref):
        for tt in range(nt):
            for ii in range(2):
                yield tt, ii, pltpu.make_async_copy(ref.at[tt, pl.ds(2 * ii * taps, taps)], wv.at[tt, ii], sem.at[tt, ii])

    @pl.when(jnp.logical_and(t == 0, i == 0))
    def _():
        @pl.when(info[0] == layer)
        def _():
            for _, _, copy in copies(own):
                copy.start()

        @pl.when(info[0] != layer)
        def _():
            for _, _, copy in copies(other):
                copy.start()

    for tt, ii, copy in copies(own):

        @pl.when(jnp.logical_and(t == tt, i == ii))
        def _():
            copy.wait()

    from_x = (info[1] == 0) == (i == 1)
    edge = i * rows
    for b in range(nb):
        v = jnp.where(jnp.full((1, c), from_x.astype(jnp.int32), jnp.int32) != 0, rx[b, 0].astype(F32), rd[b, 0].astype(F32))
        p = jnp.concatenate([down(v), v, up(v)], axis=1) * e[b, edge]
        z = zp[b, 0, 0] + dot(p.astype(BF), wv[t, i])
        hv, sv = activate(z)
        hn[b, 0, 0] = hv
        sp[b, 0, 0] = sv

        @pl.when(from_x)
        def _():
            sx[b, 0] = hv

        @pl.when(jnp.logical_not(from_x))
        def _():
            sd[b, 0] = hv


def edges(layer, info, lev, zp, rx, rd, own, other, hn, sp):
    nb, nt, rows, width, c = hn.shape
    taps = own.shape[1] // 3
    row_spec = pl.BlockSpec((nb, 1, 1, width, c), lambda t, i: (0, t, i * (rows - 1), 0, 0))
    edge_spec = pl.BlockSpec((nb, 1, width, c), lambda t, i: (0, t, 0, 0))
    edge = jax.ShapeDtypeStruct((nb, nt, width, c), BF)
    return pl.pallas_call(
        functools.partial(edge_kernel, layer, rows),
        grid=(nt, 2),
        in_specs=[
            SMEM,
            SMEM,
            pl.BlockSpec((nb, 1, 1, width, c), lambda t, i: (0, t, i, 0, 0)),
            edge_spec,
            edge_spec,
            HBM,
            HBM,
            HBM,
            HBM,
        ],
        out_specs=[row_spec, row_spec, edge_spec, edge_spec],
        out_shape=[jax.ShapeDtypeStruct(hn.shape, BF)] * 2 + [edge] * 2,
        input_output_aliases={7: 0, 8: 1},
        scratch_shapes=[pltpu.VMEM((nt, 2, taps, c), BF), pltpu.SemaphoreType.DMA((nt, 2))],
        compiler_params=pltpu.CompilerParams(vmem_limit_bytes=6 << 20),
        cost_estimate=cost(4),
        name=f"edges{layer}",
    )(info, lev, zp, rx, rd, own, other, hn, sp)


def tap_columns(ref, b, e, rows, width, gt):
    n = ref(0).shape[0]
    lane = lax.broadcasted_iota(jnp.int32, (n, width), 1)
    for s, k in ((rows, 0), (rows + 1, 0), (0, 1), (rows + 1, 1), (0, 2), (1, 2)):
        gt[0, 3 * k * n : 3 * (k + 1) * n, s * width : (s + 1) * width] = jnp.zeros((3 * n, width), gt.dtype)
    for r in range(rows):
        g = ref(r)
        left = jnp.where(lane < width - 1, pltpu.roll(g, width - 1, 1), 0.0)
        right = jnp.where(lane > 0, pltpu.roll(g, 1, 1), 0.0)
        for k in range(3):
            flag = e[b, r] if k == 0 else e[b, r + 1] if k == 2 else None
            for j, v in enumerate((left, g, right)):
                v = v if flag is None else v * flag
                at = (3 * k + j) * n
                gt[0, at : at + n, (r + k) * width : (r + k + 1) * width] = v.astype(gt.dtype)


def pack_rows(hx, rows, width, hs, row):
    hx[0:width] = hs[0]
    for r in range(rows):
        hx[(r + 1) * width : (r + 2) * width] = row(r)
    hx[(rows + 1) * width :] = hs[1]


def head_row(logit, cot, cot_r, kc, kp):
    gap = jnp.zeros((kp - kc, logit.shape[1]), F32)
    p = jax.nn.sigmoid(logit)
    q = p * (1.0 - p)
    d = [cot.astype(F32) * q[:kc], gap, cot_r.astype(F32) * q[kp : kp + kc], gap]
    return p[:kc].astype(BF), p[kp : kp + kc].astype(BF), jnp.concatenate(d, axis=0).astype(BF).T


def side(v, lane, j):
    width = v.shape[-1]
    if j == 0:
        return jnp.where(lane > 0, pltpu.roll(v, 1, 1), 0.0)
    if j == 2:
        return jnp.where(lane < width - 1, pltpu.roll(v, width - 1, 1), 0.0)
    return v


def head_kernel(
    info, lev, h, wk, wb, cb, cot, gb, cot_r,
    prob, psend, dl, gt, cb_x, cb_d, lp, bo, x, hx, lg, y,
):
    b = pl.program_id(0)
    rows, width, c = h.shape[2], h.shape[3], h.shape[4]
    kc, kb = cot.shape[2], gb.shape[1]
    kp, kq = wk.shape[1] // 2, wb.shape[0] // 18
    e = Borders(info, lev, rows)

    taps = 3 * c
    build(x, rows_of(h, (0, 0), rows), e, b)
    lg[...] = dot_nt(wk[0], x[:, :taps])
    lg[...] += dot_nt(wk[1], x[:, taps : 2 * taps])
    lg[...] += dot_nt(wk[2], x[:, 2 * taps :])

    def row(r, _):
        at = pl.ds(pl.multiple_of(r * width, width), width)
        prob[0, r], psend[0, r, :kc], dl[0, r] = head_row(lg[:, at] + cb[: 2 * kp], cot[0, r], cot_r[0, r, :kc], kc, kp)
        return 0

    lax.fori_loop(0, rows, row, 0)
    lp[0, 0] = lg[:, :width] + cb[: 2 * kp]
    lp[0, 1] = lg[:, (rows - 1) * width :] + cb[: 2 * kp]
    for r in range(rows):
        hx[r * width : (r + 1) * width] = h[0, 1, r]
    y[...] = dot_nt(wb[...], hx[...])
    n = 2 * kq
    lane = lax.broadcasted_iota(jnp.int32, (n, width), 1)
    for r in range(rows):
        v = cb[2 * kp : 2 * kp + n]
        for j in range(3):
            s = y[(3 + j) * n : (4 + j) * n, r * width : (r + 1) * width]
            if r > 0:
                s = s + y[j * n : (j + 1) * n, (r - 1) * width : r * width] * e[b, r]
            if r < rows - 1:
                s = s + y[(6 + j) * n : (7 + j) * n, (r + 1) * width : (r + 2) * width] * e[b, r + 1]
            v = v + side(s, lane, j)
        bo[0, r] = v
        rest = jnp.zeros((kp - kc - kb, width), F32)
        psend[0, r, kc:] = jnp.concatenate([v[kq : kq + kb], rest], axis=0).astype(BF)
    small = jnp.zeros((kq - kb, width), F32)
    g = gb[0].astype(F32)

    def columns(r):
        return jnp.concatenate([g[:, r], small, cot_r[0, r, kc:].astype(F32)[:kb], small], axis=0)

    tap_columns(columns, b, e, rows, width, gt)
    for i in range(2):
        s = i * (rows + 1)
        db = dot_tn(gt[0, :, s * width : (s + 1) * width], wb[...]).astype(BF)

        @pl.when((info[1] == 0) == (i == 1))
        def _():
            cb_x[0] = db

        @pl.when((info[1] == 0) == (i == 0))
        def _():
            cb_d[0] = db


def head(info, lev, h, wk, wb, cb, cot, gb, cot_r, after=()):
    nb, nt, rows, width, c = h.shape
    kc, kb, kp2, kq2 = cot.shape[2], gb.shape[1], wk.shape[1], wb.shape[0] // 9
    batches = cot.shape[0]
    m = rows * width
    ext = (rows + 2) * width

    def at_b(shape):
        return pl.BlockSpec((1,) + shape, lambda b, info: (b,) + (0,) * len(shape))

    def at_all(shape):
        return pl.BlockSpec((1,) + shape, lambda b, info: (info[0] * nb + b,) + (0,) * len(shape))

    def whole(shape):
        return pl.BlockSpec(shape, lambda b, info: (0,) * len(shape), pipeline_mode=pl.Buffered(1))

    return pl.pallas_call(
        ordered(head_kernel, 9, after),
        grid_spec=pltpu.PrefetchScalarGridSpec(
            num_scalar_prefetch=1,
            grid=(nb,),
            in_specs=[
                SMEM,
                at_b((nt, rows, width, c)),
                whole(wk.shape),
                whole(wb.shape),
                whole(cb.shape),
                at_all((rows, kc, width)),
                at_all((kb, rows, width)),
                at_b((rows, kp2 // 2, width)),
            ]
            + [ANY] * len(after),
            out_specs=[
                at_all((rows, kc, width)),
                at_b((rows, kp2 // 2, width)),
                at_b((rows, width, kp2)),
                at_b((9 * kq2, ext)),
                at_b((width, c)),
                at_b((width, c)),
                at_b((2, kp2, width)),
                at_b((rows, kq2, width)),
            ],
            scratch_shapes=[
                pltpu.VMEM((m, 9 * c), BF),
                pltpu.VMEM((m, c), BF),
                pltpu.VMEM((kp2, m), F32),
                pltpu.VMEM((9 * kq2, m), F32),
            ],
        ),
        out_shape=[
            jax.ShapeDtypeStruct((batches, rows, kc, width), BF),
            jax.ShapeDtypeStruct((nb, rows, kp2 // 2, width), BF),
            jax.ShapeDtypeStruct((nb, rows, width, kp2), BF),
            jax.ShapeDtypeStruct((nb, 9 * kq2, ext), BF),
            jax.ShapeDtypeStruct((nb, width, c), BF),
            jax.ShapeDtypeStruct((nb, width, c), BF),
            jax.ShapeDtypeStruct((nb, 2, kp2, width), F32),
            jax.ShapeDtypeStruct((nb, rows, kq2, width), F32),
        ],
        compiler_params=pltpu.CompilerParams(vmem_limit_bytes=17 << 20),
        cost_estimate=cost(14),
        name="head",
    )(info, lev, h, wk, wb, cb, cot, gb, cot_r, *after)


def head_edge_kernel(
    info, lev, rx, rd, wk, wb, lp, bo, cot, cot_r, cb_x, cb_d, prob_i, psend_i, dl_i,
    prob, psend, dl, boxo, cx, cd, hs, ds, bs, bx,
):
    i = pl.program_id(0)
    nb, nt, width, c = rx.shape
    kc, kb, rows = cot.shape[2], boxo.shape[1], boxo.shape[2]
    kp, kq = wk.shape[1] // 2, bo.shape[2] // 2
    taps = 3 * c
    n = 2 * kq
    e = Borders(info, lev, rows)
    edge = i * rows
    from_x = (info[1] == 0) == (i == 1)

    @pl.when(from_x)
    def _():
        hs[...] = rx[...]

    @pl.when(jnp.logical_not(from_x))
    def _():
        hs[...] = rd[...]

    p = []
    for b in range(nb):
        v = hs[b, 0]
        p.append(keep_if(jnp.concatenate([down(v), v, up(v)], axis=1), e[b, edge]))
    logit = dot_nt(wk[0], jnp.concatenate(p, axis=0))
    lane = lax.broadcasted_iota(jnp.int32, (n, width), 1)
    for b in range(nb):
        lg = logit[:, b * width : (b + 1) * width] + lp[b, 0]
        prob[b, 0], psend[b, 0, :kc], d = head_row(lg, cot[b, 0], cot_r[b, 0, :kc], kc, kp)
        dl[b, 0] = d
        ds[b * width : (b + 1) * width, :] = d
        y = dot_nt(wb[...], hs[b, 1]) * e[b, edge]
        v = bo[b, i * (rows - 1)]
        for j in range(3):
            v = v + side(y[j * n : (j + 1) * n, :], lane, j)
        bs[b, i] = v
        gap = jnp.zeros((kp - kc - kb, width), F32)
        psend[b, 0, kc:] = jnp.concatenate([v[kq : kq + kb], gap], axis=0).astype(BF)

    @pl.when(i == 1)
    def _():
        for b in range(nb):
            for r in range(rows):
                v = bs[b, 0] if r == 0 else bs[b, 1] if r == rows - 1 else bo[b, r]
                bx[:, r, :] = v
            boxo[b] = bx[:kb].astype(BF)

    s = dot(ds[...], wk[0]).reshape(nb, width, taps)
    dc = up(s[:, :, :c]) + s[:, :, c : 2 * c] + down(s[:, :, 2 * c :])
    for b in range(nb):
        v = keep_if(dc[b].astype(BF), e[b, edge])

        @pl.when(from_x)
        def _():
            cx[b, 0] = v
            cx[b, 1] = cb_x[b]

        @pl.when(jnp.logical_not(from_x))
        def _():
            cd[b, 0] = v
            cd[b, 1] = cb_d[b]


def head_edges(info, lev, rx, rd, wk, wb, lp, bo, cot, cot_r, cb_x, cb_d, prob, psend, dl, kb):
    nb, nt, width, c = rx.shape
    rows = cot.shape[1]
    kc, kp2, kq2 = cot.shape[2], wk.shape[1], bo.shape[2]

    def whole(shape):
        return pl.BlockSpec(shape, lambda i, info: (0,) * len(shape), pipeline_mode=pl.Buffered(1))

    def at_i(shape):
        return pl.BlockSpec(shape, lambda i, info: (0, i) + (0,) * (len(shape) - 2))

    def edge_of(shape):
        return pl.BlockSpec(shape, lambda i, info: (0, i * (rows - 1)) + (0,) * (len(shape) - 2))

    def edge_all(shape):
        return pl.BlockSpec(shape, lambda i, info: (info[0], i * (rows - 1)) + (0,) * (len(shape) - 2))

    edge = jax.ShapeDtypeStruct((nb, nt, width, c), BF)
    arrays = (prob, psend, dl)
    return pl.pallas_call(
        head_edge_kernel,
        grid_spec=pltpu.PrefetchScalarGridSpec(
            num_scalar_prefetch=1,
            grid=(2,),
            in_specs=[
                SMEM,
                whole(rx.shape),
                whole(rd.shape),
                pl.BlockSpec((1,) + wk.shape[1:], lambda i, info: (2 * i, 0, 0)),
                pl.BlockSpec((3 * kq2, c), lambda i, info: (2 * i, 0)),
                at_i((nb, 1, kp2, width)),
                whole(bo.shape),
                edge_all((nb, 1, kc, width)),
                edge_of((nb, 1, kp2 // 2, width)),
                whole(cb_x.shape),
                whole(cb_d.shape),
            ]
            + [HBM] * len(arrays),
            out_specs=[
                edge_all((nb, 1, kc, width)),
                edge_of((nb, 1, kp2 // 2, width)),
                edge_of((nb, 1, width, kp2)),
                pl.BlockSpec((nb, kb, rows, width), lambda i, info: (info[0], 0, 0, 0)),
                pl.BlockSpec(rx.shape, lambda i, info: (0, 0, 0, 0)),
                pl.BlockSpec(rx.shape, lambda i, info: (0, 0, 0, 0)),
            ],
            scratch_shapes=[
                pltpu.VMEM(rx.shape, BF),
                pltpu.VMEM((nb * width, kp2), BF),
                pltpu.VMEM((nb, 2, kq2, width), F32),
                pltpu.VMEM((kq2, rows, width), F32),
            ],
        ),
        out_shape=[jax.ShapeDtypeStruct(v.shape, BF) for v in arrays]
        + [jax.ShapeDtypeStruct((cot.shape[0], kb, rows, width), BF)]
        + [edge, edge],
        input_output_aliases={12 + i: i for i in range(len(arrays))},
        compiler_params=pltpu.CompilerParams(vmem_limit_bytes=8 << 20),
        cost_estimate=cost(6),
        name="head_edges",
    )(info, lev, rx, rd, wk, wb, lp, bo, cot, cot_r, cb_x, cb_d, *arrays)


def head_weights_kernel(info, lev, h, rx, rd, dl, gt, own, other, token, x, hx, acc, accb, small, hs, *, kc, kb):
    b, nb = pl.program_id(0), pl.num_programs(0)
    rows, width, c = h.shape[2], h.shape[3], h.shape[4]
    token[...] = jnp.zeros_like(token)
    kp, kq = dl.shape[-1] // 2, accb.shape[0] // 18
    taps = 3 * c
    e = Borders(info, lev, rows)
    pick_halo(info, rx, rd, hs, (0, 0))
    build(x, rows_of(h, (0, 0), rows), e, b, lambda: hs[0], lambda: hs[1])
    pick_halo(info, rx, rd, hs, (0, 1))
    pack_rows(hx, rows, width, hs, lambda r: h[0, 1, r])
    g = dl[0].reshape(rows * width, 2 * kp)

    @pl.when(b == 0)
    def _():
        acc[...] = jnp.zeros_like(acc)
        accb[...] = jnp.zeros_like(accb)
        small[...] = jnp.zeros_like(small)

    acc[...] += dot_tn(g, x[...])
    accb[...] += dot(gt[0], hx[...])
    small[:, : 2 * kp] += jnp.sum(g.astype(F32), axis=0, keepdims=True)
    ones = jnp.ones((8, gt.shape[2]), BF)
    s = dot_nt(ones, gt[0, 8 * kq : 10 * kq, :])[:1]
    small[:, 2 * kp :] += jnp.concatenate([s, jnp.zeros((1, LANES - 2 * kq), F32)], axis=1)

    def fill(ref, a):
        for k in range(3):
            ref[k * kc : (k + 1) * kc, :] = acc[a * kp : a * kp + kc, k * taps : (k + 1) * taps]
            at = 3 * kc + k * kq
            for j in range(3):
                first = (3 * k + j) * 2 * kq + a * kq
                ref[at : at + kq, j * c : (j + 1) * c] = accb[first : first + kq, :]
        end = 3 * (kc + kq)
        if end < ref.shape[0]:
            ref[end:, :] = jnp.zeros((ref.shape[0] - end, taps), F32)
        at = 3 * kc + kb
        ref[at : at + 1, :kp] = small[:, a * kp : (a + 1) * kp]
        ref[at : at + 1, kp : kp + LANES] = pltpu.roll(small[:, 2 * kp :], (LANES - a * kq) % LANES, 1)

    @pl.when(b == nb - 1)
    def _():
        fill(own, 1)
        other[...] = own[...].astype(BF)
        fill(own, 0)


def head_weights(info, lev, h, rx, rd, dl, gt, kc, kb, after=()):
    nb, nt, rows, width, c = h.shape
    kp2 = dl.shape[-1]
    kq2 = gt.shape[1] // 9
    m = rows * width
    size = -(-3 * (kc + kq2 // 2) // LANES) * LANES

    def at_b(shape):
        return pl.BlockSpec((1,) + shape, lambda b: (b,) + (0,) * len(shape))

    def whole(shape):
        return pl.BlockSpec(shape, lambda b: (0,) * len(shape), pipeline_mode=pl.Buffered(1))

    return pl.pallas_call(
        ordered(functools.partial(head_weights_kernel, kc=kc, kb=kb), 7, after),
        grid=(nb,),
        in_specs=[
            SMEM,
            SMEM,
            at_b((nt, rows, width, c)),
            at_b((nt, width, c)),
            at_b((nt, width, c)),
            at_b((rows, width, kp2)),
            at_b(gt.shape[1:]),
        ]
        + [ANY] * len(after),
        out_specs=[whole((size, 3 * c)), whole((size, 3 * c)), TOKEN_SPEC],
        out_shape=[jax.ShapeDtypeStruct((size, 3 * c), F32), jax.ShapeDtypeStruct((size, 3 * c), BF), TOKEN],
        scratch_shapes=[
            pltpu.VMEM((m, 9 * c), BF),
            pltpu.VMEM(((rows + 2) * width, c), BF),
            pltpu.VMEM((kp2, 9 * c), F32),
            pltpu.VMEM((9 * kq2, c), F32),
            pltpu.VMEM((1, kp2 + LANES), F32),
            pltpu.VMEM((2, width, c), BF),
        ],
        compiler_params=pltpu.CompilerParams(vmem_limit_bytes=21 << 20),
        cost_estimate=cost(12),
        name="head_weights",
    )(info, lev, h, rx, rd, dl, gt, *after)


def head_inputs_kernel(info, lev, dl, gt, rx, rd, wk, wb, sp, *rest):
    dz, sx, sd, token, *_, x, hs = rest
    token[...] = jnp.zeros_like(token)
    b = pl.program_id(0)
    rows, width, c = sp.shape[2], sp.shape[3], sp.shape[4]
    kp2 = dl.shape[-1]
    taps = 3 * c
    e = Borders(info, lev, rows)
    build(x, rows_of(dl, (0,), rows), e, b, taps=False)
    s = dot(x[:, kp2 : 2 * kp2], wk[1])
    s = s + dot(x[:, :kp2], wk[2])
    s = s + dot(x[:, 2 * kp2 :], wk[0])
    s = s.reshape(rows, width, taps)
    dc = up(s[:, :, :c]) + s[:, :, c : 2 * c] + down(s[:, :, 2 * c :])
    db = dot_tn(gt[0, :, width : (rows + 1) * width], wb[...]).reshape(rows, width, c)
    for t, dh in ((0, dc), (1, db)):
        pick_halo(info, rx, rd, hs, (0, t))
        for r in range(rows):
            v = dh[r]
            if r == 0:
                v = v + hs[0].astype(F32)
            if r == rows - 1:
                v = v + hs[1].astype(F32)
            dz[0, t, r] = (v * sp[0, t, r].astype(F32)).astype(BF)
        put_edges(info, dz[0, t, 0], dz[0, t, rows - 1], sx, sd, (0, t))


def head_inputs(info, lev, dl, gt, rx, rd, wk, wb, sp, gate, after=()):
    nb, nt, rows, width, c = sp.shape
    kp2 = dl.shape[-1]
    m = rows * width

    def at_b(shape):
        return pl.BlockSpec((1,) + shape, lambda b: (b,) + (0,) * len(shape))

    def whole(shape):
        return pl.BlockSpec(shape, lambda b: (0,) * len(shape), pipeline_mode=pl.Buffered(1))

    return pl.pallas_call(
        ordered(head_inputs_kernel, 9, gate + after),
        grid=(nb,),
        in_specs=[
            SMEM,
            SMEM,
            at_b((rows, width, kp2)),
            at_b(gt.shape[1:]),
            at_b((nt, width, c)),
            at_b((nt, width, c)),
            whole(wk.shape),
            whole(wb.shape),
            at_b((nt, rows, width, c)),
        ]
        + [ANY] * len(gate + after),
        out_specs=[at_b((nt, rows, width, c)), at_b((nt, width, c)), at_b((nt, width, c)), TOKEN_SPEC] + [ANY] * len(gate),
        out_shape=[
            jax.ShapeDtypeStruct(sp.shape, BF),
            jax.ShapeDtypeStruct((nb, nt, width, c), BF),
            jax.ShapeDtypeStruct((nb, nt, width, c), BF),
        ]
        + [TOKEN]
        + [jax.ShapeDtypeStruct(v.shape, v.dtype) for v in gate],
        input_output_aliases={9 + k: 4 + k for k in range(len(gate))},
        scratch_shapes=[pltpu.VMEM((m, 3 * kp2), BF), pltpu.VMEM((2, width, c), BF)],
        compiler_params=pltpu.CompilerParams(vmem_limit_bytes=14 << 20),
        cost_estimate=cost(9),
        name="head_inputs",
    )(info, lev, dl, gt, rx, rd, wk, wb, sp, *gate, *after)


def weights_kernel(info, lev, h, rx, rd, dz, keep, send, token, x, acc, bias, hs):
    t, b, nb = pl.program_id(0), pl.program_id(1), pl.num_programs(1)
    rows, width, c = h.shape[2], h.shape[3], h.shape[4]
    e = Borders(info, lev, rows)
    pick_halo(info, rx, rd, hs, (0, 0))
    build(x, rows_of(h, (0, 0), rows), e, b, lambda: hs[0], lambda: hs[1])
    g = dz[0, 0].reshape(rows * width, c)
    part = dot_tn(x[...], g)
    total = jnp.sum(g.astype(F32), axis=0, keepdims=True)
    taps = acc.shape[0]

    @pl.when(b == 0)
    def _():
        acc[...] = part
        bias[...] = total

    @pl.when(b != 0)
    def _():
        acc[...] += part
        bias[...] += total

    token[...] = jnp.zeros_like(token)
    for i, out in enumerate((send, keep)):

        @pl.when(jnp.logical_and(b == nb - 1, t == i))
        def _():
            out[:taps, :] = acc[...].astype(out.dtype)
            out[taps:, :] = jnp.broadcast_to(bias[...].astype(out.dtype), (out.shape[0] - taps, c))


def weights(layer, info, lev, h, rx, rd, dz, after=()):
    nb, nt, rows, width, c = h.shape

    def tower(t, info):
        return jnp.where(t == 0, 1 - info[0], info[0])

    row_spec = pl.BlockSpec((1, 1, rows, width, c), lambda t, b, info: (b, tower(t, info), 0, 0, 0))
    edge_spec = pl.BlockSpec((1, 1, width, c), lambda t, b, info: (b, tower(t, info), 0, 0))
    taps = 9 * c
    return pl.pallas_call(
        ordered(weights_kernel, 6, after),
        grid_spec=pltpu.PrefetchScalarGridSpec(
            num_scalar_prefetch=1,
            grid=(nt, nb),
            in_specs=[SMEM, row_spec, edge_spec, edge_spec, row_spec] + [ANY] * len(after),
            out_specs=[pl.BlockSpec((taps + LANES, c), lambda t, b, info: (0, 0))] * 2 + [TOKEN_SPEC],
            scratch_shapes=[
                pltpu.VMEM((rows * width, taps), BF),
                pltpu.VMEM((taps, c), F32),
                pltpu.VMEM((1, c), F32),
                pltpu.VMEM((2, width, c), BF),
            ],
        ),
        out_shape=[jax.ShapeDtypeStruct((taps + LANES, c), F32), jax.ShapeDtypeStruct((taps + LANES, c), BF), TOKEN],
        compiler_params=pltpu.CompilerParams(vmem_limit_bytes=14 << 20),
        cost_estimate=cost(8),
        name=f"weights{layer}",
    )(info, lev, h, rx, rd, dz, *after)


def inputs_kernel(layer, info, lev, dz, rx, rd, own, other, *rest):
    if layer:
        sp, out, token, sx, sd, x, wv, wt, hs, sem = rest
    else:
        out, token, *_, x, wv, wt, hs, sem = rest
    token[...] = jnp.zeros_like(token)
    t, b = pl.program_id(0), pl.program_id(1)
    rows, width, c = dz.shape[2], dz.shape[3], dz.shape[4]
    e = Borders(info, lev, rows)

    @pl.when(jnp.logical_and(t == 0, b == 0))
    def _():
        start_weights(info, layer, own, other, wv, sem)

    pick_halo(info, rx, rd, hs, (0, 0))
    build(x, rows_of(dz, (0, 0), rows), e, b, lambda: hs[0], lambda: hs[1])

    @pl.when(b == 0)
    def _():
        wait_weights(own, wv, sem, t)
        for i in range(9):
            wt[:, (8 - i) * c : (9 - i) * c] = wv[t, i * c : (i + 1) * c, :]

    dh = dot_nt(x[...], wt[...]).astype(BF)
    if not layer:
        out[0, 0] = dh.reshape(rows, width, c)
        return
    dz_next = (dh.astype(F32).reshape(rows, width, c) * sp[0, 0].astype(F32)).astype(BF)
    out[0, 0] = dz_next
    put_edges(info, dz_next[0], dz_next[rows - 1], sx, sd, (0, 0))


def inputs(layer, info, lev, dz, rx, rd, own, other, sp=None, gate=(), after=()):
    nb, nt, rows, width, c = dz.shape
    row_spec = pl.BlockSpec((1, 1, rows, width, c), lambda t, b: (b, t, 0, 0, 0))
    edge_spec = pl.BlockSpec((1, 1, width, c), lambda t, b: (b, t, 0, 0))
    edge = jax.ShapeDtypeStruct((nb, nt, width, c), BF)
    taps = own.shape[1]
    return pl.pallas_call(
        ordered(functools.partial(inputs_kernel, layer), 8 if layer else 7, gate + after),
        grid=(nt, nb),
        in_specs=[SMEM, SMEM, row_spec, edge_spec, edge_spec, HBM, HBM] + ([row_spec] if layer else []) + [ANY] * len(gate + after),
        out_specs=[row_spec, TOKEN_SPEC] + ([edge_spec, edge_spec] if layer else []) + [ANY] * len(gate),
        out_shape=[jax.ShapeDtypeStruct(dz.shape, BF)]
        + [TOKEN]
        + ([edge, edge] if layer else [])
        + [jax.ShapeDtypeStruct(v.shape, v.dtype) for v in gate],
        input_output_aliases={7 + k: 2 + k for k in range(len(gate))},
        scratch_shapes=[
            pltpu.VMEM((rows * width, taps), BF),
            pltpu.VMEM((nt, taps, c), BF),
            pltpu.VMEM((c, taps), BF),
            pltpu.VMEM((2, width, c), BF),
            pltpu.SemaphoreType.DMA((nt,)),
        ],
        compiler_params=pltpu.CompilerParams(vmem_limit_bytes=13 << 20),
        cost_estimate=cost(9),
        name=f"inputs{layer}",
    )(info, lev, dz, rx, rd, own, other, *([sp] if layer else []), *gate, *after)


def swap_section(value):
    return lax.ppermute(value, "section", [(0, 1), (1, 0)])


def swap_edges(sx, sd):
    count = lax.axis_size("tile")
    even = [p for i in range(0, count - 1, 2) for p in ((i, i + 1), (i + 1, i))]
    odd = [p for i in range(1, count - 1, 2) for p in ((i, i + 1), (i + 1, i))]
    return lax.ppermute(sx, "tile", even), lax.ppermute(sd, "tile", odd)


def combine_kernel(plan, info, *refs):
    ins, outs = list(refs[: sum(sum(p) for p in plan)]), refs[sum(sum(p) for p in plan) :]
    for counts, out in zip(plan, outs):
        lanes = out.shape[1] // len(counts)
        for i, count in enumerate(counts):
            terms = [ins.pop(0)[...].astype(F32) for _ in range(count)]
            out[:, i * lanes : (i + 1) * lanes] = functools.reduce(jnp.add, terms).astype(out.dtype)


def combine(name, info, shape, outs, gate=(), after=()):
    rows, lanes = shape
    views = [v for parts in outs for terms in parts for v in terms]

    def spec(view):
        return pl.BlockSpec(shape, lambda i, info: (view[1](info), view[2]))

    plan = [[len(terms) for terms in parts] for parts in outs]
    return pl.pallas_call(
        ordered(functools.partial(combine_kernel, plan), 1 + len(views), gate + after),
        grid_spec=pltpu.PrefetchScalarGridSpec(
            num_scalar_prefetch=1,
            grid=(1,),
            in_specs=[spec(v) for v in views] + [ANY] * len(gate + after),
            out_specs=[pl.BlockSpec((rows, lanes * len(parts)), lambda i, info: (0, 0)) for parts in outs]
            + [ANY] * len(gate),
        ),
        out_shape=[jax.ShapeDtypeStruct((rows, lanes * len(parts)), BF) for parts in outs]
        + [jax.ShapeDtypeStruct(v.shape, v.dtype) for v in gate],
        input_output_aliases={1 + len(views) + k: len(outs) + k for k in range(len(gate))},
        compiler_params=pltpu.CompilerParams(vmem_limit_bytes=7 << 20),
        cost_estimate=cost(2),
        name=name,
    )(info, *[v[0] for v in views], *gate, *after)


def join_kernel(bits, split, info, *refs):
    n = len(bits)
    for i, bit in enumerate(bits):
        cur, got = refs[2 * i], refs[2 * i + 1]
        outs = refs[2 * n :] if split else refs[2 * n + i : 2 * n + i + 1]
        m, lanes = cur.shape[0], cur.shape[1] // len(outs)
        mine = (info[2] >> bit) & 1
        for j, out in enumerate(outs):
            at = slice(j * lanes, (j + 1) * lanes)

            @pl.when(mine == 0)
            def _():
                out[:m, :] = cur[:, at]
                out[m:, :] = got[:, at]

            @pl.when(mine != 0)
            def _():
                out[:m, :] = got[:, at]
                out[m:, :] = cur[:, at]


def join(name, info, bits, pairs, split=False, after=()):
    arrays = [v for pair in pairs for v in pair]
    shapes = [(2 * cur.shape[0], cur.shape[1]) for cur, _ in pairs]
    if split:
        shapes = [(shapes[0][0], shapes[0][1] // 2)] * 2

    def whole(shape):
        return pl.BlockSpec(shape, lambda i, info: (0, 0))

    return pl.pallas_call(
        ordered(functools.partial(join_kernel, bits, split), 1 + len(arrays), after),
        grid_spec=pltpu.PrefetchScalarGridSpec(
            num_scalar_prefetch=1,
            grid=(1,),
            in_specs=[whole(v.shape) for v in arrays] + [ANY] * len(after),
            out_specs=[whole(s) for s in shapes],
        ),
        out_shape=[jax.ShapeDtypeStruct(s, BF) for s in shapes],
        compiler_params=pltpu.CompilerParams(vmem_limit_bytes=7 << 20),
        cost_estimate=cost(2),
        name=name,
    )(info, *arrays, *after)


def relay_kernel(*refs):
    del refs


def relay(name, gate, after):
    return pl.pallas_call(
        ordered(relay_kernel, 0, gate + after),
        in_specs=[ANY] * len(gate + after),
        out_specs=[ANY] * len(gate),
        out_shape=[jax.ShapeDtypeStruct(v.shape, v.dtype) for v in gate],
        input_output_aliases={k: k for k in range(len(gate))},
        compiler_params=pltpu.CompilerParams(vmem_limit_bytes=1 << 20),
        cost_estimate=cost(1),
        name=name,
    )(*gate, *after)


class TileSum:
    def __init__(self, name, info, whole, *terms):
        self.name, self.info = name, info
        rows, lanes = terms[0].shape
        self.shape = (rows, lanes // 2)
        self.parts = [[(v, lambda info: 0, i) for v in terms] for i in range(2)]
        self.count = lax.axis_size("tile")
        bits = self.count.bit_length() - 1
        near = [(0, 1), (1, 0)]
        self.plan = [("halve", step) for step in near]
        if whole or bits > 4:
            self.plan += [("add", (bit,)) for bit in range(2, bits)]
        else:
            self.plan += [("halve", (bit,)) for bit in range(2, bits)]
            self.plan += [("double", (bit,)) for bit in reversed(range(2, bits))]
        self.plan += [("double", step) for step in reversed(near)]
        self.step = 0
        self.sends = None

    def exchange(self, value, bit):
        return lax.ppermute(value, "tile", [(i, i ^ (1 << bit)) for i in range(self.count)])

    def start(self, *after, gate=()):
        kind, bits = self.plan.pop(0)
        name = f"{self.name}_{self.step}"
        self.step += 1
        if kind == "halve":
            rows, lanes = self.shape
            self.shape = (rows // 2, lanes)
            bit_of = bits * 2 if len(bits) == 1 else bits

            def half(view, bit, other):
                array, row, lane = view
                return array, lambda info: 2 * row(info) + (((info[2] >> bit) & 1) ^ other), lane

            sent = [[half(v, bit, 1) for v in terms] for terms, bit in zip(self.parts, bit_of)]
            self.parts = [[half(v, bit, 0) for v in terms] for terms, bit in zip(self.parts, bit_of)]
            outs = [sent] if len(bits) == 1 else [[terms] for terms in sent]
            sends = combine(name, self.info, self.shape, outs, gate, after)
        elif kind == "add" or self.kind != "double":
            outs = [self.parts] if len(bits) == 1 else [[terms] for terms in self.parts]
            sends = combine(name, self.info, self.shape, outs, gate, after)
        else:
            sends = join(name, self.info, self.bits, self.pairs, len(bits) > len(self.pairs), after)
        passed = tuple(sends[len(bits) :])
        sends = tuple(sends[: len(bits)])
        self.kind, self.bits, self.sends = kind, bits, sends
        got = [self.exchange(v, bit) for v, bit in zip(sends, bits)]
        if kind == "halve":
            lane = (lambda i: i) if len(bits) == 1 else (lambda i: 0)
            pick = (lambda i: got[0]) if len(bits) == 1 else (lambda i: got[i])
            self.parts = [terms + [(pick(i), lambda info: 0, lane(i))] for i, terms in enumerate(self.parts)]
        elif kind == "add":
            self.parts = [[(v, lambda info: 0, i) for v in (sends[0], got[0])] for i in range(2)]
        else:
            self.pairs = list(zip(sends, got))
        return sends + passed

    def result(self, *after):
        return join(f"{self.name}_{self.step}", self.info, self.bits, self.pairs, False, after)


def pick_kernel(info, cot, gb, out):
    rows, kc, kb = cot.shape[1], cot.shape[2], gb.shape[1]
    g = gb[0].astype(F32)
    gap = jnp.zeros((out.shape[2] - kc - kb, out.shape[3]), F32)
    for r in range(rows):
        out[0, r] = jnp.concatenate([cot[0, r].astype(F32), g[:, r], gap], axis=0).astype(BF)


def pick(info, cot, gb, nb, kp, after=()):
    def at_all(shape):
        return pl.BlockSpec((1,) + shape[1:], lambda b, info: ((1 - info[0]) * nb + b,) + (0,) * (len(shape) - 1))

    shape = (nb, cot.shape[1], kp, cot.shape[3])
    return pl.pallas_call(
        ordered(pick_kernel, 3, after),
        grid_spec=pltpu.PrefetchScalarGridSpec(
            num_scalar_prefetch=1,
            grid=(nb,),
            in_specs=[at_all(cot.shape), at_all(gb.shape)] + [ANY] * len(after),
            out_specs=pl.BlockSpec((1,) + shape[1:], lambda b, info: (b, 0, 0, 0)),
        ),
        out_shape=jax.ShapeDtypeStruct(shape, BF),
        compiler_params=pltpu.CompilerParams(vmem_limit_bytes=8 << 20),
        cost_estimate=cost(2),
        name="pick",
    )(info, cot, gb, *after)


def gather_kernel(tower, classes, boxes, out):
    out[...] = jnp.zeros_like(out)
    nt, c = tower.shape[1], tower.shape[2]
    out[:nt, :c] = tower[0]
    out[nt : nt + 1, : classes.shape[0]] = classes[...].reshape(1, -1)
    out[nt + 1 : nt + 2, : boxes.shape[0]] = boxes[...].reshape(1, -1)


def gather(tower, classes, boxes, lanes):
    return pl.pallas_call(
        gather_kernel,
        out_shape=jax.ShapeDtypeStruct((8, lanes), F32),
        compiler_params=pltpu.CompilerParams(vmem_limit_bytes=1 << 20),
        cost_estimate=cost(1),
        name="gather",
    )(tower, classes, boxes)


def pick_weights_kernel(thin, small, out):
    gap = jnp.zeros((out.shape[1] - thin.shape[1] - small.shape[1], out.shape[2]), F32)
    out[0] = jnp.concatenate([thin[0].astype(F32), small[0].astype(F32), gap], axis=0).astype(BF)


def pick_weights(thin, small, kp, after=()):
    def at_k(shape):
        return pl.BlockSpec((1,) + shape[1:], lambda k: (k, 0, 0))

    shape = (thin.shape[0], kp, thin.shape[2])
    return pl.pallas_call(
        ordered(pick_weights_kernel, 2, after),
        grid=(shape[0],),
        in_specs=[at_k(thin.shape), at_k(small.shape)] + [ANY] * len(after),
        out_specs=at_k(shape),
        out_shape=jax.ShapeDtypeStruct(shape, BF),
        compiler_params=pltpu.CompilerParams(vmem_limit_bytes=6 << 20),
        cost_estimate=cost(2),
        name="pick_weights",
    )(thin, small, *after)


def pack_kernel(own, other, bias, bias_r, wk, wb, cb, *, kc, kb, kq, towers):
    k = pl.program_id(0)
    kp = own.shape[1]
    c = wb.shape[1]
    gap = jnp.zeros((kp - kc, wk.shape[2]), F32)
    for half, v in enumerate((own, other)):
        wk[0, half * kp : (half + 1) * kp, :] = jnp.concatenate([v[0].astype(F32)[:kc], gap], axis=0).astype(BF)
    u, v = own[0].astype(F32)[kc : kc + kb], other[0].astype(F32)[kc : kc + kb]
    small = jnp.zeros((kq - kb, c), F32)
    for j in range(3):
        at = slice(j * c, (j + 1) * c)
        rows = jnp.concatenate([u[:, at], small, v[:, at], small], axis=0).astype(BF)
        wb[pl.ds(pl.multiple_of((3 * k + j) * 2 * kq, 2 * kq), 2 * kq), :] = rows

    @pl.when(k == 0)
    def _():
        wide = jnp.zeros((1, kp - kc), F32)
        thin = jnp.zeros((1, kq - kb), F32)
        rest = jnp.zeros((1, cb.shape[0] - 2 * kp - kq - kb), F32)
        classes, boxes = slice(towers, towers + 1), slice(towers + 1, towers + 2)
        parts = [bias[classes, :kc], wide, bias_r[classes, :kc], wide, bias[boxes, :kb], thin, bias_r[boxes, :kb], rest]
        cb[...] = jnp.broadcast_to(jnp.concatenate(parts, axis=1), (cb.shape[1], cb.shape[0])).T


def pack(own, other, bias, bias_r, kc, kb, kq, towers, after=()):
    k, kp, c3 = own.shape
    at_k = pl.BlockSpec((1, kp, c3), lambda k: (k, 0, 0))

    def whole(shape):
        return pl.BlockSpec(shape, lambda k: (0,) * len(shape))

    shapes = [(k, 2 * kp, c3), (18 * kq, c3 // 3), (2 * kp + LANES, LANES)]
    return pl.pallas_call(
        ordered(functools.partial(pack_kernel, kc=kc, kb=kb, kq=kq, towers=towers), 4, after),
        grid=(k,),
        in_specs=[at_k, at_k, whole(bias.shape), whole(bias.shape)] + [ANY] * len(after),
        out_specs=[pl.BlockSpec((1,) + shapes[0][1:], lambda k: (k, 0, 0)), whole(shapes[1]), whole(shapes[2])],
        out_shape=[jax.ShapeDtypeStruct(s, t) for s, t in zip(shapes, (BF, BF, F32))],
        compiler_params=pltpu.CompilerParams(vmem_limit_bytes=10 << 20),
        cost_estimate=cost(3),
        name="pack",
    )(own, other, bias, bias_r, *after)


def place_kernel(info, prob_i, box_i, got, prob, box, token, bx):
    rows, kc, kb = prob.shape[1], prob.shape[2], box.shape[1]
    for r in range(rows):
        prob[0, r] = got[0, r, :kc]
        bx[:, r, :] = got[0, r, kc:].astype(F32)[:kb]
    box[0] = bx[...].astype(BF)
    token[...] = jnp.zeros_like(token)


def place(info, prob, box, got, after=()):
    nb = got.shape[0]

    def at_all(shape):
        return pl.BlockSpec((1,) + shape[1:], lambda b, info: ((1 - info[0]) * nb + b,) + (0,) * (len(shape) - 1))

    return pl.pallas_call(
        ordered(place_kernel, 4, after),
        grid_spec=pltpu.PrefetchScalarGridSpec(
            num_scalar_prefetch=1,
            grid=(nb,),
            in_specs=[HBM, HBM, pl.BlockSpec((1,) + got.shape[1:], lambda b, info: (b, 0, 0, 0))] + [ANY] * len(after),
            out_specs=[at_all(prob.shape), at_all(box.shape), TOKEN_SPEC],
            scratch_shapes=[pltpu.VMEM(box.shape[1:], F32)],
        ),
        out_shape=[jax.ShapeDtypeStruct(v.shape, BF) for v in (prob, box)] + [TOKEN],
        input_output_aliases={1: 0, 2: 1},
        compiler_params=pltpu.CompilerParams(vmem_limit_bytes=8 << 20),
        cost_estimate=cost(2),
        name="place",
    )(info, prob, box, got, *after)


def after(value, *others):
    return lax.optimization_barrier((value,) + others)[0]


def on_device(
    features,
    levels,
    tower_weight,
    tower_bias,
    class_weight,
    class_bias,
    box_weight,
    box_bias,
    class_cotangent,
    box_cotangent,
):
    section = lax.axis_index("section")
    tile = lax.axis_index("tile")
    nb, nt, rows, width, c = features.shape
    kc, kb = class_weight.shape[-1], box_weight.shape[-1]
    kp = -(-kc // LANES) * LANES
    kq = -(-kb // 8) * 8
    taps = 9 * c
    lev = levels
    info = jnp.stack([section, tile % 2, tile]).astype(jnp.int32)
    even = tile % 2 == 0

    sx = lax.dynamic_index_in_dim(features, jnp.where(even, rows - 1, 0), 2, False)
    sd = lax.dynamic_index_in_dim(features, jnp.where(even, 0, rows - 1), 2, False)
    rx0, rd0 = swap_edges(sx, sd)
    bias = gather(tower_bias, class_bias, box_bias, kp)
    bias_r = swap_section(bias)
    w_own = tower_weight.reshape(nt, taps, c)
    w_other = swap_section(w_own)

    h1, sp0, zp, token = forward(0, info, lev, features, w_own, w_other, bias, bias_r, (sx, sd))
    thin, small = class_weight.transpose(0, 2, 1), box_weight.transpose(0, 2, 1)
    cot, gb = class_cotangent.transpose(0, 1, 3, 2), box_cotangent.transpose(0, 3, 1, 2)
    w_out = pick_weights(thin, small, kp, (token,))
    w_out_r = swap_section(w_out)
    cot_r = swap_section(pick(info, cot, gb, nb, kp, (token,)))
    h1, sp0, sx, sd = edges(0, info, lev, zp, rx0, rd0, w_own, w_other, h1, sp0)
    rx1, rd1 = swap_edges(sx, sd)
    h2, sp1, zp, _ = forward(1, info, lev, h1, w_own, w_other, bias, bias_r)
    wk, wb, cb = pack(w_out, w_out_r, bias, bias_r, kc, kb, kq, nt, (zp,))
    h2, sp1, sx, sd = edges(1, info, lev, zp, rx1, rd1, w_own, w_other, h2, sp1)
    rx2, rd2 = swap_edges(sx, sd)
    prob, psend, dl, gt, cb_x, cb_d, lp, bo = head(info, lev, h2, wk, wb, cb, cot, gb, cot_r)
    prob, psend, dl, boxo, cx, cd = head_edges(
        info, lev, rx2, rd2, wk, wb, lp, bo, cot, cot_r, cb_x, cb_d, prob, psend, dl, kb
    )
    rx, rd = swap_edges(cx, cd)

    keep, send, token = head_weights(info, lev, h2, rx2, rd2, dl, gt, kc, kb)
    (send,) = relay("send_head", (send,), (token, rx, rd))
    head_sum = TileSum("sum_head", info, True, keep, swap_section(send))
    s = head_sum.start()
    dz1, sx, sd, token = head_inputs(info, lev, dl, gt, rx, rd, wk, wb, sp1, (), s)
    rx, rd = swap_edges(sx, sd)
    s = head_sum.start(token)
    keep1, send1, token = weights(1, info, lev, h1, rx1, rd1, dz1, s)
    *s, send1 = head_sum.start(token, rx, rd, gate=(send1,))
    dz0, token, sx, sd = inputs(1, info, lev, dz1, rx, rd, w_own, w_other, sp0, (), tuple(s))
    *s, psend = head_sum.start(token, gate=(psend,))
    prob_r = swap_section(psend)
    sum1 = TileSum("sum_one", info, False, keep1, swap_section(send1))
    s = tuple(s)
    s = s + sum1.start(*s)
    keep0, send0, token = weights(0, info, lev, features, rx0, rd0, dz0, s)
    *s, send0 = sum1.start(token, gate=(send0,))
    sum0 = TileSum("sum_zero", info, False, keep0, swap_section(send0))
    s = tuple(s) + sum0.start(*s)
    prob, boxo, token = place(info, prob, boxo, prob_r, tuple(s))
    *s, sx, sd = sum0.start(token, gate=(sx, sd))
    rx, rd = swap_edges(sx, sd)
    s = tuple(s)
    s = s + sum1.start(*s)
    s = s + sum0.start(*s)
    s = s + head_sum.start(*s)
    feature_grad, token = inputs(0, info, lev, dz0, rx, rd, w_own, w_other, None, (), s)
    done = (token,)
    while sum0.plan:
        s = sum0.start(*done)
        done = ()
        for other in (head_sum, sum1):
            if other.plan:
                other.start(*s)
    head_done, l1, l0 = (jnp.concatenate(v.result(), axis=1) for v in (head_sum, sum1, sum0))

    mine_l = jnp.where(section == 0, l0, l1)
    other_l = swap_section(jnp.where(section == 0, l1, l0))
    towers = jnp.where(section == 0, jnp.stack([mine_l[:taps], other_l[:taps]]), jnp.stack([other_l[:taps], mine_l[:taps]]))
    biases = jnp.where(section == 0, jnp.stack([mine_l[taps], other_l[taps]]), jnp.stack([other_l[taps], mine_l[taps]]))
    end = 3 * kc
    box = head_done[end : end + 3 * kq].astype(F32)
    return (
        prob.transpose(0, 1, 3, 2),
        boxo.transpose(0, 2, 3, 1),
        feature_grad,
        towers.astype(F32).reshape(1, nt, 3, 3 * c, c),
        biases.astype(F32).reshape(1, nt, c),
        head_done[:end].astype(F32).reshape(3, kc, 3 * c).transpose(0, 2, 1),
        box[kb, :kc],
        box.reshape(3, kq, 3 * c)[:, :kb].transpose(0, 2, 1),
        box[kb, kp : kp + kb],
    )


def solution(mesh):
    in_specs = (
        P("section", None, "tile", None, None),
        P(),
        P("section", None, None, None, None),
        P("section", None, None),
        P(None, None, "section"),
        P("section"),
        P(None, None, "section"),
        P("section"),
        P(None, "tile", None, "section"),
        P(None, "tile", None, "section"),
    )
    out_specs = (
        P(None, "tile", None, "section"),
        P(None, "tile", None, "section"),
        P("section", None, "tile", None, None),
        P("section", None, None, None, None),
        P("section", None, None),
        P(None, None, "section"),
        P("section"),
        P(None, None, "section"),
        P("section"),
    )
    return jax.shard_map(on_device, mesh=mesh, in_specs=in_specs, out_specs=out_specs, check_vma=False)
```

```python
import functools

import jax
import jax.numpy as jnp
from jax import lax
from jax.experimental import pallas as pl
from jax.experimental.pallas import tpu as pltpu
from jax.sharding import PartitionSpec as P

BF = jnp.bfloat16
F32 = jnp.float32
LANES = 128


def cost(us):
    return pl.CostEstimate(flops=int(us * 2e9), bytes_accessed=0, transcendentals=0)


def ordered(kernel, inputs, after):
    def body(*refs):
        return kernel(*refs[:inputs], *refs[inputs + len(after) :])

    return body
SMEM = pl.BlockSpec(memory_space=pltpu.SMEM)
HBM = pl.BlockSpec(memory_space=pltpu.HBM)
ANY = pl.BlockSpec(memory_space=pl.ANY)


TOKEN = jax.ShapeDtypeStruct((8, LANES), F32)
TOKEN_SPEC = pl.BlockSpec((8, LANES), lambda *_: (0, 0))


def dot(a, b):
    return jnp.dot(a, b, preferred_element_type=F32)


def dot_nt(a, b):
    return lax.dot_general(a, b, (((1,), (1,)), ((), ())), preferred_element_type=F32)


def dot_tn(a, b):
    return lax.dot_general(a, b, (((0,), (0,)), ((), ())), preferred_element_type=F32)


def down(v):
    return jnp.concatenate([jnp.zeros_like(v[..., :1, :]), v[..., :-1, :]], axis=-2)


def up(v):
    return jnp.concatenate([v[..., 1:, :], jnp.zeros_like(v[..., :1, :])], axis=-2)


def keep_if(v, flag):
    return v * jnp.full((1, v.shape[-1]), flag, F32).astype(v.dtype)


def build(x, rows, e, b, before=None, after=None, taps=True):
    count = len(rows)
    width = rows[0]().shape[0]
    for q in range(-1, count + 1):
        if q < 0:
            get = before
        elif q < count:
            get = rows[q]
        else:
            get = after
        if get is None:
            dest = 0 if q < 0 else count - 1
            part = x.shape[1] // 3
            first = 0 if q < 0 else 2 * part
            x[dest * width : (dest + 1) * width, first : first + part] = jnp.zeros((width, part), x.dtype)
            continue
        v = get()
        p = jnp.concatenate([down(v), v, up(v)], axis=1) if taps else v
        n = p.shape[1]
        if 0 <= q < count:
            x[q * width : (q + 1) * width, n : 2 * n] = p
        if q + 1 < count:
            x[(q + 1) * width : (q + 2) * width, 0:n] = keep_if(p, e[b, q + 1])
        if q >= 1:
            x[(q - 1) * width : q * width, 2 * n : 3 * n] = keep_if(p, e[b, q])


class Borders:
    def __init__(self, info, lev, rows):
        self.info, self.lev, self.rows = info, lev, rows

    def __getitem__(self, at):
        b, i = at
        lines, count = self.lev.shape
        line = self.info[0] * (lines // 2) + b
        r = self.info[2] * self.rows + i
        same = self.lev[line, jnp.maximum(r - 1, 0)] == self.lev[line, jnp.minimum(r, count - 1)]
        return jnp.where(jnp.logical_and(same, jnp.logical_and(r > 0, r < count)), 1.0, 0.0)


def rows_of(ref, lead, count):
    return [functools.partial(lambda r: ref[lead + (r,)], r) for r in range(count)]


def pick_halo(info, rx, rd, hs, lead):
    @pl.when(info[1] == 0)
    def _():
        hs[0] = rd[lead]
        hs[1] = rx[lead]

    @pl.when(info[1] != 0)
    def _():
        hs[0] = rx[lead]
        hs[1] = rd[lead]


def put_edges(info, first, last, sx, sd, lead):
    @pl.when(info[1] == 0)
    def _():
        sx[lead] = last
        sd[lead] = first

    @pl.when(info[1] != 0)
    def _():
        sx[lead] = first
        sd[lead] = last


def start_weights(info, layer, own, other, wv, sem):
    for t in range(wv.shape[0]):

        @pl.when(info[0] == layer)
        def _():
            pltpu.make_async_copy(own.at[t], wv.at[t], sem.at[t]).start()

        @pl.when(info[0] != layer)
        def _():
            pltpu.make_async_copy(other.at[t], wv.at[t], sem.at[t]).start()


def wait_weights(own, wv, sem, t):
    for i in range(wv.shape[0]):

        @pl.when(t == i)
        def _():
            pltpu.make_async_copy(own.at[i], wv.at[i], sem.at[i]).wait()


def activate(z):
    sg = jax.nn.sigmoid(z)
    hv = z * sg
    return hv.astype(BF), (sg + hv * (1.0 - sg)).astype(BF)


def forward_kernel(layer, info, lev, h, own, other, bias, bias_r, hn, sp, zp, token, x, wv, sem):
    t, b = pl.program_id(0), pl.program_id(1)
    rows, width = h.shape[2], h.shape[3]
    e = Borders(info, lev, rows)

    @pl.when(jnp.logical_and(t == 0, b == 0))
    def _():
        start_weights(info, layer, own, other, wv, sem)

    build(x, rows_of(h, (0, 0), rows), e, b)

    @pl.when(b == 0)
    def _():
        wait_weights(own, wv, sem, t)

    c = h.shape[4]
    chosen = jnp.full((1, c), info[0] == layer, jnp.int32) != 0
    row = pl.ds(t, 1)
    z = dot(x[...], wv[t]) + jnp.where(chosen, bias[row, :c], bias_r[row, :c])
    hv, sv = activate(z)
    hn[0, 0] = hv.reshape(h.shape[2:])
    sp[0, 0] = sv.reshape(h.shape[2:])
    zp[0, 0, 0] = z[:width]
    zp[0, 0, 1] = z[(rows - 1) * width :]
    token[...] = jnp.zeros_like(token)


def forward(layer, info, lev, h, own, other, bias, bias_r, after=()):
    nb, nt, rows, width, c = h.shape
    row_spec = pl.BlockSpec((1, 1, rows, width, c), lambda t, b: (b, t, 0, 0, 0))
    taps = own.shape[1]
    return pl.pallas_call(
        ordered(functools.partial(forward_kernel, layer), 7, after),
        grid=(nt, nb),
        in_specs=[SMEM, SMEM, row_spec, HBM, HBM] + [pl.BlockSpec(bias.shape, lambda t, b: (0, 0))] * 2 + [ANY] * len(after),
        out_specs=[row_spec, row_spec, pl.BlockSpec((1, 1, 2, width, c), lambda t, b: (b, t, 0, 0, 0)), TOKEN_SPEC],
        out_shape=[jax.ShapeDtypeStruct(h.shape, BF)] * 2 + [jax.ShapeDtypeStruct((nb, nt, 2, width, c), F32), TOKEN],
        scratch_shapes=[
            pltpu.VMEM((rows * width, taps), BF),
            pltpu.VMEM((nt, taps, c), BF),
            pltpu.SemaphoreType.DMA((nt,)),
        ],
        compiler_params=pltpu.CompilerParams(vmem_limit_bytes=12 << 20),
        cost_estimate=cost(8),
        name=f"forward{layer}",
    )(info, lev, h, own, other, bias, bias_r, *after)


def edge_kernel(layer, rows, info, lev, zp, rx, rd, own, other, hin, sin, hn, sp, sx, sd, wv, sem):
    i = pl.program_id(0)
    nb, nt, width, c = zp.shape[0], zp.shape[1], zp.shape[3], zp.shape[4]
    taps = wv.shape[2]
    e = Borders(info, lev, rows)

    def copies(ref, ii):
        for t in range(nt):
            yield pltpu.make_async_copy(ref.at[t, pl.ds(2 * ii * taps, taps)], wv.at[ii, t], sem.at[ii, t])

    for ii in range(2):
        for ref, chosen in ((own, info[0] == layer), (other, info[0] != layer)):

            @pl.when(jnp.logical_and(i == 0, chosen))
            def _():
                for copy in copies(ref, ii):
                    copy.start()

    from_x = (info[1] == 0) == (i == 1)
    edge = i * rows
    mask = jnp.full((1, c), from_x.astype(jnp.int32), jnp.int32) != 0
    parts = []
    for t in range(nt):
        p = []
        for b in range(nb):
            v = jnp.where(mask, rx[b, t].astype(F32), rd[b, t].astype(F32))
            p.append((jnp.concatenate([down(v), v, up(v)], axis=1) * e[b, edge]).astype(BF))
        parts.append(jnp.concatenate(p, axis=0))

    for ii in range(2):

        @pl.when(i == ii)
        def _():
            for copy in copies(own, ii):
                copy.wait()

    for t in range(nt):
        z = dot(parts[t], wv[i, t])
        for b in range(nb):
            hv, sv = activate(zp[b, t, 0] + z[b * width : (b + 1) * width])
            hn[b, t, 0] = hv
            sp[b, t, 0] = sv

            @pl.when(from_x)
            def _():
                sx[b, t] = hv

            @pl.when(jnp.logical_not(from_x))
            def _():
                sd[b, t] = hv


def edges(layer, info, lev, zp, rx, rd, own, other, hn, sp):
    nb, nt, rows, width, c = hn.shape
    taps = own.shape[1] // 3
    row_spec = pl.BlockSpec((nb, nt, 1, width, c), lambda i: (0, 0, i * (rows - 1), 0, 0))
    edge_spec = pl.BlockSpec((nb, nt, width, c), lambda i: (0, 0, 0, 0))
    edge = jax.ShapeDtypeStruct((nb, nt, width, c), BF)
    return pl.pallas_call(
        functools.partial(edge_kernel, layer, rows),
        grid=(2,),
        in_specs=[
            SMEM,
            SMEM,
            pl.BlockSpec((nb, nt, 1, width, c), lambda i: (0, 0, i, 0, 0)),
            edge_spec,
            edge_spec,
            HBM,
            HBM,
            HBM,
            HBM,
        ],
        out_specs=[row_spec, row_spec, edge_spec, edge_spec],
        out_shape=[jax.ShapeDtypeStruct(hn.shape, BF)] * 2 + [edge] * 2,
        input_output_aliases={7: 0, 8: 1},
        scratch_shapes=[pltpu.VMEM((2, nt, taps, c), BF), pltpu.SemaphoreType.DMA((2, nt))],
        compiler_params=pltpu.CompilerParams(vmem_limit_bytes=8 << 20),
        cost_estimate=cost(4),
        name=f"edges{layer}",
    )(info, lev, zp, rx, rd, own, other, hn, sp)


def tap_columns(ref, b, e, rows, width, gt):
    n = ref(0).shape[0]
    lane = lax.broadcasted_iota(jnp.int32, (n, width), 1)
    for s, k in ((rows, 0), (rows + 1, 0), (0, 1), (rows + 1, 1), (0, 2), (1, 2)):
        gt[0, 3 * k * n : 3 * (k + 1) * n, s * width : (s + 1) * width] = jnp.zeros((3 * n, width), gt.dtype)
    for r in range(rows):
        g = ref(r)
        left = jnp.where(lane < width - 1, pltpu.roll(g, width - 1, 1), 0.0)
        right = jnp.where(lane > 0, pltpu.roll(g, 1, 1), 0.0)
        for k in range(3):
            flag = e[b, r] if k == 0 else e[b, r + 1] if k == 2 else None
            for j, v in enumerate((left, g, right)):
                v = v if flag is None else v * flag
                at = (3 * k + j) * n
                gt[0, at : at + n, (r + k) * width : (r + k + 1) * width] = v.astype(gt.dtype)


def pack_rows(hx, rows, width, hs, row):
    hx[0:width] = hs[0]
    for r in range(rows):
        hx[(r + 1) * width : (r + 2) * width] = row(r)
    hx[(rows + 1) * width :] = hs[1]


def head_row(logit, cot, cot_r, kc, kp):
    gap = jnp.zeros((kp - kc, logit.shape[1]), F32)
    p = jax.nn.sigmoid(logit)
    q = p * (1.0 - p)
    d = [cot.astype(F32) * q[:kc], gap, cot_r.astype(F32) * q[kp : kp + kc], gap]
    return p[:kc].astype(BF), p[kp : kp + kc].astype(BF), jnp.concatenate(d, axis=0).astype(BF).T


def side(v, lane, j):
    width = v.shape[-1]
    if j == 0:
        return jnp.where(lane > 0, pltpu.roll(v, 1, 1), 0.0)
    if j == 2:
        return jnp.where(lane < width - 1, pltpu.roll(v, width - 1, 1), 0.0)
    return v


def head_kernel(
    info, lev, h, wk, wb, cb, cot, gb, cot_r,
    prob, psend, dl, gt, cb_x, cb_d, lp, bo, x, hx, lg, y,
):
    b = pl.program_id(0)
    rows, width, c = h.shape[2], h.shape[3], h.shape[4]
    kc, kb = cot.shape[2], gb.shape[1]
    kp, kq = wk.shape[1] // 2, wb.shape[0] // 18
    e = Borders(info, lev, rows)

    taps = 3 * c
    build(x, rows_of(h, (0, 0), rows), e, b)
    lg[...] = dot_nt(wk[0], x[:, :taps])
    lg[...] += dot_nt(wk[1], x[:, taps : 2 * taps])
    lg[...] += dot_nt(wk[2], x[:, 2 * taps :])

    def row(r, _):
        at = pl.ds(pl.multiple_of(r * width, width), width)
        prob[0, r], psend[0, r, :kc], dl[0, r] = head_row(lg[:, at] + cb[: 2 * kp], cot[0, r], cot_r[0, r, :kc], kc, kp)
        return 0

    lax.fori_loop(0, rows, row, 0)
    lp[0, 0] = lg[:, :width] + cb[: 2 * kp]
    lp[0, 1] = lg[:, (rows - 1) * width :] + cb[: 2 * kp]
    for r in range(rows):
        hx[r * width : (r + 1) * width] = h[0, 1, r]
    y[...] = dot_nt(wb[...], hx[...])
    n = 2 * kq
    lane = lax.broadcasted_iota(jnp.int32, (n, width), 1)
    for r in range(rows):
        v = cb[2 * kp : 2 * kp + n]
        for j in range(3):
            s = y[(3 + j) * n : (4 + j) * n, r * width : (r + 1) * width]
            if r > 0:
                s = s + y[j * n : (j + 1) * n, (r - 1) * width : r * width] * e[b, r]
            if r < rows - 1:
                s = s + y[(6 + j) * n : (7 + j) * n, (r + 1) * width : (r + 2) * width] * e[b, r + 1]
            v = v + side(s, lane, j)
        bo[0, r] = v
        rest = jnp.zeros((kp - kc - kb, width), F32)
        psend[0, r, kc:] = jnp.concatenate([v[kq : kq + kb], rest], axis=0).astype(BF)
    small = jnp.zeros((kq - kb, width), F32)
    g = gb[0].astype(F32)

    def columns(r):
        return jnp.concatenate([g[:, r], small, cot_r[0, r, kc:].astype(F32)[:kb], small], axis=0)

    tap_columns(columns, b, e, rows, width, gt)
    for i in range(2):
        s = i * (rows + 1)
        db = dot_tn(gt[0, :, s * width : (s + 1) * width], wb[...]).astype(BF)

        @pl.when((info[1] == 0) == (i == 1))
        def _():
            cb_x[0] = db

        @pl.when((info[1] == 0) == (i == 0))
        def _():
            cb_d[0] = db


def head(info, lev, h, wk, wb, cb, cot, gb, cot_r, after=()):
    nb, nt, rows, width, c = h.shape
    kc, kb, kp2, kq2 = cot.shape[2], gb.shape[1], wk.shape[1], wb.shape[0] // 9
    batches = cot.shape[0]
    m = rows * width
    ext = (rows + 2) * width

    def at_b(shape):
        return pl.BlockSpec((1,) + shape, lambda b, info: (b,) + (0,) * len(shape))

    def at_all(shape):
        return pl.BlockSpec((1,) + shape, lambda b, info: (info[0] * nb + b,) + (0,) * len(shape))

    def whole(shape):
        return pl.BlockSpec(shape, lambda b, info: (0,) * len(shape), pipeline_mode=pl.Buffered(1))

    return pl.pallas_call(
        ordered(head_kernel, 9, after),
        grid_spec=pltpu.PrefetchScalarGridSpec(
            num_scalar_prefetch=1,
            grid=(nb,),
            in_specs=[
                SMEM,
                at_b((nt, rows, width, c)),
                whole(wk.shape),
                whole(wb.shape),
                whole(cb.shape),
                at_all((rows, kc, width)),
                at_all((kb, rows, width)),
                at_b((rows, kp2 // 2, width)),
            ]
            + [ANY] * len(after),
            out_specs=[
                at_all((rows, kc, width)),
                at_b((rows, kp2 // 2, width)),
                at_b((rows, width, kp2)),
                at_b((9 * kq2, ext)),
                at_b((width, c)),
                at_b((width, c)),
                at_b((2, kp2, width)),
                at_b((rows, kq2, width)),
            ],
            scratch_shapes=[
                pltpu.VMEM((m, 9 * c), BF),
                pltpu.VMEM((m, c), BF),
                pltpu.VMEM((kp2, m), F32),
                pltpu.VMEM((9 * kq2, m), F32),
            ],
        ),
        out_shape=[
            jax.ShapeDtypeStruct((batches, rows, kc, width), BF),
            jax.ShapeDtypeStruct((nb, rows, kp2 // 2, width), BF),
            jax.ShapeDtypeStruct((nb, rows, width, kp2), BF),
            jax.ShapeDtypeStruct((nb, 9 * kq2, ext), BF),
            jax.ShapeDtypeStruct((nb, width, c), BF),
            jax.ShapeDtypeStruct((nb, width, c), BF),
            jax.ShapeDtypeStruct((nb, 2, kp2, width), F32),
            jax.ShapeDtypeStruct((nb, rows, kq2, width), F32),
        ],
        compiler_params=pltpu.CompilerParams(vmem_limit_bytes=17 << 20),
        cost_estimate=cost(14),
        name="head",
    )(info, lev, h, wk, wb, cb, cot, gb, cot_r, *after)


def head_edge_kernel(
    info, lev, rx, rd, wk, wb, lp, bo, cot, cot_r, cb_x, cb_d, prob_i, psend_i, dl_i,
    prob, psend, dl, boxo, cx, cd, hs, ds, bs, bx,
):
    i = pl.program_id(0)
    nb, nt, width, c = rx.shape
    kc, kb, rows = cot.shape[2], boxo.shape[1], boxo.shape[2]
    kp, kq = wk.shape[1] // 2, bo.shape[2] // 2
    taps = 3 * c
    n = 2 * kq
    e = Borders(info, lev, rows)
    edge = i * rows
    from_x = (info[1] == 0) == (i == 1)

    @pl.when(from_x)
    def _():
        hs[...] = rx[...]

    @pl.when(jnp.logical_not(from_x))
    def _():
        hs[...] = rd[...]

    p = []
    for b in range(nb):
        v = hs[b, 0]
        p.append(keep_if(jnp.concatenate([down(v), v, up(v)], axis=1), e[b, edge]))
    logit = dot_nt(wk[0], jnp.concatenate(p, axis=0))
    lane = lax.broadcasted_iota(jnp.int32, (n, width), 1)
    for b in range(nb):
        lg = logit[:, b * width : (b + 1) * width] + lp[b, 0]
        prob[b, 0], psend[b, 0, :kc], d = head_row(lg, cot[b, 0], cot_r[b, 0, :kc], kc, kp)
        dl[b, 0] = d
        ds[b * width : (b + 1) * width, :] = d
        y = dot_nt(wb[...], hs[b, 1]) * e[b, edge]
        v = bo[b, i * (rows - 1)]
        for j in range(3):
            v = v + side(y[j * n : (j + 1) * n, :], lane, j)
        bs[b, i] = v
        gap = jnp.zeros((kp - kc - kb, width), F32)
        psend[b, 0, kc:] = jnp.concatenate([v[kq : kq + kb], gap], axis=0).astype(BF)

    @pl.when(i == 1)
    def _():
        for b in range(nb):
            for r in range(rows):
                v = bs[b, 0] if r == 0 else bs[b, 1] if r == rows - 1 else bo[b, r]
                bx[:, r, :] = v
            boxo[b] = bx[:kb].astype(BF)

    s = dot(ds[...], wk[0]).reshape(nb, width, taps)
    dc = up(s[:, :, :c]) + s[:, :, c : 2 * c] + down(s[:, :, 2 * c :])
    for b in range(nb):
        v = keep_if(dc[b].astype(BF), e[b, edge])

        @pl.when(from_x)
        def _():
            cx[b, 0] = v
            cx[b, 1] = cb_x[b]

        @pl.when(jnp.logical_not(from_x))
        def _():
            cd[b, 0] = v
            cd[b, 1] = cb_d[b]


def head_edges(info, lev, rx, rd, wk, wb, lp, bo, cot, cot_r, cb_x, cb_d, prob, psend, dl, kb):
    nb, nt, width, c = rx.shape
    rows = cot.shape[1]
    kc, kp2, kq2 = cot.shape[2], wk.shape[1], bo.shape[2]

    def whole(shape):
        return pl.BlockSpec(shape, lambda i, info: (0,) * len(shape), pipeline_mode=pl.Buffered(1))

    def at_i(shape):
        return pl.BlockSpec(shape, lambda i, info: (0, i) + (0,) * (len(shape) - 2))

    def edge_of(shape):
        return pl.BlockSpec(shape, lambda i, info: (0, i * (rows - 1)) + (0,) * (len(shape) - 2))

    def edge_all(shape):
        return pl.BlockSpec(shape, lambda i, info: (info[0], i * (rows - 1)) + (0,) * (len(shape) - 2))

    edge = jax.ShapeDtypeStruct((nb, nt, width, c), BF)
    arrays = (prob, psend, dl)
    return pl.pallas_call(
        head_edge_kernel,
        grid_spec=pltpu.PrefetchScalarGridSpec(
            num_scalar_prefetch=1,
            grid=(2,),
            in_specs=[
                SMEM,
                whole(rx.shape),
                whole(rd.shape),
                pl.BlockSpec((1,) + wk.shape[1:], lambda i, info: (2 * i, 0, 0)),
                pl.BlockSpec((3 * kq2, c), lambda i, info: (2 * i, 0)),
                at_i((nb, 1, kp2, width)),
                whole(bo.shape),
                edge_all((nb, 1, kc, width)),
                edge_of((nb, 1, kp2 // 2, width)),
                whole(cb_x.shape),
                whole(cb_d.shape),
            ]
            + [HBM] * len(arrays),
            out_specs=[
                edge_all((nb, 1, kc, width)),
                edge_of((nb, 1, kp2 // 2, width)),
                edge_of((nb, 1, width, kp2)),
                pl.BlockSpec((nb, kb, rows, width), lambda i, info: (info[0], 0, 0, 0)),
                pl.BlockSpec(rx.shape, lambda i, info: (0, 0, 0, 0)),
                pl.BlockSpec(rx.shape, lambda i, info: (0, 0, 0, 0)),
            ],
            scratch_shapes=[
                pltpu.VMEM(rx.shape, BF),
                pltpu.VMEM((nb * width, kp2), BF),
                pltpu.VMEM((nb, 2, kq2, width), F32),
                pltpu.VMEM((kq2, rows, width), F32),
            ],
        ),
        out_shape=[jax.ShapeDtypeStruct(v.shape, BF) for v in arrays]
        + [jax.ShapeDtypeStruct((cot.shape[0], kb, rows, width), BF)]
        + [edge, edge],
        input_output_aliases={12 + i: i for i in range(len(arrays))},
        compiler_params=pltpu.CompilerParams(vmem_limit_bytes=8 << 20),
        cost_estimate=cost(6),
        name="head_edges",
    )(info, lev, rx, rd, wk, wb, lp, bo, cot, cot_r, cb_x, cb_d, *arrays)


def head_weights_kernel(info, lev, h, rx, rd, dl, gt, own, other, token, x, hx, acc, accb, small, sums, hs, *, kc, kb):
    b, nb = pl.program_id(0), pl.num_programs(0)
    rows, width, c = h.shape[2], h.shape[3], h.shape[4]
    token[...] = jnp.zeros_like(token)
    kp, kq = dl.shape[-1] // 2, accb.shape[0] // 18
    taps = 3 * c
    e = Borders(info, lev, rows)
    pick_halo(info, rx, rd, hs, (0, 0))
    build(x, rows_of(h, (0, 0), rows), e, b, lambda: hs[0], lambda: hs[1])
    pick_halo(info, rx, rd, hs, (0, 1))
    pack_rows(hx, rows, width, hs, lambda r: h[0, 1, r])
    g = dl[0].reshape(rows * width, 2 * kp)

    @pl.when(b == 0)
    def _():
        acc[...] = jnp.zeros_like(acc)
        accb[...] = jnp.zeros_like(accb)
        small[...] = jnp.zeros_like(small)

    acc[...] += dot_tn(g, x[...])
    accb[...] += dot(gt[0], hx[...])
    small[:, : 2 * kp] += jnp.sum(g.astype(F32), axis=0, keepdims=True)
    ones = jnp.ones((8, gt.shape[2]), BF)
    s = dot_nt(ones, gt[0, 8 * kq : 10 * kq, :])[:1]
    small[:, 2 * kp :] += jnp.concatenate([s, jnp.zeros((1, LANES - 2 * kq), F32)], axis=1)

    def fill(ref, a):
        for k in range(3):
            ref[k * kc : (k + 1) * kc, :] = acc[a * kp : a * kp + kc, k * taps : (k + 1) * taps]
            at = 3 * kc + k * kq
            for j in range(3):
                first = (3 * k + j) * 2 * kq + a * kq
                ref[at : at + kq, j * c : (j + 1) * c] = accb[first : first + kq, :]
        end = 3 * (kc + kq)
        if end < ref.shape[0]:
            ref[end:, :] = jnp.zeros((ref.shape[0] - end, taps), F32)
        at = 3 * kc + kb
        ref[at : at + 1, :kp] = small[:, a * kp : (a + 1) * kp]
        ref[at : at + 1, kp : kp + LANES] = pltpu.roll(small[:, 2 * kp :], (LANES - a * kq) % LANES, 1)

    @pl.when(b == nb - 1)
    def _():
        for a, out in ((1, other), (0, own)):
            fill(sums, a)
            out[...] = sums[...].astype(BF)


def head_weights(info, lev, h, rx, rd, dl, gt, kc, kb, after=()):
    nb, nt, rows, width, c = h.shape
    kp2 = dl.shape[-1]
    kq2 = gt.shape[1] // 9
    m = rows * width
    size = -(-3 * (kc + kq2 // 2) // LANES) * LANES

    def at_b(shape):
        return pl.BlockSpec((1,) + shape, lambda b: (b,) + (0,) * len(shape))

    def whole(shape):
        return pl.BlockSpec(shape, lambda b: (0,) * len(shape), pipeline_mode=pl.Buffered(1))

    return pl.pallas_call(
        ordered(functools.partial(head_weights_kernel, kc=kc, kb=kb), 7, after),
        grid=(nb,),
        in_specs=[
            SMEM,
            SMEM,
            at_b((nt, rows, width, c)),
            at_b((nt, width, c)),
            at_b((nt, width, c)),
            at_b((rows, width, kp2)),
            at_b(gt.shape[1:]),
        ]
        + [ANY] * len(after),
        out_specs=[whole((size, 3 * c)), whole((size, 3 * c)), TOKEN_SPEC],
        out_shape=[jax.ShapeDtypeStruct((size, 3 * c), BF)] * 2 + [TOKEN],
        scratch_shapes=[
            pltpu.VMEM((m, 9 * c), BF),
            pltpu.VMEM(((rows + 2) * width, c), BF),
            pltpu.VMEM((kp2, 9 * c), F32),
            pltpu.VMEM((9 * kq2, c), F32),
            pltpu.VMEM((1, kp2 + LANES), F32),
            pltpu.VMEM((size, 3 * c), F32),
            pltpu.VMEM((2, width, c), BF),
        ],
        compiler_params=pltpu.CompilerParams(vmem_limit_bytes=21 << 20),
        cost_estimate=cost(12),
        name="head_weights",
    )(info, lev, h, rx, rd, dl, gt, *after)


def head_inputs_kernel(info, lev, dl, gt, rx, rd, wk, wb, sp, *rest):
    dz, sx, sd, token, *_, x, hs = rest
    token[...] = jnp.zeros_like(token)
    b = pl.program_id(0)
    rows, width, c = sp.shape[2], sp.shape[3], sp.shape[4]
    kp2 = dl.shape[-1]
    taps = 3 * c
    e = Borders(info, lev, rows)
    build(x, rows_of(dl, (0,), rows), e, b, taps=False)
    s = dot(x[:, kp2 : 2 * kp2], wk[1])
    s = s + dot(x[:, :kp2], wk[2])
    s = s + dot(x[:, 2 * kp2 :], wk[0])
    s = s.reshape(rows, width, taps)
    dc = up(s[:, :, :c]) + s[:, :, c : 2 * c] + down(s[:, :, 2 * c :])
    db = dot_tn(gt[0, :, width : (rows + 1) * width], wb[...]).reshape(rows, width, c)
    for t, dh in ((0, dc), (1, db)):
        pick_halo(info, rx, rd, hs, (0, t))
        for r in range(rows):
            v = dh[r]
            if r == 0:
                v = v + hs[0].astype(F32)
            if r == rows - 1:
                v = v + hs[1].astype(F32)
            dz[0, t, r] = (v * sp[0, t, r].astype(F32)).astype(BF)
        put_edges(info, dz[0, t, 0], dz[0, t, rows - 1], sx, sd, (0, t))


def head_inputs(info, lev, dl, gt, rx, rd, wk, wb, sp, gate, after=()):
    nb, nt, rows, width, c = sp.shape
    kp2 = dl.shape[-1]
    m = rows * width

    def at_b(shape):
        return pl.BlockSpec((1,) + shape, lambda b: (b,) + (0,) * len(shape))

    def whole(shape):
        return pl.BlockSpec(shape, lambda b: (0,) * len(shape), pipeline_mode=pl.Buffered(1))

    return pl.pallas_call(
        ordered(head_inputs_kernel, 9, gate + after),
        grid=(nb,),
        in_specs=[
            SMEM,
            SMEM,
            at_b((rows, width, kp2)),
            at_b(gt.shape[1:]),
            at_b((nt, width, c)),
            at_b((nt, width, c)),
            whole(wk.shape),
            whole(wb.shape),
            at_b((nt, rows, width, c)),
        ]
        + [ANY] * len(gate + after),
        out_specs=[at_b((nt, rows, width, c)), at_b((nt, width, c)), at_b((nt, width, c)), TOKEN_SPEC] + [ANY] * len(gate),
        out_shape=[
            jax.ShapeDtypeStruct(sp.shape, BF),
            jax.ShapeDtypeStruct((nb, nt, width, c), BF),
            jax.ShapeDtypeStruct((nb, nt, width, c), BF),
        ]
        + [TOKEN]
        + [jax.ShapeDtypeStruct(v.shape, v.dtype) for v in gate],
        input_output_aliases={9 + k: 4 + k for k in range(len(gate))},
        scratch_shapes=[pltpu.VMEM((m, 3 * kp2), BF), pltpu.VMEM((2, width, c), BF)],
        compiler_params=pltpu.CompilerParams(vmem_limit_bytes=14 << 20),
        cost_estimate=cost(9),
        name="head_inputs",
    )(info, lev, dl, gt, rx, rd, wk, wb, sp, *gate, *after)


def weights_kernel(info, lev, h, rx, rd, dz, keep, send, token, x, acc, bias, hs):
    t, b, nb = pl.program_id(0), pl.program_id(1), pl.num_programs(1)
    rows, width, c = h.shape[2], h.shape[3], h.shape[4]
    e = Borders(info, lev, rows)
    pick_halo(info, rx, rd, hs, (0, 0))
    build(x, rows_of(h, (0, 0), rows), e, b, lambda: hs[0], lambda: hs[1])
    g = dz[0, 0].reshape(rows * width, c)
    part = dot_tn(x[...], g)
    total = jnp.sum(g.astype(F32), axis=0, keepdims=True)
    taps = acc.shape[0]

    @pl.when(b == 0)
    def _():
        acc[...] = part
        bias[...] = total

    @pl.when(b != 0)
    def _():
        acc[...] += part
        bias[...] += total

    token[...] = jnp.zeros_like(token)
    for i, out in enumerate((send, keep)):

        @pl.when(jnp.logical_and(b == nb - 1, t == i))
        def _():
            out[:taps, :] = acc[...].astype(out.dtype)
            out[taps:, :] = jnp.broadcast_to(bias[...].astype(out.dtype), (out.shape[0] - taps, c))


def weights(layer, info, lev, h, rx, rd, dz, after=()):
    nb, nt, rows, width, c = h.shape

    def tower(t, info):
        return jnp.where(t == 0, 1 - info[0], info[0])

    row_spec = pl.BlockSpec((1, 1, rows, width, c), lambda t, b, info: (b, tower(t, info), 0, 0, 0))
    edge_spec = pl.BlockSpec((1, 1, width, c), lambda t, b, info: (b, tower(t, info), 0, 0))
    taps = 9 * c
    return pl.pallas_call(
        ordered(weights_kernel, 6, after),
        grid_spec=pltpu.PrefetchScalarGridSpec(
            num_scalar_prefetch=1,
            grid=(nt, nb),
            in_specs=[SMEM, row_spec, edge_spec, edge_spec, row_spec] + [ANY] * len(after),
            out_specs=[pl.BlockSpec((taps + LANES, c), lambda t, b, info: (0, 0))] * 2 + [TOKEN_SPEC],
            scratch_shapes=[
                pltpu.VMEM((rows * width, taps), BF),
                pltpu.VMEM((taps, c), F32),
                pltpu.VMEM((1, c), F32),
                pltpu.VMEM((2, width, c), BF),
            ],
        ),
        out_shape=[jax.ShapeDtypeStruct((taps + LANES, c), BF)] * 2 + [TOKEN],
        compiler_params=pltpu.CompilerParams(vmem_limit_bytes=14 << 20),
        cost_estimate=cost(8),
        name=f"weights{layer}",
    )(info, lev, h, rx, rd, dz, *after)


def inputs_kernel(layer, info, lev, dz, rx, rd, own, other, *rest):
    if layer:
        sp, out, token, sx, sd, x, wv, wt, hs, sem = rest
    else:
        out, token, *_, x, wv, wt, hs, sem = rest
    token[...] = jnp.zeros_like(token)
    t, b = pl.program_id(0), pl.program_id(1)
    rows, width, c = dz.shape[2], dz.shape[3], dz.shape[4]
    e = Borders(info, lev, rows)

    @pl.when(jnp.logical_and(t == 0, b == 0))
    def _():
        start_weights(info, layer, own, other, wv, sem)

    pick_halo(info, rx, rd, hs, (0, 0))
    build(x, rows_of(dz, (0, 0), rows), e, b, lambda: hs[0], lambda: hs[1])

    @pl.when(b == 0)
    def _():
        wait_weights(own, wv, sem, t)
        for i in range(9):
            wt[:, (8 - i) * c : (9 - i) * c] = wv[t, i * c : (i + 1) * c, :]

    dh = dot_nt(x[...], wt[...]).astype(BF)
    if not layer:
        out[0, 0] = dh.reshape(rows, width, c)
        return
    dz_next = (dh.astype(F32).reshape(rows, width, c) * sp[0, 0].astype(F32)).astype(BF)
    out[0, 0] = dz_next
    put_edges(info, dz_next[0], dz_next[rows - 1], sx, sd, (0, 0))


def inputs(layer, info, lev, dz, rx, rd, own, other, sp=None, gate=(), after=()):
    nb, nt, rows, width, c = dz.shape
    row_spec = pl.BlockSpec((1, 1, rows, width, c), lambda t, b: (b, t, 0, 0, 0))
    edge_spec = pl.BlockSpec((1, 1, width, c), lambda t, b: (b, t, 0, 0))
    edge = jax.ShapeDtypeStruct((nb, nt, width, c), BF)
    taps = own.shape[1]
    return pl.pallas_call(
        ordered(functools.partial(inputs_kernel, layer), 8 if layer else 7, gate + after),
        grid=(nt, nb),
        in_specs=[SMEM, SMEM, row_spec, edge_spec, edge_spec, HBM, HBM] + ([row_spec] if layer else []) + [ANY] * len(gate + after),
        out_specs=[row_spec, TOKEN_SPEC] + ([edge_spec, edge_spec] if layer else []) + [ANY] * len(gate),
        out_shape=[jax.ShapeDtypeStruct(dz.shape, BF)]
        + [TOKEN]
        + ([edge, edge] if layer else [])
        + [jax.ShapeDtypeStruct(v.shape, v.dtype) for v in gate],
        input_output_aliases={7 + k: 2 + k for k in range(len(gate))},
        scratch_shapes=[
            pltpu.VMEM((rows * width, taps), BF),
            pltpu.VMEM((nt, taps, c), BF),
            pltpu.VMEM((c, taps), BF),
            pltpu.VMEM((2, width, c), BF),
            pltpu.SemaphoreType.DMA((nt,)),
        ],
        compiler_params=pltpu.CompilerParams(vmem_limit_bytes=13 << 20),
        cost_estimate=cost(9),
        name=f"inputs{layer}",
    )(info, lev, dz, rx, rd, own, other, *([sp] if layer else []), *gate, *after)


def swap_section(value):
    return lax.ppermute(value, "section", [(0, 1), (1, 0)])


def swap_edges(sx, sd):
    count = lax.axis_size("tile")
    even = [p for i in range(0, count - 1, 2) for p in ((i, i + 1), (i + 1, i))]
    odd = [p for i in range(1, count - 1, 2) for p in ((i, i + 1), (i + 1, i))]
    return lax.ppermute(sx, "tile", even), lax.ppermute(sd, "tile", odd)


def combine_kernel(plan, info, *refs):
    ins, outs = list(refs[: sum(sum(p) for p in plan)]), refs[sum(sum(p) for p in plan) :]
    for counts, out in zip(plan, outs):
        lanes = out.shape[1] // len(counts)
        for i, count in enumerate(counts):
            terms = [ins.pop(0)[...].astype(F32) for _ in range(count)]
            out[:, i * lanes : (i + 1) * lanes] = functools.reduce(jnp.add, terms).astype(out.dtype)


def combine(name, info, shape, outs, gate=(), after=()):
    rows, lanes = shape
    views = [v for parts in outs for terms in parts for v in terms]

    def spec(view):
        return pl.BlockSpec(shape, lambda i, info: (view[1](info), view[2]))

    plan = [[len(terms) for terms in parts] for parts in outs]
    return pl.pallas_call(
        ordered(functools.partial(combine_kernel, plan), 1 + len(views), gate + after),
        grid_spec=pltpu.PrefetchScalarGridSpec(
            num_scalar_prefetch=1,
            grid=(1,),
            in_specs=[spec(v) for v in views] + [ANY] * len(gate + after),
            out_specs=[pl.BlockSpec((rows, lanes * len(parts)), lambda i, info: (0, 0)) for parts in outs]
            + [ANY] * len(gate),
        ),
        out_shape=[jax.ShapeDtypeStruct((rows, lanes * len(parts)), BF) for parts in outs]
        + [jax.ShapeDtypeStruct(v.shape, v.dtype) for v in gate],
        input_output_aliases={1 + len(views) + k: len(outs) + k for k in range(len(gate))},
        compiler_params=pltpu.CompilerParams(vmem_limit_bytes=7 << 20),
        cost_estimate=cost(2),
        name=name,
    )(info, *[v[0] for v in views], *gate, *after)


def join_kernel(bits, split, info, *refs):
    n = len(bits)
    for i, bit in enumerate(bits):
        cur, got = refs[2 * i], refs[2 * i + 1]
        outs = refs[2 * n :] if split else refs[2 * n + i : 2 * n + i + 1]
        m, lanes = cur.shape[0], cur.shape[1] // len(outs)
        mine = (info[2] >> bit) & 1
        for j, out in enumerate(outs):
            at = slice(j * lanes, (j + 1) * lanes)

            @pl.when(mine == 0)
            def _():
                out[:m, :] = cur[:, at]
                out[m:, :] = got[:, at]

            @pl.when(mine != 0)
            def _():
                out[:m, :] = got[:, at]
                out[m:, :] = cur[:, at]


def join(name, info, bits, pairs, split=False, after=()):
    arrays = [v for pair in pairs for v in pair]
    shapes = [(2 * cur.shape[0], cur.shape[1]) for cur, _ in pairs]
    if split:
        shapes = [(shapes[0][0], shapes[0][1] // 2)] * 2

    def whole(shape):
        return pl.BlockSpec(shape, lambda i, info: (0, 0))

    return pl.pallas_call(
        ordered(functools.partial(join_kernel, bits, split), 1 + len(arrays), after),
        grid_spec=pltpu.PrefetchScalarGridSpec(
            num_scalar_prefetch=1,
            grid=(1,),
            in_specs=[whole(v.shape) for v in arrays] + [ANY] * len(after),
            out_specs=[whole(s) for s in shapes],
        ),
        out_shape=[jax.ShapeDtypeStruct(s, BF) for s in shapes],
        compiler_params=pltpu.CompilerParams(vmem_limit_bytes=7 << 20),
        cost_estimate=cost(2),
        name=name,
    )(info, *arrays, *after)


def relay_kernel(*refs):
    del refs


def relay(name, gate, after):
    return pl.pallas_call(
        ordered(relay_kernel, 0, gate + after),
        in_specs=[ANY] * len(gate + after),
        out_specs=[ANY] * len(gate),
        out_shape=[jax.ShapeDtypeStruct(v.shape, v.dtype) for v in gate],
        input_output_aliases={k: k for k in range(len(gate))},
        compiler_params=pltpu.CompilerParams(vmem_limit_bytes=1 << 20),
        cost_estimate=cost(1),
        name=name,
    )(*gate, *after)


class TileSum:
    def __init__(self, name, info, whole, *terms):
        self.name, self.info = name, info
        rows, lanes = terms[0].shape
        self.shape = (rows, lanes // 2)
        self.parts = [[(v, lambda info: 0, i) for v in terms] for i in range(2)]
        self.count = lax.axis_size("tile")
        bits = self.count.bit_length() - 1
        near = [(0, 1), (1, 0)]
        self.plan = [("halve", step) for step in near]
        if whole or bits > 4:
            self.plan += [("add", (bit,)) for bit in range(2, bits)]
        else:
            self.plan += [("halve", (bit,)) for bit in range(2, bits)]
            self.plan += [("double", (bit,)) for bit in reversed(range(2, bits))]
        self.plan += [("double", step) for step in reversed(near)]
        self.step = 0
        self.sends = None

    def exchange(self, value, bit):
        return lax.ppermute(value, "tile", [(i, i ^ (1 << bit)) for i in range(self.count)])

    def start(self, *after, gate=()):
        kind, bits = self.plan.pop(0)
        name = f"{self.name}_{self.step}"
        self.step += 1
        if kind == "halve":
            rows, lanes = self.shape
            self.shape = (rows // 2, lanes)
            bit_of = bits * 2 if len(bits) == 1 else bits

            def half(view, bit, other):
                array, row, lane = view
                return array, lambda info: 2 * row(info) + (((info[2] >> bit) & 1) ^ other), lane

            sent = [[half(v, bit, 1) for v in terms] for terms, bit in zip(self.parts, bit_of)]
            self.parts = [[half(v, bit, 0) for v in terms] for terms, bit in zip(self.parts, bit_of)]
            outs = [sent] if len(bits) == 1 else [[terms] for terms in sent]
            sends = combine(name, self.info, self.shape, outs, gate, after)
        elif kind == "add" or self.kind != "double":
            outs = [self.parts] if len(bits) == 1 else [[terms] for terms in self.parts]
            sends = combine(name, self.info, self.shape, outs, gate, after)
        else:
            sends = join(name, self.info, self.bits, self.pairs, len(bits) > len(self.pairs), after)
        passed = tuple(sends[len(bits) :])
        sends = tuple(sends[: len(bits)])
        self.kind, self.bits, self.sends = kind, bits, sends
        got = [self.exchange(v, bit) for v, bit in zip(sends, bits)]
        if kind == "halve":
            lane = (lambda i: i) if len(bits) == 1 else (lambda i: 0)
            pick = (lambda i: got[0]) if len(bits) == 1 else (lambda i: got[i])
            self.parts = [terms + [(pick(i), lambda info: 0, lane(i))] for i, terms in enumerate(self.parts)]
        elif kind == "add":
            self.parts = [[(v, lambda info: 0, i) for v in (sends[0], got[0])] for i in range(2)]
        else:
            self.pairs = list(zip(sends, got))
        return sends + passed

    def result(self, *after):
        return join(f"{self.name}_{self.step}", self.info, self.bits, self.pairs, False, after)


def pick_kernel(info, cot, gb, out):
    rows, kc, kb = cot.shape[1], cot.shape[2], gb.shape[1]
    g = gb[0].astype(F32)
    gap = jnp.zeros((out.shape[2] - kc - kb, out.shape[3]), F32)
    for r in range(rows):
        out[0, r] = jnp.concatenate([cot[0, r].astype(F32), g[:, r], gap], axis=0).astype(BF)


def pick(info, cot, gb, nb, kp, after=()):
    def at_all(shape):
        return pl.BlockSpec((1,) + shape[1:], lambda b, info: ((1 - info[0]) * nb + b,) + (0,) * (len(shape) - 1))

    shape = (nb, cot.shape[1], kp, cot.shape[3])
    return pl.pallas_call(
        ordered(pick_kernel, 3, after),
        grid_spec=pltpu.PrefetchScalarGridSpec(
            num_scalar_prefetch=1,
            grid=(nb,),
            in_specs=[at_all(cot.shape), at_all(gb.shape)] + [ANY] * len(after),
            out_specs=pl.BlockSpec((1,) + shape[1:], lambda b, info: (b, 0, 0, 0)),
        ),
        out_shape=jax.ShapeDtypeStruct(shape, BF),
        compiler_params=pltpu.CompilerParams(vmem_limit_bytes=8 << 20),
        cost_estimate=cost(2),
        name="pick",
    )(info, cot, gb, *after)


def gather_kernel(tower, classes, boxes, out):
    out[...] = jnp.zeros_like(out)
    nt, c = tower.shape[1], tower.shape[2]
    out[:nt, :c] = tower[0]
    out[nt : nt + 1, : classes.shape[0]] = classes[...].reshape(1, -1)
    out[nt + 1 : nt + 2, : boxes.shape[0]] = boxes[...].reshape(1, -1)


def gather(tower, classes, boxes, lanes):
    return pl.pallas_call(
        gather_kernel,
        out_shape=jax.ShapeDtypeStruct((8, lanes), F32),
        cost_estimate=cost(1),
        name="gather",
    )(tower, classes, boxes)


def pick_weights_kernel(thin, small, out):
    gap = jnp.zeros((out.shape[1] - thin.shape[1] - small.shape[1], out.shape[2]), F32)
    out[0] = jnp.concatenate([thin[0].astype(F32), small[0].astype(F32), gap], axis=0).astype(BF)


def pick_weights(thin, small, kp, after=()):
    def at_k(shape):
        return pl.BlockSpec((1,) + shape[1:], lambda k: (k, 0, 0))

    shape = (thin.shape[0], kp, thin.shape[2])
    return pl.pallas_call(
        ordered(pick_weights_kernel, 2, after),
        grid=(shape[0],),
        in_specs=[at_k(thin.shape), at_k(small.shape)] + [ANY] * len(after),
        out_specs=at_k(shape),
        out_shape=jax.ShapeDtypeStruct(shape, BF),
        compiler_params=pltpu.CompilerParams(vmem_limit_bytes=6 << 20),
        cost_estimate=cost(2),
        name="pick_weights",
    )(thin, small, *after)


def pack_kernel(own, other, bias, bias_r, wk, wb, cb, *, kc, kb, kq, towers):
    k = pl.program_id(0)
    kp = own.shape[1]
    c = wb.shape[1]
    gap = jnp.zeros((kp - kc, wk.shape[2]), F32)
    for half, v in enumerate((own, other)):
        wk[0, half * kp : (half + 1) * kp, :] = jnp.concatenate([v[0].astype(F32)[:kc], gap], axis=0).astype(BF)
    u, v = own[0].astype(F32)[kc : kc + kb], other[0].astype(F32)[kc : kc + kb]
    small = jnp.zeros((kq - kb, c), F32)
    for j in range(3):
        at = slice(j * c, (j + 1) * c)
        rows = jnp.concatenate([u[:, at], small, v[:, at], small], axis=0).astype(BF)
        wb[pl.ds(pl.multiple_of((3 * k + j) * 2 * kq, 2 * kq), 2 * kq), :] = rows

    @pl.when(k == 0)
    def _():
        wide = jnp.zeros((1, kp - kc), F32)
        thin = jnp.zeros((1, kq - kb), F32)
        rest = jnp.zeros((1, cb.shape[0] - 2 * kp - kq - kb), F32)
        classes, boxes = slice(towers, towers + 1), slice(towers + 1, towers + 2)
        parts = [bias[classes, :kc], wide, bias_r[classes, :kc], wide, bias[boxes, :kb], thin, bias_r[boxes, :kb], rest]
        cb[...] = jnp.broadcast_to(jnp.concatenate(parts, axis=1), (cb.shape[1], cb.shape[0])).T


def pack(own, other, bias, bias_r, kc, kb, kq, towers, after=()):
    k, kp, c3 = own.shape
    at_k = pl.BlockSpec((1, kp, c3), lambda k: (k, 0, 0))

    def whole(shape):
        return pl.BlockSpec(shape, lambda k: (0,) * len(shape))

    shapes = [(k, 2 * kp, c3), (18 * kq, c3 // 3), (2 * kp + LANES, LANES)]
    return pl.pallas_call(
        ordered(functools.partial(pack_kernel, kc=kc, kb=kb, kq=kq, towers=towers), 4, after),
        grid=(k,),
        in_specs=[at_k, at_k, whole(bias.shape), whole(bias.shape)] + [ANY] * len(after),
        out_specs=[pl.BlockSpec((1,) + shapes[0][1:], lambda k: (k, 0, 0)), whole(shapes[1]), whole(shapes[2])],
        out_shape=[jax.ShapeDtypeStruct(s, t) for s, t in zip(shapes, (BF, BF, F32))],
        compiler_params=pltpu.CompilerParams(vmem_limit_bytes=10 << 20),
        cost_estimate=cost(3),
        name="pack",
    )(own, other, bias, bias_r, *after)


def place_kernel(info, prob_i, box_i, got, prob, box, token, bx):
    rows, kc, kb = prob.shape[1], prob.shape[2], box.shape[1]
    for r in range(rows):
        prob[0, r] = got[0, r, :kc]
        bx[:, r, :] = got[0, r, kc:].astype(F32)[:kb]
    box[0] = bx[...].astype(BF)
    token[...] = jnp.zeros_like(token)


def place(info, prob, box, got, after=()):
    nb = got.shape[0]

    def at_all(shape):
        return pl.BlockSpec((1,) + shape[1:], lambda b, info: ((1 - info[0]) * nb + b,) + (0,) * (len(shape) - 1))

    return pl.pallas_call(
        ordered(place_kernel, 4, after),
        grid_spec=pltpu.PrefetchScalarGridSpec(
            num_scalar_prefetch=1,
            grid=(nb,),
            in_specs=[HBM, HBM, pl.BlockSpec((1,) + got.shape[1:], lambda b, info: (b, 0, 0, 0))] + [ANY] * len(after),
            out_specs=[at_all(prob.shape), at_all(box.shape), TOKEN_SPEC],
            scratch_shapes=[pltpu.VMEM(box.shape[1:], F32)],
        ),
        out_shape=[jax.ShapeDtypeStruct(v.shape, BF) for v in (prob, box)] + [TOKEN],
        input_output_aliases={1: 0, 2: 1},
        compiler_params=pltpu.CompilerParams(vmem_limit_bytes=8 << 20),
        cost_estimate=cost(2),
        name="place",
    )(info, prob, box, got, *after)


def after(value, *others):
    return lax.optimization_barrier((value,) + others)[0]


def on_device(
    features,
    levels,
    tower_weight,
    tower_bias,
    class_weight,
    class_bias,
    box_weight,
    box_bias,
    class_cotangent,
    box_cotangent,
):
    section = lax.axis_index("section")
    tile = lax.axis_index("tile")
    nb, nt, rows, width, c = features.shape
    kc, kb = class_weight.shape[-1], box_weight.shape[-1]
    kp = -(-kc // LANES) * LANES
    kq = -(-kb // 8) * 8
    taps = 9 * c
    lev = levels
    info = jnp.stack([section, tile % 2, tile]).astype(jnp.int32)
    even = tile % 2 == 0

    sx = lax.dynamic_index_in_dim(features, jnp.where(even, rows - 1, 0), 2, False)
    sd = lax.dynamic_index_in_dim(features, jnp.where(even, 0, rows - 1), 2, False)
    rx0, rd0 = swap_edges(sx, sd)
    bias = gather(tower_bias, class_bias, box_bias, kp)
    bias_r = swap_section(bias)
    w_own = tower_weight.reshape(nt, taps, c)
    w_other = swap_section(w_own)

    h1, sp0, zp, token = forward(0, info, lev, features, w_own, w_other, bias, bias_r, (sx, sd))
    thin, small = class_weight.transpose(0, 2, 1), box_weight.transpose(0, 2, 1)
    cot, gb = class_cotangent.transpose(0, 1, 3, 2), box_cotangent.transpose(0, 3, 1, 2)
    w_out = pick_weights(thin, small, kp, (token,))
    w_out_r = swap_section(w_out)
    cot_r = swap_section(pick(info, cot, gb, nb, kp, (token,)))
    h1, sp0, sx, sd = edges(0, info, lev, zp, rx0, rd0, w_own, w_other, h1, sp0)
    rx1, rd1 = swap_edges(sx, sd)
    h2, sp1, zp, _ = forward(1, info, lev, h1, w_own, w_other, bias, bias_r)
    wk, wb, cb = pack(w_out, w_out_r, bias, bias_r, kc, kb, kq, nt, (zp,))
    h2, sp1, sx, sd = edges(1, info, lev, zp, rx1, rd1, w_own, w_other, h2, sp1)
    rx2, rd2 = swap_edges(sx, sd)
    prob, psend, dl, gt, cb_x, cb_d, lp, bo = head(info, lev, h2, wk, wb, cb, cot, gb, cot_r)
    prob, psend, dl, boxo, cx, cd = head_edges(
        info, lev, rx2, rd2, wk, wb, lp, bo, cot, cot_r, cb_x, cb_d, prob, psend, dl, kb
    )
    rx, rd = swap_edges(cx, cd)

    keep, send, token = head_weights(info, lev, h2, rx2, rd2, dl, gt, kc, kb)
    (send,) = relay("send_head", (send,), (token, rx, rd))
    head_sum = TileSum("sum_head", info, True, keep, swap_section(send))
    s = head_sum.start()
    dz1, sx, sd, token = head_inputs(info, lev, dl, gt, rx, rd, wk, wb, sp1, (), s)
    rx, rd = swap_edges(sx, sd)
    s = head_sum.start(token)
    keep1, send1, token = weights(1, info, lev, h1, rx1, rd1, dz1, s)
    *s, send1 = head_sum.start(token, rx, rd, gate=(send1,))
    dz0, token, sx, sd = inputs(1, info, lev, dz1, rx, rd, w_own, w_other, sp0, (), tuple(s))
    *s, psend = head_sum.start(token, gate=(psend,))
    prob_r = swap_section(psend)
    sum1 = TileSum("sum_one", info, False, keep1, swap_section(send1))
    s = tuple(s)
    s = s + sum1.start(*s)
    keep0, send0, token = weights(0, info, lev, features, rx0, rd0, dz0, s)
    sum0 = TileSum("sum_zero", info, False, keep0, swap_section(send0))
    s = sum0.start()
    s = s + sum1.start(*s)
    prob, boxo, token = place(info, prob, boxo, prob_r, tuple(s))
    *s, sx, sd = sum0.start(token, gate=(sx, sd))
    rx, rd = swap_edges(sx, sd)
    s = tuple(s)
    s = s + sum1.start(*s)
    s = s + sum0.start(*s)
    s = s + head_sum.start(*s)
    s = s + sum1.start(*s)
    feature_grad, token = inputs(0, info, lev, dz0, rx, rd, w_own, w_other, None, (), s)
    done = (token,)
    while sum0.plan:
        s = sum0.start(*done)
        done = ()
        for other in (head_sum, sum1):
            if other.plan:
                other.start(*s)
    head_done, l1, l0 = (jnp.concatenate(v.result(), axis=1) for v in (head_sum, sum1, sum0))

    mine_l = jnp.where(section == 0, l0, l1)
    other_l = swap_section(jnp.where(section == 0, l1, l0))
    towers = jnp.where(section == 0, jnp.stack([mine_l[:taps], other_l[:taps]]), jnp.stack([other_l[:taps], mine_l[:taps]]))
    biases = jnp.where(section == 0, jnp.stack([mine_l[taps], other_l[taps]]), jnp.stack([other_l[taps], mine_l[taps]]))
    end = 3 * kc
    box = head_done[end : end + 3 * kq].astype(F32)
    return (
        prob.transpose(0, 1, 3, 2),
        boxo.transpose(0, 2, 3, 1),
        feature_grad,
        towers.astype(F32).reshape(1, nt, 3, 3 * c, c),
        biases.astype(F32).reshape(1, nt, c),
        head_done[:end].astype(F32).reshape(3, kc, 3 * c).transpose(0, 2, 1),
        box[kb, :kc],
        box.reshape(3, kq, 3 * c)[:, :kb].transpose(0, 2, 1),
        box[kb, kp : kp + kb],
    )


def solution(mesh):
    in_specs = (
        P("section", None, "tile", None, None),
        P(),
        P("section", None, None, None, None),
        P("section", None, None),
        P(None, None, "section"),
        P("section"),
        P(None, None, "section"),
        P("section"),
        P(None, "tile", None, "section"),
        P(None, "tile", None, "section"),
    )
    out_specs = (
        P(None, "tile", None, "section"),
        P(None, "tile", None, "section"),
        P("section", None, "tile", None, None),
        P("section", None, None, None, None),
        P("section", None, None),
        P(None, None, "section"),
        P("section"),
        P(None, None, "section"),
        P("section"),
    )
    return jax.shard_map(on_device, mesh=mesh, in_specs=in_specs, out_specs=out_specs, check_vma=False)
```

```python
import functools

import jax
import jax.numpy as jnp
from jax import lax
from jax.experimental import pallas as pl
from jax.experimental.pallas import tpu as pltpu
from jax.sharding import PartitionSpec as P

BF = jnp.bfloat16
F32 = jnp.float32
LANES = 128


def cost(us):
    return pl.CostEstimate(flops=int(us * 2e9), bytes_accessed=0, transcendentals=0)


def ordered(kernel, inputs, after):
    def body(*refs):
        return kernel(*refs[:inputs], *refs[inputs + len(after) :])

    return body
SMEM = pl.BlockSpec(memory_space=pltpu.SMEM)
HBM = pl.BlockSpec(memory_space=pltpu.HBM)
ANY = pl.BlockSpec(memory_space=pl.ANY)


TOKEN = jax.ShapeDtypeStruct((8, LANES), F32)
TOKEN_SPEC = pl.BlockSpec((8, LANES), lambda *_: (0, 0))


def dot(a, b):
    return jnp.dot(a, b, preferred_element_type=F32)


def dot_nt(a, b):
    return lax.dot_general(a, b, (((1,), (1,)), ((), ())), preferred_element_type=F32)


def dot_tn(a, b):
    return lax.dot_general(a, b, (((0,), (0,)), ((), ())), preferred_element_type=F32)


def down(v):
    return jnp.concatenate([jnp.zeros_like(v[..., :1, :]), v[..., :-1, :]], axis=-2)


def up(v):
    return jnp.concatenate([v[..., 1:, :], jnp.zeros_like(v[..., :1, :])], axis=-2)


def keep_if(v, flag):
    return v * jnp.full((1, v.shape[-1]), flag, F32).astype(v.dtype)


def build(x, rows, e, b, before=None, after=None, taps=True):
    count = len(rows)
    width = rows[0]().shape[0]
    for q in range(-1, count + 1):
        if q < 0:
            get = before
        elif q < count:
            get = rows[q]
        else:
            get = after
        if get is None:
            dest = 0 if q < 0 else count - 1
            part = x.shape[1] // 3
            first = 0 if q < 0 else 2 * part
            x[dest * width : (dest + 1) * width, first : first + part] = jnp.zeros((width, part), x.dtype)
            continue
        v = get()
        p = jnp.concatenate([down(v), v, up(v)], axis=1) if taps else v
        n = p.shape[1]
        if 0 <= q < count:
            x[q * width : (q + 1) * width, n : 2 * n] = p
        if q + 1 < count:
            x[(q + 1) * width : (q + 2) * width, 0:n] = keep_if(p, e[b, q + 1])
        if q >= 1:
            x[(q - 1) * width : q * width, 2 * n : 3 * n] = keep_if(p, e[b, q])


class Borders:
    def __init__(self, info, lev, rows):
        self.info, self.lev, self.rows = info, lev, rows

    def __getitem__(self, at):
        b, i = at
        lines, count = self.lev.shape
        line = self.info[0] * (lines // 2) + b
        r = self.info[2] * self.rows + i
        same = self.lev[line, jnp.maximum(r - 1, 0)] == self.lev[line, jnp.minimum(r, count - 1)]
        return jnp.where(jnp.logical_and(same, jnp.logical_and(r > 0, r < count)), 1.0, 0.0)


def rows_of(ref, lead, count):
    return [functools.partial(lambda r: ref[lead + (r,)], r) for r in range(count)]


def pick_halo(info, rx, rd, hs, lead):
    @pl.when(info[1] == 0)
    def _():
        hs[0] = rd[lead]
        hs[1] = rx[lead]

    @pl.when(info[1] != 0)
    def _():
        hs[0] = rx[lead]
        hs[1] = rd[lead]


def put_edges(info, first, last, sx, sd, lead):
    @pl.when(info[1] == 0)
    def _():
        sx[lead] = last
        sd[lead] = first

    @pl.when(info[1] != 0)
    def _():
        sx[lead] = first
        sd[lead] = last


def start_weights(info, layer, own, other, wv, sem):
    for t in range(wv.shape[0]):

        @pl.when(info[0] == layer)
        def _():
            pltpu.make_async_copy(own.at[t], wv.at[t], sem.at[t]).start()

        @pl.when(info[0] != layer)
        def _():
            pltpu.make_async_copy(other.at[t], wv.at[t], sem.at[t]).start()


def wait_weights(own, wv, sem, t):
    for i in range(wv.shape[0]):

        @pl.when(t == i)
        def _():
            pltpu.make_async_copy(own.at[i], wv.at[i], sem.at[i]).wait()


def activate(z):
    sg = jax.nn.sigmoid(z)
    hv = z * sg
    return hv.astype(BF), (sg + hv * (1.0 - sg)).astype(BF)


def forward_kernel(layer, info, lev, h, own, other, bias, bias_r, hn, sp, zp, token, x, wv, sem):
    t, b = pl.program_id(0), pl.program_id(1)
    rows, width = h.shape[2], h.shape[3]
    e = Borders(info, lev, rows)

    @pl.when(jnp.logical_and(t == 0, b == 0))
    def _():
        start_weights(info, layer, own, other, wv, sem)

    build(x, rows_of(h, (0, 0), rows), e, b)

    @pl.when(b == 0)
    def _():
        wait_weights(own, wv, sem, t)

    c = h.shape[4]
    chosen = jnp.full((1, c), info[0] == layer, jnp.int32) != 0
    row = pl.ds(t, 1)
    z = dot(x[...], wv[t]) + jnp.where(chosen, bias[row, :c], bias_r[row, :c])
    hv, sv = activate(z)
    hn[0, 0] = hv.reshape(h.shape[2:])
    sp[0, 0] = sv.reshape(h.shape[2:])
    zp[0, 0, 0] = z[:width]
    zp[0, 0, 1] = z[(rows - 1) * width :]
    token[...] = jnp.zeros_like(token)


def forward(layer, info, lev, h, own, other, bias, bias_r, after=()):
    nb, nt, rows, width, c = h.shape
    row_spec = pl.BlockSpec((1, 1, rows, width, c), lambda t, b: (b, t, 0, 0, 0))
    taps = own.shape[1]
    return pl.pallas_call(
        ordered(functools.partial(forward_kernel, layer), 7, after),
        grid=(nt, nb),
        in_specs=[SMEM, SMEM, row_spec, HBM, HBM] + [pl.BlockSpec(bias.shape, lambda t, b: (0, 0))] * 2 + [ANY] * len(after),
        out_specs=[row_spec, row_spec, pl.BlockSpec((1, 1, 2, width, c), lambda t, b: (b, t, 0, 0, 0)), TOKEN_SPEC],
        out_shape=[jax.ShapeDtypeStruct(h.shape, BF)] * 2 + [jax.ShapeDtypeStruct((nb, nt, 2, width, c), F32), TOKEN],
        scratch_shapes=[
            pltpu.VMEM((rows * width, taps), BF),
            pltpu.VMEM((nt, taps, c), BF),
            pltpu.SemaphoreType.DMA((nt,)),
        ],
        compiler_params=pltpu.CompilerParams(vmem_limit_bytes=12 << 20),
        cost_estimate=cost(8),
        name=f"forward{layer}",
    )(info, lev, h, own, other, bias, bias_r, *after)


def edge_kernel(layer, rows, info, lev, zp, rx, rd, own, other, hin, sin, hn, sp, sx, sd, wv, sem):
    i = pl.program_id(0)
    nb, nt, width, c = zp.shape[0], zp.shape[1], zp.shape[3], zp.shape[4]
    taps = wv.shape[2]
    e = Borders(info, lev, rows)

    def copies(ref, ii):
        for t in range(nt):
            yield pltpu.make_async_copy(ref.at[t, pl.ds(2 * ii * taps, taps)], wv.at[ii, t], sem.at[ii, t])

    for ii in range(2):
        for ref, chosen in ((own, info[0] == layer), (other, info[0] != layer)):

            @pl.when(jnp.logical_and(i == 0, chosen))
            def _():
                for copy in copies(ref, ii):
                    copy.start()

    from_x = (info[1] == 0) == (i == 1)
    edge = i * rows
    mask = jnp.full((1, c), from_x.astype(jnp.int32), jnp.int32) != 0
    parts = []
    for t in range(nt):
        p = []
        for b in range(nb):
            v = jnp.where(mask, rx[b, t].astype(F32), rd[b, t].astype(F32))
            p.append((jnp.concatenate([down(v), v, up(v)], axis=1) * e[b, edge]).astype(BF))
        parts.append(jnp.concatenate(p, axis=0))

    for ii in range(2):

        @pl.when(i == ii)
        def _():
            for copy in copies(own, ii):
                copy.wait()

    for t in range(nt):
        z = dot(parts[t], wv[i, t])
        for b in range(nb):
            hv, sv = activate(zp[b, t, 0] + z[b * width : (b + 1) * width])
            hn[b, t, 0] = hv
            sp[b, t, 0] = sv

            @pl.when(from_x)
            def _():
                sx[b, t] = hv

            @pl.when(jnp.logical_not(from_x))
            def _():
                sd[b, t] = hv


def edges(layer, info, lev, zp, rx, rd, own, other, hn, sp):
    nb, nt, rows, width, c = hn.shape
    taps = own.shape[1] // 3
    row_spec = pl.BlockSpec((nb, nt, 1, width, c), lambda i: (0, 0, i * (rows - 1), 0, 0))
    edge_spec = pl.BlockSpec((nb, nt, width, c), lambda i: (0, 0, 0, 0))
    edge = jax.ShapeDtypeStruct((nb, nt, width, c), BF)
    return pl.pallas_call(
        functools.partial(edge_kernel, layer, rows),
        grid=(2,),
        in_specs=[
            SMEM,
            SMEM,
            pl.BlockSpec((nb, nt, 1, width, c), lambda i: (0, 0, i, 0, 0)),
            edge_spec,
            edge_spec,
            HBM,
            HBM,
            HBM,
            HBM,
        ],
        out_specs=[row_spec, row_spec, edge_spec, edge_spec],
        out_shape=[jax.ShapeDtypeStruct(hn.shape, BF)] * 2 + [edge] * 2,
        input_output_aliases={7: 0, 8: 1},
        scratch_shapes=[pltpu.VMEM((2, nt, taps, c), BF), pltpu.SemaphoreType.DMA((2, nt))],
        compiler_params=pltpu.CompilerParams(vmem_limit_bytes=8 << 20),
        cost_estimate=cost(4),
        name=f"edges{layer}",
    )(info, lev, zp, rx, rd, own, other, hn, sp)


def tap_columns(ref, b, e, rows, width, gt):
    n = ref(0).shape[0]
    lane = lax.broadcasted_iota(jnp.int32, (n, width), 1)
    for s, k in ((rows, 0), (rows + 1, 0), (0, 1), (rows + 1, 1), (0, 2), (1, 2)):
        gt[0, 3 * k * n : 3 * (k + 1) * n, s * width : (s + 1) * width] = jnp.zeros((3 * n, width), gt.dtype)
    for r in range(rows):
        g = ref(r)
        left = jnp.where(lane < width - 1, pltpu.roll(g, width - 1, 1), 0.0)
        right = jnp.where(lane > 0, pltpu.roll(g, 1, 1), 0.0)
        for k in range(3):
            flag = e[b, r] if k == 0 else e[b, r + 1] if k == 2 else None
            for j, v in enumerate((left, g, right)):
                v = v if flag is None else v * flag
                at = (3 * k + j) * n
                gt[0, at : at + n, (r + k) * width : (r + k + 1) * width] = v.astype(gt.dtype)


def pack_rows(hx, rows, width, hs, row):
    hx[0:width] = hs[0]
    for r in range(rows):
        hx[(r + 1) * width : (r + 2) * width] = row(r)
    hx[(rows + 1) * width :] = hs[1]


def head_row(logit, cot, cot_r, kc, kp):
    gap = jnp.zeros((kp - kc, logit.shape[1]), F32)
    p = jax.nn.sigmoid(logit)
    q = p * (1.0 - p)
    d = [cot.astype(F32) * q[:kc], gap, cot_r.astype(F32) * q[kp : kp + kc], gap]
    return p[:kc].astype(BF), p[kp : kp + kc].astype(BF), jnp.concatenate(d, axis=0).astype(BF).T


def side(v, lane, j):
    width = v.shape[-1]
    if j == 0:
        return jnp.where(lane > 0, pltpu.roll(v, 1, 1), 0.0)
    if j == 2:
        return jnp.where(lane < width - 1, pltpu.roll(v, width - 1, 1), 0.0)
    return v


def head_kernel(
    info, lev, h, wk, wb, cb, cot, gb, cot_r,
    prob, psend, dl, gt, cb_x, cb_d, lp, bo, x, hx, lg, y,
):
    b = pl.program_id(0)
    rows, width, c = h.shape[2], h.shape[3], h.shape[4]
    kc, kb = cot.shape[2], gb.shape[1]
    kp, kq = wk.shape[1] // 2, wb.shape[0] // 18
    e = Borders(info, lev, rows)

    taps = 3 * c
    build(x, rows_of(h, (0, 0), rows), e, b)
    lg[...] = dot_nt(wk[0], x[:, :taps])
    lg[...] += dot_nt(wk[1], x[:, taps : 2 * taps])
    lg[...] += dot_nt(wk[2], x[:, 2 * taps :])

    def row(r, _):
        at = pl.ds(pl.multiple_of(r * width, width), width)
        prob[0, r], psend[0, r, :kc], dl[0, r] = head_row(lg[:, at] + cb[: 2 * kp], cot[0, r], cot_r[0, r, :kc], kc, kp)
        return 0

    lax.fori_loop(0, rows, row, 0)
    lp[0, 0] = lg[:, :width] + cb[: 2 * kp]
    lp[0, 1] = lg[:, (rows - 1) * width :] + cb[: 2 * kp]
    for r in range(rows):
        hx[r * width : (r + 1) * width] = h[0, 1, r]
    y[...] = dot_nt(wb[...], hx[...])
    n = 2 * kq
    lane = lax.broadcasted_iota(jnp.int32, (n, width), 1)
    for r in range(rows):
        v = cb[2 * kp : 2 * kp + n]
        for j in range(3):
            s = y[(3 + j) * n : (4 + j) * n, r * width : (r + 1) * width]
            if r > 0:
                s = s + y[j * n : (j + 1) * n, (r - 1) * width : r * width] * e[b, r]
            if r < rows - 1:
                s = s + y[(6 + j) * n : (7 + j) * n, (r + 1) * width : (r + 2) * width] * e[b, r + 1]
            v = v + side(s, lane, j)
        bo[0, r] = v
        rest = jnp.zeros((kp - kc - kb, width), F32)
        psend[0, r, kc:] = jnp.concatenate([v[kq : kq + kb], rest], axis=0).astype(BF)
    small = jnp.zeros((kq - kb, width), F32)
    g = gb[0].astype(F32)

    def columns(r):
        return jnp.concatenate([g[:, r], small, cot_r[0, r, kc:].astype(F32)[:kb], small], axis=0)

    tap_columns(columns, b, e, rows, width, gt)
    for i in range(2):
        s = i * (rows + 1)
        db = dot_tn(gt[0, :, s * width : (s + 1) * width], wb[...]).astype(BF)

        @pl.when((info[1] == 0) == (i == 1))
        def _():
            cb_x[0] = db

        @pl.when((info[1] == 0) == (i == 0))
        def _():
            cb_d[0] = db


def head(info, lev, h, wk, wb, cb, cot, gb, cot_r, after=()):
    nb, nt, rows, width, c = h.shape
    kc, kb, kp2, kq2 = cot.shape[2], gb.shape[1], wk.shape[1], wb.shape[0] // 9
    batches = cot.shape[0]
    m = rows * width
    ext = (rows + 2) * width

    def at_b(shape):
        return pl.BlockSpec((1,) + shape, lambda b, info: (b,) + (0,) * len(shape))

    def at_all(shape):
        return pl.BlockSpec((1,) + shape, lambda b, info: (info[0] * nb + b,) + (0,) * len(shape))

    def whole(shape):
        return pl.BlockSpec(shape, lambda b, info: (0,) * len(shape), pipeline_mode=pl.Buffered(1))

    return pl.pallas_call(
        ordered(head_kernel, 9, after),
        grid_spec=pltpu.PrefetchScalarGridSpec(
            num_scalar_prefetch=1,
            grid=(nb,),
            in_specs=[
                SMEM,
                at_b((nt, rows, width, c)),
                whole(wk.shape),
                whole(wb.shape),
                whole(cb.shape),
                at_all((rows, kc, width)),
                at_all((kb, rows, width)),
                at_b((rows, kp2 // 2, width)),
            ]
            + [ANY] * len(after),
            out_specs=[
                at_all((rows, kc, width)),
                at_b((rows, kp2 // 2, width)),
                at_b((rows, width, kp2)),
                at_b((9 * kq2, ext)),
                at_b((width, c)),
                at_b((width, c)),
                at_b((2, kp2, width)),
                at_b((rows, kq2, width)),
            ],
            scratch_shapes=[
                pltpu.VMEM((m, 9 * c), BF),
                pltpu.VMEM((m, c), BF),
                pltpu.VMEM((kp2, m), F32),
                pltpu.VMEM((9 * kq2, m), F32),
            ],
        ),
        out_shape=[
            jax.ShapeDtypeStruct((batches, rows, kc, width), BF),
            jax.ShapeDtypeStruct((nb, rows, kp2 // 2, width), BF),
            jax.ShapeDtypeStruct((nb, rows, width, kp2), BF),
            jax.ShapeDtypeStruct((nb, 9 * kq2, ext), BF),
            jax.ShapeDtypeStruct((nb, width, c), BF),
            jax.ShapeDtypeStruct((nb, width, c), BF),
            jax.ShapeDtypeStruct((nb, 2, kp2, width), F32),
            jax.ShapeDtypeStruct((nb, rows, kq2, width), F32),
        ],
        compiler_params=pltpu.CompilerParams(vmem_limit_bytes=17 << 20),
        cost_estimate=cost(14),
        name="head",
    )(info, lev, h, wk, wb, cb, cot, gb, cot_r, *after)


def head_edge_kernel(
    info, lev, rx, rd, wk, wb, lp, bo, cot, cot_r, cb_x, cb_d, prob_i, psend_i, dl_i,
    prob, psend, dl, boxo, cx, cd, hs, ds, bs, bx,
):
    i = pl.program_id(0)
    nb, nt, width, c = rx.shape
    kc, kb, rows = cot.shape[2], boxo.shape[1], boxo.shape[2]
    kp, kq = wk.shape[1] // 2, bo.shape[2] // 2
    taps = 3 * c
    n = 2 * kq
    e = Borders(info, lev, rows)
    edge = i * rows
    from_x = (info[1] == 0) == (i == 1)

    @pl.when(from_x)
    def _():
        hs[...] = rx[...]

    @pl.when(jnp.logical_not(from_x))
    def _():
        hs[...] = rd[...]

    p = []
    for b in range(nb):
        v = hs[b, 0]
        p.append(keep_if(jnp.concatenate([down(v), v, up(v)], axis=1), e[b, edge]))
    logit = dot_nt(wk[0], jnp.concatenate(p, axis=0))
    lane = lax.broadcasted_iota(jnp.int32, (n, width), 1)
    for b in range(nb):
        lg = logit[:, b * width : (b + 1) * width] + lp[b, 0]
        prob[b, 0], psend[b, 0, :kc], d = head_row(lg, cot[b, 0], cot_r[b, 0, :kc], kc, kp)
        dl[b, 0] = d
        ds[b * width : (b + 1) * width, :] = d
        y = dot_nt(wb[...], hs[b, 1]) * e[b, edge]
        v = bo[b, i * (rows - 1)]
        for j in range(3):
            v = v + side(y[j * n : (j + 1) * n, :], lane, j)
        bs[b, i] = v
        gap = jnp.zeros((kp - kc - kb, width), F32)
        psend[b, 0, kc:] = jnp.concatenate([v[kq : kq + kb], gap], axis=0).astype(BF)

    @pl.when(i == 1)
    def _():
        for b in range(nb):
            for r in range(rows):
                v = bs[b, 0] if r == 0 else bs[b, 1] if r == rows - 1 else bo[b, r]
                bx[:, r, :] = v
            boxo[b] = bx[:kb].astype(BF)

    s = dot(ds[...], wk[0]).reshape(nb, width, taps)
    dc = up(s[:, :, :c]) + s[:, :, c : 2 * c] + down(s[:, :, 2 * c :])
    for b in range(nb):
        v = keep_if(dc[b].astype(BF), e[b, edge])

        @pl.when(from_x)
        def _():
            cx[b, 0] = v
            cx[b, 1] = cb_x[b]

        @pl.when(jnp.logical_not(from_x))
        def _():
            cd[b, 0] = v
            cd[b, 1] = cb_d[b]


def head_edges(info, lev, rx, rd, wk, wb, lp, bo, cot, cot_r, cb_x, cb_d, prob, psend, dl, kb):
    nb, nt, width, c = rx.shape
    rows = cot.shape[1]
    kc, kp2, kq2 = cot.shape[2], wk.shape[1], bo.shape[2]

    def whole(shape):
        return pl.BlockSpec(shape, lambda i, info: (0,) * len(shape), pipeline_mode=pl.Buffered(1))

    def at_i(shape):
        return pl.BlockSpec(shape, lambda i, info: (0, i) + (0,) * (len(shape) - 2))

    def edge_of(shape):
        return pl.BlockSpec(shape, lambda i, info: (0, i * (rows - 1)) + (0,) * (len(shape) - 2))

    def edge_all(shape):
        return pl.BlockSpec(shape, lambda i, info: (info[0], i * (rows - 1)) + (0,) * (len(shape) - 2))

    edge = jax.ShapeDtypeStruct((nb, nt, width, c), BF)
    arrays = (prob, psend, dl)
    return pl.pallas_call(
        head_edge_kernel,
        grid_spec=pltpu.PrefetchScalarGridSpec(
            num_scalar_prefetch=1,
            grid=(2,),
            in_specs=[
                SMEM,
                whole(rx.shape),
                whole(rd.shape),
                pl.BlockSpec((1,) + wk.shape[1:], lambda i, info: (2 * i, 0, 0)),
                pl.BlockSpec((3 * kq2, c), lambda i, info: (2 * i, 0)),
                at_i((nb, 1, kp2, width)),
                whole(bo.shape),
                edge_all((nb, 1, kc, width)),
                edge_of((nb, 1, kp2 // 2, width)),
                whole(cb_x.shape),
                whole(cb_d.shape),
            ]
            + [HBM] * len(arrays),
            out_specs=[
                edge_all((nb, 1, kc, width)),
                edge_of((nb, 1, kp2 // 2, width)),
                edge_of((nb, 1, width, kp2)),
                pl.BlockSpec((nb, kb, rows, width), lambda i, info: (info[0], 0, 0, 0)),
                pl.BlockSpec(rx.shape, lambda i, info: (0, 0, 0, 0)),
                pl.BlockSpec(rx.shape, lambda i, info: (0, 0, 0, 0)),
            ],
            scratch_shapes=[
                pltpu.VMEM(rx.shape, BF),
                pltpu.VMEM((nb * width, kp2), BF),
                pltpu.VMEM((nb, 2, kq2, width), F32),
                pltpu.VMEM((kq2, rows, width), F32),
            ],
        ),
        out_shape=[jax.ShapeDtypeStruct(v.shape, BF) for v in arrays]
        + [jax.ShapeDtypeStruct((cot.shape[0], kb, rows, width), BF)]
        + [edge, edge],
        input_output_aliases={12 + i: i for i in range(len(arrays))},
        compiler_params=pltpu.CompilerParams(vmem_limit_bytes=8 << 20),
        cost_estimate=cost(6),
        name="head_edges",
    )(info, lev, rx, rd, wk, wb, lp, bo, cot, cot_r, cb_x, cb_d, *arrays)


def head_weights_kernel(info, lev, h, rx, rd, dl, gt, own, other, token, x, hx, acc, accb, small, sums, hs, *, kc, kb):
    b, nb = pl.program_id(0), pl.num_programs(0)
    rows, width, c = h.shape[2], h.shape[3], h.shape[4]
    token[...] = jnp.zeros_like(token)
    kp, kq = dl.shape[-1] // 2, accb.shape[0] // 18
    taps = 3 * c
    e = Borders(info, lev, rows)
    pick_halo(info, rx, rd, hs, (0, 0))
    build(x, rows_of(h, (0, 0), rows), e, b, lambda: hs[0], lambda: hs[1])
    pick_halo(info, rx, rd, hs, (0, 1))
    pack_rows(hx, rows, width, hs, lambda r: h[0, 1, r])
    g = dl[0].reshape(rows * width, 2 * kp)

    @pl.when(b == 0)
    def _():
        acc[...] = jnp.zeros_like(acc)
        accb[...] = jnp.zeros_like(accb)
        small[...] = jnp.zeros_like(small)

    acc[...] += dot_tn(g, x[...])
    accb[...] += dot(gt[0], hx[...])
    small[:, : 2 * kp] += jnp.sum(g.astype(F32), axis=0, keepdims=True)
    ones = jnp.ones((8, gt.shape[2]), BF)
    s = dot_nt(ones, gt[0, 8 * kq : 10 * kq, :])[:1]
    small[:, 2 * kp :] += jnp.concatenate([s, jnp.zeros((1, LANES - 2 * kq), F32)], axis=1)

    def fill(ref, a):
        for k in range(3):
            ref[k * kc : (k + 1) * kc, :] = acc[a * kp : a * kp + kc, k * taps : (k + 1) * taps]
            at = 3 * kc + k * kq
            for j in range(3):
                first = (3 * k + j) * 2 * kq + a * kq
                ref[at : at + kq, j * c : (j + 1) * c] = accb[first : first + kq, :]
        end = 3 * (kc + kq)
        if end < ref.shape[0]:
            ref[end:, :] = jnp.zeros((ref.shape[0] - end, taps), F32)
        at = 3 * kc + kb
        ref[at : at + 1, :kp] = small[:, a * kp : (a + 1) * kp]
        ref[at : at + 1, kp : kp + LANES] = pltpu.roll(small[:, 2 * kp :], (LANES - a * kq) % LANES, 1)

    @pl.when(b == nb - 1)
    def _():
        for a, out in ((1, other), (0, own)):
            fill(sums, a)
            out[...] = sums[...].astype(BF)


def head_weights(info, lev, h, rx, rd, dl, gt, kc, kb, after=()):
    nb, nt, rows, width, c = h.shape
    kp2 = dl.shape[-1]
    kq2 = gt.shape[1] // 9
    m = rows * width
    size = -(-3 * (kc + kq2 // 2) // LANES) * LANES

    def at_b(shape):
        return pl.BlockSpec((1,) + shape, lambda b: (b,) + (0,) * len(shape))

    def whole(shape):
        return pl.BlockSpec(shape, lambda b: (0,) * len(shape), pipeline_mode=pl.Buffered(1))

    return pl.pallas_call(
        ordered(functools.partial(head_weights_kernel, kc=kc, kb=kb), 7, after),
        grid=(nb,),
        in_specs=[
            SMEM,
            SMEM,
            at_b((nt, rows, width, c)),
            at_b((nt, width, c)),
            at_b((nt, width, c)),
            at_b((rows, width, kp2)),
            at_b(gt.shape[1:]),
        ]
        + [ANY] * len(after),
        out_specs=[whole((size, 3 * c)), whole((size, 3 * c)), TOKEN_SPEC],
        out_shape=[jax.ShapeDtypeStruct((size, 3 * c), BF)] * 2 + [TOKEN],
        scratch_shapes=[
            pltpu.VMEM((m, 9 * c), BF),
            pltpu.VMEM(((rows + 2) * width, c), BF),
            pltpu.VMEM((kp2, 9 * c), F32),
            pltpu.VMEM((9 * kq2, c), F32),
            pltpu.VMEM((1, kp2 + LANES), F32),
            pltpu.VMEM((size, 3 * c), F32),
            pltpu.VMEM((2, width, c), BF),
        ],
        compiler_params=pltpu.CompilerParams(vmem_limit_bytes=21 << 20),
        cost_estimate=cost(12),
        name="head_weights",
    )(info, lev, h, rx, rd, dl, gt, *after)


def head_inputs_kernel(info, lev, dl, gt, rx, rd, wk, wb, sp, *rest):
    dz, sx, sd, token, *_, x, hs = rest
    token[...] = jnp.zeros_like(token)
    b = pl.program_id(0)
    rows, width, c = sp.shape[2], sp.shape[3], sp.shape[4]
    kp2 = dl.shape[-1]
    taps = 3 * c
    e = Borders(info, lev, rows)
    build(x, rows_of(dl, (0,), rows), e, b, taps=False)
    s = dot(x[:, kp2 : 2 * kp2], wk[1])
    s = s + dot(x[:, :kp2], wk[2])
    s = s + dot(x[:, 2 * kp2 :], wk[0])
    s = s.reshape(rows, width, taps)
    dc = up(s[:, :, :c]) + s[:, :, c : 2 * c] + down(s[:, :, 2 * c :])
    db = dot_tn(gt[0, :, width : (rows + 1) * width], wb[...]).reshape(rows, width, c)
    for t, dh in ((0, dc), (1, db)):
        pick_halo(info, rx, rd, hs, (0, t))
        for r in range(rows):
            v = dh[r]
            if r == 0:
                v = v + hs[0].astype(F32)
            if r == rows - 1:
                v = v + hs[1].astype(F32)
            dz[0, t, r] = (v * sp[0, t, r].astype(F32)).astype(BF)
        put_edges(info, dz[0, t, 0], dz[0, t, rows - 1], sx, sd, (0, t))


def head_inputs(info, lev, dl, gt, rx, rd, wk, wb, sp, gate, after=()):
    nb, nt, rows, width, c = sp.shape
    kp2 = dl.shape[-1]
    m = rows * width

    def at_b(shape):
        return pl.BlockSpec((1,) + shape, lambda b: (b,) + (0,) * len(shape))

    def whole(shape):
        return pl.BlockSpec(shape, lambda b: (0,) * len(shape), pipeline_mode=pl.Buffered(1))

    return pl.pallas_call(
        ordered(head_inputs_kernel, 9, gate + after),
        grid=(nb,),
        in_specs=[
            SMEM,
            SMEM,
            at_b((rows, width, kp2)),
            at_b(gt.shape[1:]),
            at_b((nt, width, c)),
            at_b((nt, width, c)),
            whole(wk.shape),
            whole(wb.shape),
            at_b((nt, rows, width, c)),
        ]
        + [ANY] * len(gate + after),
        out_specs=[at_b((nt, rows, width, c)), at_b((nt, width, c)), at_b((nt, width, c)), TOKEN_SPEC] + [ANY] * len(gate),
        out_shape=[
            jax.ShapeDtypeStruct(sp.shape, BF),
            jax.ShapeDtypeStruct((nb, nt, width, c), BF),
            jax.ShapeDtypeStruct((nb, nt, width, c), BF),
        ]
        + [TOKEN]
        + [jax.ShapeDtypeStruct(v.shape, v.dtype) for v in gate],
        input_output_aliases={9 + k: 4 + k for k in range(len(gate))},
        scratch_shapes=[pltpu.VMEM((m, 3 * kp2), BF), pltpu.VMEM((2, width, c), BF)],
        compiler_params=pltpu.CompilerParams(vmem_limit_bytes=14 << 20),
        cost_estimate=cost(9),
        name="head_inputs",
    )(info, lev, dl, gt, rx, rd, wk, wb, sp, *gate, *after)


def weights_kernel(info, lev, h, rx, rd, dz, keep, send, token, x, acc, bias, hs):
    t, b, nb = pl.program_id(0), pl.program_id(1), pl.num_programs(1)
    rows, width, c = h.shape[2], h.shape[3], h.shape[4]
    e = Borders(info, lev, rows)
    pick_halo(info, rx, rd, hs, (0, 0))
    build(x, rows_of(h, (0, 0), rows), e, b, lambda: hs[0], lambda: hs[1])
    g = dz[0, 0].reshape(rows * width, c)
    part = dot_tn(x[...], g)
    total = jnp.sum(g.astype(F32), axis=0, keepdims=True)
    taps = acc.shape[0]

    @pl.when(b == 0)
    def _():
        acc[...] = part
        bias[...] = total

    @pl.when(b != 0)
    def _():
        acc[...] += part
        bias[...] += total

    token[...] = jnp.zeros_like(token)
    for i, out in enumerate((send, keep)):

        @pl.when(jnp.logical_and(b == nb - 1, t == i))
        def _():
            out[:taps, :] = acc[...].astype(out.dtype)
            out[taps:, :] = jnp.broadcast_to(bias[...].astype(out.dtype), (out.shape[0] - taps, c))


def weights(layer, info, lev, h, rx, rd, dz, after=()):
    nb, nt, rows, width, c = h.shape

    def tower(t, info):
        return jnp.where(t == 0, 1 - info[0], info[0])

    row_spec = pl.BlockSpec((1, 1, rows, width, c), lambda t, b, info: (b, tower(t, info), 0, 0, 0))
    edge_spec = pl.BlockSpec((1, 1, width, c), lambda t, b, info: (b, tower(t, info), 0, 0))
    taps = 9 * c
    return pl.pallas_call(
        ordered(weights_kernel, 6, after),
        grid_spec=pltpu.PrefetchScalarGridSpec(
            num_scalar_prefetch=1,
            grid=(nt, nb),
            in_specs=[SMEM, row_spec, edge_spec, edge_spec, row_spec] + [ANY] * len(after),
            out_specs=[pl.BlockSpec((taps + LANES, c), lambda t, b, info: (0, 0))] * 2 + [TOKEN_SPEC],
            scratch_shapes=[
                pltpu.VMEM((rows * width, taps), BF),
                pltpu.VMEM((taps, c), F32),
                pltpu.VMEM((1, c), F32),
                pltpu.VMEM((2, width, c), BF),
            ],
        ),
        out_shape=[jax.ShapeDtypeStruct((taps + LANES, c), BF)] * 2 + [TOKEN],
        compiler_params=pltpu.CompilerParams(vmem_limit_bytes=14 << 20),
        cost_estimate=cost(8),
        name=f"weights{layer}",
    )(info, lev, h, rx, rd, dz, *after)


def inputs_kernel(layer, info, lev, dz, rx, rd, own, other, *rest):
    if layer:
        sp, out, token, sx, sd, x, wv, wt, hs, sem = rest
    else:
        out, token, *_, x, wv, wt, hs, sem = rest
    token[...] = jnp.zeros_like(token)
    t, b = pl.program_id(0), pl.program_id(1)
    rows, width, c = dz.shape[2], dz.shape[3], dz.shape[4]
    e = Borders(info, lev, rows)

    @pl.when(jnp.logical_and(t == 0, b == 0))
    def _():
        start_weights(info, layer, own, other, wv, sem)

    pick_halo(info, rx, rd, hs, (0, 0))
    build(x, rows_of(dz, (0, 0), rows), e, b, lambda: hs[0], lambda: hs[1])

    @pl.when(b == 0)
    def _():
        wait_weights(own, wv, sem, t)
        for i in range(9):
            wt[:, (8 - i) * c : (9 - i) * c] = wv[t, i * c : (i + 1) * c, :]

    dh = dot_nt(x[...], wt[...]).astype(BF)
    if not layer:
        out[0, 0] = dh.reshape(rows, width, c)
        return
    dz_next = (dh.astype(F32).reshape(rows, width, c) * sp[0, 0].astype(F32)).astype(BF)
    out[0, 0] = dz_next
    put_edges(info, dz_next[0], dz_next[rows - 1], sx, sd, (0, 0))


def inputs(layer, info, lev, dz, rx, rd, own, other, sp=None, gate=(), after=()):
    nb, nt, rows, width, c = dz.shape
    row_spec = pl.BlockSpec((1, 1, rows, width, c), lambda t, b: (b, t, 0, 0, 0))
    edge_spec = pl.BlockSpec((1, 1, width, c), lambda t, b: (b, t, 0, 0))
    edge = jax.ShapeDtypeStruct((nb, nt, width, c), BF)
    taps = own.shape[1]
    return pl.pallas_call(
        ordered(functools.partial(inputs_kernel, layer), 8 if layer else 7, gate + after),
        grid=(nt, nb),
        in_specs=[SMEM, SMEM, row_spec, edge_spec, edge_spec, HBM, HBM] + ([row_spec] if layer else []) + [ANY] * len(gate + after),
        out_specs=[row_spec, TOKEN_SPEC] + ([edge_spec, edge_spec] if layer else []) + [ANY] * len(gate),
        out_shape=[jax.ShapeDtypeStruct(dz.shape, BF)]
        + [TOKEN]
        + ([edge, edge] if layer else [])
        + [jax.ShapeDtypeStruct(v.shape, v.dtype) for v in gate],
        input_output_aliases={7 + k: 2 + k for k in range(len(gate))},
        scratch_shapes=[
            pltpu.VMEM((rows * width, taps), BF),
            pltpu.VMEM((nt, taps, c), BF),
            pltpu.VMEM((c, taps), BF),
            pltpu.VMEM((2, width, c), BF),
            pltpu.SemaphoreType.DMA((nt,)),
        ],
        compiler_params=pltpu.CompilerParams(vmem_limit_bytes=13 << 20),
        cost_estimate=cost(9),
        name=f"inputs{layer}",
    )(info, lev, dz, rx, rd, own, other, *([sp] if layer else []), *gate, *after)


def swap_section(value):
    return lax.ppermute(value, "section", [(0, 1), (1, 0)])


def swap_edges(sx, sd):
    count = lax.axis_size("tile")
    even = [p for i in range(0, count - 1, 2) for p in ((i, i + 1), (i + 1, i))]
    odd = [p for i in range(1, count - 1, 2) for p in ((i, i + 1), (i + 1, i))]
    return lax.ppermute(sx, "tile", even), lax.ppermute(sd, "tile", odd)


def combine_kernel(plan, info, *refs):
    ins, outs = list(refs[: sum(sum(p) for p in plan)]), refs[sum(sum(p) for p in plan) :]
    for counts, out in zip(plan, outs):
        lanes = out.shape[1] // len(counts)
        for i, count in enumerate(counts):
            terms = [ins.pop(0)[...].astype(F32) for _ in range(count)]
            out[:, i * lanes : (i + 1) * lanes] = functools.reduce(jnp.add, terms).astype(out.dtype)


def combine(name, info, shape, outs, gate=(), after=()):
    rows, lanes = shape
    views = [v for parts in outs for terms in parts for v in terms]

    def spec(view):
        return pl.BlockSpec(shape, lambda i, info: (view[1](info), view[2]))

    plan = [[len(terms) for terms in parts] for parts in outs]
    return pl.pallas_call(
        ordered(functools.partial(combine_kernel, plan), 1 + len(views), gate + after),
        grid_spec=pltpu.PrefetchScalarGridSpec(
            num_scalar_prefetch=1,
            grid=(1,),
            in_specs=[spec(v) for v in views] + [ANY] * len(gate + after),
            out_specs=[pl.BlockSpec((rows, lanes * len(parts)), lambda i, info: (0, 0)) for parts in outs]
            + [ANY] * len(gate),
        ),
        out_shape=[jax.ShapeDtypeStruct((rows, lanes * len(parts)), BF) for parts in outs]
        + [jax.ShapeDtypeStruct(v.shape, v.dtype) for v in gate],
        input_output_aliases={1 + len(views) + k: len(outs) + k for k in range(len(gate))},
        compiler_params=pltpu.CompilerParams(vmem_limit_bytes=7 << 20),
        cost_estimate=cost(2),
        name=name,
    )(info, *[v[0] for v in views], *gate, *after)


def join_kernel(bits, split, info, *refs):
    n = len(bits)
    for i, bit in enumerate(bits):
        cur, got = refs[2 * i], refs[2 * i + 1]
        outs = refs[2 * n :] if split else refs[2 * n + i : 2 * n + i + 1]
        m, lanes = cur.shape[0], cur.shape[1] // len(outs)
        mine = (info[2] >> bit) & 1
        for j, out in enumerate(outs):
            at = slice(j * lanes, (j + 1) * lanes)

            @pl.when(mine == 0)
            def _():
                out[:m, :] = cur[:, at]
                out[m:, :] = got[:, at]

            @pl.when(mine != 0)
            def _():
                out[:m, :] = got[:, at]
                out[m:, :] = cur[:, at]


def join(name, info, bits, pairs, split=False, after=()):
    arrays = [v for pair in pairs for v in pair]
    shapes = [(2 * cur.shape[0], cur.shape[1]) for cur, _ in pairs]
    if split:
        shapes = [(shapes[0][0], shapes[0][1] // 2)] * 2

    def whole(shape):
        return pl.BlockSpec(shape, lambda i, info: (0, 0))

    return pl.pallas_call(
        ordered(functools.partial(join_kernel, bits, split), 1 + len(arrays), after),
        grid_spec=pltpu.PrefetchScalarGridSpec(
            num_scalar_prefetch=1,
            grid=(1,),
            in_specs=[whole(v.shape) for v in arrays] + [ANY] * len(after),
            out_specs=[whole(s) for s in shapes],
        ),
        out_shape=[jax.ShapeDtypeStruct(s, BF) for s in shapes],
        compiler_params=pltpu.CompilerParams(vmem_limit_bytes=7 << 20),
        cost_estimate=cost(2),
        name=name,
    )(info, *arrays, *after)


def relay_kernel(*refs):
    del refs


def relay(name, gate, after):
    return pl.pallas_call(
        ordered(relay_kernel, 0, gate + after),
        in_specs=[ANY] * len(gate + after),
        out_specs=[ANY] * len(gate),
        out_shape=[jax.ShapeDtypeStruct(v.shape, v.dtype) for v in gate],
        input_output_aliases={k: k for k in range(len(gate))},
        compiler_params=pltpu.CompilerParams(vmem_limit_bytes=1 << 20),
        cost_estimate=cost(1),
        name=name,
    )(*gate, *after)


class TileSum:
    def __init__(self, name, info, whole, *terms):
        self.name, self.info = name, info
        rows, lanes = terms[0].shape
        self.shape = (rows, lanes // 2)
        self.parts = [[(v, lambda info: 0, i) for v in terms] for i in range(2)]
        self.count = lax.axis_size("tile")
        bits = self.count.bit_length() - 1
        near = [(0, 1), (1, 0)]
        self.plan = [("halve", step) for step in near]
        if whole or bits > 4:
            self.plan += [("add", (bit,)) for bit in range(2, bits)]
        else:
            self.plan += [("halve", (bit,)) for bit in range(2, bits - 1)]
            self.plan += [("add", (bit,)) for bit in range(max(bits - 1, 2), bits)]
            self.plan += [("double", (bit,)) for bit in reversed(range(2, bits - 1))]
        self.plan += [("double", step) for step in reversed(near)]
        self.step = 0
        self.sends = None

    def exchange(self, value, bit):
        return lax.ppermute(value, "tile", [(i, i ^ (1 << bit)) for i in range(self.count)])

    def start(self, *after, gate=()):
        kind, bits = self.plan.pop(0)
        name = f"{self.name}_{self.step}"
        self.step += 1
        if kind == "halve":
            rows, lanes = self.shape
            self.shape = (rows // 2, lanes)
            bit_of = bits * 2 if len(bits) == 1 else bits

            def half(view, bit, other):
                array, row, lane = view
                return array, lambda info: 2 * row(info) + (((info[2] >> bit) & 1) ^ other), lane

            sent = [[half(v, bit, 1) for v in terms] for terms, bit in zip(self.parts, bit_of)]
            self.parts = [[half(v, bit, 0) for v in terms] for terms, bit in zip(self.parts, bit_of)]
            outs = [sent] if len(bits) == 1 else [[terms] for terms in sent]
            sends = combine(name, self.info, self.shape, outs, gate, after)
        elif kind == "add" or self.kind != "double":
            outs = [self.parts] if len(bits) == 1 else [[terms] for terms in self.parts]
            sends = combine(name, self.info, self.shape, outs, gate, after)
        else:
            sends = join(name, self.info, self.bits, self.pairs, len(bits) > len(self.pairs), after)
        passed = tuple(sends[len(bits) :])
        sends = tuple(sends[: len(bits)])
        self.kind, self.bits, self.sends = kind, bits, sends
        got = [self.exchange(v, bit) for v, bit in zip(sends, bits)]
        if kind == "halve":
            lane = (lambda i: i) if len(bits) == 1 else (lambda i: 0)
            pick = (lambda i: got[0]) if len(bits) == 1 else (lambda i: got[i])
            self.parts = [terms + [(pick(i), lambda info: 0, lane(i))] for i, terms in enumerate(self.parts)]
        elif kind == "add":
            self.parts = [[(v, lambda info: 0, i) for v in (sends[0], got[0])] for i in range(2)]
        else:
            self.pairs = list(zip(sends, got))
        return sends + passed

    def result(self, *after):
        return join(f"{self.name}_{self.step}", self.info, self.bits, self.pairs, False, after)


def pick_kernel(info, cot, gb, out):
    rows, kc, kb = cot.shape[1], cot.shape[2], gb.shape[1]
    g = gb[0].astype(F32)
    gap = jnp.zeros((out.shape[2] - kc - kb, out.shape[3]), F32)
    for r in range(rows):
        out[0, r] = jnp.concatenate([cot[0, r].astype(F32), g[:, r], gap], axis=0).astype(BF)


def pick(info, cot, gb, nb, kp, after=()):
    def at_all(shape):
        return pl.BlockSpec((1,) + shape[1:], lambda b, info: ((1 - info[0]) * nb + b,) + (0,) * (len(shape) - 1))

    shape = (nb, cot.shape[1], kp, cot.shape[3])
    return pl.pallas_call(
        ordered(pick_kernel, 3, after),
        grid_spec=pltpu.PrefetchScalarGridSpec(
            num_scalar_prefetch=1,
            grid=(nb,),
            in_specs=[at_all(cot.shape), at_all(gb.shape)] + [ANY] * len(after),
            out_specs=pl.BlockSpec((1,) + shape[1:], lambda b, info: (b, 0, 0, 0)),
        ),
        out_shape=jax.ShapeDtypeStruct(shape, BF),
        compiler_params=pltpu.CompilerParams(vmem_limit_bytes=8 << 20),
        cost_estimate=cost(2),
        name="pick",
    )(info, cot, gb, *after)


def gather_kernel(tower, classes, boxes, out):
    out[...] = jnp.zeros_like(out)
    nt, c = tower.shape[1], tower.shape[2]
    out[:nt, :c] = tower[0]
    out[nt : nt + 1, : classes.shape[0]] = classes[...].reshape(1, -1)
    out[nt + 1 : nt + 2, : boxes.shape[0]] = boxes[...].reshape(1, -1)


def gather(tower, classes, boxes, lanes):
    return pl.pallas_call(
        gather_kernel,
        out_shape=jax.ShapeDtypeStruct((8, lanes), F32),
        cost_estimate=cost(1),
        name="gather",
    )(tower, classes, boxes)


def pick_weights_kernel(thin, small, out):
    gap = jnp.zeros((out.shape[1] - thin.shape[1] - small.shape[1], out.shape[2]), F32)
    out[0] = jnp.concatenate([thin[0].astype(F32), small[0].astype(F32), gap], axis=0).astype(BF)


def pick_weights(thin, small, kp, after=()):
    def at_k(shape):
        return pl.BlockSpec((1,) + shape[1:], lambda k: (k, 0, 0))

    shape = (thin.shape[0], kp, thin.shape[2])
    return pl.pallas_call(
        ordered(pick_weights_kernel, 2, after),
        grid=(shape[0],),
        in_specs=[at_k(thin.shape), at_k(small.shape)] + [ANY] * len(after),
        out_specs=at_k(shape),
        out_shape=jax.ShapeDtypeStruct(shape, BF),
        compiler_params=pltpu.CompilerParams(vmem_limit_bytes=6 << 20),
        cost_estimate=cost(2),
        name="pick_weights",
    )(thin, small, *after)


def pack_kernel(own, other, bias, bias_r, wk, wb, cb, *, kc, kb, kq, towers):
    k = pl.program_id(0)
    kp = own.shape[1]
    c = wb.shape[1]
    gap = jnp.zeros((kp - kc, wk.shape[2]), F32)
    for half, v in enumerate((own, other)):
        wk[0, half * kp : (half + 1) * kp, :] = jnp.concatenate([v[0].astype(F32)[:kc], gap], axis=0).astype(BF)
    u, v = own[0].astype(F32)[kc : kc + kb], other[0].astype(F32)[kc : kc + kb]
    small = jnp.zeros((kq - kb, c), F32)
    for j in range(3):
        at = slice(j * c, (j + 1) * c)
        rows = jnp.concatenate([u[:, at], small, v[:, at], small], axis=0).astype(BF)
        wb[pl.ds(pl.multiple_of((3 * k + j) * 2 * kq, 2 * kq), 2 * kq), :] = rows

    @pl.when(k == 0)
    def _():
        wide = jnp.zeros((1, kp - kc), F32)
        thin = jnp.zeros((1, kq - kb), F32)
        rest = jnp.zeros((1, cb.shape[0] - 2 * kp - kq - kb), F32)
        classes, boxes = slice(towers, towers + 1), slice(towers + 1, towers + 2)
        parts = [bias[classes, :kc], wide, bias_r[classes, :kc], wide, bias[boxes, :kb], thin, bias_r[boxes, :kb], rest]
        cb[...] = jnp.broadcast_to(jnp.concatenate(parts, axis=1), (cb.shape[1], cb.shape[0])).T


def pack(own, other, bias, bias_r, kc, kb, kq, towers, after=()):
    k, kp, c3 = own.shape
    at_k = pl.BlockSpec((1, kp, c3), lambda k: (k, 0, 0))

    def whole(shape):
        return pl.BlockSpec(shape, lambda k: (0,) * len(shape))

    shapes = [(k, 2 * kp, c3), (18 * kq, c3 // 3), (2 * kp + LANES, LANES)]
    return pl.pallas_call(
        ordered(functools.partial(pack_kernel, kc=kc, kb=kb, kq=kq, towers=towers), 4, after),
        grid=(k,),
        in_specs=[at_k, at_k, whole(bias.shape), whole(bias.shape)] + [ANY] * len(after),
        out_specs=[pl.BlockSpec((1,) + shapes[0][1:], lambda k: (k, 0, 0)), whole(shapes[1]), whole(shapes[2])],
        out_shape=[jax.ShapeDtypeStruct(s, t) for s, t in zip(shapes, (BF, BF, F32))],
        compiler_params=pltpu.CompilerParams(vmem_limit_bytes=10 << 20),
        cost_estimate=cost(3),
        name="pack",
    )(own, other, bias, bias_r, *after)


def place_kernel(info, prob_i, box_i, got, prob, box, token, bx):
    rows, kc, kb = prob.shape[1], prob.shape[2], box.shape[1]
    for r in range(rows):
        prob[0, r] = got[0, r, :kc]
        bx[:, r, :] = got[0, r, kc:].astype(F32)[:kb]
    box[0] = bx[...].astype(BF)
    token[...] = jnp.zeros_like(token)


def place(info, prob, box, got, after=()):
    nb = got.shape[0]

    def at_all(shape):
        return pl.BlockSpec((1,) + shape[1:], lambda b, info: ((1 - info[0]) * nb + b,) + (0,) * (len(shape) - 1))

    return pl.pallas_call(
        ordered(place_kernel, 4, after),
        grid_spec=pltpu.PrefetchScalarGridSpec(
            num_scalar_prefetch=1,
            grid=(nb,),
            in_specs=[HBM, HBM, pl.BlockSpec((1,) + got.shape[1:], lambda b, info: (b, 0, 0, 0))] + [ANY] * len(after),
            out_specs=[at_all(prob.shape), at_all(box.shape), TOKEN_SPEC],
            scratch_shapes=[pltpu.VMEM(box.shape[1:], F32)],
        ),
        out_shape=[jax.ShapeDtypeStruct(v.shape, BF) for v in (prob, box)] + [TOKEN],
        input_output_aliases={1: 0, 2: 1},
        compiler_params=pltpu.CompilerParams(vmem_limit_bytes=8 << 20),
        cost_estimate=cost(2),
        name="place",
    )(info, prob, box, got, *after)


def after(value, *others):
    return lax.optimization_barrier((value,) + others)[0]


def on_device(
    features,
    levels,
    tower_weight,
    tower_bias,
    class_weight,
    class_bias,
    box_weight,
    box_bias,
    class_cotangent,
    box_cotangent,
):
    section = lax.axis_index("section")
    tile = lax.axis_index("tile")
    nb, nt, rows, width, c = features.shape
    kc, kb = class_weight.shape[-1], box_weight.shape[-1]
    kp = -(-kc // LANES) * LANES
    kq = -(-kb // 8) * 8
    taps = 9 * c
    lev = levels
    info = jnp.stack([section, tile % 2, tile]).astype(jnp.int32)
    even = tile % 2 == 0

    sx = lax.dynamic_index_in_dim(features, jnp.where(even, rows - 1, 0), 2, False)
    sd = lax.dynamic_index_in_dim(features, jnp.where(even, 0, rows - 1), 2, False)
    rx0, rd0 = swap_edges(sx, sd)
    bias = gather(tower_bias, class_bias, box_bias, kp)
    bias_r = swap_section(bias)
    w_own = tower_weight.reshape(nt, taps, c)
    w_other = swap_section(w_own)

    h1, sp0, zp, token = forward(0, info, lev, features, w_own, w_other, bias, bias_r, (sx, sd))
    thin, small = class_weight.transpose(0, 2, 1), box_weight.transpose(0, 2, 1)
    cot, gb = class_cotangent.transpose(0, 1, 3, 2), box_cotangent.transpose(0, 3, 1, 2)
    w_out = pick_weights(thin, small, kp, (token,))
    w_out_r = swap_section(w_out)
    cot_r = swap_section(pick(info, cot, gb, nb, kp, (token,)))
    h1, sp0, sx, sd = edges(0, info, lev, zp, rx0, rd0, w_own, w_other, h1, sp0)
    rx1, rd1 = swap_edges(sx, sd)
    h2, sp1, zp, _ = forward(1, info, lev, h1, w_own, w_other, bias, bias_r)
    wk, wb, cb = pack(w_out, w_out_r, bias, bias_r, kc, kb, kq, nt, (zp,))
    h2, sp1, sx, sd = edges(1, info, lev, zp, rx1, rd1, w_own, w_other, h2, sp1)
    rx2, rd2 = swap_edges(sx, sd)
    prob, psend, dl, gt, cb_x, cb_d, lp, bo = head(info, lev, h2, wk, wb, cb, cot, gb, cot_r)
    prob, psend, dl, boxo, cx, cd = head_edges(
        info, lev, rx2, rd2, wk, wb, lp, bo, cot, cot_r, cb_x, cb_d, prob, psend, dl, kb
    )
    rx, rd = swap_edges(cx, cd)

    keep, send, token = head_weights(info, lev, h2, rx2, rd2, dl, gt, kc, kb)
    (send,) = relay("send_head", (send,), (token, rx, rd))
    head_sum = TileSum("sum_head", info, True, keep, swap_section(send))
    s = head_sum.start()
    dz1, sx, sd, token = head_inputs(info, lev, dl, gt, rx, rd, wk, wb, sp1, (), s)
    rx, rd = swap_edges(sx, sd)
    s = head_sum.start(token)
    keep1, send1, token = weights(1, info, lev, h1, rx1, rd1, dz1, s)
    *s, send1 = head_sum.start(token, rx, rd, gate=(send1,))
    dz0, token, sx, sd = inputs(1, info, lev, dz1, rx, rd, w_own, w_other, sp0, (), tuple(s))
    *s, psend = head_sum.start(token, gate=(psend,))
    prob_r = swap_section(psend)
    sum1 = TileSum("sum_one", info, False, keep1, swap_section(send1))
    s = tuple(s)
    s = s + sum1.start(*s)
    keep0, send0, token = weights(0, info, lev, features, rx0, rd0, dz0, s)
    sum0 = TileSum("sum_zero", info, False, keep0, swap_section(send0))
    s = sum0.start()
    s = s + sum1.start(*s)
    prob, boxo, token = place(info, prob, boxo, prob_r, tuple(s))
    *s, sx, sd = sum0.start(token, gate=(sx, sd))
    rx, rd = swap_edges(sx, sd)
    s = tuple(s)
    s = s + sum1.start(*s)
    s = s + sum0.start(*s)
    s = s + head_sum.start(*s)
    s = s + sum1.start(*s)
    feature_grad, token = inputs(0, info, lev, dz0, rx, rd, w_own, w_other, None, (), s)
    done = (token,)
    while sum0.plan:
        s = sum0.start(*done)
        done = ()
        for other in (head_sum, sum1):
            if other.plan:
                other.start(*s)
    head_done, l1, l0 = (jnp.concatenate(v.result(), axis=1) for v in (head_sum, sum1, sum0))

    mine_l = jnp.where(section == 0, l0, l1)
    other_l = swap_section(jnp.where(section == 0, l1, l0))
    towers = jnp.where(section == 0, jnp.stack([mine_l[:taps], other_l[:taps]]), jnp.stack([other_l[:taps], mine_l[:taps]]))
    biases = jnp.where(section == 0, jnp.stack([mine_l[taps], other_l[taps]]), jnp.stack([other_l[taps], mine_l[taps]]))
    end = 3 * kc
    box = head_done[end : end + 3 * kq].astype(F32)
    return (
        prob.transpose(0, 1, 3, 2),
        boxo.transpose(0, 2, 3, 1),
        feature_grad,
        towers.astype(F32).reshape(1, nt, 3, 3 * c, c),
        biases.astype(F32).reshape(1, nt, c),
        head_done[:end].astype(F32).reshape(3, kc, 3 * c).transpose(0, 2, 1),
        box[kb, :kc],
        box.reshape(3, kq, 3 * c)[:, :kb].transpose(0, 2, 1),
        box[kb, kp : kp + kb],
    )


def solution(mesh):
    in_specs = (
        P("section", None, "tile", None, None),
        P(),
        P("section", None, None, None, None),
        P("section", None, None),
        P(None, None, "section"),
        P("section"),
        P(None, None, "section"),
        P("section"),
        P(None, "tile", None, "section"),
        P(None, "tile", None, "section"),
    )
    out_specs = (
        P(None, "tile", None, "section"),
        P(None, "tile", None, "section"),
        P("section", None, "tile", None, None),
        P("section", None, None, None, None),
        P("section", None, None),
        P(None, None, "section"),
        P("section"),
        P(None, None, "section"),
        P("section"),
    )
    return jax.shard_map(on_device, mesh=mesh, in_specs=in_specs, out_specs=out_specs, check_vma=False)
```

```python
import functools

import jax
import jax.numpy as jnp
from jax import lax
from jax.experimental import pallas as pl
from jax.experimental.pallas import tpu as pltpu
from jax.sharding import PartitionSpec as P

BF = jnp.bfloat16
F32 = jnp.float32
LANES = 128


def cost(us):
    return pl.CostEstimate(flops=int(us * 2e9), bytes_accessed=0, transcendentals=0)


def ordered(kernel, inputs, after):
    def body(*refs):
        return kernel(*refs[:inputs], *refs[inputs + len(after) :])

    return body
SMEM = pl.BlockSpec(memory_space=pltpu.SMEM)
HBM = pl.BlockSpec(memory_space=pltpu.HBM)
ANY = pl.BlockSpec(memory_space=pl.ANY)


TOKEN = jax.ShapeDtypeStruct((8, LANES), F32)
TOKEN_SPEC = pl.BlockSpec((8, LANES), lambda *_: (0, 0))


def dot(a, b):
    return jnp.dot(a, b, preferred_element_type=F32)


def dot_nt(a, b):
    return lax.dot_general(a, b, (((1,), (1,)), ((), ())), preferred_element_type=F32)


def dot_tn(a, b):
    return lax.dot_general(a, b, (((0,), (0,)), ((), ())), preferred_element_type=F32)


def down(v):
    return jnp.concatenate([jnp.zeros_like(v[..., :1, :]), v[..., :-1, :]], axis=-2)


def up(v):
    return jnp.concatenate([v[..., 1:, :], jnp.zeros_like(v[..., :1, :])], axis=-2)


def keep_if(v, flag):
    return v * jnp.full((1, v.shape[-1]), flag, F32).astype(v.dtype)


def build(x, rows, e, b, before=None, after=None, taps=True):
    count = len(rows)
    width = rows[0]().shape[0]
    for q in range(-1, count + 1):
        if q < 0:
            get = before
        elif q < count:
            get = rows[q]
        else:
            get = after
        if get is None:
            dest = 0 if q < 0 else count - 1
            part = x.shape[1] // 3
            first = 0 if q < 0 else 2 * part
            x[dest * width : (dest + 1) * width, first : first + part] = jnp.zeros((width, part), x.dtype)
            continue
        v = get()
        p = jnp.concatenate([down(v), v, up(v)], axis=1) if taps else v
        n = p.shape[1]
        if 0 <= q < count:
            x[q * width : (q + 1) * width, n : 2 * n] = p
        if q + 1 < count:
            x[(q + 1) * width : (q + 2) * width, 0:n] = keep_if(p, e[b, q + 1])
        if q >= 1:
            x[(q - 1) * width : q * width, 2 * n : 3 * n] = keep_if(p, e[b, q])


class Borders:
    def __init__(self, info, lev, rows):
        self.info, self.lev, self.rows = info, lev, rows

    def __getitem__(self, at):
        b, i = at
        lines, count = self.lev.shape
        line = self.info[0] * (lines // 2) + b
        r = self.info[2] * self.rows + i
        same = self.lev[line, jnp.maximum(r - 1, 0)] == self.lev[line, jnp.minimum(r, count - 1)]
        return jnp.where(jnp.logical_and(same, jnp.logical_and(r > 0, r < count)), 1.0, 0.0)


def rows_of(ref, lead, count):
    return [functools.partial(lambda r: ref[lead + (r,)], r) for r in range(count)]


def pick_halo(info, rx, rd, hs, lead):
    @pl.when(info[1] == 0)
    def _():
        hs[0] = rd[lead]
        hs[1] = rx[lead]

    @pl.when(info[1] != 0)
    def _():
        hs[0] = rx[lead]
        hs[1] = rd[lead]


def put_edges(info, first, last, sx, sd, lead):
    @pl.when(info[1] == 0)
    def _():
        sx[lead] = last
        sd[lead] = first

    @pl.when(info[1] != 0)
    def _():
        sx[lead] = first
        sd[lead] = last


def start_weights(info, layer, own, other, wv, sem):
    for t in range(wv.shape[0]):

        @pl.when(info[0] == layer)
        def _():
            pltpu.make_async_copy(own.at[t], wv.at[t], sem.at[t]).start()

        @pl.when(info[0] != layer)
        def _():
            pltpu.make_async_copy(other.at[t], wv.at[t], sem.at[t]).start()


def wait_weights(own, wv, sem, t):
    for i in range(wv.shape[0]):

        @pl.when(t == i)
        def _():
            pltpu.make_async_copy(own.at[i], wv.at[i], sem.at[i]).wait()


def activate(z):
    sg = jax.nn.sigmoid(z)
    hv = z * sg
    return hv.astype(BF), (sg + hv * (1.0 - sg)).astype(BF)


def forward_kernel(layer, info, lev, h, own, other, bias, bias_r, hn, sp, zp, token, x, wv, wt, sem):
    t, b = pl.program_id(0), pl.program_id(1)
    rows, width = h.shape[2], h.shape[3]
    e = Borders(info, lev, rows)

    @pl.when(jnp.logical_and(t == 0, b == 0))
    def _():
        start_weights(info, layer, own, other, wv, sem)

    build(x, rows_of(h, (0, 0), rows), e, b, taps=False)
    c = h.shape[4]

    @pl.when(b == 0)
    def _():
        wait_weights(own, wv, sem, t)
        for i in range(9):
            k, j = divmod(i, 3)
            wt[k * c : (k + 1) * c, j * c : (j + 1) * c] = wv[t, i * c : (i + 1) * c, :]

    chosen = jnp.full((1, c), info[0] == layer, jnp.int32) != 0
    row = pl.ds(t, 1)
    s = dot(x[...], wt[...]).reshape(rows, width, 3 * c)
    z = down(s[:, :, :c]) + s[:, :, c : 2 * c] + up(s[:, :, 2 * c :])
    z = z + jnp.where(chosen, bias[row, :c], bias_r[row, :c])
    hv, sv = activate(z)
    hn[0, 0] = hv
    sp[0, 0] = sv
    zp[0, 0, 0] = z[0]
    zp[0, 0, 1] = z[rows - 1]
    token[...] = jnp.zeros_like(token)


def forward(layer, info, lev, h, own, other, bias, bias_r, after=()):
    nb, nt, rows, width, c = h.shape
    row_spec = pl.BlockSpec((1, 1, rows, width, c), lambda t, b: (b, t, 0, 0, 0))
    taps = own.shape[1]
    return pl.pallas_call(
        ordered(functools.partial(forward_kernel, layer), 7, after),
        grid=(nt, nb),
        in_specs=[SMEM, SMEM, row_spec, HBM, HBM] + [pl.BlockSpec(bias.shape, lambda t, b: (0, 0))] * 2 + [ANY] * len(after),
        out_specs=[row_spec, row_spec, pl.BlockSpec((1, 1, 2, width, c), lambda t, b: (b, t, 0, 0, 0)), TOKEN_SPEC],
        out_shape=[jax.ShapeDtypeStruct(h.shape, BF)] * 2 + [jax.ShapeDtypeStruct((nb, nt, 2, width, c), F32), TOKEN],
        scratch_shapes=[
            pltpu.VMEM((rows * width, 3 * c), BF),
            pltpu.VMEM((nt, taps, c), BF),
            pltpu.VMEM((3 * c, 3 * c), BF),
            pltpu.SemaphoreType.DMA((nt,)),
        ],
        compiler_params=pltpu.CompilerParams(vmem_limit_bytes=12 << 20),
        cost_estimate=cost(8),
        name=f"forward{layer}",
    )(info, lev, h, own, other, bias, bias_r, *after)


def edge_kernel(layer, rows, info, lev, zp, rx, rd, own, other, hin, sin, hn, sp, sx, sd, wv, sem):
    i = pl.program_id(0)
    nb, nt, width, c = zp.shape[0], zp.shape[1], zp.shape[3], zp.shape[4]
    taps = wv.shape[2]
    e = Borders(info, lev, rows)

    def copies(ref, ii):
        for t in range(nt):
            yield pltpu.make_async_copy(ref.at[t, pl.ds(2 * ii * taps, taps)], wv.at[ii, t], sem.at[ii, t])

    for ii in range(2):
        for ref, chosen in ((own, info[0] == layer), (other, info[0] != layer)):

            @pl.when(jnp.logical_and(i == 0, chosen))
            def _():
                for copy in copies(ref, ii):
                    copy.start()

    from_x = (info[1] == 0) == (i == 1)
    edge = i * rows
    mask = jnp.full((1, c), from_x.astype(jnp.int32), jnp.int32) != 0
    parts = []
    for t in range(nt):
        p = []
        for b in range(nb):
            v = jnp.where(mask, rx[b, t].astype(F32), rd[b, t].astype(F32))
            p.append((jnp.concatenate([down(v), v, up(v)], axis=1) * e[b, edge]).astype(BF))
        parts.append(jnp.concatenate(p, axis=0))

    for ii in range(2):

        @pl.when(i == ii)
        def _():
            for copy in copies(own, ii):
                copy.wait()

    for t in range(nt):
        z = dot(parts[t], wv[i, t])
        for b in range(nb):
            hv, sv = activate(zp[b, t, 0] + z[b * width : (b + 1) * width])
            hn[b, t, 0] = hv
            sp[b, t, 0] = sv

            @pl.when(from_x)
            def _():
                sx[b, t] = hv

            @pl.when(jnp.logical_not(from_x))
            def _():
                sd[b, t] = hv


def edges(layer, info, lev, zp, rx, rd, own, other, hn, sp):
    nb, nt, rows, width, c = hn.shape
    taps = own.shape[1] // 3
    row_spec = pl.BlockSpec((nb, nt, 1, width, c), lambda i: (0, 0, i * (rows - 1), 0, 0))
    edge_spec = pl.BlockSpec((nb, nt, width, c), lambda i: (0, 0, 0, 0))
    edge = jax.ShapeDtypeStruct((nb, nt, width, c), BF)
    return pl.pallas_call(
        functools.partial(edge_kernel, layer, rows),
        grid=(2,),
        in_specs=[
            SMEM,
            SMEM,
            pl.BlockSpec((nb, nt, 1, width, c), lambda i: (0, 0, i, 0, 0)),
            edge_spec,
            edge_spec,
            HBM,
            HBM,
            HBM,
            HBM,
        ],
        out_specs=[row_spec, row_spec, edge_spec, edge_spec],
        out_shape=[jax.ShapeDtypeStruct(hn.shape, BF)] * 2 + [edge] * 2,
        input_output_aliases={7: 0, 8: 1},
        scratch_shapes=[pltpu.VMEM((2, nt, taps, c), BF), pltpu.SemaphoreType.DMA((2, nt))],
        compiler_params=pltpu.CompilerParams(vmem_limit_bytes=8 << 20),
        cost_estimate=cost(4),
        name=f"edges{layer}",
    )(info, lev, zp, rx, rd, own, other, hn, sp)


def tap_columns(ref, b, e, rows, width, gt):
    n = ref(0).shape[0]
    lane = lax.broadcasted_iota(jnp.int32, (n, width), 1)
    for s, k in ((rows, 0), (rows + 1, 0), (0, 1), (rows + 1, 1), (0, 2), (1, 2)):
        gt[0, 3 * k * n : 3 * (k + 1) * n, s * width : (s + 1) * width] = jnp.zeros((3 * n, width), gt.dtype)
    for r in range(rows):
        g = ref(r)
        left = jnp.where(lane < width - 1, pltpu.roll(g, width - 1, 1), 0.0)
        right = jnp.where(lane > 0, pltpu.roll(g, 1, 1), 0.0)
        for k in range(3):
            flag = e[b, r] if k == 0 else e[b, r + 1] if k == 2 else None
            for j, v in enumerate((left, g, right)):
                v = v if flag is None else v * flag
                at = (3 * k + j) * n
                gt[0, at : at + n, (r + k) * width : (r + k + 1) * width] = v.astype(gt.dtype)


def pack_rows(hx, rows, width, hs, row):
    hx[0:width] = hs[0]
    for r in range(rows):
        hx[(r + 1) * width : (r + 2) * width] = row(r)
    hx[(rows + 1) * width :] = hs[1]


def head_row(logit, cot, cot_r, kc, kp):
    gap = jnp.zeros((kp - kc, logit.shape[1]), F32)
    p = jax.nn.sigmoid(logit)
    q = p * (1.0 - p)
    d = [cot.astype(F32) * q[:kc], gap, cot_r.astype(F32) * q[kp : kp + kc], gap]
    return p[:kc].astype(BF), p[kp : kp + kc].astype(BF), jnp.concatenate(d, axis=0).astype(BF).T


def side(v, lane, j):
    width = v.shape[-1]
    if j == 0:
        return jnp.where(lane > 0, pltpu.roll(v, 1, 1), 0.0)
    if j == 2:
        return jnp.where(lane < width - 1, pltpu.roll(v, width - 1, 1), 0.0)
    return v


def head_kernel(
    info, lev, h, wk, wb, cb, cot, gb, cot_r,
    prob, psend, dl, gt, cb_x, cb_d, lp, bo, x, hx, lg, y,
):
    b = pl.program_id(0)
    rows, width, c = h.shape[2], h.shape[3], h.shape[4]
    kc, kb = cot.shape[2], gb.shape[1]
    kp, kq = wk.shape[1] // 2, wb.shape[0] // 18
    e = Borders(info, lev, rows)

    taps = 3 * c
    build(x, rows_of(h, (0, 0), rows), e, b)
    lg[...] = dot_nt(wk[0], x[:, :taps])
    lg[...] += dot_nt(wk[1], x[:, taps : 2 * taps])
    lg[...] += dot_nt(wk[2], x[:, 2 * taps :])

    def row(r, _):
        at = pl.ds(pl.multiple_of(r * width, width), width)
        prob[0, r], psend[0, r, :kc], dl[0, r] = head_row(lg[:, at] + cb[: 2 * kp], cot[0, r], cot_r[0, r, :kc], kc, kp)
        return 0

    lax.fori_loop(0, rows, row, 0, unroll=2)
    lp[0, 0] = lg[:, :width] + cb[: 2 * kp]
    lp[0, 1] = lg[:, (rows - 1) * width :] + cb[: 2 * kp]
    for r in range(rows):
        hx[r * width : (r + 1) * width] = h[0, 1, r]
    y[...] = dot_nt(wb[...], hx[...])
    n = 2 * kq
    lane = lax.broadcasted_iota(jnp.int32, (n, width), 1)
    for r in range(rows):
        v = cb[2 * kp : 2 * kp + n]
        for j in range(3):
            s = y[(3 + j) * n : (4 + j) * n, r * width : (r + 1) * width]
            if r > 0:
                s = s + y[j * n : (j + 1) * n, (r - 1) * width : r * width] * e[b, r]
            if r < rows - 1:
                s = s + y[(6 + j) * n : (7 + j) * n, (r + 1) * width : (r + 2) * width] * e[b, r + 1]
            v = v + side(s, lane, j)
        bo[0, r] = v
        rest = jnp.zeros((kp - kc - kb, width), F32)
        psend[0, r, kc:] = jnp.concatenate([v[kq : kq + kb], rest], axis=0).astype(BF)
    small = jnp.zeros((kq - kb, width), F32)
    g = gb[0].astype(F32)

    def columns(r):
        return jnp.concatenate([g[:, r], small, cot_r[0, r, kc:].astype(F32)[:kb], small], axis=0)

    tap_columns(columns, b, e, rows, width, gt)
    for i in range(2):
        s = i * (rows + 1)
        db = dot_tn(gt[0, :, s * width : (s + 1) * width], wb[...]).astype(BF)

        @pl.when((info[1] == 0) == (i == 1))
        def _():
            cb_x[0] = db

        @pl.when((info[1] == 0) == (i == 0))
        def _():
            cb_d[0] = db


def head(info, lev, h, wk, wb, cb, cot, gb, cot_r, after=()):
    nb, nt, rows, width, c = h.shape
    kc, kb, kp2, kq2 = cot.shape[2], gb.shape[1], wk.shape[1], wb.shape[0] // 9
    batches = cot.shape[0]
    m = rows * width
    ext = (rows + 2) * width

    def at_b(shape):
        return pl.BlockSpec((1,) + shape, lambda b, info: (b,) + (0,) * len(shape))

    def at_all(shape):
        return pl.BlockSpec((1,) + shape, lambda b, info: (info[0] * nb + b,) + (0,) * len(shape))

    def whole(shape):
        return pl.BlockSpec(shape, lambda b, info: (0,) * len(shape), pipeline_mode=pl.Buffered(1))

    return pl.pallas_call(
        ordered(head_kernel, 9, after),
        grid_spec=pltpu.PrefetchScalarGridSpec(
            num_scalar_prefetch=1,
            grid=(nb,),
            in_specs=[
                SMEM,
                at_b((nt, rows, width, c)),
                whole(wk.shape),
                whole(wb.shape),
                whole(cb.shape),
                at_all((rows, kc, width)),
                at_all((kb, rows, width)),
                at_b((rows, kp2 // 2, width)),
            ]
            + [ANY] * len(after),
            out_specs=[
                at_all((rows, kc, width)),
                at_b((rows, kp2 // 2, width)),
                at_b((rows, width, kp2)),
                at_b((9 * kq2, ext)),
                at_b((width, c)),
                at_b((width, c)),
                at_b((2, kp2, width)),
                at_b((rows, kq2, width)),
            ],
            scratch_shapes=[
                pltpu.VMEM((m, 9 * c), BF),
                pltpu.VMEM((m, c), BF),
                pltpu.VMEM((kp2, m), F32),
                pltpu.VMEM((9 * kq2, m), F32),
            ],
        ),
        out_shape=[
            jax.ShapeDtypeStruct((batches, rows, kc, width), BF),
            jax.ShapeDtypeStruct((nb, rows, kp2 // 2, width), BF),
            jax.ShapeDtypeStruct((nb, rows, width, kp2), BF),
            jax.ShapeDtypeStruct((nb, 9 * kq2, ext), BF),
            jax.ShapeDtypeStruct((nb, width, c), BF),
            jax.ShapeDtypeStruct((nb, width, c), BF),
            jax.ShapeDtypeStruct((nb, 2, kp2, width), F32),
            jax.ShapeDtypeStruct((nb, rows, kq2, width), F32),
        ],
        compiler_params=pltpu.CompilerParams(vmem_limit_bytes=17 << 20),
        cost_estimate=cost(14),
        name="head",
    )(info, lev, h, wk, wb, cb, cot, gb, cot_r, *after)


def head_edge_kernel(
    info, lev, rx, rd, wk, wb, lp, bo, cot, cot_r, cb_x, cb_d, prob_i, psend_i, dl_i,
    prob, psend, dl, boxo, cx, cd, hs, ds, bs, bx,
):
    i = pl.program_id(0)
    nb, nt, width, c = rx.shape
    kc, kb, rows = cot.shape[2], boxo.shape[1], boxo.shape[2]
    kp, kq = wk.shape[1] // 2, bo.shape[2] // 2
    taps = 3 * c
    n = 2 * kq
    e = Borders(info, lev, rows)
    edge = i * rows
    from_x = (info[1] == 0) == (i == 1)

    @pl.when(from_x)
    def _():
        hs[...] = rx[...]

    @pl.when(jnp.logical_not(from_x))
    def _():
        hs[...] = rd[...]

    p = []
    for b in range(nb):
        v = hs[b, 0]
        p.append(keep_if(jnp.concatenate([down(v), v, up(v)], axis=1), e[b, edge]))
    logit = dot_nt(wk[0], jnp.concatenate(p, axis=0))
    lane = lax.broadcasted_iota(jnp.int32, (n, width), 1)
    for b in range(nb):
        lg = logit[:, b * width : (b + 1) * width] + lp[b, 0]
        prob[b, 0], psend[b, 0, :kc], d = head_row(lg, cot[b, 0], cot_r[b, 0, :kc], kc, kp)
        dl[b, 0] = d
        ds[b * width : (b + 1) * width, :] = d
        y = dot_nt(wb[...], hs[b, 1]) * e[b, edge]
        v = bo[b, i * (rows - 1)]
        for j in range(3):
            v = v + side(y[j * n : (j + 1) * n, :], lane, j)
        bs[b, i] = v
        gap = jnp.zeros((kp - kc - kb, width), F32)
        psend[b, 0, kc:] = jnp.concatenate([v[kq : kq + kb], gap], axis=0).astype(BF)

    @pl.when(i == 1)
    def _():
        for b in range(nb):
            for r in range(rows):
                v = bs[b, 0] if r == 0 else bs[b, 1] if r == rows - 1 else bo[b, r]
                bx[:, r, :] = v
            boxo[b] = bx[:kb].astype(BF)

    s = dot(ds[...], wk[0]).reshape(nb, width, taps)
    dc = up(s[:, :, :c]) + s[:, :, c : 2 * c] + down(s[:, :, 2 * c :])
    for b in range(nb):
        v = keep_if(dc[b].astype(BF), e[b, edge])

        @pl.when(from_x)
        def _():
            cx[b, 0] = v
            cx[b, 1] = cb_x[b]

        @pl.when(jnp.logical_not(from_x))
        def _():
            cd[b, 0] = v
            cd[b, 1] = cb_d[b]


def head_edges(info, lev, rx, rd, wk, wb, lp, bo, cot, cot_r, cb_x, cb_d, prob, psend, dl, kb):
    nb, nt, width, c = rx.shape
    rows = cot.shape[1]
    kc, kp2, kq2 = cot.shape[2], wk.shape[1], bo.shape[2]

    def whole(shape):
        return pl.BlockSpec(shape, lambda i, info: (0,) * len(shape), pipeline_mode=pl.Buffered(1))

    def at_i(shape):
        return pl.BlockSpec(shape, lambda i, info: (0, i) + (0,) * (len(shape) - 2))

    def edge_of(shape):
        return pl.BlockSpec(shape, lambda i, info: (0, i * (rows - 1)) + (0,) * (len(shape) - 2))

    def edge_all(shape):
        return pl.BlockSpec(shape, lambda i, info: (info[0], i * (rows - 1)) + (0,) * (len(shape) - 2))

    edge = jax.ShapeDtypeStruct((nb, nt, width, c), BF)
    arrays = (prob, psend, dl)
    return pl.pallas_call(
        head_edge_kernel,
        grid_spec=pltpu.PrefetchScalarGridSpec(
            num_scalar_prefetch=1,
            grid=(2,),
            in_specs=[
                SMEM,
                whole(rx.shape),
                whole(rd.shape),
                pl.BlockSpec((1,) + wk.shape[1:], lambda i, info: (2 * i, 0, 0)),
                pl.BlockSpec((3 * kq2, c), lambda i, info: (2 * i, 0)),
                at_i((nb, 1, kp2, width)),
                whole(bo.shape),
                edge_all((nb, 1, kc, width)),
                edge_of((nb, 1, kp2 // 2, width)),
                whole(cb_x.shape),
                whole(cb_d.shape),
            ]
            + [HBM] * len(arrays),
            out_specs=[
                edge_all((nb, 1, kc, width)),
                edge_of((nb, 1, kp2 // 2, width)),
                edge_of((nb, 1, width, kp2)),
                pl.BlockSpec((nb, kb, rows, width), lambda i, info: (info[0], 0, 0, 0)),
                pl.BlockSpec(rx.shape, lambda i, info: (0, 0, 0, 0)),
                pl.BlockSpec(rx.shape, lambda i, info: (0, 0, 0, 0)),
            ],
            scratch_shapes=[
                pltpu.VMEM(rx.shape, BF),
                pltpu.VMEM((nb * width, kp2), BF),
                pltpu.VMEM((nb, 2, kq2, width), F32),
                pltpu.VMEM((kq2, rows, width), F32),
            ],
        ),
        out_shape=[jax.ShapeDtypeStruct(v.shape, BF) for v in arrays]
        + [jax.ShapeDtypeStruct((cot.shape[0], kb, rows, width), BF)]
        + [edge, edge],
        input_output_aliases={12 + i: i for i in range(len(arrays))},
        compiler_params=pltpu.CompilerParams(vmem_limit_bytes=8 << 20),
        cost_estimate=cost(6),
        name="head_edges",
    )(info, lev, rx, rd, wk, wb, lp, bo, cot, cot_r, cb_x, cb_d, *arrays)


def head_weights_kernel(info, lev, h, rx, rd, dl, gt, own, other, token, x, hx, acc, accb, small, sums, hs, *, kc, kb):
    b, nb = pl.program_id(0), pl.num_programs(0)
    rows, width, c = h.shape[2], h.shape[3], h.shape[4]
    token[...] = jnp.zeros_like(token)
    kp, kq = dl.shape[-1] // 2, accb.shape[0] // 18
    taps = 3 * c
    e = Borders(info, lev, rows)
    pick_halo(info, rx, rd, hs, (0, 0))
    build(x, rows_of(h, (0, 0), rows), e, b, lambda: hs[0], lambda: hs[1])
    pick_halo(info, rx, rd, hs, (0, 1))
    pack_rows(hx, rows, width, hs, lambda r: h[0, 1, r])
    g = dl[0].reshape(rows * width, 2 * kp)

    @pl.when(b == 0)
    def _():
        acc[...] = jnp.zeros_like(acc)
        accb[...] = jnp.zeros_like(accb)
        small[...] = jnp.zeros_like(small)

    acc[...] += dot_tn(g, x[...])
    accb[...] += dot(gt[0], hx[...])
    small[:, : 2 * kp] += jnp.sum(g.astype(F32), axis=0, keepdims=True)
    ones = jnp.ones((8, gt.shape[2]), BF)
    s = dot_nt(ones, gt[0, 8 * kq : 10 * kq, :])[:1]
    small[:, 2 * kp :] += jnp.concatenate([s, jnp.zeros((1, LANES - 2 * kq), F32)], axis=1)

    def fill(ref, a):
        for k in range(3):
            ref[k * kc : (k + 1) * kc, :] = acc[a * kp : a * kp + kc, k * taps : (k + 1) * taps]
            at = 3 * kc + k * kq
            for j in range(3):
                first = (3 * k + j) * 2 * kq + a * kq
                ref[at : at + kq, j * c : (j + 1) * c] = accb[first : first + kq, :]
        end = 3 * (kc + kq)
        if end < ref.shape[0]:
            ref[end:, :] = jnp.zeros((ref.shape[0] - end, taps), F32)
        at = 3 * kc + kb
        ref[at : at + 1, :kp] = small[:, a * kp : (a + 1) * kp]
        ref[at : at + 1, kp : kp + LANES] = pltpu.roll(small[:, 2 * kp :], (LANES - a * kq) % LANES, 1)

    @pl.when(b == nb - 1)
    def _():
        for a, out in ((1, other), (0, own)):
            fill(sums, a)
            out[...] = sums[...].astype(BF)


def head_weights(info, lev, h, rx, rd, dl, gt, kc, kb, after=()):
    nb, nt, rows, width, c = h.shape
    kp2 = dl.shape[-1]
    kq2 = gt.shape[1] // 9
    m = rows * width
    size = -(-3 * (kc + kq2 // 2) // LANES) * LANES

    def at_b(shape):
        return pl.BlockSpec((1,) + shape, lambda b: (b,) + (0,) * len(shape))

    def whole(shape):
        return pl.BlockSpec(shape, lambda b: (0,) * len(shape), pipeline_mode=pl.Buffered(1))

    return pl.pallas_call(
        ordered(functools.partial(head_weights_kernel, kc=kc, kb=kb), 7, after),
        grid=(nb,),
        in_specs=[
            SMEM,
            SMEM,
            at_b((nt, rows, width, c)),
            at_b((nt, width, c)),
            at_b((nt, width, c)),
            at_b((rows, width, kp2)),
            at_b(gt.shape[1:]),
        ]
        + [ANY] * len(after),
        out_specs=[whole((size, 3 * c)), whole((size, 3 * c)), TOKEN_SPEC],
        out_shape=[jax.ShapeDtypeStruct((size, 3 * c), BF)] * 2 + [TOKEN],
        scratch_shapes=[
            pltpu.VMEM((m, 9 * c), BF),
            pltpu.VMEM(((rows + 2) * width, c), BF),
            pltpu.VMEM((kp2, 9 * c), F32),
            pltpu.VMEM((9 * kq2, c), F32),
            pltpu.VMEM((1, kp2 + LANES), F32),
            pltpu.VMEM((size, 3 * c), F32),
            pltpu.VMEM((2, width, c), BF),
        ],
        compiler_params=pltpu.CompilerParams(vmem_limit_bytes=21 << 20),
        cost_estimate=cost(12),
        name="head_weights",
    )(info, lev, h, rx, rd, dl, gt, *after)


def head_inputs_kernel(info, lev, dl, gt, rx, rd, wk, wb, sp, *rest):
    dz, sx, sd, token, *_, x, hs = rest
    token[...] = jnp.zeros_like(token)
    b = pl.program_id(0)
    rows, width, c = sp.shape[2], sp.shape[3], sp.shape[4]
    kp2 = dl.shape[-1]
    taps = 3 * c
    e = Borders(info, lev, rows)
    build(x, rows_of(dl, (0,), rows), e, b, taps=False)
    s = dot(x[:, kp2 : 2 * kp2], wk[1])
    s = s + dot(x[:, :kp2], wk[2])
    s = s + dot(x[:, 2 * kp2 :], wk[0])
    s = s.reshape(rows, width, taps)
    dc = up(s[:, :, :c]) + s[:, :, c : 2 * c] + down(s[:, :, 2 * c :])
    db = dot_tn(gt[0, :, width : (rows + 1) * width], wb[...]).reshape(rows, width, c)
    for t, dh in ((0, dc), (1, db)):
        pick_halo(info, rx, rd, hs, (0, t))
        for r in range(rows):
            v = dh[r]
            if r == 0:
                v = v + hs[0].astype(F32)
            if r == rows - 1:
                v = v + hs[1].astype(F32)
            dz[0, t, r] = (v * sp[0, t, r].astype(F32)).astype(BF)
        put_edges(info, dz[0, t, 0], dz[0, t, rows - 1], sx, sd, (0, t))


def head_inputs(info, lev, dl, gt, rx, rd, wk, wb, sp, gate, after=()):
    nb, nt, rows, width, c = sp.shape
    kp2 = dl.shape[-1]
    m = rows * width

    def at_b(shape):
        return pl.BlockSpec((1,) + shape, lambda b: (b,) + (0,) * len(shape))

    def whole(shape):
        return pl.BlockSpec(shape, lambda b: (0,) * len(shape), pipeline_mode=pl.Buffered(1))

    return pl.pallas_call(
        ordered(head_inputs_kernel, 9, gate + after),
        grid=(nb,),
        in_specs=[
            SMEM,
            SMEM,
            at_b((rows, width, kp2)),
            at_b(gt.shape[1:]),
            at_b((nt, width, c)),
            at_b((nt, width, c)),
            whole(wk.shape),
            whole(wb.shape),
            at_b((nt, rows, width, c)),
        ]
        + [ANY] * len(gate + after),
        out_specs=[at_b((nt, rows, width, c)), at_b((nt, width, c)), at_b((nt, width, c)), TOKEN_SPEC] + [ANY] * len(gate),
        out_shape=[
            jax.ShapeDtypeStruct(sp.shape, BF),
            jax.ShapeDtypeStruct((nb, nt, width, c), BF),
            jax.ShapeDtypeStruct((nb, nt, width, c), BF),
        ]
        + [TOKEN]
        + [jax.ShapeDtypeStruct(v.shape, v.dtype) for v in gate],
        input_output_aliases={9 + k: 4 + k for k in range(len(gate))},
        scratch_shapes=[pltpu.VMEM((m, 3 * kp2), BF), pltpu.VMEM((2, width, c), BF)],
        compiler_params=pltpu.CompilerParams(vmem_limit_bytes=14 << 20),
        cost_estimate=cost(9),
        name="head_inputs",
    )(info, lev, dl, gt, rx, rd, wk, wb, sp, *gate, *after)


def weights_kernel(info, lev, h, rx, rd, dz, keep, send, token, x, acc, bias, hs):
    t, b, nb = pl.program_id(0), pl.program_id(1), pl.num_programs(1)
    rows, width, c = h.shape[2], h.shape[3], h.shape[4]
    e = Borders(info, lev, rows)
    pick_halo(info, rx, rd, hs, (0, 0))
    build(x, rows_of(h, (0, 0), rows), e, b, lambda: hs[0], lambda: hs[1])
    g = dz[0, 0].reshape(rows * width, c)
    part = dot_tn(x[...], g)
    total = jnp.sum(g.astype(F32), axis=0, keepdims=True)
    taps = acc.shape[0]

    @pl.when(b == 0)
    def _():
        acc[...] = part
        bias[...] = total

    @pl.when(b != 0)
    def _():
        acc[...] += part
        bias[...] += total

    token[...] = jnp.zeros_like(token)
    for i, out in enumerate((send, keep)):

        @pl.when(jnp.logical_and(b == nb - 1, t == i))
        def _():
            out[:taps, :] = acc[...].astype(out.dtype)
            out[taps:, :] = jnp.broadcast_to(bias[...].astype(out.dtype), (out.shape[0] - taps, c))


def weights(layer, info, lev, h, rx, rd, dz, after=()):
    nb, nt, rows, width, c = h.shape

    def tower(t, info):
        return jnp.where(t == 0, 1 - info[0], info[0])

    row_spec = pl.BlockSpec((1, 1, rows, width, c), lambda t, b, info: (b, tower(t, info), 0, 0, 0))
    edge_spec = pl.BlockSpec((1, 1, width, c), lambda t, b, info: (b, tower(t, info), 0, 0))
    taps = 9 * c
    return pl.pallas_call(
        ordered(weights_kernel, 6, after),
        grid_spec=pltpu.PrefetchScalarGridSpec(
            num_scalar_prefetch=1,
            grid=(nt, nb),
            in_specs=[SMEM, row_spec, edge_spec, edge_spec, row_spec] + [ANY] * len(after),
            out_specs=[pl.BlockSpec((taps + LANES, c), lambda t, b, info: (0, 0))] * 2 + [TOKEN_SPEC],
            scratch_shapes=[
                pltpu.VMEM((rows * width, taps), BF),
                pltpu.VMEM((taps, c), F32),
                pltpu.VMEM((1, c), F32),
                pltpu.VMEM((2, width, c), BF),
            ],
        ),
        out_shape=[jax.ShapeDtypeStruct((taps + LANES, c), BF)] * 2 + [TOKEN],
        compiler_params=pltpu.CompilerParams(vmem_limit_bytes=14 << 20),
        cost_estimate=cost(8),
        name=f"weights{layer}",
    )(info, lev, h, rx, rd, dz, *after)


def inputs_kernel(layer, info, lev, dz, rx, rd, own, other, *rest):
    if layer:
        sp, out, token, sx, sd, x, wv, wt, hs, sem = rest
    else:
        out, token, *_, x, wv, wt, hs, sem = rest
    token[...] = jnp.zeros_like(token)
    t, b = pl.program_id(0), pl.program_id(1)
    rows, width, c = dz.shape[2], dz.shape[3], dz.shape[4]
    e = Borders(info, lev, rows)

    @pl.when(jnp.logical_and(t == 0, b == 0))
    def _():
        start_weights(info, layer, own, other, wv, sem)

    pick_halo(info, rx, rd, hs, (0, 0))
    build(x, rows_of(dz, (0, 0), rows), e, b, lambda: hs[0], lambda: hs[1], taps=False)

    @pl.when(b == 0)
    def _():
        wait_weights(own, wv, sem, t)
        for k in range(3):
            wt[:, (2 - k) * c : (3 - k) * c] = wv[t, 3 * k * c : 3 * (k + 1) * c, :]

    s = dot_nt(x[...], wt[...]).reshape(rows, width, 3 * c)
    dh = (up(s[:, :, :c]) + s[:, :, c : 2 * c] + down(s[:, :, 2 * c :])).astype(BF)
    if not layer:
        out[0, 0] = dh
        return
    dz_next = (dh.astype(F32) * sp[0, 0].astype(F32)).astype(BF)
    out[0, 0] = dz_next
    put_edges(info, dz_next[0], dz_next[rows - 1], sx, sd, (0, 0))


def inputs(layer, info, lev, dz, rx, rd, own, other, sp=None, gate=(), after=()):
    nb, nt, rows, width, c = dz.shape
    row_spec = pl.BlockSpec((1, 1, rows, width, c), lambda t, b: (b, t, 0, 0, 0))
    edge_spec = pl.BlockSpec((1, 1, width, c), lambda t, b: (b, t, 0, 0))
    edge = jax.ShapeDtypeStruct((nb, nt, width, c), BF)
    taps = own.shape[1]
    return pl.pallas_call(
        ordered(functools.partial(inputs_kernel, layer), 8 if layer else 7, gate + after),
        grid=(nt, nb),
        in_specs=[SMEM, SMEM, row_spec, edge_spec, edge_spec, HBM, HBM] + ([row_spec] if layer else []) + [ANY] * len(gate + after),
        out_specs=[row_spec, TOKEN_SPEC] + ([edge_spec, edge_spec] if layer else []) + [ANY] * len(gate),
        out_shape=[jax.ShapeDtypeStruct(dz.shape, BF)]
        + [TOKEN]
        + ([edge, edge] if layer else [])
        + [jax.ShapeDtypeStruct(v.shape, v.dtype) for v in gate],
        input_output_aliases={7 + k: 2 + k for k in range(len(gate))},
        scratch_shapes=[
            pltpu.VMEM((rows * width, 3 * c), BF),
            pltpu.VMEM((nt, taps, c), BF),
            pltpu.VMEM((3 * c, 3 * c), BF),
            pltpu.VMEM((2, width, c), BF),
            pltpu.SemaphoreType.DMA((nt,)),
        ],
        compiler_params=pltpu.CompilerParams(vmem_limit_bytes=13 << 20),
        cost_estimate=cost(9),
        name=f"inputs{layer}",
    )(info, lev, dz, rx, rd, own, other, *([sp] if layer else []), *gate, *after)


def swap_section(value):
    return lax.ppermute(value, "section", [(0, 1), (1, 0)])


def swap_edges(sx, sd):
    count = lax.axis_size("tile")
    even = [p for i in range(0, count - 1, 2) for p in ((i, i + 1), (i + 1, i))]
    odd = [p for i in range(1, count - 1, 2) for p in ((i, i + 1), (i + 1, i))]
    return lax.ppermute(sx, "tile", even), lax.ppermute(sd, "tile", odd)


def combine_kernel(plan, info, *refs):
    ins, outs = list(refs[: sum(sum(p) for p in plan)]), refs[sum(sum(p) for p in plan) :]
    for counts, out in zip(plan, outs):
        lanes = out.shape[1] // len(counts)
        for i, count in enumerate(counts):
            terms = [ins.pop(0)[...].astype(F32) for _ in range(count)]
            out[:, i * lanes : (i + 1) * lanes] = functools.reduce(jnp.add, terms).astype(out.dtype)


def combine(name, info, shape, outs, gate=(), after=()):
    rows, lanes = shape
    views = [v for parts in outs for terms in parts for v in terms]

    def spec(view):
        return pl.BlockSpec(shape, lambda i, info: (view[1](info), view[2]))

    plan = [[len(terms) for terms in parts] for parts in outs]
    return pl.pallas_call(
        ordered(functools.partial(combine_kernel, plan), 1 + len(views), gate + after),
        grid_spec=pltpu.PrefetchScalarGridSpec(
            num_scalar_prefetch=1,
            grid=(1,),
            in_specs=[spec(v) for v in views] + [ANY] * len(gate + after),
            out_specs=[pl.BlockSpec((rows, lanes * len(parts)), lambda i, info: (0, 0)) for parts in outs]
            + [ANY] * len(gate),
        ),
        out_shape=[jax.ShapeDtypeStruct((rows, lanes * len(parts)), BF) for parts in outs]
        + [jax.ShapeDtypeStruct(v.shape, v.dtype) for v in gate],
        input_output_aliases={1 + len(views) + k: len(outs) + k for k in range(len(gate))},
        compiler_params=pltpu.CompilerParams(vmem_limit_bytes=7 << 20),
        cost_estimate=cost(2),
        name=name,
    )(info, *[v[0] for v in views], *gate, *after)


def join_kernel(bits, split, info, *refs):
    n = len(bits)
    for i, bit in enumerate(bits):
        cur, got = refs[2 * i], refs[2 * i + 1]
        outs = refs[2 * n :] if split else refs[2 * n + i : 2 * n + i + 1]
        m, lanes = cur.shape[0], cur.shape[1] // len(outs)
        mine = (info[2] >> bit) & 1
        for j, out in enumerate(outs):
            at = slice(j * lanes, (j + 1) * lanes)

            @pl.when(mine == 0)
            def _():
                out[:m, :] = cur[:, at]
                out[m:, :] = got[:, at]

            @pl.when(mine != 0)
            def _():
                out[:m, :] = got[:, at]
                out[m:, :] = cur[:, at]


def join(name, info, bits, pairs, split=False, after=()):
    arrays = [v for pair in pairs for v in pair]
    shapes = [(2 * cur.shape[0], cur.shape[1]) for cur, _ in pairs]
    if split:
        shapes = [(shapes[0][0], shapes[0][1] // 2)] * 2

    def whole(shape):
        return pl.BlockSpec(shape, lambda i, info: (0, 0))

    return pl.pallas_call(
        ordered(functools.partial(join_kernel, bits, split), 1 + len(arrays), after),
        grid_spec=pltpu.PrefetchScalarGridSpec(
            num_scalar_prefetch=1,
            grid=(1,),
            in_specs=[whole(v.shape) for v in arrays] + [ANY] * len(after),
            out_specs=[whole(s) for s in shapes],
        ),
        out_shape=[jax.ShapeDtypeStruct(s, BF) for s in shapes],
        compiler_params=pltpu.CompilerParams(vmem_limit_bytes=7 << 20),
        cost_estimate=cost(2),
        name=name,
    )(info, *arrays, *after)


def relay_kernel(*refs):
    del refs


def relay(name, gate, after):
    return pl.pallas_call(
        ordered(relay_kernel, 0, gate + after),
        in_specs=[ANY] * len(gate + after),
        out_specs=[ANY] * len(gate),
        out_shape=[jax.ShapeDtypeStruct(v.shape, v.dtype) for v in gate],
        input_output_aliases={k: k for k in range(len(gate))},
        compiler_params=pltpu.CompilerParams(vmem_limit_bytes=1 << 20),
        cost_estimate=cost(1),
        name=name,
    )(*gate, *after)


class TileSum:
    def __init__(self, name, info, whole, *terms):
        self.name, self.info = name, info
        rows, lanes = terms[0].shape
        self.shape = (rows, lanes // 2)
        self.parts = [[(v, lambda info: 0, i) for v in terms] for i in range(2)]
        self.count = lax.axis_size("tile")
        bits = self.count.bit_length() - 1
        near = [(0, 1), (1, 0)]
        self.plan = [("halve", step) for step in near]
        if whole or bits > 4:
            self.plan += [("add", (bit,)) for bit in range(2, bits)]
        else:
            self.plan += [("halve", (bit,)) for bit in range(2, bits - 1)]
            self.plan += [("add", (bit,)) for bit in range(max(bits - 1, 2), bits)]
            self.plan += [("double", (bit,)) for bit in reversed(range(2, bits - 1))]
        self.plan += [("double", step) for step in reversed(near)]
        self.step = 0
        self.sends = None

    def exchange(self, value, bit):
        return lax.ppermute(value, "tile", [(i, i ^ (1 << bit)) for i in range(self.count)])

    def start(self, *after, gate=()):
        kind, bits = self.plan.pop(0)
        name = f"{self.name}_{self.step}"
        self.step += 1
        if kind == "halve":
            rows, lanes = self.shape
            self.shape = (rows // 2, lanes)
            bit_of = bits * 2 if len(bits) == 1 else bits

            def half(view, bit, other):
                array, row, lane = view
                return array, lambda info: 2 * row(info) + (((info[2] >> bit) & 1) ^ other), lane

            sent = [[half(v, bit, 1) for v in terms] for terms, bit in zip(self.parts, bit_of)]
            self.parts = [[half(v, bit, 0) for v in terms] for terms, bit in zip(self.parts, bit_of)]
            outs = [sent] if len(bits) == 1 else [[terms] for terms in sent]
            sends = combine(name, self.info, self.shape, outs, gate, after)
        elif kind == "add" or self.kind != "double":
            outs = [self.parts] if len(bits) == 1 else [[terms] for terms in self.parts]
            sends = combine(name, self.info, self.shape, outs, gate, after)
        else:
            sends = join(name, self.info, self.bits, self.pairs, len(bits) > len(self.pairs), after)
        passed = tuple(sends[len(bits) :])
        sends = tuple(sends[: len(bits)])
        self.kind, self.bits, self.sends = kind, bits, sends
        got = [self.exchange(v, bit) for v, bit in zip(sends, bits)]
        if kind == "halve":
            lane = (lambda i: i) if len(bits) == 1 else (lambda i: 0)
            pick = (lambda i: got[0]) if len(bits) == 1 else (lambda i: got[i])
            self.parts = [terms + [(pick(i), lambda info: 0, lane(i))] for i, terms in enumerate(self.parts)]
        elif kind == "add":
            self.parts = [[(v, lambda info: 0, i) for v in (sends[0], got[0])] for i in range(2)]
        else:
            self.pairs = list(zip(sends, got))
        return sends + passed

    def result(self, *after):
        return join(f"{self.name}_{self.step}", self.info, self.bits, self.pairs, False, after)


def pick_kernel(info, cot, gb, out):
    rows, kc, kb = cot.shape[1], cot.shape[2], gb.shape[1]
    g = gb[0].astype(F32)
    gap = jnp.zeros((out.shape[2] - kc - kb, out.shape[3]), F32)
    for r in range(rows):
        out[0, r] = jnp.concatenate([cot[0, r].astype(F32), g[:, r], gap], axis=0).astype(BF)


def pick(info, cot, gb, nb, kp, after=()):
    def at_all(shape):
        return pl.BlockSpec((1,) + shape[1:], lambda b, info: ((1 - info[0]) * nb + b,) + (0,) * (len(shape) - 1))

    shape = (nb, cot.shape[1], kp, cot.shape[3])
    return pl.pallas_call(
        ordered(pick_kernel, 3, after),
        grid_spec=pltpu.PrefetchScalarGridSpec(
            num_scalar_prefetch=1,
            grid=(nb,),
            in_specs=[at_all(cot.shape), at_all(gb.shape)] + [ANY] * len(after),
            out_specs=pl.BlockSpec((1,) + shape[1:], lambda b, info: (b, 0, 0, 0)),
        ),
        out_shape=jax.ShapeDtypeStruct(shape, BF),
        compiler_params=pltpu.CompilerParams(vmem_limit_bytes=8 << 20),
        cost_estimate=cost(2),
        name="pick",
    )(info, cot, gb, *after)


def gather_kernel(tower, classes, boxes, out):
    out[...] = jnp.zeros_like(out)
    nt, c = tower.shape[1], tower.shape[2]
    out[:nt, :c] = tower[0]
    out[nt : nt + 1, : classes.shape[0]] = classes[...].reshape(1, -1)
    out[nt + 1 : nt + 2, : boxes.shape[0]] = boxes[...].reshape(1, -1)


def gather(tower, classes, boxes, lanes):
    return pl.pallas_call(
        gather_kernel,
        out_shape=jax.ShapeDtypeStruct((8, lanes), F32),
        cost_estimate=cost(1),
        name="gather",
    )(tower, classes, boxes)


def pick_weights_kernel(thin, small, out):
    gap = jnp.zeros((out.shape[1] - thin.shape[1] - small.shape[1], out.shape[2]), F32)
    out[0] = jnp.concatenate([thin[0].astype(F32), small[0].astype(F32), gap], axis=0).astype(BF)


def pick_weights(thin, small, kp, after=()):
    def at_k(shape):
        return pl.BlockSpec((1,) + shape[1:], lambda k: (k, 0, 0))

    shape = (thin.shape[0], kp, thin.shape[2])
    return pl.pallas_call(
        ordered(pick_weights_kernel, 2, after),
        grid=(shape[0],),
        in_specs=[at_k(thin.shape), at_k(small.shape)] + [ANY] * len(after),
        out_specs=at_k(shape),
        out_shape=jax.ShapeDtypeStruct(shape, BF),
        compiler_params=pltpu.CompilerParams(vmem_limit_bytes=6 << 20),
        cost_estimate=cost(2),
        name="pick_weights",
    )(thin, small, *after)


def pack_kernel(own, other, bias, bias_r, wk, wb, cb, *, kc, kb, kq, towers):
    k = pl.program_id(0)
    kp = own.shape[1]
    c = wb.shape[1]
    gap = jnp.zeros((kp - kc, wk.shape[2]), F32)
    for half, v in enumerate((own, other)):
        wk[0, half * kp : (half + 1) * kp, :] = jnp.concatenate([v[0].astype(F32)[:kc], gap], axis=0).astype(BF)
    u, v = own[0].astype(F32)[kc : kc + kb], other[0].astype(F32)[kc : kc + kb]
    small = jnp.zeros((kq - kb, c), F32)
    for j in range(3):
        at = slice(j * c, (j + 1) * c)
        rows = jnp.concatenate([u[:, at], small, v[:, at], small], axis=0).astype(BF)
        wb[pl.ds(pl.multiple_of((3 * k + j) * 2 * kq, 2 * kq), 2 * kq), :] = rows

    @pl.when(k == 0)
    def _():
        wide = jnp.zeros((1, kp - kc), F32)
        thin = jnp.zeros((1, kq - kb), F32)
        rest = jnp.zeros((1, cb.shape[0] - 2 * kp - kq - kb), F32)
        classes, boxes = slice(towers, towers + 1), slice(towers + 1, towers + 2)
        parts = [bias[classes, :kc], wide, bias_r[classes, :kc], wide, bias[boxes, :kb], thin, bias_r[boxes, :kb], rest]
        cb[...] = jnp.broadcast_to(jnp.concatenate(parts, axis=1), (cb.shape[1], cb.shape[0])).T


def pack(own, other, bias, bias_r, kc, kb, kq, towers, after=()):
    k, kp, c3 = own.shape
    at_k = pl.BlockSpec((1, kp, c3), lambda k: (k, 0, 0))

    def whole(shape):
        return pl.BlockSpec(shape, lambda k: (0,) * len(shape))

    shapes = [(k, 2 * kp, c3), (18 * kq, c3 // 3), (2 * kp + LANES, LANES)]
    return pl.pallas_call(
        ordered(functools.partial(pack_kernel, kc=kc, kb=kb, kq=kq, towers=towers), 4, after),
        grid=(k,),
        in_specs=[at_k, at_k, whole(bias.shape), whole(bias.shape)] + [ANY] * len(after),
        out_specs=[pl.BlockSpec((1,) + shapes[0][1:], lambda k: (k, 0, 0)), whole(shapes[1]), whole(shapes[2])],
        out_shape=[jax.ShapeDtypeStruct(s, t) for s, t in zip(shapes, (BF, BF, F32))],
        compiler_params=pltpu.CompilerParams(vmem_limit_bytes=10 << 20),
        cost_estimate=cost(3),
        name="pack",
    )(own, other, bias, bias_r, *after)


def place_kernel(info, prob_i, box_i, got, prob, box, token, bx):
    rows, kc, kb = prob.shape[1], prob.shape[2], box.shape[1]
    for r in range(rows):
        prob[0, r] = got[0, r, :kc]
        bx[:, r, :] = got[0, r, kc:].astype(F32)[:kb]
    box[0] = bx[...].astype(BF)
    token[...] = jnp.zeros_like(token)


def place(info, prob, box, got, after=()):
    nb = got.shape[0]

    def at_all(shape):
        return pl.BlockSpec((1,) + shape[1:], lambda b, info: ((1 - info[0]) * nb + b,) + (0,) * (len(shape) - 1))

    return pl.pallas_call(
        ordered(place_kernel, 4, after),
        grid_spec=pltpu.PrefetchScalarGridSpec(
            num_scalar_prefetch=1,
            grid=(nb,),
            in_specs=[HBM, HBM, pl.BlockSpec((1,) + got.shape[1:], lambda b, info: (b, 0, 0, 0))] + [ANY] * len(after),
            out_specs=[at_all(prob.shape), at_all(box.shape), TOKEN_SPEC],
            scratch_shapes=[pltpu.VMEM(box.shape[1:], F32)],
        ),
        out_shape=[jax.ShapeDtypeStruct(v.shape, BF) for v in (prob, box)] + [TOKEN],
        input_output_aliases={1: 0, 2: 1},
        compiler_params=pltpu.CompilerParams(vmem_limit_bytes=8 << 20),
        cost_estimate=cost(2),
        name="place",
    )(info, prob, box, got, *after)


def after(value, *others):
    return lax.optimization_barrier((value,) + others)[0]


def on_device(
    features,
    levels,
    tower_weight,
    tower_bias,
    class_weight,
    class_bias,
    box_weight,
    box_bias,
    class_cotangent,
    box_cotangent,
):
    section = lax.axis_index("section")
    tile = lax.axis_index("tile")
    nb, nt, rows, width, c = features.shape
    kc, kb = class_weight.shape[-1], box_weight.shape[-1]
    kp = -(-kc // LANES) * LANES
    kq = -(-kb // 8) * 8
    taps = 9 * c
    lev = levels
    info = jnp.stack([section, tile % 2, tile]).astype(jnp.int32)
    even = tile % 2 == 0

    sx = lax.dynamic_index_in_dim(features, jnp.where(even, rows - 1, 0), 2, False)
    sd = lax.dynamic_index_in_dim(features, jnp.where(even, 0, rows - 1), 2, False)
    rx0, rd0 = swap_edges(sx, sd)
    bias = gather(tower_bias, class_bias, box_bias, kp)
    bias_r = swap_section(bias)
    w_own = tower_weight.reshape(nt, taps, c)
    w_other = swap_section(w_own)

    h1, sp0, zp, token = forward(0, info, lev, features, w_own, w_other, bias, bias_r, (sx, sd))
    thin, small = class_weight.transpose(0, 2, 1), box_weight.transpose(0, 2, 1)
    cot, gb = class_cotangent.transpose(0, 1, 3, 2), box_cotangent.transpose(0, 3, 1, 2)
    w_out = pick_weights(thin, small, kp, (token,))
    w_out_r = swap_section(w_out)
    cot_r = swap_section(pick(info, cot, gb, nb, kp, (token,)))
    h1, sp0, sx, sd = edges(0, info, lev, zp, rx0, rd0, w_own, w_other, h1, sp0)
    rx1, rd1 = swap_edges(sx, sd)
    h2, sp1, zp, _ = forward(1, info, lev, h1, w_own, w_other, bias, bias_r)
    wk, wb, cb = pack(w_out, w_out_r, bias, bias_r, kc, kb, kq, nt, (zp,))
    h2, sp1, sx, sd = edges(1, info, lev, zp, rx1, rd1, w_own, w_other, h2, sp1)
    rx2, rd2 = swap_edges(sx, sd)
    prob, psend, dl, gt, cb_x, cb_d, lp, bo = head(info, lev, h2, wk, wb, cb, cot, gb, cot_r)
    prob, psend, dl, boxo, cx, cd = head_edges(
        info, lev, rx2, rd2, wk, wb, lp, bo, cot, cot_r, cb_x, cb_d, prob, psend, dl, kb
    )
    rx, rd = swap_edges(cx, cd)

    keep, send, token = head_weights(info, lev, h2, rx2, rd2, dl, gt, kc, kb)
    (send,) = relay("send_head", (send,), (token, rx, rd))
    head_sum = TileSum("sum_head", info, True, keep, swap_section(send))
    s = head_sum.start()
    dz1, sx, sd, token = head_inputs(info, lev, dl, gt, rx, rd, wk, wb, sp1, (), s)
    rx, rd = swap_edges(sx, sd)
    s = head_sum.start(token)
    keep1, send1, token = weights(1, info, lev, h1, rx1, rd1, dz1, s)
    *s, send1 = head_sum.start(token, rx, rd, gate=(send1,))
    dz0, token, sx, sd = inputs(1, info, lev, dz1, rx, rd, w_own, w_other, sp0, (), tuple(s))
    *s, psend = head_sum.start(token, gate=(psend,))
    prob_r = swap_section(psend)
    sum1 = TileSum("sum_one", info, False, keep1, swap_section(send1))
    s = tuple(s)
    s = s + sum1.start(*s)
    keep0, send0, token = weights(0, info, lev, features, rx0, rd0, dz0, s)
    sum0 = TileSum("sum_zero", info, False, keep0, swap_section(send0))
    s = sum0.start()
    s = s + sum1.start(*s)
    prob, boxo, token = place(info, prob, boxo, prob_r, tuple(s))
    *s, sx, sd = sum0.start(token, gate=(sx, sd))
    rx, rd = swap_edges(sx, sd)
    s = tuple(s)
    s = s + sum1.start(*s)
    s = s + sum0.start(*s)
    s = s + head_sum.start(*s)
    s = s + sum1.start(*s)
    feature_grad, token = inputs(0, info, lev, dz0, rx, rd, w_own, w_other, None, (), s)
    done = (token,)
    while sum0.plan:
        s = sum0.start(*done)
        done = ()
        for other in (head_sum, sum1):
            if other.plan:
                other.start(*s)
    head_done, l1, l0 = (jnp.concatenate(v.result(), axis=1) for v in (head_sum, sum1, sum0))

    mine_l = jnp.where(section == 0, l0, l1)
    other_l = swap_section(jnp.where(section == 0, l1, l0))
    towers = jnp.where(section == 0, jnp.stack([mine_l[:taps], other_l[:taps]]), jnp.stack([other_l[:taps], mine_l[:taps]]))
    biases = jnp.where(section == 0, jnp.stack([mine_l[taps], other_l[taps]]), jnp.stack([other_l[taps], mine_l[taps]]))
    end = 3 * kc
    box = head_done[end : end + 3 * kq].astype(F32)
    return (
        prob.transpose(0, 1, 3, 2),
        boxo.transpose(0, 2, 3, 1),
        feature_grad,
        towers.astype(F32).reshape(1, nt, 3, 3 * c, c),
        biases.astype(F32).reshape(1, nt, c),
        head_done[:end].astype(F32).reshape(3, kc, 3 * c).transpose(0, 2, 1),
        box[kb, :kc],
        box.reshape(3, kq, 3 * c)[:, :kb].transpose(0, 2, 1),
        box[kb, kp : kp + kb],
    )


def solution(mesh):
    in_specs = (
        P("section", None, "tile", None, None),
        P(),
        P("section", None, None, None, None),
        P("section", None, None),
        P(None, None, "section"),
        P("section"),
        P(None, None, "section"),
        P("section"),
        P(None, "tile", None, "section"),
        P(None, "tile", None, "section"),
    )
    out_specs = (
        P(None, "tile", None, "section"),
        P(None, "tile", None, "section"),
        P("section", None, "tile", None, None),
        P("section", None, None, None, None),
        P("section", None, None),
        P(None, None, "section"),
        P("section"),
        P(None, None, "section"),
        P("section"),
    )
    return jax.shard_map(on_device, mesh=mesh, in_specs=in_specs, out_specs=out_specs, check_vma=False)
```

```python
import functools

import jax
import jax.numpy as jnp
from jax import lax
from jax.experimental import pallas as pl
from jax.experimental.pallas import tpu as pltpu
from jax.sharding import PartitionSpec as P

BF = jnp.bfloat16
F32 = jnp.float32
LANES = 128


def cost(us):
    return pl.CostEstimate(flops=int(us * 2e9), bytes_accessed=0, transcendentals=0)


def ordered(kernel, inputs, after):
    def body(*refs):
        return kernel(*refs[:inputs], *refs[inputs + len(after) :])

    return body
SMEM = pl.BlockSpec(memory_space=pltpu.SMEM)
HBM = pl.BlockSpec(memory_space=pltpu.HBM)
ANY = pl.BlockSpec(memory_space=pl.ANY)


TOKEN = jax.ShapeDtypeStruct((8, LANES), F32)
TOKEN_SPEC = pl.BlockSpec((8, LANES), lambda *_: (0, 0))


def dot(a, b):
    return jnp.dot(a, b, preferred_element_type=F32)


def dot_nt(a, b):
    return lax.dot_general(a, b, (((1,), (1,)), ((), ())), preferred_element_type=F32)


def dot_tn(a, b):
    return lax.dot_general(a, b, (((0,), (0,)), ((), ())), preferred_element_type=F32)


def down(v):
    return jnp.concatenate([jnp.zeros_like(v[..., :1, :]), v[..., :-1, :]], axis=-2)


def up(v):
    return jnp.concatenate([v[..., 1:, :], jnp.zeros_like(v[..., :1, :])], axis=-2)


def keep_if(v, flag):
    return v * jnp.full((1, v.shape[-1]), flag, F32).astype(v.dtype)


def build(x, rows, e, b, before=None, after=None, taps=True):
    count = len(rows)
    width = rows[0]().shape[0]
    for q in range(-1, count + 1):
        if q < 0:
            get = before
        elif q < count:
            get = rows[q]
        else:
            get = after
        if get is None:
            dest = 0 if q < 0 else count - 1
            part = x.shape[1] // 3
            first = 0 if q < 0 else 2 * part
            x[dest * width : (dest + 1) * width, first : first + part] = jnp.zeros((width, part), x.dtype)
            continue
        v = get()
        p = jnp.concatenate([down(v), v, up(v)], axis=1) if taps else v
        n = p.shape[1]
        if 0 <= q < count:
            x[q * width : (q + 1) * width, n : 2 * n] = p
        if q + 1 < count:
            x[(q + 1) * width : (q + 2) * width, 0:n] = keep_if(p, e[b, q + 1])
        if q >= 1:
            x[(q - 1) * width : q * width, 2 * n : 3 * n] = keep_if(p, e[b, q])


class Borders:
    def __init__(self, info, lev, rows):
        self.info, self.lev, self.rows = info, lev, rows

    def __getitem__(self, at):
        b, i = at
        lines, count = self.lev.shape
        line = self.info[0] * (lines // 2) + b
        r = self.info[2] * self.rows + i
        same = self.lev[line, jnp.maximum(r - 1, 0)] == self.lev[line, jnp.minimum(r, count - 1)]
        return jnp.where(jnp.logical_and(same, jnp.logical_and(r > 0, r < count)), 1.0, 0.0)


def rows_of(ref, lead, count):
    return [functools.partial(lambda r: ref[lead + (r,)], r) for r in range(count)]


def pick_halo(info, rx, rd, hs, lead):
    @pl.when(info[1] == 0)
    def _():
        hs[0] = rd[lead]
        hs[1] = rx[lead]

    @pl.when(info[1] != 0)
    def _():
        hs[0] = rx[lead]
        hs[1] = rd[lead]


def put_edges(info, first, last, sx, sd, lead):
    @pl.when(info[1] == 0)
    def _():
        sx[lead] = last
        sd[lead] = first

    @pl.when(info[1] != 0)
    def _():
        sx[lead] = first
        sd[lead] = last


def start_weights(info, layer, own, other, wv, sem):
    for t in range(wv.shape[0]):

        @pl.when(info[0] == layer)
        def _():
            pltpu.make_async_copy(own.at[t], wv.at[t], sem.at[t]).start()

        @pl.when(info[0] != layer)
        def _():
            pltpu.make_async_copy(other.at[t], wv.at[t], sem.at[t]).start()


def wait_weights(own, wv, sem, t):
    for i in range(wv.shape[0]):

        @pl.when(t == i)
        def _():
            pltpu.make_async_copy(own.at[i], wv.at[i], sem.at[i]).wait()


def activate(z):
    sg = jax.nn.sigmoid(z)
    hv = z * sg
    return hv.astype(BF), (sg + hv * (1.0 - sg)).astype(BF)


def forward_kernel(layer, info, lev, h, own, other, bias, bias_r, hn, sp, zp, token, x, wv, wt, sem):
    t, b = pl.program_id(0), pl.program_id(1)
    rows, width = h.shape[2], h.shape[3]
    e = Borders(info, lev, rows)

    @pl.when(jnp.logical_and(t == 0, b == 0))
    def _():
        start_weights(info, layer, own, other, wv, sem)

    build(x, rows_of(h, (0, 0), rows), e, b, taps=False)
    c = h.shape[4]

    @pl.when(b == 0)
    def _():
        wait_weights(own, wv, sem, t)
        for i in range(9):
            k, j = divmod(i, 3)
            wt[k * c : (k + 1) * c, j * c : (j + 1) * c] = wv[t, i * c : (i + 1) * c, :]

    chosen = jnp.full((1, c), info[0] == layer, jnp.int32) != 0
    row = pl.ds(t, 1)
    s = dot(x[...], wt[...]).reshape(rows, width, 3 * c)
    z = down(s[:, :, :c]) + s[:, :, c : 2 * c] + up(s[:, :, 2 * c :])
    z = z + jnp.where(chosen, bias[row, :c], bias_r[row, :c])
    hv, sv = activate(z)
    hn[0, 0] = hv
    sp[0, 0] = sv
    zp[0, 0, 0] = z[0]
    zp[0, 0, 1] = z[rows - 1]
    token[...] = jnp.zeros_like(token)


def forward(layer, info, lev, h, own, other, bias, bias_r, after=()):
    nb, nt, rows, width, c = h.shape
    row_spec = pl.BlockSpec((1, 1, rows, width, c), lambda t, b: (b, t, 0, 0, 0))
    taps = own.shape[1]
    return pl.pallas_call(
        ordered(functools.partial(forward_kernel, layer), 7, after),
        grid=(nt, nb),
        in_specs=[SMEM, SMEM, row_spec, HBM, HBM] + [pl.BlockSpec(bias.shape, lambda t, b: (0, 0))] * 2 + [ANY] * len(after),
        out_specs=[row_spec, row_spec, pl.BlockSpec((1, 1, 2, width, c), lambda t, b: (b, t, 0, 0, 0)), TOKEN_SPEC],
        out_shape=[jax.ShapeDtypeStruct(h.shape, BF)] * 2 + [jax.ShapeDtypeStruct((nb, nt, 2, width, c), F32), TOKEN],
        scratch_shapes=[
            pltpu.VMEM((rows * width, 3 * c), BF),
            pltpu.VMEM((nt, taps, c), BF),
            pltpu.VMEM((3 * c, 3 * c), BF),
            pltpu.SemaphoreType.DMA((nt,)),
        ],
        compiler_params=pltpu.CompilerParams(vmem_limit_bytes=12 << 20),
        cost_estimate=cost(8),
        name=f"forward{layer}",
    )(info, lev, h, own, other, bias, bias_r, *after)


def edge_kernel(layer, rows, info, lev, zp, rx, rd, own, other, hin, sin, hn, sp, sx, sd, wv, sem):
    i = pl.program_id(0)
    nb, nt, width, c = zp.shape[0], zp.shape[1], zp.shape[3], zp.shape[4]
    taps = wv.shape[2]
    e = Borders(info, lev, rows)

    def copies(ref, ii):
        for t in range(nt):
            yield pltpu.make_async_copy(ref.at[t, pl.ds(2 * ii * taps, taps)], wv.at[ii, t], sem.at[ii, t])

    for ii in range(2):
        for ref, chosen in ((own, info[0] == layer), (other, info[0] != layer)):

            @pl.when(jnp.logical_and(i == 0, chosen))
            def _():
                for copy in copies(ref, ii):
                    copy.start()

    from_x = (info[1] == 0) == (i == 1)
    edge = i * rows
    mask = jnp.full((1, c), from_x.astype(jnp.int32), jnp.int32) != 0
    parts = []
    for t in range(nt):
        p = []
        for b in range(nb):
            v = jnp.where(mask, rx[b, t].astype(F32), rd[b, t].astype(F32))
            p.append((jnp.concatenate([down(v), v, up(v)], axis=1) * e[b, edge]).astype(BF))
        parts.append(jnp.concatenate(p, axis=0))

    for ii in range(2):

        @pl.when(i == ii)
        def _():
            for copy in copies(own, ii):
                copy.wait()

    for t in range(nt):
        z = dot(parts[t], wv[i, t])
        for b in range(nb):
            hv, sv = activate(zp[b, t, 0] + z[b * width : (b + 1) * width])
            hn[b, t, 0] = hv
            sp[b, t, 0] = sv

            @pl.when(from_x)
            def _():
                sx[b, t] = hv

            @pl.when(jnp.logical_not(from_x))
            def _():
                sd[b, t] = hv


def edges(layer, info, lev, zp, rx, rd, own, other, hn, sp):
    nb, nt, rows, width, c = hn.shape
    taps = own.shape[1] // 3
    row_spec = pl.BlockSpec((nb, nt, 1, width, c), lambda i: (0, 0, i * (rows - 1), 0, 0))
    edge_spec = pl.BlockSpec((nb, nt, width, c), lambda i: (0, 0, 0, 0))
    edge = jax.ShapeDtypeStruct((nb, nt, width, c), BF)
    return pl.pallas_call(
        functools.partial(edge_kernel, layer, rows),
        grid=(2,),
        in_specs=[
            SMEM,
            SMEM,
            pl.BlockSpec((nb, nt, 1, width, c), lambda i: (0, 0, i, 0, 0)),
            edge_spec,
            edge_spec,
            HBM,
            HBM,
            HBM,
            HBM,
        ],
        out_specs=[row_spec, row_spec, edge_spec, edge_spec],
        out_shape=[jax.ShapeDtypeStruct(hn.shape, BF)] * 2 + [edge] * 2,
        input_output_aliases={7: 0, 8: 1},
        scratch_shapes=[pltpu.VMEM((2, nt, taps, c), BF), pltpu.SemaphoreType.DMA((2, nt))],
        compiler_params=pltpu.CompilerParams(vmem_limit_bytes=8 << 20),
        cost_estimate=cost(4),
        name=f"edges{layer}",
    )(info, lev, zp, rx, rd, own, other, hn, sp)


def tap_columns(ref, b, e, rows, width, gt):
    n = ref(0).shape[0]
    lane = lax.broadcasted_iota(jnp.int32, (n, width), 1)
    for s, k in ((rows, 0), (rows + 1, 0), (0, 1), (rows + 1, 1), (0, 2), (1, 2)):
        gt[0, 3 * k * n : 3 * (k + 1) * n, s * width : (s + 1) * width] = jnp.zeros((3 * n, width), gt.dtype)
    for r in range(rows):
        g = ref(r)
        left = jnp.where(lane < width - 1, pltpu.roll(g, width - 1, 1), 0.0)
        right = jnp.where(lane > 0, pltpu.roll(g, 1, 1), 0.0)
        for k in range(3):
            flag = e[b, r] if k == 0 else e[b, r + 1] if k == 2 else None
            for j, v in enumerate((left, g, right)):
                v = v if flag is None else v * flag
                at = (3 * k + j) * n
                gt[0, at : at + n, (r + k) * width : (r + k + 1) * width] = v.astype(gt.dtype)


def pack_rows(hx, rows, width, hs, row):
    hx[0:width] = hs[0]
    for r in range(rows):
        hx[(r + 1) * width : (r + 2) * width] = row(r)
    hx[(rows + 1) * width :] = hs[1]


def head_row(logit, cot, cot_r, kc, kp):
    gap = jnp.zeros((kp - kc, logit.shape[1]), F32)
    p = jax.nn.sigmoid(logit)
    q = p * (1.0 - p)
    d = [cot.astype(F32) * q[:kc], gap, cot_r.astype(F32) * q[kp : kp + kc], gap]
    return p[:kc].astype(BF), p[kp : kp + kc], jnp.concatenate(d, axis=0).astype(BF).T


def side(v, lane, j):
    width = v.shape[-1]
    if j == 0:
        return jnp.where(lane > 0, pltpu.roll(v, 1, 1), 0.0)
    if j == 2:
        return jnp.where(lane < width - 1, pltpu.roll(v, width - 1, 1), 0.0)
    return v


def head_kernel(
    info, lev, h, wk, wb, cb, cot, gb, cot_r,
    prob, psend, dl, gt, cb_x, cb_d, lp, bo, x, hx, lg, y,
):
    b = pl.program_id(0)
    rows, width, c = h.shape[2], h.shape[3], h.shape[4]
    kc, kb = cot.shape[2], gb.shape[1]
    kp, kq = wk.shape[1] // 2, wb.shape[0] // 18
    e = Borders(info, lev, rows)

    taps = 3 * c
    build(x, rows_of(h, (0, 0), rows), e, b)
    lg[...] = dot_nt(wk[0], x[:, :taps])
    lg[...] += dot_nt(wk[1], x[:, taps : 2 * taps])
    lg[...] += dot_nt(wk[2], x[:, 2 * taps :])

    for r in range(rows):
        hx[r * width : (r + 1) * width] = h[0, 1, r]
    y[...] = dot_nt(wb[...], hx[...])
    n = 2 * kq
    lane = lax.broadcasted_iota(jnp.int32, (n, width), 1)
    for r in range(rows):
        v = cb[2 * kp : 2 * kp + n]
        for j in range(3):
            s = y[(3 + j) * n : (4 + j) * n, r * width : (r + 1) * width]
            if r > 0:
                s = s + y[j * n : (j + 1) * n, (r - 1) * width : r * width] * e[b, r]
            if r < rows - 1:
                s = s + y[(6 + j) * n : (7 + j) * n, (r + 1) * width : (r + 2) * width] * e[b, r + 1]
            v = v + side(s, lane, j)
        bo[0, r] = v
    def row(r, _):
        at = pl.ds(pl.multiple_of(r * width, width), width)
        got = cot_r[0, r].astype(F32)[:kc]
        prob[0, r], other, dl[0, r] = head_row(lg[:, at] + cb[: 2 * kp], cot[0, r], got, kc, kp)
        rest = jnp.zeros((kp - kc - kb, width), F32)
        psend[0, r] = jnp.concatenate([other, bo[0, r, kq : kq + kb, :], rest], axis=0).astype(BF)
        return 0

    lax.fori_loop(0, rows, row, 0, unroll=2)
    lp[0, 0] = lg[:, :width] + cb[: 2 * kp]
    lp[0, 1] = lg[:, (rows - 1) * width :] + cb[: 2 * kp]
    small = jnp.zeros((kq - kb, width), F32)
    g = gb[0].astype(F32)

    def columns(r):
        return jnp.concatenate([g[:, r], small, cot_r[0, r].astype(F32)[kc : kc + kb], small], axis=0)

    tap_columns(columns, b, e, rows, width, gt)
    for i in range(2):
        s = i * (rows + 1)
        db = dot_tn(gt[0, :, s * width : (s + 1) * width], wb[...]).astype(BF)

        @pl.when((info[1] == 0) == (i == 1))
        def _():
            cb_x[0] = db

        @pl.when((info[1] == 0) == (i == 0))
        def _():
            cb_d[0] = db


def head(info, lev, h, wk, wb, cb, cot, gb, cot_r, after=()):
    nb, nt, rows, width, c = h.shape
    kc, kb, kp2, kq2 = cot.shape[2], gb.shape[1], wk.shape[1], wb.shape[0] // 9
    batches = cot.shape[0]
    m = rows * width
    ext = (rows + 2) * width

    def at_b(shape):
        return pl.BlockSpec((1,) + shape, lambda b, info: (b,) + (0,) * len(shape))

    def at_all(shape):
        return pl.BlockSpec((1,) + shape, lambda b, info: (info[0] * nb + b,) + (0,) * len(shape))

    def whole(shape):
        return pl.BlockSpec(shape, lambda b, info: (0,) * len(shape), pipeline_mode=pl.Buffered(1))

    return pl.pallas_call(
        ordered(head_kernel, 9, after),
        grid_spec=pltpu.PrefetchScalarGridSpec(
            num_scalar_prefetch=1,
            grid=(nb,),
            in_specs=[
                SMEM,
                at_b((nt, rows, width, c)),
                whole(wk.shape),
                whole(wb.shape),
                whole(cb.shape),
                at_all((rows, kc, width)),
                at_all((kb, rows, width)),
                at_b((rows, kp2 // 2, width)),
            ]
            + [ANY] * len(after),
            out_specs=[
                at_all((rows, kc, width)),
                at_b((rows, kp2 // 2, width)),
                at_b((rows, width, kp2)),
                at_b((9 * kq2, ext)),
                at_b((width, c)),
                at_b((width, c)),
                at_b((2, kp2, width)),
                at_b((rows, kq2, width)),
            ],
            scratch_shapes=[
                pltpu.VMEM((m, 9 * c), BF),
                pltpu.VMEM((m, c), BF),
                pltpu.VMEM((kp2, m), F32),
                pltpu.VMEM((9 * kq2, m), F32),
            ],
        ),
        out_shape=[
            jax.ShapeDtypeStruct((batches, rows, kc, width), BF),
            jax.ShapeDtypeStruct((nb, rows, kp2 // 2, width), BF),
            jax.ShapeDtypeStruct((nb, rows, width, kp2), BF),
            jax.ShapeDtypeStruct((nb, 9 * kq2, ext), BF),
            jax.ShapeDtypeStruct((nb, width, c), BF),
            jax.ShapeDtypeStruct((nb, width, c), BF),
            jax.ShapeDtypeStruct((nb, 2, kp2, width), F32),
            jax.ShapeDtypeStruct((nb, rows, kq2, width), F32),
        ],
        compiler_params=pltpu.CompilerParams(vmem_limit_bytes=17 << 20),
        cost_estimate=cost(14),
        name="head",
    )(info, lev, h, wk, wb, cb, cot, gb, cot_r, *after)


def head_edge_kernel(
    info, lev, rx, rd, wk, wb, lp, bo, cot, cot_r, cb_x, cb_d, prob_i, psend_i, dl_i,
    prob, psend, dl, boxo, cx, cd, hs, ds, bs, bx,
):
    i = pl.program_id(0)
    nb, nt, width, c = rx.shape
    kc, kb, rows = cot.shape[2], boxo.shape[1], boxo.shape[2]
    kp, kq = wk.shape[1] // 2, bo.shape[2] // 2
    taps = 3 * c
    n = 2 * kq
    e = Borders(info, lev, rows)
    edge = i * rows
    from_x = (info[1] == 0) == (i == 1)

    @pl.when(from_x)
    def _():
        hs[...] = rx[...]

    @pl.when(jnp.logical_not(from_x))
    def _():
        hs[...] = rd[...]

    p = []
    for b in range(nb):
        v = hs[b, 0]
        p.append(keep_if(jnp.concatenate([down(v), v, up(v)], axis=1), e[b, edge]))
    logit = dot_nt(wk[0], jnp.concatenate(p, axis=0))
    lane = lax.broadcasted_iota(jnp.int32, (n, width), 1)
    for b in range(nb):
        lg = logit[:, b * width : (b + 1) * width] + lp[b, 0]
        prob[b, 0], other, d = head_row(lg, cot[b, 0], cot_r[b, 0].astype(F32)[:kc], kc, kp)
        dl[b, 0] = d
        ds[b * width : (b + 1) * width, :] = d
        y = dot_nt(wb[...], hs[b, 1]) * e[b, edge]
        v = bo[b, i * (rows - 1)]
        for j in range(3):
            v = v + side(y[j * n : (j + 1) * n, :], lane, j)
        bs[b, i] = v
        gap = jnp.zeros((kp - kc - kb, width), F32)
        psend[b, 0] = jnp.concatenate([other, v[kq : kq + kb], gap], axis=0).astype(BF)

    @pl.when(i == 1)
    def _():
        for b in range(nb):
            for r in range(rows):
                v = bs[b, 0] if r == 0 else bs[b, 1] if r == rows - 1 else bo[b, r]
                bx[:, r, :] = v
            boxo[b] = bx[:kb].astype(BF)

    s = dot(ds[...], wk[0]).reshape(nb, width, taps)
    dc = up(s[:, :, :c]) + s[:, :, c : 2 * c] + down(s[:, :, 2 * c :])
    for b in range(nb):
        v = keep_if(dc[b].astype(BF), e[b, edge])

        @pl.when(from_x)
        def _():
            cx[b, 0] = v
            cx[b, 1] = cb_x[b]

        @pl.when(jnp.logical_not(from_x))
        def _():
            cd[b, 0] = v
            cd[b, 1] = cb_d[b]


def head_edges(info, lev, rx, rd, wk, wb, lp, bo, cot, cot_r, cb_x, cb_d, prob, psend, dl, kb):
    nb, nt, width, c = rx.shape
    rows = cot.shape[1]
    kc, kp2, kq2 = cot.shape[2], wk.shape[1], bo.shape[2]

    def whole(shape):
        return pl.BlockSpec(shape, lambda i, info: (0,) * len(shape), pipeline_mode=pl.Buffered(1))

    def at_i(shape):
        return pl.BlockSpec(shape, lambda i, info: (0, i) + (0,) * (len(shape) - 2))

    def edge_of(shape):
        return pl.BlockSpec(shape, lambda i, info: (0, i * (rows - 1)) + (0,) * (len(shape) - 2))

    def edge_all(shape):
        return pl.BlockSpec(shape, lambda i, info: (info[0], i * (rows - 1)) + (0,) * (len(shape) - 2))

    edge = jax.ShapeDtypeStruct((nb, nt, width, c), BF)
    arrays = (prob, psend, dl)
    return pl.pallas_call(
        head_edge_kernel,
        grid_spec=pltpu.PrefetchScalarGridSpec(
            num_scalar_prefetch=1,
            grid=(2,),
            in_specs=[
                SMEM,
                whole(rx.shape),
                whole(rd.shape),
                pl.BlockSpec((1,) + wk.shape[1:], lambda i, info: (2 * i, 0, 0)),
                pl.BlockSpec((3 * kq2, c), lambda i, info: (2 * i, 0)),
                at_i((nb, 1, kp2, width)),
                whole(bo.shape),
                edge_all((nb, 1, kc, width)),
                edge_of((nb, 1, kp2 // 2, width)),
                whole(cb_x.shape),
                whole(cb_d.shape),
            ]
            + [HBM] * len(arrays),
            out_specs=[
                edge_all((nb, 1, kc, width)),
                edge_of((nb, 1, kp2 // 2, width)),
                edge_of((nb, 1, width, kp2)),
                pl.BlockSpec((nb, kb, rows, width), lambda i, info: (info[0], 0, 0, 0)),
                pl.BlockSpec(rx.shape, lambda i, info: (0, 0, 0, 0)),
                pl.BlockSpec(rx.shape, lambda i, info: (0, 0, 0, 0)),
            ],
            scratch_shapes=[
                pltpu.VMEM(rx.shape, BF),
                pltpu.VMEM((nb * width, kp2), BF),
                pltpu.VMEM((nb, 2, kq2, width), F32),
                pltpu.VMEM((kq2, rows, width), F32),
            ],
        ),
        out_shape=[jax.ShapeDtypeStruct(v.shape, BF) for v in arrays]
        + [jax.ShapeDtypeStruct((cot.shape[0], kb, rows, width), BF)]
        + [edge, edge],
        input_output_aliases={12 + i: i for i in range(len(arrays))},
        compiler_params=pltpu.CompilerParams(vmem_limit_bytes=8 << 20),
        cost_estimate=cost(6),
        name="head_edges",
    )(info, lev, rx, rd, wk, wb, lp, bo, cot, cot_r, cb_x, cb_d, *arrays)


def head_weights_kernel(info, lev, h, rx, rd, dl, gt, own, other, token, x, hx, acc, accb, small, sums, hs, *, kc, kb):
    b, nb = pl.program_id(0), pl.num_programs(0)
    rows, width, c = h.shape[2], h.shape[3], h.shape[4]
    token[...] = jnp.zeros_like(token)
    kp, kq = dl.shape[-1] // 2, accb.shape[0] // 18
    taps = 3 * c
    e = Borders(info, lev, rows)
    pick_halo(info, rx, rd, hs, (0, 0))
    build(x, rows_of(h, (0, 0), rows), e, b, lambda: hs[0], lambda: hs[1])
    pick_halo(info, rx, rd, hs, (0, 1))
    pack_rows(hx, rows, width, hs, lambda r: h[0, 1, r])
    g = dl[0].reshape(rows * width, 2 * kp)

    @pl.when(b == 0)
    def _():
        acc[...] = jnp.zeros_like(acc)
        accb[...] = jnp.zeros_like(accb)
        small[...] = jnp.zeros_like(small)

    acc[...] += dot_tn(g, x[...])
    accb[...] += dot(gt[0], hx[...])
    small[:, : 2 * kp] += jnp.sum(g.astype(F32), axis=0, keepdims=True)
    ones = jnp.ones((8, gt.shape[2]), BF)
    s = dot_nt(ones, gt[0, 8 * kq : 10 * kq, :])[:1]
    small[:, 2 * kp :] += jnp.concatenate([s, jnp.zeros((1, LANES - 2 * kq), F32)], axis=1)

    def fill(ref, a):
        for k in range(3):
            ref[k * kc : (k + 1) * kc, :] = acc[a * kp : a * kp + kc, k * taps : (k + 1) * taps]
            at = 3 * kc + k * kq
            for j in range(3):
                first = (3 * k + j) * 2 * kq + a * kq
                ref[at : at + kq, j * c : (j + 1) * c] = accb[first : first + kq, :]
        end = 3 * (kc + kq)
        if end < ref.shape[0]:
            ref[end:, :] = jnp.zeros((ref.shape[0] - end, taps), F32)
        at = 3 * kc + kb
        ref[at : at + 1, :kp] = small[:, a * kp : (a + 1) * kp]
        ref[at : at + 1, kp : kp + LANES] = pltpu.roll(small[:, 2 * kp :], (LANES - a * kq) % LANES, 1)

    @pl.when(b == nb - 1)
    def _():
        for a, out in ((1, other), (0, own)):
            fill(sums, a)
            out[...] = sums[...].astype(BF)


def head_weights(info, lev, h, rx, rd, dl, gt, kc, kb, after=()):
    nb, nt, rows, width, c = h.shape
    kp2 = dl.shape[-1]
    kq2 = gt.shape[1] // 9
    m = rows * width
    size = -(-3 * (kc + kq2 // 2) // LANES) * LANES

    def at_b(shape):
        return pl.BlockSpec((1,) + shape, lambda b: (b,) + (0,) * len(shape))

    def whole(shape):
        return pl.BlockSpec(shape, lambda b: (0,) * len(shape), pipeline_mode=pl.Buffered(1))

    return pl.pallas_call(
        ordered(functools.partial(head_weights_kernel, kc=kc, kb=kb), 7, after),
        grid=(nb,),
        in_specs=[
            SMEM,
            SMEM,
            at_b((nt, rows, width, c)),
            at_b((nt, width, c)),
            at_b((nt, width, c)),
            at_b((rows, width, kp2)),
            at_b(gt.shape[1:]),
        ]
        + [ANY] * len(after),
        out_specs=[whole((size, 3 * c)), whole((size, 3 * c)), TOKEN_SPEC],
        out_shape=[jax.ShapeDtypeStruct((size, 3 * c), BF)] * 2 + [TOKEN],
        scratch_shapes=[
            pltpu.VMEM((m, 9 * c), BF),
            pltpu.VMEM(((rows + 2) * width, c), BF),
            pltpu.VMEM((kp2, 9 * c), F32),
            pltpu.VMEM((9 * kq2, c), F32),
            pltpu.VMEM((1, kp2 + LANES), F32),
            pltpu.VMEM((size, 3 * c), F32),
            pltpu.VMEM((2, width, c), BF),
        ],
        compiler_params=pltpu.CompilerParams(vmem_limit_bytes=21 << 20),
        cost_estimate=cost(12),
        name="head_weights",
    )(info, lev, h, rx, rd, dl, gt, *after)


def head_inputs_kernel(info, lev, dl, gt, rx, rd, wk, wb, sp, *rest):
    dz, sx, sd, token, *_, x, hs = rest
    token[...] = jnp.zeros_like(token)
    b = pl.program_id(0)
    rows, width, c = sp.shape[2], sp.shape[3], sp.shape[4]
    kp2 = dl.shape[-1]
    taps = 3 * c
    e = Borders(info, lev, rows)
    build(x, rows_of(dl, (0,), rows), e, b, taps=False)
    s = dot(x[:, kp2 : 2 * kp2], wk[1])
    s = s + dot(x[:, :kp2], wk[2])
    s = s + dot(x[:, 2 * kp2 :], wk[0])
    s = s.reshape(rows, width, taps)
    dc = up(s[:, :, :c]) + s[:, :, c : 2 * c] + down(s[:, :, 2 * c :])
    db = dot_tn(gt[0, :, width : (rows + 1) * width], wb[...]).reshape(rows, width, c)
    for t, dh in ((0, dc), (1, db)):
        pick_halo(info, rx, rd, hs, (0, t))
        for r in range(rows):
            v = dh[r]
            if r == 0:
                v = v + hs[0].astype(F32)
            if r == rows - 1:
                v = v + hs[1].astype(F32)
            dz[0, t, r] = (v * sp[0, t, r].astype(F32)).astype(BF)
        put_edges(info, dz[0, t, 0], dz[0, t, rows - 1], sx, sd, (0, t))


def head_inputs(info, lev, dl, gt, rx, rd, wk, wb, sp, gate, after=()):
    nb, nt, rows, width, c = sp.shape
    kp2 = dl.shape[-1]
    m = rows * width

    def at_b(shape):
        return pl.BlockSpec((1,) + shape, lambda b: (b,) + (0,) * len(shape))

    def whole(shape):
        return pl.BlockSpec(shape, lambda b: (0,) * len(shape), pipeline_mode=pl.Buffered(1))

    return pl.pallas_call(
        ordered(head_inputs_kernel, 9, gate + after),
        grid=(nb,),
        in_specs=[
            SMEM,
            SMEM,
            at_b((rows, width, kp2)),
            at_b(gt.shape[1:]),
            at_b((nt, width, c)),
            at_b((nt, width, c)),
            whole(wk.shape),
            whole(wb.shape),
            at_b((nt, rows, width, c)),
        ]
        + [ANY] * len(gate + after),
        out_specs=[at_b((nt, rows, width, c)), at_b((nt, width, c)), at_b((nt, width, c)), TOKEN_SPEC] + [ANY] * len(gate),
        out_shape=[
            jax.ShapeDtypeStruct(sp.shape, BF),
            jax.ShapeDtypeStruct((nb, nt, width, c), BF),
            jax.ShapeDtypeStruct((nb, nt, width, c), BF),
        ]
        + [TOKEN]
        + [jax.ShapeDtypeStruct(v.shape, v.dtype) for v in gate],
        input_output_aliases={9 + k: 4 + k for k in range(len(gate))},
        scratch_shapes=[pltpu.VMEM((m, 3 * kp2), BF), pltpu.VMEM((2, width, c), BF)],
        compiler_params=pltpu.CompilerParams(vmem_limit_bytes=14 << 20),
        cost_estimate=cost(9),
        name="head_inputs",
    )(info, lev, dl, gt, rx, rd, wk, wb, sp, *gate, *after)


def weights_kernel(info, lev, h, rx, rd, dz, keep, send, token, x, acc, bias, hs):
    t, b, nb = pl.program_id(0), pl.program_id(1), pl.num_programs(1)
    rows, width, c = h.shape[2], h.shape[3], h.shape[4]
    e = Borders(info, lev, rows)
    pick_halo(info, rx, rd, hs, (0, 0))
    build(x, rows_of(h, (0, 0), rows), e, b, lambda: hs[0], lambda: hs[1])
    g = dz[0, 0].reshape(rows * width, c)
    part = dot_tn(x[...], g)
    total = jnp.sum(g.astype(F32), axis=0, keepdims=True)
    taps = acc.shape[0]

    @pl.when(b == 0)
    def _():
        acc[...] = part
        bias[...] = total

    @pl.when(b != 0)
    def _():
        acc[...] += part
        bias[...] += total

    token[...] = jnp.zeros_like(token)
    for i, out in enumerate((send, keep)):

        @pl.when(jnp.logical_and(b == nb - 1, t == i))
        def _():
            out[:taps, :] = acc[...].astype(out.dtype)
            out[taps:, :] = jnp.broadcast_to(bias[...].astype(out.dtype), (out.shape[0] - taps, c))


def weights(layer, info, lev, h, rx, rd, dz, after=()):
    nb, nt, rows, width, c = h.shape

    def tower(t, info):
        return jnp.where(t == 0, 1 - info[0], info[0])

    row_spec = pl.BlockSpec((1, 1, rows, width, c), lambda t, b, info: (b, tower(t, info), 0, 0, 0))
    edge_spec = pl.BlockSpec((1, 1, width, c), lambda t, b, info: (b, tower(t, info), 0, 0))
    taps = 9 * c
    return pl.pallas_call(
        ordered(weights_kernel, 6, after),
        grid_spec=pltpu.PrefetchScalarGridSpec(
            num_scalar_prefetch=1,
            grid=(nt, nb),
            in_specs=[SMEM, row_spec, edge_spec, edge_spec, row_spec] + [ANY] * len(after),
            out_specs=[pl.BlockSpec((taps + LANES, c), lambda t, b, info: (0, 0))] * 2 + [TOKEN_SPEC],
            scratch_shapes=[
                pltpu.VMEM((rows * width, taps), BF),
                pltpu.VMEM((taps, c), F32),
                pltpu.VMEM((1, c), F32),
                pltpu.VMEM((2, width, c), BF),
            ],
        ),
        out_shape=[jax.ShapeDtypeStruct((taps + LANES, c), BF)] * 2 + [TOKEN],
        compiler_params=pltpu.CompilerParams(vmem_limit_bytes=14 << 20),
        cost_estimate=cost(8),
        name=f"weights{layer}",
    )(info, lev, h, rx, rd, dz, *after)


def inputs_kernel(layer, info, lev, dz, rx, rd, own, other, *rest):
    if layer:
        sp, out, token, sx, sd, x, wv, wt, hs, sem = rest
    else:
        out, token, *_, x, wv, wt, hs, sem = rest
    token[...] = jnp.zeros_like(token)
    t, b = pl.program_id(0), pl.program_id(1)
    rows, width, c = dz.shape[2], dz.shape[3], dz.shape[4]
    e = Borders(info, lev, rows)

    @pl.when(jnp.logical_and(t == 0, b == 0))
    def _():
        start_weights(info, layer, own, other, wv, sem)

    pick_halo(info, rx, rd, hs, (0, 0))
    build(x, rows_of(dz, (0, 0), rows), e, b, lambda: hs[0], lambda: hs[1], taps=False)

    @pl.when(b == 0)
    def _():
        wait_weights(own, wv, sem, t)
        for k in range(3):
            wt[:, (2 - k) * c : (3 - k) * c] = wv[t, 3 * k * c : 3 * (k + 1) * c, :]

    s = dot_nt(x[...], wt[...]).reshape(rows, width, 3 * c)
    dh = (up(s[:, :, :c]) + s[:, :, c : 2 * c] + down(s[:, :, 2 * c :])).astype(BF)
    if not layer:
        out[0, 0] = dh
        return
    dz_next = (dh.astype(F32) * sp[0, 0].astype(F32)).astype(BF)
    out[0, 0] = dz_next
    put_edges(info, dz_next[0], dz_next[rows - 1], sx, sd, (0, 0))


def inputs(layer, info, lev, dz, rx, rd, own, other, sp=None, gate=(), after=()):
    nb, nt, rows, width, c = dz.shape
    row_spec = pl.BlockSpec((1, 1, rows, width, c), lambda t, b: (b, t, 0, 0, 0))
    edge_spec = pl.BlockSpec((1, 1, width, c), lambda t, b: (b, t, 0, 0))
    edge = jax.ShapeDtypeStruct((nb, nt, width, c), BF)
    taps = own.shape[1]
    return pl.pallas_call(
        ordered(functools.partial(inputs_kernel, layer), 8 if layer else 7, gate + after),
        grid=(nt, nb),
        in_specs=[SMEM, SMEM, row_spec, edge_spec, edge_spec, HBM, HBM] + ([row_spec] if layer else []) + [ANY] * len(gate + after),
        out_specs=[row_spec, TOKEN_SPEC] + ([edge_spec, edge_spec] if layer else []) + [ANY] * len(gate),
        out_shape=[jax.ShapeDtypeStruct(dz.shape, BF)]
        + [TOKEN]
        + ([edge, edge] if layer else [])
        + [jax.ShapeDtypeStruct(v.shape, v.dtype) for v in gate],
        input_output_aliases={7 + k: 2 + k for k in range(len(gate))},
        scratch_shapes=[
            pltpu.VMEM((rows * width, 3 * c), BF),
            pltpu.VMEM((nt, taps, c), BF),
            pltpu.VMEM((3 * c, 3 * c), BF),
            pltpu.VMEM((2, width, c), BF),
            pltpu.SemaphoreType.DMA((nt,)),
        ],
        compiler_params=pltpu.CompilerParams(vmem_limit_bytes=13 << 20),
        cost_estimate=cost(9),
        name=f"inputs{layer}",
    )(info, lev, dz, rx, rd, own, other, *([sp] if layer else []), *gate, *after)


def swap_section(value):
    return lax.ppermute(value, "section", [(0, 1), (1, 0)])


def swap_edges(sx, sd):
    count = lax.axis_size("tile")
    even = [p for i in range(0, count - 1, 2) for p in ((i, i + 1), (i + 1, i))]
    odd = [p for i in range(1, count - 1, 2) for p in ((i, i + 1), (i + 1, i))]
    return lax.ppermute(sx, "tile", even), lax.ppermute(sd, "tile", odd)


def combine_kernel(plan, info, *refs):
    ins, outs = list(refs[: sum(sum(p) for p in plan)]), refs[sum(sum(p) for p in plan) :]
    for counts, out in zip(plan, outs):
        lanes = out.shape[1] // len(counts)
        for i, count in enumerate(counts):
            terms = [ins.pop(0)[...].astype(F32) for _ in range(count)]
            out[:, i * lanes : (i + 1) * lanes] = functools.reduce(jnp.add, terms).astype(out.dtype)


def combine(name, info, shape, outs, gate=(), after=()):
    rows, lanes = shape
    views = [v for parts in outs for terms in parts for v in terms]

    def spec(view):
        return pl.BlockSpec(shape, lambda i, info: (view[1](info), view[2]))

    plan = [[len(terms) for terms in parts] for parts in outs]
    return pl.pallas_call(
        ordered(functools.partial(combine_kernel, plan), 1 + len(views), gate + after),
        grid_spec=pltpu.PrefetchScalarGridSpec(
            num_scalar_prefetch=1,
            grid=(1,),
            in_specs=[spec(v) for v in views] + [ANY] * len(gate + after),
            out_specs=[pl.BlockSpec((rows, lanes * len(parts)), lambda i, info: (0, 0)) for parts in outs]
            + [ANY] * len(gate),
        ),
        out_shape=[jax.ShapeDtypeStruct((rows, lanes * len(parts)), BF) for parts in outs]
        + [jax.ShapeDtypeStruct(v.shape, v.dtype) for v in gate],
        input_output_aliases={1 + len(views) + k: len(outs) + k for k in range(len(gate))},
        compiler_params=pltpu.CompilerParams(vmem_limit_bytes=7 << 20),
        cost_estimate=cost(2),
        name=name,
    )(info, *[v[0] for v in views], *gate, *after)


def join_kernel(bits, split, info, *refs):
    n = len(bits)
    for i, bit in enumerate(bits):
        cur, got = refs[2 * i], refs[2 * i + 1]
        outs = refs[2 * n :] if split else refs[2 * n + i : 2 * n + i + 1]
        m, lanes = cur.shape[0], cur.shape[1] // len(outs)
        mine = (info[2] >> bit) & 1
        for j, out in enumerate(outs):
            at = slice(j * lanes, (j + 1) * lanes)

            @pl.when(mine == 0)
            def _():
                out[:m, :] = cur[:, at]
                out[m:, :] = got[:, at]

            @pl.when(mine != 0)
            def _():
                out[:m, :] = got[:, at]
                out[m:, :] = cur[:, at]


def join(name, info, bits, pairs, split=False, after=()):
    arrays = [v for pair in pairs for v in pair]
    shapes = [(2 * cur.shape[0], cur.shape[1]) for cur, _ in pairs]
    if split:
        shapes = [(shapes[0][0], shapes[0][1] // 2)] * 2

    def whole(shape):
        return pl.BlockSpec(shape, lambda i, info: (0, 0))

    return pl.pallas_call(
        ordered(functools.partial(join_kernel, bits, split), 1 + len(arrays), after),
        grid_spec=pltpu.PrefetchScalarGridSpec(
            num_scalar_prefetch=1,
            grid=(1,),
            in_specs=[whole(v.shape) for v in arrays] + [ANY] * len(after),
            out_specs=[whole(s) for s in shapes],
        ),
        out_shape=[jax.ShapeDtypeStruct(s, BF) for s in shapes],
        compiler_params=pltpu.CompilerParams(vmem_limit_bytes=7 << 20),
        cost_estimate=cost(2),
        name=name,
    )(info, *arrays, *after)


def relay_kernel(*refs):
    del refs


def relay(name, gate, after):
    return pl.pallas_call(
        ordered(relay_kernel, 0, gate + after),
        in_specs=[ANY] * len(gate + after),
        out_specs=[ANY] * len(gate),
        out_shape=[jax.ShapeDtypeStruct(v.shape, v.dtype) for v in gate],
        input_output_aliases={k: k for k in range(len(gate))},
        compiler_params=pltpu.CompilerParams(vmem_limit_bytes=1 << 20),
        cost_estimate=cost(1),
        name=name,
    )(*gate, *after)


class TileSum:
    def __init__(self, name, info, whole, *terms):
        self.name, self.info = name, info
        rows, lanes = terms[0].shape
        self.shape = (rows, lanes // 2)
        self.parts = [[(v, lambda info: 0, i) for v in terms] for i in range(2)]
        self.count = lax.axis_size("tile")
        bits = self.count.bit_length() - 1
        near = [(0, 1), (1, 0)]
        self.plan = [("halve", step) for step in near]
        if whole or bits > 4:
            self.plan += [("add", (bit,)) for bit in range(2, bits)]
        else:
            self.plan += [("halve", (bit,)) for bit in range(2, bits - 1)]
            self.plan += [("add", (bit,)) for bit in range(max(bits - 1, 2), bits)]
            self.plan += [("double", (bit,)) for bit in reversed(range(2, bits - 1))]
        self.plan += [("double", step) for step in reversed(near)]
        self.step = 0
        self.sends = None

    def exchange(self, value, bit):
        return lax.ppermute(value, "tile", [(i, i ^ (1 << bit)) for i in range(self.count)])

    def start(self, *after, gate=()):
        kind, bits = self.plan.pop(0)
        name = f"{self.name}_{self.step}"
        self.step += 1
        if kind == "halve":
            rows, lanes = self.shape
            self.shape = (rows // 2, lanes)
            bit_of = bits * 2 if len(bits) == 1 else bits

            def half(view, bit, other):
                array, row, lane = view
                return array, lambda info: 2 * row(info) + (((info[2] >> bit) & 1) ^ other), lane

            sent = [[half(v, bit, 1) for v in terms] for terms, bit in zip(self.parts, bit_of)]
            self.parts = [[half(v, bit, 0) for v in terms] for terms, bit in zip(self.parts, bit_of)]
            outs = [sent] if len(bits) == 1 else [[terms] for terms in sent]
            sends = combine(name, self.info, self.shape, outs, gate, after)
        elif kind == "add" or self.kind != "double":
            outs = [self.parts] if len(bits) == 1 else [[terms] for terms in self.parts]
            sends = combine(name, self.info, self.shape, outs, gate, after)
        else:
            sends = join(name, self.info, self.bits, self.pairs, len(bits) > len(self.pairs), after)
        passed = tuple(sends[len(bits) :])
        sends = tuple(sends[: len(bits)])
        self.kind, self.bits, self.sends = kind, bits, sends
        got = [self.exchange(v, bit) for v, bit in zip(sends, bits)]
        if kind == "halve":
            lane = (lambda i: i) if len(bits) == 1 else (lambda i: 0)
            pick = (lambda i: got[0]) if len(bits) == 1 else (lambda i: got[i])
            self.parts = [terms + [(pick(i), lambda info: 0, lane(i))] for i, terms in enumerate(self.parts)]
        elif kind == "add":
            self.parts = [[(v, lambda info: 0, i) for v in (sends[0], got[0])] for i in range(2)]
        else:
            self.pairs = list(zip(sends, got))
        return sends + passed

    def result(self, *after):
        return join(f"{self.name}_{self.step}", self.info, self.bits, self.pairs, False, after)


def pick_kernel(info, cot, gb, out):
    rows, kc, kb = cot.shape[1], cot.shape[2], gb.shape[1]
    g = gb[0].astype(F32)
    gap = jnp.zeros((out.shape[2] - kc - kb, out.shape[3]), F32)
    for r in range(rows):
        out[0, r] = jnp.concatenate([cot[0, r].astype(F32), g[:, r], gap], axis=0).astype(BF)


def pick(info, cot, gb, nb, kp, after=()):
    def at_all(shape):
        return pl.BlockSpec((1,) + shape[1:], lambda b, info: ((1 - info[0]) * nb + b,) + (0,) * (len(shape) - 1))

    shape = (nb, cot.shape[1], kp, cot.shape[3])
    return pl.pallas_call(
        ordered(pick_kernel, 3, after),
        grid_spec=pltpu.PrefetchScalarGridSpec(
            num_scalar_prefetch=1,
            grid=(nb,),
            in_specs=[at_all(cot.shape), at_all(gb.shape)] + [ANY] * len(after),
            out_specs=pl.BlockSpec((1,) + shape[1:], lambda b, info: (b, 0, 0, 0)),
        ),
        out_shape=jax.ShapeDtypeStruct(shape, BF),
        compiler_params=pltpu.CompilerParams(vmem_limit_bytes=8 << 20),
        cost_estimate=cost(2),
        name="pick",
    )(info, cot, gb, *after)


def gather_kernel(tower, classes, boxes, out):
    out[...] = jnp.zeros_like(out)
    nt, c = tower.shape[1], tower.shape[2]
    out[:nt, :c] = tower[0]
    out[nt : nt + 1, : classes.shape[0]] = classes[...].reshape(1, -1)
    out[nt + 1 : nt + 2, : boxes.shape[0]] = boxes[...].reshape(1, -1)


def gather(tower, classes, boxes, lanes):
    return pl.pallas_call(
        gather_kernel,
        out_shape=jax.ShapeDtypeStruct((8, lanes), F32),
        cost_estimate=cost(1),
        name="gather",
    )(tower, classes, boxes)


def pick_weights_kernel(thin, small, out):
    gap = jnp.zeros((out.shape[1] - thin.shape[1] - small.shape[1], out.shape[2]), F32)
    out[0] = jnp.concatenate([thin[0].astype(F32), small[0].astype(F32), gap], axis=0).astype(BF)


def pick_weights(thin, small, kp, after=()):
    def at_k(shape):
        return pl.BlockSpec((1,) + shape[1:], lambda k: (k, 0, 0))

    shape = (thin.shape[0], kp, thin.shape[2])
    return pl.pallas_call(
        ordered(pick_weights_kernel, 2, after),
        grid=(shape[0],),
        in_specs=[at_k(thin.shape), at_k(small.shape)] + [ANY] * len(after),
        out_specs=at_k(shape),
        out_shape=jax.ShapeDtypeStruct(shape, BF),
        compiler_params=pltpu.CompilerParams(vmem_limit_bytes=6 << 20),
        cost_estimate=cost(2),
        name="pick_weights",
    )(thin, small, *after)


def pack_kernel(own, other, bias, bias_r, wk, wb, cb, *, kc, kb, kq, towers):
    k = pl.program_id(0)
    kp = own.shape[1]
    c = wb.shape[1]
    gap = jnp.zeros((kp - kc, wk.shape[2]), F32)
    for half, v in enumerate((own, other)):
        wk[0, half * kp : (half + 1) * kp, :] = jnp.concatenate([v[0].astype(F32)[:kc], gap], axis=0).astype(BF)
    u, v = own[0].astype(F32)[kc : kc + kb], other[0].astype(F32)[kc : kc + kb]
    small = jnp.zeros((kq - kb, c), F32)
    for j in range(3):
        at = slice(j * c, (j + 1) * c)
        rows = jnp.concatenate([u[:, at], small, v[:, at], small], axis=0).astype(BF)
        wb[pl.ds(pl.multiple_of((3 * k + j) * 2 * kq, 2 * kq), 2 * kq), :] = rows

    @pl.when(k == 0)
    def _():
        wide = jnp.zeros((1, kp - kc), F32)
        thin = jnp.zeros((1, kq - kb), F32)
        rest = jnp.zeros((1, cb.shape[0] - 2 * kp - kq - kb), F32)
        classes, boxes = slice(towers, towers + 1), slice(towers + 1, towers + 2)
        parts = [bias[classes, :kc], wide, bias_r[classes, :kc], wide, bias[boxes, :kb], thin, bias_r[boxes, :kb], rest]
        cb[...] = jnp.broadcast_to(jnp.concatenate(parts, axis=1), (cb.shape[1], cb.shape[0])).T


def pack(own, other, bias, bias_r, kc, kb, kq, towers, after=()):
    k, kp, c3 = own.shape
    at_k = pl.BlockSpec((1, kp, c3), lambda k: (k, 0, 0))

    def whole(shape):
        return pl.BlockSpec(shape, lambda k: (0,) * len(shape))

    shapes = [(k, 2 * kp, c3), (18 * kq, c3 // 3), (2 * kp + LANES, LANES)]
    return pl.pallas_call(
        ordered(functools.partial(pack_kernel, kc=kc, kb=kb, kq=kq, towers=towers), 4, after),
        grid=(k,),
        in_specs=[at_k, at_k, whole(bias.shape), whole(bias.shape)] + [ANY] * len(after),
        out_specs=[pl.BlockSpec((1,) + shapes[0][1:], lambda k: (k, 0, 0)), whole(shapes[1]), whole(shapes[2])],
        out_shape=[jax.ShapeDtypeStruct(s, t) for s, t in zip(shapes, (BF, BF, F32))],
        compiler_params=pltpu.CompilerParams(vmem_limit_bytes=10 << 20),
        cost_estimate=cost(3),
        name="pack",
    )(own, other, bias, bias_r, *after)


def place_kernel(info, prob_i, box_i, got, prob, box, token, bx):
    rows, kc, kb = prob.shape[1], prob.shape[2], box.shape[1]
    for r in range(rows):
        v = got[0, r].astype(F32)
        prob[0, r] = v[:kc].astype(BF)
        bx[:, r, :] = v[kc : kc + kb]
    box[0] = bx[...].astype(BF)
    token[...] = jnp.zeros_like(token)


def place(info, prob, box, got, after=()):
    nb = got.shape[0]

    def at_all(shape):
        return pl.BlockSpec((1,) + shape[1:], lambda b, info: ((1 - info[0]) * nb + b,) + (0,) * (len(shape) - 1))

    return pl.pallas_call(
        ordered(place_kernel, 4, after),
        grid_spec=pltpu.PrefetchScalarGridSpec(
            num_scalar_prefetch=1,
            grid=(nb,),
            in_specs=[HBM, HBM, pl.BlockSpec((1,) + got.shape[1:], lambda b, info: (b, 0, 0, 0))] + [ANY] * len(after),
            out_specs=[at_all(prob.shape), at_all(box.shape), TOKEN_SPEC],
            scratch_shapes=[pltpu.VMEM(box.shape[1:], F32)],
        ),
        out_shape=[jax.ShapeDtypeStruct(v.shape, BF) for v in (prob, box)] + [TOKEN],
        input_output_aliases={1: 0, 2: 1},
        compiler_params=pltpu.CompilerParams(vmem_limit_bytes=8 << 20),
        cost_estimate=cost(2),
        name="place",
    )(info, prob, box, got, *after)


def after(value, *others):
    return lax.optimization_barrier((value,) + others)[0]


def on_device(
    features,
    levels,
    tower_weight,
    tower_bias,
    class_weight,
    class_bias,
    box_weight,
    box_bias,
    class_cotangent,
    box_cotangent,
):
    section = lax.axis_index("section")
    tile = lax.axis_index("tile")
    nb, nt, rows, width, c = features.shape
    kc, kb = class_weight.shape[-1], box_weight.shape[-1]
    kp = -(-kc // LANES) * LANES
    kq = -(-kb // 8) * 8
    taps = 9 * c
    lev = levels
    info = jnp.stack([section, tile % 2, tile]).astype(jnp.int32)
    even = tile % 2 == 0

    sx = lax.dynamic_index_in_dim(features, jnp.where(even, rows - 1, 0), 2, False)
    sd = lax.dynamic_index_in_dim(features, jnp.where(even, 0, rows - 1), 2, False)
    rx0, rd0 = swap_edges(sx, sd)
    bias = gather(tower_bias, class_bias, box_bias, kp)
    bias_r = swap_section(bias)
    w_own = tower_weight.reshape(nt, taps, c)
    w_other = swap_section(w_own)

    h1, sp0, zp, token = forward(0, info, lev, features, w_own, w_other, bias, bias_r, (sx, sd))
    thin, small = class_weight.transpose(0, 2, 1), box_weight.transpose(0, 2, 1)
    cot, gb = class_cotangent.transpose(0, 1, 3, 2), box_cotangent.transpose(0, 3, 1, 2)
    w_out = pick_weights(thin, small, kp, (token,))
    w_out_r = swap_section(w_out)
    cot_r = swap_section(pick(info, cot, gb, nb, kp, (token,)))
    h1, sp0, sx, sd = edges(0, info, lev, zp, rx0, rd0, w_own, w_other, h1, sp0)
    rx1, rd1 = swap_edges(sx, sd)
    h2, sp1, zp, _ = forward(1, info, lev, h1, w_own, w_other, bias, bias_r)
    wk, wb, cb = pack(w_out, w_out_r, bias, bias_r, kc, kb, kq, nt, (zp,))
    h2, sp1, sx, sd = edges(1, info, lev, zp, rx1, rd1, w_own, w_other, h2, sp1)
    rx2, rd2 = swap_edges(sx, sd)
    prob, psend, dl, gt, cb_x, cb_d, lp, bo = head(info, lev, h2, wk, wb, cb, cot, gb, cot_r)
    prob, psend, dl, boxo, cx, cd = head_edges(
        info, lev, rx2, rd2, wk, wb, lp, bo, cot, cot_r, cb_x, cb_d, prob, psend, dl, kb
    )
    rx, rd = swap_edges(cx, cd)

    keep, send, token = head_weights(info, lev, h2, rx2, rd2, dl, gt, kc, kb)
    (send,) = relay("send_head", (send,), (token, rx, rd))
    head_sum = TileSum("sum_head", info, True, keep, swap_section(send))
    s = head_sum.start()
    dz1, sx, sd, token = head_inputs(info, lev, dl, gt, rx, rd, wk, wb, sp1, (), s)
    rx, rd = swap_edges(sx, sd)
    s = head_sum.start(token)
    keep1, send1, token = weights(1, info, lev, h1, rx1, rd1, dz1, s)
    *s, send1 = head_sum.start(token, rx, rd, gate=(send1,))
    dz0, token, sx, sd = inputs(1, info, lev, dz1, rx, rd, w_own, w_other, sp0, (), tuple(s))
    *s, psend = head_sum.start(token, gate=(psend,))
    prob_r = swap_section(psend)
    sum1 = TileSum("sum_one", info, False, keep1, swap_section(send1))
    s = tuple(s)
    s = s + sum1.start(*s)
    keep0, send0, token = weights(0, info, lev, features, rx0, rd0, dz0, s)
    sum0 = TileSum("sum_zero", info, False, keep0, swap_section(send0))
    s = sum0.start()
    s = s + sum1.start(*s)
    prob, boxo, token = place(info, prob, boxo, prob_r, tuple(s))
    *s, sx, sd = sum0.start(token, gate=(sx, sd))
    rx, rd = swap_edges(sx, sd)
    s = tuple(s)
    s = s + sum1.start(*s)
    s = s + sum0.start(*s)
    s = s + head_sum.start(*s)
    s = s + sum1.start(*s)
    feature_grad, token = inputs(0, info, lev, dz0, rx, rd, w_own, w_other, None, (), s)
    done = (token,)
    while sum0.plan:
        s = sum0.start(*done)
        done = ()
        for other in (head_sum, sum1):
            if other.plan:
                other.start(*s)
    head_done, l1, l0 = (jnp.concatenate(v.result(), axis=1) for v in (head_sum, sum1, sum0))

    mine_l = jnp.where(section == 0, l0, l1)
    other_l = swap_section(jnp.where(section == 0, l1, l0))
    towers = jnp.where(section == 0, jnp.stack([mine_l[:taps], other_l[:taps]]), jnp.stack([other_l[:taps], mine_l[:taps]]))
    biases = jnp.where(section == 0, jnp.stack([mine_l[taps], other_l[taps]]), jnp.stack([other_l[taps], mine_l[taps]]))
    end = 3 * kc
    box = head_done[end : end + 3 * kq].astype(F32)
    return (
        prob.transpose(0, 1, 3, 2),
        boxo.transpose(0, 2, 3, 1),
        feature_grad,
        towers.astype(F32).reshape(1, nt, 3, 3 * c, c),
        biases.astype(F32).reshape(1, nt, c),
        head_done[:end].astype(F32).reshape(3, kc, 3 * c).transpose(0, 2, 1),
        box[kb, :kc],
        box.reshape(3, kq, 3 * c)[:, :kb].transpose(0, 2, 1),
        box[kb, kp : kp + kb],
    )


def solution(mesh):
    in_specs = (
        P("section", None, "tile", None, None),
        P(),
        P("section", None, None, None, None),
        P("section", None, None),
        P(None, None, "section"),
        P("section"),
        P(None, None, "section"),
        P("section"),
        P(None, "tile", None, "section"),
        P(None, "tile", None, "section"),
    )
    out_specs = (
        P(None, "tile", None, "section"),
        P(None, "tile", None, "section"),
        P("section", None, "tile", None, None),
        P("section", None, None, None, None),
        P("section", None, None),
        P(None, None, "section"),
        P("section"),
        P(None, None, "section"),
        P("section"),
    )
    return jax.shard_map(on_device, mesh=mesh, in_specs=in_specs, out_specs=out_specs, check_vma=False)
```
